128 devices in a mesh: ctx: 64 (over x, z_lo, y, core), head: 2 (over z_hi).
Axes of the slice: x: 4, y: 4, z: 4 (z_hi: 2, z_lo: 2; z = z_hi * 2 + z_lo), core: 2. Of those that a mesh axis runs over, the one named last changes fastest.
Arguments:
- img_q: bfloat16 [2048, 1536], P('ctx', 'head'), may hold values from -12 to 12
- img_k: bfloat16 [2048, 1536], P('ctx', 'head'), may hold values from -12 to 12
- img_v: bfloat16 [2048, 1536], P('ctx', 'head'), may hold values from -6 to 6
- txt_ids: int32 [512], replicated, may hold values from 0 to 32767
- concept_ids: int32 [1024], replicated, may hold values from 0 to 32767
- step_index: int32 [1], replicated, may hold values from 0 to 27
- token_table: bfloat16 [32768, 3072], P(('ctx', 'head')), may hold values from -6 to 6
- modulation: float32 [28, 2, 3072], replicated, may hold values from -3 to 3
- txt_qkv: bfloat16 [3072, 3, 1536], P(None, None, 'head'), may hold values from -0.109375 to 0.109375
- qk_gain: float32 [2, 128], replicated, may hold values from 0.25 to 1.75
Outputs:
- img_out: bfloat16 [2048, 1536], P('ctx', 'head')
- saliency: float32 [1024, 2048], P(None, 'ctx')
The draws below stay inside these ranges and needn't reach their ends.
All inputs are finite; a program needn't handle non-finite values.
Results may differ from the reference program's by a relative error of at most 0.013.
Values may be sent and summed in bfloat16 or wider, within the bound.
No kernel may reach another device: no remote copies, remote signals or barrier semaphores. Data moves between devices by JAX's collectives and lax.ppermute only.
A program may use at most 128 MiB of HBM per device.

```python
import jax
import jax.numpy as jnp
from jax import lax

D = 3072
HD = 128
TEXT = 512
HEADS = 12
CONCEPTS = 1024
VOCAB = 32768
STEPS = 28
IMAGES = 2048


def draw_img_k(key, part):
    key = jax.random.fold_in(key, 3)
    first = jax.random.fold_in(key, 0)
    values = jax.random.normal(first, (IMAGES, HEADS * HD), jnp.float32)
    return jnp.clip(values, -12.0, 12.0).astype(jnp.bfloat16)


def set_ends(drawn, rng, smallest, largest):
    longest = drawn.shape.index(max(drawn.shape))
    spots = []
    for shift in (0, 1):
        where = [jax.random.randint(jax.random.fold_in(rng, axis), (), 0, length) for axis, length in enumerate(drawn.shape)]
        where[longest] = (where[longest] + shift) % drawn.shape[longest]
        spots.append(tuple(where))
    return drawn.at[spots[0]].set(smallest).at[spots[1]].set(largest)


def levels(key, dims, pieces, smallest, largest):
    loudness = 1.0
    for dim, parts in pieces:
        draws = jax.random.uniform(jax.random.fold_in(jax.random.fold_in(key, 6), dim), (parts,), jnp.float32, smallest / len(pieces), largest / len(pieces))
        loudness = loudness * jnp.repeat(jnp.exp(draws), dims[dim] // parts).reshape((-1,) + (1,) * (len(dims) - 1 - dim))
    return loudness


def bell_draw(key, shape, scale, reach, cuts=(), kind=jnp.bfloat16):
    level = levels(key, shape, cuts, -0.22, 0.18) if cuts else 1.0
    entries = jax.random.normal(key, shape, jnp.float32) * scale * level
    return jnp.minimum(jnp.maximum(entries, -reach), reach).astype(kind)


def setup_inputs(seed: int = 0) -> dict:
    key_of = jax.random.split(jax.random.key(seed), 11)
    return {
        "img_q": bell_draw(key_of[0], (IMAGES, HEADS * HD), 2.0, 12.0, ((0, 64), (1, 2))),
        "img_k": draw_img_k(jax.random.fold_in(key_of[10], 71), 0),
        "img_v": bell_draw(key_of[2], (IMAGES, HEADS * HD), 1.0, 6.0, ((0, 64), (1, 2))),
        "txt_ids": set_ends(jax.random.randint(key_of[3], (TEXT,), 0, VOCAB), jax.random.fold_in(key_of[3], 1), 0, VOCAB - 1).astype(jnp.int32),
        "concept_ids": set_ends(jax.random.randint(key_of[4], (CONCEPTS,), 0, VOCAB), jax.random.fold_in(key_of[4], 1), 0, VOCAB - 1).astype(jnp.int32),
        "step_index": jax.random.randint(key_of[5], (1,), 0, STEPS).astype(jnp.int32),
        "token_table": bell_draw(key_of[6], (VOCAB, D), 1.0, 6.0, ((0, 128),)),
        "modulation": bell_draw(key_of[7], (STEPS, 2, D), 0.5, 3.0, (), jnp.float32),
        "txt_qkv": bell_draw(key_of[8], (D, 3, HEADS * HD), D ** -0.5, 0.109375, ((2, 2),)),
        "qk_gain": jnp.clip(1.0 + 0.15 * jax.random.normal(key_of[9], (2, HD), jnp.float32), 0.25, 1.75),
    }


def modulate(rows, shift_scale):
    values = rows.astype(jnp.float32)
    mean = lax.optimization_barrier(jnp.mean(values, axis=1, keepdims=True))
    centered = values - mean
    var = lax.optimization_barrier(jnp.mean(centered * centered, axis=1, keepdims=True))
    normed = centered * lax.rsqrt(var + 1e-06)
    return (normed * (1.0 + shift_scale[1]) + shift_scale[0]).astype(jnp.bfloat16)

def head_norm(values, gain):
    shaped = values.reshape(values.shape[0], HEADS, HD)
    meansq = lax.optimization_barrier(jnp.mean(shaped * shaped, axis=2, keepdims=True))
    return (shaped * lax.rsqrt(meansq + 1e-06) * gain).reshape(values.shape[0], HEADS * HD)

def attend(queries, keys, values):
    rows = queries.shape[0]
    block = min(512, rows)
    key_f = keys.reshape(-1, HEADS, HD).astype(jnp.float32)
    val_f = values.reshape(-1, HEADS, HD).astype(jnp.float32)
    blocks = queries.reshape(rows // block, block, HEADS, HD)

    def one(query_block):
        scores = jnp.einsum('bhd,khd->hbk', query_block.astype(jnp.float32), key_f) * HD ** (-0.5)
        peak = lax.optimization_barrier(jnp.max(scores, axis=2, keepdims=True))
        weights = jnp.exp(scores - peak)
        total = lax.optimization_barrier(jnp.sum(weights, axis=2))
        rounded = lax.optimization_barrier(weights.astype(jnp.bfloat16))
        summed = jnp.einsum('hbk,khd->bhd', rounded.astype(jnp.float32), val_f)
        return (summed / jnp.transpose(total)[:, :, None]).reshape(block, HEADS * HD)
    return lax.map(one, blocks).reshape(rows, HEADS * HD).astype(jnp.bfloat16)

def reference(img_q, img_k, img_v, txt_ids, concept_ids, step_index, token_table, modulation, txt_qkv, qk_gain):
    shift_scale = lax.dynamic_index_in_dim(modulation, step_index[0], 0, keepdims=False)
    text_mod = modulate(jnp.take(token_table, txt_ids, axis=0), shift_scale)
    concept_mod = modulate(jnp.take(token_table, concept_ids, axis=0), shift_scale)
    txt_k = head_norm(jnp.dot(text_mod, txt_qkv[:, 1], preferred_element_type=jnp.float32), qk_gain[1]).astype(jnp.bfloat16)
    txt_v = jnp.dot(text_mod, txt_qkv[:, 2], preferred_element_type=jnp.float32).astype(jnp.bfloat16)
    con_q = head_norm(jnp.dot(concept_mod, txt_qkv[:, 0], preferred_element_type=jnp.float32), qk_gain[0]).astype(jnp.bfloat16)
    con_k = head_norm(jnp.dot(concept_mod, txt_qkv[:, 1], preferred_element_type=jnp.float32), qk_gain[1]).astype(jnp.bfloat16)
    con_v = jnp.dot(concept_mod, txt_qkv[:, 2], preferred_element_type=jnp.float32).astype(jnp.bfloat16)
    img_out = attend(img_q, jnp.concatenate([txt_k, img_k], axis=0), jnp.concatenate([txt_v, img_v], axis=0))
    con_out = attend(con_q, jnp.concatenate([con_k, img_k], axis=0), jnp.concatenate([con_v, img_v], axis=0))
    dots = jnp.dot(con_out, jnp.transpose(img_out), preferred_element_type=jnp.float32)
    con_f = con_out.astype(jnp.float32)
    img_f = img_out.astype(jnp.float32)
    width = HEADS * HD
    con_rms = jnp.sqrt(lax.optimization_barrier(jnp.sum(con_f * con_f, axis=1)) / width + 1e-06)
    img_rms = jnp.sqrt(lax.optimization_barrier(jnp.sum(img_f * img_f, axis=1)) / width + 1e-06)
    saliency = dots / (jnp.sqrt(jnp.float32(width)) * con_rms[:, None] * img_rms[None, :])
    return (img_out, saliency)
```

```python
import jax
import jax.numpy as jnp
from jax import lax
from jax.sharding import PartitionSpec as P


def modulate(rows, shift_scale):
    values = rows.astype(jnp.float32)
    mean = jnp.mean(values, axis=1, keepdims=True)
    centered = values - mean
    var = jnp.mean(centered * centered, axis=1, keepdims=True)
    normed = centered * lax.rsqrt(var + 1e-06)
    return (normed * (1.0 + shift_scale[1]) + shift_scale[0]).astype(jnp.bfloat16)


def head_norm(values, gain, head_dim):
    shaped = values.reshape(values.shape[0], -1, head_dim)
    meansq = jnp.mean(shaped * shaped, axis=2, keepdims=True)
    return (shaped * lax.rsqrt(meansq + 1e-06) * gain).reshape(values.shape[0], -1)


def block_stats(queries, keys, values):
    scores = jnp.einsum(
        "rgd,kgd->grk", queries, keys, preferred_element_type=jnp.float32
    ) * queries.shape[-1] ** (-0.5)
    peak = jnp.max(scores, axis=2)
    weights = jnp.exp(scores - peak[:, :, None])
    total = jnp.sum(weights, axis=2)
    summed = jnp.einsum(
        "grk,kgd->grd", weights.astype(jnp.bfloat16), values, preferred_element_type=jnp.float32
    )
    return (peak, total, summed)


def combine_stats(first, second):
    peak = jnp.maximum(first[0], second[0])
    left = jnp.exp(first[0] - peak)
    right = jnp.exp(second[0] - peak)
    total = first[1] * left + second[1] * right
    summed = first[2] * left[:, :, None] + second[2] * right[:, :, None]
    return (peak, total, summed)


def scaled_scores(dots, concept_sq, image_sq, width):
    concept_rms = jnp.sqrt(concept_sq / width + 1e-06)
    image_rms = jnp.sqrt(image_sq / width + 1e-06)
    return dots / (jnp.sqrt(jnp.float32(width)) * concept_rms[:, None] * image_rms[None, :])


def gather_ctx(block):
    n_ctx = lax.axis_size("ctx")
    spread = jnp.broadcast_to(block[None], (n_ctx,) + block.shape)
    return lax.all_to_all(spread, "ctx", 0, 0, tiled=True)


def on_device(
    img_q, img_k, img_v, txt_ids, concept_ids, step_index, token_table, modulation, txt_qkv, qk_gain
):
    n_ctx = lax.axis_size("ctx")
    n_head = lax.axis_size("head")
    head_dim = qk_gain.shape[1]
    group = img_q.shape[1] // head_dim
    text_dev = txt_ids.shape[0] // n_ctx
    concept_dev = concept_ids.shape[0] // n_ctx
    vocab_dev = token_table.shape[0]
    combined = jnp.concatenate(
        [txt_ids.reshape(n_ctx, text_dev), concept_ids.reshape(n_ctx, concept_dev)], axis=1
    ).reshape(-1)
    offset = lax.axis_index(("ctx", "head")) * vocab_dev
    wanted = combined - offset
    inside = (wanted >= 0) & (wanted < vocab_dev)
    picked = jnp.take(token_table, jnp.clip(wanted, 0, vocab_dev - 1), axis=0)
    n_all = n_ctx * n_head
    mine = jnp.where(inside[:, None], picked, jnp.zeros((), picked.dtype))
    parts = lax.all_to_all(
        mine.reshape(n_all, -1, mine.shape[1]), ("ctx", "head"), 0, 0, tiled=True
    )
    own_rows = jnp.sum(parts.astype(jnp.float32), axis=0)
    prompt_rows = lax.all_gather(own_rows.astype(jnp.bfloat16), "head", axis=0, tiled=True)
    shift_scale = lax.dynamic_index_in_dim(modulation, step_index[0], 0, keepdims=False)
    modded = modulate(prompt_rows, shift_scale)
    text_mod = modded[:text_dev]
    concept_mod = modded[text_dev:]
    text_kv = jnp.einsum(
        "rd,dgc->rgc", text_mod, txt_qkv[:, 1:], preferred_element_type=jnp.float32
    )
    concept_qkv = jnp.einsum(
        "rd,dgc->rgc", concept_mod, txt_qkv, preferred_element_type=jnp.float32
    )
    text_keys = head_norm(text_kv[:, 0], qk_gain[1], head_dim).astype(jnp.bfloat16)
    text_values = text_kv[:, 1].astype(jnp.bfloat16)
    concept_queries = head_norm(concept_qkv[:, 0], qk_gain[0], head_dim).astype(jnp.bfloat16)
    concept_keys = head_norm(concept_qkv[:, 1], qk_gain[1], head_dim).astype(jnp.bfloat16)
    concept_values = concept_qkv[:, 2].astype(jnp.bfloat16)
    local_kv = jnp.stack(
        [
            jnp.concatenate([text_keys, concept_keys], axis=0),
            jnp.concatenate([text_values, concept_values], axis=0),
        ]
    )
    prompt_kv = gather_ctx(local_kv)
    text_part = jnp.swapaxes(prompt_kv[:, :, :text_dev], 0, 1).reshape(2, -1, group, head_dim)
    concept_part = jnp.swapaxes(prompt_kv[:, :, text_dev:], 0, 1).reshape(2, -1, group, head_dim)
    image_queries = img_q.reshape(-1, group, head_dim)
    concept_q3 = concept_queries.reshape(-1, group, head_dim)
    first = block_stats(image_queries, text_part[0], text_part[1])
    second = block_stats(concept_q3, concept_part[0], concept_part[1])
    start_stats = (
        jnp.concatenate([first[0], second[0]], axis=1),
        jnp.concatenate([first[1], second[1]], axis=1),
        jnp.concatenate([first[2], second[2]], axis=1),
    )
    all_queries = jnp.concatenate([image_queries, concept_q3], axis=0)
    keys = lax.all_gather(img_k, "ctx", axis=0, tiled=True).reshape(-1, group, head_dim)
    values = lax.all_gather(img_v, "ctx", axis=0, tiled=True).reshape(-1, group, head_dim)
    peak, total, summed = combine_stats(start_stats, block_stats(all_queries, keys, values))
    attended = (
        jnp.transpose(summed / total[:, :, None], (1, 0, 2))
        .reshape(all_queries.shape[0], -1)
        .astype(jnp.bfloat16)
    )
    img_rows = img_q.shape[0]
    img_out = attended[:img_rows]
    concept_out = attended[img_rows:]
    concept_all = gather_ctx(concept_out).reshape(-1, concept_out.shape[1])
    dots = lax.dot_general(
        concept_all, img_out, (((1,), (1,)), ((), ())), preferred_element_type=jnp.float32
    )
    image_f = img_out.astype(jnp.float32)
    concept_f = concept_all.astype(jnp.float32)
    image_sq = jnp.sum(image_f * image_f, axis=1)
    concept_sq = jnp.sum(concept_f * concept_f, axis=1)
    width = group * head_dim * n_head
    sums = jnp.concatenate(
        [
            jnp.concatenate([dots, concept_sq[:, None]], axis=1),
            jnp.concatenate([image_sq, jnp.zeros((1,), jnp.float32)])[None],
        ]
    ).astype(jnp.bfloat16)
    other = lax.ppermute(sums, "head", [(0, 1), (1, 0)])
    sums = sums.astype(jnp.float32) + other.astype(jnp.float32)
    concepts = dots.shape[0]
    dots_total = sums[:concepts, : img_rows]
    concept_total = sums[:concepts, img_rows]
    image_total = sums[concepts, :img_rows]
    saliency = scaled_scores(dots_total, concept_total, image_total, width)
    return (img_out, saliency)


def solution(mesh):
    return jax.shard_map(
        on_device,
        mesh=mesh,
        in_specs=(
            P("ctx", "head"),
            P("ctx", "head"),
            P("ctx", "head"),
            P(),
            P(),
            P(),
            P(("ctx", "head"), None),
            P(),
            P(None, None, "head"),
            P(),
        ),
        out_specs=(P("ctx", "head"), P(None, "ctx")),
        check_vma=False,
    )
```

```python
import math

import jax
import jax.numpy as jnp
from jax import lax
from jax.experimental import pallas as pl
from jax.experimental.pallas import tpu as pltpu
from jax.sharding import PartitionSpec as P

BF = jnp.bfloat16
F32 = jnp.float32
HD = 128
SLOTS = 32
CON = 112
TXT = 64
ROWS = CON + TXT
MIB = 1 << 20


def modulate(rows, shift_scale):
    values = rows.astype(F32)
    mean = jnp.mean(values, axis=1, keepdims=True)
    centered = values - mean
    var = jnp.mean(centered * centered, axis=1, keepdims=True)
    normed = centered * lax.rsqrt(var + 1e-06)
    return (normed * (1.0 + shift_scale[1]) + shift_scale[0]).astype(BF)


def head_norm(values, gain, head_dim):
    shaped = values.reshape(values.shape[0], -1, head_dim)
    meansq = jnp.mean(shaped * shaped, axis=2, keepdims=True)
    return (shaped * lax.rsqrt(meansq + 1e-06) * gain).reshape(values.shape[0], -1)


def block_stats(queries, keys, values):
    scores = jnp.einsum("rgd,kgd->grk", queries, keys, preferred_element_type=F32)
    scores = scores * queries.shape[-1] ** (-0.5)
    peak = jnp.max(scores, axis=2)
    weights = jnp.exp(scores - peak[:, :, None])
    total = jnp.sum(weights, axis=2)
    summed = jnp.einsum("grk,kgd->grd", weights.astype(BF), values, preferred_element_type=F32)
    return (peak, total, summed)


def combine_stats(first, second):
    peak = jnp.maximum(first[0], second[0])
    left = jnp.exp(first[0] - peak)
    right = jnp.exp(second[0] - peak)
    total = first[1] * left + second[1] * right
    summed = first[2] * left[:, :, None] + second[2] * right[:, :, None]
    return (peak, total, summed)


def scaled_scores(dots, concept_sq, image_sq, width):
    concept_rms = jnp.sqrt(concept_sq / width + 1e-06)
    image_rms = jnp.sqrt(image_sq / width + 1e-06)
    return dots / (jnp.sqrt(F32(width)) * concept_rms[:, None] * image_rms[None, :])


def gather_ctx(block):
    n_ctx = lax.axis_size("ctx")
    spread = jnp.broadcast_to(block[None], (n_ctx,) + block.shape)
    return lax.all_to_all(spread, "ctx", 0, 0, tiled=True)


def general(
    img_q, img_k, img_v, txt_ids, concept_ids, step_index, token_table, modulation, txt_qkv, qk_gain
):
    n_ctx = lax.axis_size("ctx")
    n_head = lax.axis_size("head")
    head_dim = qk_gain.shape[1]
    group = img_q.shape[1] // head_dim
    text_dev = txt_ids.shape[0] // n_ctx
    concept_dev = concept_ids.shape[0] // n_ctx
    vocab_dev = token_table.shape[0]
    combined = jnp.concatenate(
        [txt_ids.reshape(n_ctx, text_dev), concept_ids.reshape(n_ctx, concept_dev)], axis=1
    ).reshape(-1)
    offset = lax.axis_index(("ctx", "head")) * vocab_dev
    wanted = combined - offset
    inside = (wanted >= 0) & (wanted < vocab_dev)
    picked = jnp.take(token_table, jnp.clip(wanted, 0, vocab_dev - 1), axis=0)
    n_all = n_ctx * n_head
    mine = jnp.where(inside[:, None], picked, jnp.zeros((), picked.dtype))
    parts = lax.all_to_all(
        mine.reshape(n_all, -1, mine.shape[1]), ("ctx", "head"), 0, 0, tiled=True
    )
    own_rows = jnp.sum(parts.astype(F32), axis=0)
    prompt_rows = lax.all_gather(own_rows.astype(BF), "head", axis=0, tiled=True)
    shift_scale = lax.dynamic_index_in_dim(modulation, step_index[0], 0, keepdims=False)
    modded = modulate(prompt_rows, shift_scale)
    text_mod = modded[:text_dev]
    concept_mod = modded[text_dev:]
    text_kv = jnp.einsum("rd,dgc->rgc", text_mod, txt_qkv[:, 1:], preferred_element_type=F32)
    concept_qkv = jnp.einsum("rd,dgc->rgc", concept_mod, txt_qkv, preferred_element_type=F32)
    text_keys = head_norm(text_kv[:, 0], qk_gain[1], head_dim).astype(BF)
    text_values = text_kv[:, 1].astype(BF)
    concept_queries = head_norm(concept_qkv[:, 0], qk_gain[0], head_dim).astype(BF)
    concept_keys = head_norm(concept_qkv[:, 1], qk_gain[1], head_dim).astype(BF)
    concept_values = concept_qkv[:, 2].astype(BF)
    local_kv = jnp.stack(
        [
            jnp.concatenate([text_keys, concept_keys], axis=0),
            jnp.concatenate([text_values, concept_values], axis=0),
        ]
    )
    prompt_kv = gather_ctx(local_kv)
    text_part = jnp.swapaxes(prompt_kv[:, :, :text_dev], 0, 1).reshape(2, -1, group, head_dim)
    concept_part = jnp.swapaxes(prompt_kv[:, :, text_dev:], 0, 1).reshape(2, -1, group, head_dim)
    image_queries = img_q.reshape(-1, group, head_dim)
    concept_q3 = concept_queries.reshape(-1, group, head_dim)
    first = block_stats(image_queries, text_part[0], text_part[1])
    second = block_stats(concept_q3, concept_part[0], concept_part[1])
    start_stats = (
        jnp.concatenate([first[0], second[0]], axis=1),
        jnp.concatenate([first[1], second[1]], axis=1),
        jnp.concatenate([first[2], second[2]], axis=1),
    )
    all_queries = jnp.concatenate([image_queries, concept_q3], axis=0)
    image_kv = gather_ctx(jnp.stack([img_k, img_v]))
    keys = image_kv[:, 0].reshape(-1, group, head_dim)
    values = image_kv[:, 1].reshape(-1, group, head_dim)
    peak, total, summed = combine_stats(start_stats, block_stats(all_queries, keys, values))
    attended = (
        jnp.transpose(summed / total[:, :, None], (1, 0, 2))
        .reshape(all_queries.shape[0], -1)
        .astype(BF)
    )
    img_rows = img_q.shape[0]
    img_out = attended[:img_rows]
    concept_out = attended[img_rows:]
    concept_all = gather_ctx(concept_out).reshape(-1, concept_out.shape[1])
    dots = lax.dot_general(
        concept_all, img_out, (((1,), (1,)), ((), ())), preferred_element_type=F32
    )
    image_f = img_out.astype(F32)
    concept_f = concept_all.astype(F32)
    image_sq = jnp.sum(image_f * image_f, axis=1)
    concept_sq = jnp.sum(concept_f * concept_f, axis=1)
    width = group * head_dim * n_head
    sums = jnp.concatenate(
        [
            jnp.concatenate([dots, concept_sq[:, None]], axis=1),
            jnp.concatenate([image_sq, jnp.zeros((1,), F32)])[None],
        ]
    ).astype(BF)
    other = lax.ppermute(sums, "head", [(0, 1), (1, 0)])
    sums = sums.astype(F32) + other.astype(F32)
    concepts = dots.shape[0]
    saliency = scaled_scores(
        sums[:concepts, :img_rows], sums[:concepts, img_rows], sums[concepts, :img_rows], width
    )
    return (img_out, saliency)


def place(x, zl, y, c, g):
    return ((((x * 2 + zl) * 4 + y) * 2 + c) * 2) + g


def pairs(move):
    found = []
    for x in range(4):
        for zl in range(2):
            for y in range(4):
                for c in range(2):
                    for g in range(2):
                        found.append((place(x, zl, y, c, g), place(*move(x, zl, y, c, g))))
    return found


def along_z(s):
    def move(x, zl, y, c, g):
        z = (2 * g + zl + s) % 4
        return x, z % 2, y, c, z // 2

    return pairs(move)


def along_u(s):
    def move(x, zl, y, c, g):
        if c == 0:
            return (x + s) % 4, zl, y, c, g
        return x, zl, (y + s) % 4, c, g

    return pairs(move)


def along_v(s):
    def move(x, zl, y, c, g):
        if c == 0:
            return x, zl, (y + s) % 4, c, g
        return (x + s) % 4, zl, y, c, g

    return pairs(move)


def swap(dzl, dc, dg):
    return pairs(lambda x, zl, y, c, g: (x, zl ^ dzl, y, c ^ dc, g ^ dg))


def send(array, pairing):
    return lax.ppermute(array, ("ctx", "head"), pairing)


def nt(a, b, **kw):
    return lax.dot_general(a, b, (((1,), (1,)), ((), ())), preferred_element_type=F32, **kw)


def nn(a, b):
    return lax.dot_general(a, b, (((1,), (0,)), ((), ())), preferred_element_type=F32)


def call(kernel, outs, scratch=(), limit=48, flops=0, nbytes=0, smem=1):
    def run(*args):
        vm = pl.BlockSpec(memory_space=pltpu.VMEM)
        sm = pl.BlockSpec(memory_space=pltpu.SMEM)
        return pl.pallas_call(
            kernel,
            out_shape=outs,
            in_specs=[sm] * smem + [vm] * (len(args) - smem),
            out_specs=jax.tree.map(lambda _: vm, outs),
            scratch_shapes=list(scratch),
            compiler_params=pltpu.CompilerParams(vmem_limit_bytes=limit * MIB),
            cost_estimate=pl.CostEstimate(flops=flops, bytes_accessed=nbytes, transcendentals=0),
        )(*args)

    return run


def sds(shape, dtype=BF):
    return jax.ShapeDtypeStruct(shape, dtype)


def column_of(owner):
    ctx = owner >> 1
    return ((ctx >> 4) << 2) | ((ctx >> 1) & 3)


def ranks(keys, classes, resets):
    n = keys.shape[1]
    blk = 256
    row = lax.broadcasted_iota(jnp.int32, (blk, blk), 0)
    col = lax.broadcasted_iota(jnp.int32, (blk, blk), 1)
    earlier = (row < col).astype(F32).astype(BF)
    label = lax.broadcasted_iota(jnp.int32, (classes, blk), 0)
    carry = jnp.zeros((classes, 1), F32)
    found, peaks = [], []
    for b in range(n // blk):
        if b in resets:
            peaks.append(jnp.max(carry, axis=0, keepdims=True))
            carry = jnp.zeros((classes, 1), F32)
        hot = (label == keys[:, b * blk : (b + 1) * blk]).astype(F32)
        before = nn(hot.astype(BF), earlier) + carry
        found.append(jnp.sum(hot * before, axis=0, keepdims=True))
        carry = carry + jnp.sum(hot, axis=1, keepdims=True)
    peaks.append(jnp.max(carry, axis=0, keepdims=True))
    return jnp.concatenate(found, axis=1).astype(jnp.int32), peaks


def plan_kernel(at, ids_ref, table_ref, rows_ref, plan_ref):
    ids = ids_ref[...]
    n = ids.shape[1]
    vocab_dev = table_ref.shape[0]
    owner = ids >> int(math.log2(vocab_dev))
    rank, (most,) = ranks(owner, 128, ())
    hot_slot = lax.broadcasted_iota(jnp.int32, (SLOTS, n), 0) == rank
    hot_slot = (hot_slot & (owner == at[0])).astype(F32).astype(BF)
    hot_row = lax.broadcasted_iota(jnp.int32, (vocab_dev, n), 0) == (ids & (vocab_dev - 1))
    pick = nt(hot_slot, hot_row.astype(F32).astype(BF)).astype(BF)
    rows_ref[...] = nn(pick, table_ref[...]).astype(BF)
    spot, (con_most, txt_most) = ranks(column_of(owner), 16, (n * 2 // 3 // 256,))
    plan_ref[0:1, :] = rank
    plan_ref[1:2, :] = spot
    plan_ref[2:3, :] = jnp.broadcast_to(most.astype(jnp.int32), (1, n))
    plan_ref[3:4, :] = jnp.broadcast_to(con_most.astype(jnp.int32), (1, n))
    plan_ref[4:5, :] = jnp.broadcast_to(txt_most.astype(jnp.int32), (1, n))
    plan_ref[5:8, :] = jnp.zeros((3, n), jnp.int32)


def pack_kernel(at, ids_ref, plan_ref, out_ref):
    ids = ids_ref[...]
    n = ids.shape[1]
    owner = ids >> 8
    here = column_of(owner) == at[1]
    rank = plan_ref[0:1, :]
    spot = plan_ref[1:2, :]
    concept = lax.broadcasted_iota(jnp.int32, (1, n), 1) < (n * 2 // 3)
    target = jnp.where(
        concept, jnp.where(spot < CON, spot, -1), jnp.where(spot < TXT, spot + CON, -1)
    )
    z = ((owner & 1) << 1) | ((owner >> 4) & 1)
    core = (owner >> 1) & 1
    piece = jnp.where(core == at[2], 0, 4) + ((at[3] - z) & 3)
    source = jnp.where(rank < SLOTS, piece * SLOTS + rank, -1)
    target = jnp.where(here, target, -1)
    source = jnp.where(here, source, -1)
    hot_t = (lax.broadcasted_iota(jnp.int32, (ROWS, n), 0) == target).astype(F32).astype(BF)
    hot_s = (lax.broadcasted_iota(jnp.int32, (8 * SLOTS, n), 0) == source).astype(F32).astype(BF)
    out_ref[...] = nt(hot_t, hot_s).astype(BF)


def project_kernel(at, pack_ref, *refs):
    rows, (mod_ref, gain_ref, w_ref), outs, (x_ref,) = refs[:8], refs[8:11], refs[11:15], refs[15:]
    shift = mod_ref[0:1, :]
    scale = 1.0 + mod_ref[1:2, :]
    for i, ref in enumerate(rows):
        values = ref[...].astype(F32)
        mean = jnp.mean(values, axis=1, keepdims=True)
        centered = values - mean
        var = jnp.mean(centered * centered, axis=1, keepdims=True)
        x_ref[i * SLOTS : (i + 1) * SLOTS, :] = (
            centered * lax.rsqrt(var + 1e-06) * scale + shift
        ).astype(BF)
    x = nn(pack_ref[...], x_ref[...]).astype(BF)

    def normed(u, gain):
        meansq = jnp.mean(u * u, axis=1, keepdims=True)
        return u * lax.rsqrt(meansq + 1e-06) * gain

    q = nn(x[:CON], w_ref[0])
    k = nn(x, w_ref[1])
    v = nn(x, w_ref[2])
    heads = []
    for h in range(3):
        lanes = slice(h * HD, (h + 1) * HD)
        heads.append(
            (
                normed(q[:, lanes], gain_ref[0:1, :]).astype(BF),
                normed(k[:, lanes], gain_ref[1:2, :]).astype(BF),
                v[:, lanes].astype(BF),
            )
        )
    for s, out in enumerate(outs):
        head = (at[4] + s) & 3
        out[CON:, 0:HD] = jnp.zeros((TXT, HD), BF)
        for h in range(3):

            @pl.when(jnp.minimum(head, 2) == h)
            def _(h=h, out=out):
                out[0:CON, 0:HD] = heads[h][0]
                out[:, HD : 2 * HD] = heads[h][1]
                out[:, 2 * HD : 3 * HD] = heads[h][2]


def join_kernel(a, b, c, d, out):
    for i, ref in enumerate((a, b, c, d)):
        out[i * CON : (i + 1) * CON, :] = ref[0:CON, :]
        out[4 * CON + i * TXT : 4 * CON + (i + 1) * TXT, :] = ref[CON:, :]


def image_halves_kernel(at, q, kv, kvz, mine, theirs):
    half = q.shape[1] // 2
    n, m = q.shape[0], kv.shape[0]
    for out, core in ((mine, at[2]), (theirs, 1 - at[2])):
        lanes = pl.ds(pl.multiple_of(core * half, half), half)
        out[0:n, :] = q[:, lanes]
        out[n : n + m, :] = kv[:, lanes]
        out[n + m : n + 2 * m, :] = kvz[:, lanes]


def image_heads_kernel(at, mine, other, *outs):
    n = mine.shape[0]
    for s, out in enumerate(outs):
        head = jnp.minimum((at[4] + s) & 3, 2)
        lanes = pl.ds(pl.multiple_of(head * HD, HD), HD)
        out[0:n, :] = mine[:, lanes]
        out[n:, :] = other[:, lanes]


def image_join_kernel(a, b, c, d, q_out, kv_out):
    n = 32
    for i, ref in enumerate((a, b, c, d)):
        for j in range(2):
            base = j * 5 * n
            q_out[(2 * i + j) * n : (2 * i + j + 1) * n, :] = ref[base : base + n, :]
            for m in range(2):
                row = (4 * i + 2 * j + m) * n
                src = base + (1 + 2 * m) * n
                kv_out[row : row + n, :] = ref[src : src + n, :]
                kv_out[16 * n + row : 16 * n + row + n, :] = ref[src + n : src + 2 * n, :]


def attend(q, keys, values):
    scores = nt(q, keys)
    peak = jnp.max(scores, axis=1, keepdims=True)
    weights = jnp.exp2((scores - peak) * (HD ** (-0.5) * math.log2(math.e)))
    total = jnp.sum(weights, axis=1, keepdims=True)
    return (nn(weights.astype(BF), values) / total).astype(BF)


def attention_kernel(pc, pt, c0, c1, c2, c3, i0, i1, i2, i3, q, o0, o1, o2, o3, qc, keys, vals, co):
    chunks = (c0, c1, c2, c3)
    con = sum(
        nn(pc[:, a * 4 * CON : (a + 1) * 4 * CON], ref[0 : 4 * CON, :])
        for a, ref in enumerate(chunks)
    ).astype(BF)
    txt = sum(
        nn(pt[:, a * 4 * TXT : (a + 1) * 4 * TXT], ref[4 * CON :, HD:])
        for a, ref in enumerate(chunks)
    ).astype(BF)
    n_con, n_txt, n_img = con.shape[0], txt.shape[0], 4 * i0.shape[0] // 2
    qc[...] = con[:, 0:HD]
    keys[0:n_txt, :] = txt[:, 0:HD]
    vals[0:n_txt, :] = txt[:, HD:]
    part = n_img // 4
    for i, ref in enumerate((i0, i1, i2, i3)):
        row = n_txt + i * part
        keys[row : row + part, :] = ref[0:part, :]
        vals[row : row + part, :] = ref[part:, :]
    keys[n_txt + n_img :, :] = con[:, HD : 2 * HD]
    vals[n_txt + n_img :, :] = con[:, 2 * HD :]
    for b in range(n_con // 256):
        rows = slice(b * 256, (b + 1) * 256)
        co[rows, :] = attend(qc[rows, :], keys[n_txt:, :], vals[n_txt:, :])
    img = attend(q[...], keys[0 : n_txt + n_img, :], vals[0 : n_txt + n_img, :])
    con_out = co[...]
    dots = nt(img, con_out).astype(BF)
    con_f = con_out.astype(F32)
    con_sq = nt(jnp.ones((16, HD), F32), con_f * con_f, precision=lax.Precision.HIGHEST).astype(BF)
    for s, out in enumerate((o0, o1, o2, o3)):
        rows = slice(s * 64, (s + 1) * 64)
        out[0:64, 0:n_con] = dots[rows]
        out[0:64, n_con:] = img[rows]
        out[64:80, 0:n_con] = con_sq
        out[64:80, n_con:] = jnp.zeros((16, HD), BF)


def head_sum_kernel(at, b0, b1, b2, b3, own, core, diag, out_own):
    n_con = b0.shape[1] - HD
    total = jnp.zeros((80, n_con), F32)
    outs = [jnp.zeros((64, HD), BF) for _ in range(3)]
    for s, ref in enumerate((b0, b1, b2, b3)):
        head = (at[4] + s) & 3
        total = total + jnp.where(head < 3, ref[:, 0:n_con].astype(F32), 0.0)
        for h in range(3):
            outs[h] = jnp.where(head == h, ref[0:64, n_con:], outs[h])
    image_sq = jnp.zeros((64, 1), F32)
    for h in range(3):
        out_f = outs[h].astype(F32)
        image_sq = image_sq + jnp.sum(out_f * out_f, axis=1, keepdims=True)
    image_sq = jnp.broadcast_to(image_sq, (64, HD)).astype(BF)
    total = total.astype(BF)
    for ref, row in ((own, 0), (core, 32), (diag, 32)):
        ref[0:32, 0:n_con] = total[row : row + 32]
        ref[32:48, 0:n_con] = total[64:80]
        ref[0:32, n_con : n_con + HD] = image_sq[row : row + 32]
        ref[32:48, n_con : n_con + HD] = jnp.zeros((16, HD), BF)
    for h in range(3):
        lanes = slice(n_con + (1 + h) * HD, n_con + (2 + h) * HD)
        core[0:32, lanes] = outs[h][32:64]
        core[32:48, lanes] = jnp.zeros((16, HD), BF)
        out_own[:, h * HD : (h + 1) * HD] = outs[h][0:32]


def finish_kernel(at, own, core, head, diag, out_own, img_ref, sal_ref):
    n_con = own.shape[1] - HD
    width = 12 * HD
    cols = n_con + HD
    near = own[...].astype(F32) + core[:, 0:cols].astype(F32)
    far = head[...].astype(F32) + diag[...].astype(F32)
    total = near + far
    con_rms = jnp.sqrt(total[32:33, 0:n_con] / width + 1e-06)
    img_rms = jnp.sqrt(total[0:32, n_con : n_con + 1] / width + 1e-06)
    sal = total[0:32, 0:n_con] / (math.sqrt(width) * con_rms * img_rms)
    sal_ref[...] = jnp.transpose(sal)
    half = 3 * HD
    mine = pl.ds(pl.multiple_of(at[2] * half, half), half)
    theirs = pl.ds(pl.multiple_of((1 - at[2]) * half, half), half)
    img_ref[:, mine] = out_own[...]
    img_ref[:, theirs] = core[0:32, cols:]


def packed(
    img_q, img_k, img_v, txt_ids, concept_ids, step_index, token_table, modulation, txt_qkv, qk_gain
):
    n_con, n_txt = concept_ids.shape[0], txt_ids.shape[0]
    ctx = lax.axis_index("ctx")
    g = lax.axis_index("head")
    c = ctx & 1
    y = (ctx >> 1) & 3
    zl = (ctx >> 3) & 1
    x = ctx >> 4
    u = jnp.where(c == 0, x, y)
    v = jnp.where(c == 0, y, x)
    at = jnp.stack([ctx * 2 + g, x * 4 + y, c, 2 * g + zl, u, v]).astype(jnp.int32)
    ids = jnp.concatenate([concept_ids, txt_ids])[None, :]
    n = n_con + n_txt
    width = token_table.shape[1]

    kv = jnp.concatenate([img_k, img_v], axis=0)
    kvz = send(kv, swap(1, 0, 0))

    own_rows, plan = call(
        plan_kernel, (sds((SLOTS, width)), sds((8, n), jnp.int32)), nbytes=2 * MIB, flops=10**9
    )(at, ids, token_table)
    column_rows = [own_rows] + [send(own_rows, along_z(s)) for s in (1, 2, 3)]
    other_rows = [send(r, swap(0, 1, 0)) for r in column_rows]

    pack = call(pack_kernel, sds((ROWS, 8 * SLOTS)), nbytes=MIB, flops=10**9)(at, ids, plan)

    owner = ids[0] >> 8
    item_x = owner >> 5
    item_y = (owner >> 2) & 3
    item_u = jnp.where(c == 0, item_x, item_y)
    item_v = jnp.where(c == 0, item_y, item_x)
    block = ((v - item_v) & 3) * 4 + ((u - item_u) & 3)
    spot = plan[1]
    con_slot = block[:n_con] * CON + spot[:n_con]
    txt_slot = block[n_con:] * TXT + spot[n_con:]
    pick_con = (con_slot[:, None] == jnp.arange(16 * CON)[None, :]).astype(BF)
    pick_txt = (txt_slot[:, None] == jnp.arange(16 * TXT)[None, :]).astype(BF)

    half = txt_qkv.shape[2] // 2
    weights = lax.dynamic_slice_in_dim(jnp.transpose(txt_qkv, (1, 0, 2)), c * half, half, axis=2)
    shift_scale = lax.dynamic_index_in_dim(modulation, step_index[0], 0, keepdims=False)

    n_img = img_q.shape[0]
    mine, theirs = call(
        image_halves_kernel, (sds((5 * n_img, half)), sds((5 * n_img, half))), nbytes=MIB // 2
    )(at, img_q, kv, kvz)
    other = send(theirs, swap(0, 1, 0))
    image_blocks = call(
        image_heads_kernel, tuple(sds((10 * n_img, HD)) for _ in range(4)), nbytes=MIB // 2
    )(at, mine, other)
    image_blocks = [image_blocks[0]] + [send(image_blocks[s], along_u(s)) for s in (1, 2, 3)]
    image_q, image_kv = call(
        image_join_kernel, (sds((8 * n_img, HD)), sds((32 * n_img, HD))), nbytes=MIB // 2, smem=0
    )(*image_blocks)
    image_kvs = [image_kv] + [send(image_kv, along_v(s)) for s in (1, 2, 3)]

    qkv = call(
        project_kernel,
        tuple(sds((ROWS, 3 * HD)) for _ in range(4)),
        scratch=(pltpu.VMEM((8 * SLOTS, width), BF),),
        nbytes=10 * MIB,
        flops=10**9,
    )(at, pack, *column_rows, *other_rows, shift_scale, qk_gain, weights)
    qkv = [qkv[0]] + [send(qkv[s], along_u(s)) for s in (1, 2, 3)]
    joined = call(join_kernel, sds((4 * ROWS, 3 * HD)), nbytes=MIB, smem=0)(*qkv)
    chunks = [joined] + [send(joined, along_v(s)) for s in (1, 2, 3)]

    n_keys = n_txt + 64 * n_img + n_con
    blocks = call(
        attention_kernel,
        tuple(sds((80, n_con + HD)) for _ in range(4)),
        scratch=(
            pltpu.VMEM((n_con, HD), BF),
            pltpu.VMEM((n_keys, HD), BF),
            pltpu.VMEM((n_keys, HD), BF),
            pltpu.VMEM((n_con, HD), BF),
        ),
        nbytes=10 * MIB,
        flops=4 * 10**9,
        smem=0,
    )(pick_con, pick_txt, *chunks, *image_kvs, image_q)
    blocks = [blocks[0]] + [send(blocks[s], along_u(-s)) for s in (1, 2, 3)]
    own, core, diag, out_own = call(
        head_sum_kernel,
        (sds((48, n_con + HD)), sds((48, n_con + 4 * HD)), sds((48, n_con + HD)), sds((32, half))),
        nbytes=MIB,
    )(at, *blocks)
    from_head = send(own, swap(0, 0, 1))
    from_diag = send(diag, swap(0, 1, 1))
    from_core = send(core, swap(0, 1, 0))
    img_out, saliency = call(
        finish_kernel, (sds((n_img, 2 * half)), sds((n_con, n_img), F32)), nbytes=MIB
    )(at, own, from_core, from_head, from_diag, out_own)
    fits = (plan[2, 0] <= SLOTS) & (plan[3, 0] <= CON) & (plan[4, 0] <= TXT)
    return img_out, saliency, fits


def on_device(*args):
    img_out, saliency, fits = packed(*args)
    return lax.cond(fits, lambda: (img_out, saliency), lambda: general(*args))


def solution(mesh):
    return jax.shard_map(
        on_device,
        mesh=mesh,
        in_specs=(
            P("ctx", "head"),
            P("ctx", "head"),
            P("ctx", "head"),
            P(),
            P(),
            P(),
            P(("ctx", "head"), None),
            P(),
            P(None, None, "head"),
            P(),
        ),
        out_specs=(P("ctx", "head"), P(None, "ctx")),
        check_vma=False,
    )
```

```python
import math

import jax
import jax.numpy as jnp
from jax import lax
from jax.experimental import pallas as pl
from jax.experimental.pallas import tpu as pltpu
from jax.sharding import PartitionSpec as P

BF = jnp.bfloat16
F32 = jnp.float32
HD = 128
SLOTS = 32
CON = 96
TXT = 64
ROWS = CON + TXT
MIB = 1 << 20


def modulate(rows, shift_scale):
    values = rows.astype(F32)
    mean = jnp.mean(values, axis=1, keepdims=True)
    centered = values - mean
    var = jnp.mean(centered * centered, axis=1, keepdims=True)
    normed = centered * lax.rsqrt(var + 1e-06)
    return (normed * (1.0 + shift_scale[1]) + shift_scale[0]).astype(BF)


def head_norm(values, gain, head_dim):
    shaped = values.reshape(values.shape[0], -1, head_dim)
    meansq = jnp.mean(shaped * shaped, axis=2, keepdims=True)
    return (shaped * lax.rsqrt(meansq + 1e-06) * gain).reshape(values.shape[0], -1)


def block_stats(queries, keys, values):
    scores = jnp.einsum("rgd,kgd->grk", queries, keys, preferred_element_type=F32)
    scores = scores * queries.shape[-1] ** (-0.5)
    peak = jnp.max(scores, axis=2)
    weights = jnp.exp(scores - peak[:, :, None])
    total = jnp.sum(weights, axis=2)
    summed = jnp.einsum("grk,kgd->grd", weights.astype(BF), values, preferred_element_type=F32)
    return (peak, total, summed)


def combine_stats(first, second):
    peak = jnp.maximum(first[0], second[0])
    left = jnp.exp(first[0] - peak)
    right = jnp.exp(second[0] - peak)
    total = first[1] * left + second[1] * right
    summed = first[2] * left[:, :, None] + second[2] * right[:, :, None]
    return (peak, total, summed)


def scaled_scores(dots, concept_sq, image_sq, width):
    concept_rms = jnp.sqrt(concept_sq / width + 1e-06)
    image_rms = jnp.sqrt(image_sq / width + 1e-06)
    return dots / (jnp.sqrt(F32(width)) * concept_rms[:, None] * image_rms[None, :])


def gather_ctx(block):
    n_ctx = lax.axis_size("ctx")
    spread = jnp.broadcast_to(block[None], (n_ctx,) + block.shape)
    return lax.all_to_all(spread, "ctx", 0, 0, tiled=True)


def general(
    img_q, img_k, img_v, txt_ids, concept_ids, step_index, token_table, modulation, txt_qkv, qk_gain
):
    n_ctx = lax.axis_size("ctx")
    n_head = lax.axis_size("head")
    head_dim = qk_gain.shape[1]
    group = img_q.shape[1] // head_dim
    text_dev = txt_ids.shape[0] // n_ctx
    concept_dev = concept_ids.shape[0] // n_ctx
    vocab_dev = token_table.shape[0]
    combined = jnp.concatenate(
        [txt_ids.reshape(n_ctx, text_dev), concept_ids.reshape(n_ctx, concept_dev)], axis=1
    ).reshape(-1)
    offset = lax.axis_index(("ctx", "head")) * vocab_dev
    wanted = combined - offset
    inside = (wanted >= 0) & (wanted < vocab_dev)
    picked = jnp.take(token_table, jnp.clip(wanted, 0, vocab_dev - 1), axis=0)
    n_all = n_ctx * n_head
    mine = jnp.where(inside[:, None], picked, jnp.zeros((), picked.dtype))
    parts = lax.all_to_all(
        mine.reshape(n_all, -1, mine.shape[1]), ("ctx", "head"), 0, 0, tiled=True
    )
    own_rows = jnp.sum(parts.astype(F32), axis=0)
    prompt_rows = lax.all_gather(own_rows.astype(BF), "head", axis=0, tiled=True)
    shift_scale = lax.dynamic_index_in_dim(modulation, step_index[0], 0, keepdims=False)
    modded = modulate(prompt_rows, shift_scale)
    text_mod = modded[:text_dev]
    concept_mod = modded[text_dev:]
    text_kv = jnp.einsum("rd,dgc->rgc", text_mod, txt_qkv[:, 1:], preferred_element_type=F32)
    concept_qkv = jnp.einsum("rd,dgc->rgc", concept_mod, txt_qkv, preferred_element_type=F32)
    text_keys = head_norm(text_kv[:, 0], qk_gain[1], head_dim).astype(BF)
    text_values = text_kv[:, 1].astype(BF)
    concept_queries = head_norm(concept_qkv[:, 0], qk_gain[0], head_dim).astype(BF)
    concept_keys = head_norm(concept_qkv[:, 1], qk_gain[1], head_dim).astype(BF)
    concept_values = concept_qkv[:, 2].astype(BF)
    local_kv = jnp.stack(
        [
            jnp.concatenate([text_keys, concept_keys], axis=0),
            jnp.concatenate([text_values, concept_values], axis=0),
        ]
    )
    prompt_kv = gather_ctx(local_kv)
    text_part = jnp.swapaxes(prompt_kv[:, :, :text_dev], 0, 1).reshape(2, -1, group, head_dim)
    concept_part = jnp.swapaxes(prompt_kv[:, :, text_dev:], 0, 1).reshape(2, -1, group, head_dim)
    image_queries = img_q.reshape(-1, group, head_dim)
    concept_q3 = concept_queries.reshape(-1, group, head_dim)
    first = block_stats(image_queries, text_part[0], text_part[1])
    second = block_stats(concept_q3, concept_part[0], concept_part[1])
    start_stats = (
        jnp.concatenate([first[0], second[0]], axis=1),
        jnp.concatenate([first[1], second[1]], axis=1),
        jnp.concatenate([first[2], second[2]], axis=1),
    )
    all_queries = jnp.concatenate([image_queries, concept_q3], axis=0)
    image_kv = gather_ctx(jnp.stack([img_k, img_v]))
    keys = image_kv[:, 0].reshape(-1, group, head_dim)
    values = image_kv[:, 1].reshape(-1, group, head_dim)
    peak, total, summed = combine_stats(start_stats, block_stats(all_queries, keys, values))
    attended = (
        jnp.transpose(summed / total[:, :, None], (1, 0, 2))
        .reshape(all_queries.shape[0], -1)
        .astype(BF)
    )
    img_rows = img_q.shape[0]
    img_out = attended[:img_rows]
    concept_out = attended[img_rows:]
    concept_all = gather_ctx(concept_out).reshape(-1, concept_out.shape[1])
    dots = lax.dot_general(
        concept_all, img_out, (((1,), (1,)), ((), ())), preferred_element_type=F32
    )
    image_f = img_out.astype(F32)
    concept_f = concept_all.astype(F32)
    image_sq = jnp.sum(image_f * image_f, axis=1)
    concept_sq = jnp.sum(concept_f * concept_f, axis=1)
    width = group * head_dim * n_head
    sums = jnp.concatenate(
        [
            jnp.concatenate([dots, concept_sq[:, None]], axis=1),
            jnp.concatenate([image_sq, jnp.zeros((1,), F32)])[None],
        ]
    ).astype(BF)
    other = lax.ppermute(sums, "head", [(0, 1), (1, 0)])
    sums = sums.astype(F32) + other.astype(F32)
    concepts = dots.shape[0]
    saliency = scaled_scores(
        sums[:concepts, :img_rows], sums[:concepts, img_rows], sums[concepts, :img_rows], width
    )
    return (img_out, saliency)


def place(x, zl, y, c, g):
    return ((((x * 2 + zl) * 4 + y) * 2 + c) * 2) + g


def pairs(move):
    found = []
    for x in range(4):
        for zl in range(2):
            for y in range(4):
                for c in range(2):
                    for g in range(2):
                        found.append((place(x, zl, y, c, g), place(*move(x, zl, y, c, g))))
    return found


def along_z(s):
    def move(x, zl, y, c, g):
        z = (2 * g + zl + s) % 4
        return x, z % 2, y, c, z // 2

    return pairs(move)


def along_u(s):
    def move(x, zl, y, c, g):
        if c == 0:
            return (x + s) % 4, zl, y, c, g
        return x, zl, (y + s) % 4, c, g

    return pairs(move)


def along_v(s):
    def move(x, zl, y, c, g):
        if c == 0:
            return x, zl, (y + s) % 4, c, g
        return (x + s) % 4, zl, y, c, g

    return pairs(move)


def swap(dzl, dc, dg):
    return pairs(lambda x, zl, y, c, g: (x, zl ^ dzl, y, c ^ dc, g ^ dg))


def send(array, pairing):
    return lax.ppermute(array, ("ctx", "head"), pairing)


def nt(a, b, **kw):
    return lax.dot_general(a, b, (((1,), (1,)), ((), ())), preferred_element_type=F32, **kw)


def nn(a, b):
    return lax.dot_general(a, b, (((1,), (0,)), ((), ())), preferred_element_type=F32)


def call(kernel, outs, scratch=(), limit=48, flops=0, nbytes=0, smem=1, in_hbm=0):
    def run(*args):
        vm = pl.BlockSpec(memory_space=pltpu.VMEM)
        sm = pl.BlockSpec(memory_space=pltpu.SMEM)
        return pl.pallas_call(
            kernel,
            out_shape=outs,
            in_specs=[sm] * smem
            + [vm] * (len(args) - smem - in_hbm)
            + [pl.BlockSpec(memory_space=pl.ANY)] * in_hbm,
            out_specs=jax.tree.map(lambda _: vm, outs),
            scratch_shapes=list(scratch),
            compiler_params=pltpu.CompilerParams(vmem_limit_bytes=limit * MIB),
            cost_estimate=pl.CostEstimate(flops=flops, bytes_accessed=nbytes, transcendentals=0),
        )(*args)

    return run


def sds(shape, dtype=BF):
    return jax.ShapeDtypeStruct(shape, dtype)


def column_of(owner):
    ctx = owner >> 1
    return ((ctx >> 4) << 2) | ((ctx >> 1) & 3)


def ranks(keys, classes, resets):
    n = keys.shape[1]
    blk = 256
    row = lax.broadcasted_iota(jnp.int32, (blk, blk), 0)
    col = lax.broadcasted_iota(jnp.int32, (blk, blk), 1)
    earlier = (row < col).astype(F32).astype(BF)
    label = lax.broadcasted_iota(jnp.int32, (classes, blk), 0)
    carry = jnp.zeros((classes, 1), F32)
    found, peaks = [], []
    for b in range(n // blk):
        if b in resets:
            peaks.append(jnp.max(carry, axis=0, keepdims=True))
            carry = jnp.zeros((classes, 1), F32)
        hot = (label == keys[:, b * blk : (b + 1) * blk]).astype(F32)
        before = nn(hot.astype(BF), earlier) + carry
        found.append(jnp.sum(hot * before, axis=0, keepdims=True))
        carry = carry + jnp.sum(hot, axis=1, keepdims=True)
    peaks.append(jnp.max(carry, axis=0, keepdims=True))
    return jnp.concatenate(found, axis=1).astype(jnp.int32), peaks


def plan_kernel(at, ids_ref, table_ref, rows_ref, plan_ref):
    ids = ids_ref[...]
    n = ids.shape[1]
    vocab_dev = table_ref.shape[0]
    owner = ids >> int(math.log2(vocab_dev))
    rank, (most,) = ranks(owner, 128, ())
    hot_slot = lax.broadcasted_iota(jnp.int32, (SLOTS, n), 0) == rank
    hot_slot = (hot_slot & (owner == at[0])).astype(F32).astype(BF)
    hot_row = lax.broadcasted_iota(jnp.int32, (vocab_dev, n), 0) == (ids & (vocab_dev - 1))
    pick = nt(hot_slot, hot_row.astype(F32).astype(BF)).astype(BF)
    rows_ref[...] = nn(pick, table_ref[...]).astype(BF)
    plan_ref[0:1, :] = rank
    plan_ref[1:2, :] = jnp.broadcast_to(most.astype(jnp.int32), (1, n))
    plan_ref[2:8, :] = jnp.zeros((6, n), jnp.int32)


def pack_kernel(at, ids_ref, plan_ref, out_ref, spot_ref):
    ids = ids_ref[...]
    n = ids.shape[1]
    owner = ids >> 8
    column = column_of(owner)
    spot, (con_most, txt_most) = ranks(column, 16, (n * 2 // 3 // 256,))
    spot_ref[0:1, :] = spot
    spot_ref[1:2, :] = jnp.broadcast_to(con_most.astype(jnp.int32), (1, n))
    spot_ref[2:3, :] = jnp.broadcast_to(txt_most.astype(jnp.int32), (1, n))
    spot_ref[3:8, :] = jnp.zeros((5, n), jnp.int32)
    here = column == at[1]
    rank = plan_ref[0:1, :]
    concept = lax.broadcasted_iota(jnp.int32, (1, n), 1) < (n * 2 // 3)
    target = jnp.where(
        concept, jnp.where(spot < CON, spot, -1), jnp.where(spot < TXT, spot + CON, -1)
    )
    z = ((owner & 1) << 1) | ((owner >> 4) & 1)
    core = (owner >> 1) & 1
    piece = jnp.where(core == at[2], 0, 4) + ((at[3] - z) & 3)
    source = jnp.where(rank < SLOTS, piece * SLOTS + rank, -1)
    target = jnp.where(here, target, -1)
    source = jnp.where(here, source, -1)
    hot_t = (lax.broadcasted_iota(jnp.int32, (ROWS, n), 0) == target).astype(F32).astype(BF)
    hot_s = (lax.broadcasted_iota(jnp.int32, (8 * SLOTS, n), 0) == source).astype(F32).astype(BF)
    out_ref[...] = nt(hot_t, hot_s).astype(BF)


def project_kernel(at, pack_ref, *refs):
    rows, (mod_ref, gain_ref, w_hbm), outs = refs[:8], refs[8:11], refs[11:15]
    raw_ref, x_ref, w_ref, sems = refs[15:]
    half = w_ref.shape[2]
    lanes = pl.ds(pl.multiple_of(at[2] * half, half), half)
    copies = [
        pltpu.make_async_copy(w_hbm.at[j, :, lanes], w_ref.at[j], sems.at[j]) for j in range(3)
    ]
    for copy in copies:
        copy.start()
    for i, ref in enumerate(rows):
        raw_ref[i * SLOTS : (i + 1) * SLOTS, :] = ref[...]
    shift = mod_ref[0:1, :]
    scale = 1.0 + mod_ref[1:2, :]
    for i in range(ROWS // 32):
        block = slice(i * 32, (i + 1) * 32)
        values = nn(pack_ref[block, :], raw_ref[...])
        mean = jnp.mean(values, axis=1, keepdims=True)
        centered = values - mean
        var = jnp.mean(centered * centered, axis=1, keepdims=True)
        x_ref[block, :] = (centered * lax.rsqrt(var + 1e-06) * scale + shift).astype(BF)

    def normed(u, gain):
        meansq = jnp.mean(u * u, axis=1, keepdims=True)
        return u * lax.rsqrt(meansq + 1e-06) * gain

    copies[0].wait()
    q = nn(x_ref[0:CON, :], w_ref[0])
    copies[1].wait()
    k = nn(x_ref[...], w_ref[1])
    copies[2].wait()
    v = nn(x_ref[...], w_ref[2])
    heads = []
    for h in range(3):
        cols = slice(h * HD, (h + 1) * HD)
        heads.append(
            (
                normed(q[:, cols], gain_ref[0:1, :]).astype(BF),
                normed(k[:, cols], gain_ref[1:2, :]).astype(BF),
                v[:, cols].astype(BF),
            )
        )
    for s, out in enumerate(outs):
        head = jnp.minimum((at[4] + s) & 3, 2)
        for h in range(3):

            @pl.when(head == h)
            def _(h=h, out=out):
                out[0:ROWS, 0:HD] = heads[h][1]
                out[0:ROWS, HD:] = heads[h][2]
                out[ROWS:, 0:HD] = heads[h][0][: CON // 2]
                out[ROWS:, HD:] = heads[h][0][CON // 2 :]


def join_kernel(a, b, c, d, q_out, kv_out):
    for i, ref in enumerate((a, b, c, d)):
        kv_out[i * CON : (i + 1) * CON, :] = ref[0:CON, :]
        kv_out[4 * CON + i * TXT : 4 * CON + (i + 1) * TXT, :] = ref[CON:ROWS, :]
        q_out[i * CON : i * CON + CON // 2, :] = ref[ROWS:, 0:HD]
        q_out[i * CON + CON // 2 : (i + 1) * CON, :] = ref[ROWS:, HD:]


def image_halves_kernel(at, q, k, v, own, to_core, to_zl, to_diag):
    half = q.shape[1] // 2
    n = q.shape[0]
    for whole, part, core in ((own, to_zl, at[2]), (to_core, to_diag, 1 - at[2])):
        lanes = pl.ds(pl.multiple_of(core * half, half), half)
        for i, ref in enumerate((q, k, v)):
            piece = ref[:, lanes]
            whole[i * n : (i + 1) * n, :] = piece
            if i:
                part[(i - 1) * n : i * n, :] = piece


def image_heads_kernel(at, own, core, zl, diag, *outs):
    n = zl.shape[0] // 2
    for s, out in enumerate(outs):
        head = jnp.minimum((at[4] + s) & 3, 2)
        lanes = pl.ds(pl.multiple_of(head * HD, HD), HD)
        out[0:n, :] = own[0:n, lanes]
        out[n : 2 * n, :] = core[0:n, lanes]
        for i in range(2):
            for j, (ref, skip) in enumerate(((own, n), (core, n), (zl, 0), (diag, 0))):
                row = (2 + 4 * i + j) * n
                out[row : row + n, :] = ref[skip + i * n : skip + (i + 1) * n, lanes]


def image_join_kernel(a, b, c, d, q_out, kv_out):
    n = a.shape[0] // 10
    for i, ref in enumerate((a, b, c, d)):
        q_out[2 * n * i : 2 * n * (i + 1), :] = ref[0 : 2 * n, :]
        kv_out[4 * n * i : 4 * n * (i + 1), :] = ref[2 * n : 6 * n, :]
        kv_out[4 * n * (4 + i) : 4 * n * (5 + i), :] = ref[6 * n :, :]


def attend(q, keys, values):
    scores = nt(q, keys)
    factor = HD ** (-0.5) * math.log2(math.e)
    peak = jnp.max(scores, axis=1, keepdims=True)
    weights = jnp.exp2((scores - peak) * factor)
    total = jnp.sum(weights, axis=1, keepdims=True)
    return peak * factor, total, nn(weights.astype(BF), values)


def merge(first, second):
    peak = jnp.maximum(first[0], second[0])
    left = jnp.exp2(first[0] - peak)
    right = jnp.exp2(second[0] - peak)
    return (first[2] * left + second[2] * right) / (first[1] * left + second[1] * right)


def image_self_kernel(i0, i1, i2, i3, q, keys, vals, peak, total, summed):
    part = i0.shape[0] // 2
    for i, ref in enumerate((i0, i1, i2, i3)):
        keys[i * part : (i + 1) * part, :] = ref[0:part, :]
        vals[i * part : (i + 1) * part, :] = ref[part:, :]
    peak[...], total[...], summed[...] = attend(q[...], keys[...], vals[...])


def concept_image_kernel(pick, q0, q1, q2, q3, keys, vals, q_out, peak, total, summed):
    n = q0.shape[0]
    q_out[...] = sum(
        nn(pick[:, a * n : (a + 1) * n], ref[...]) for a, ref in enumerate((q0, q1, q2, q3))
    ).astype(BF)
    for b in range(q_out.shape[0] // 256):
        rows = slice(b * 256, (b + 1) * 256)
        peak[rows, :], total[rows, :], summed[rows, :] = attend(
            q_out[rows, :], keys[...], vals[...]
        )


def prompt_kernel(pick_con, pick_txt, c0, c1, c2, c3, cq, cm, cl, co, iq, im, il, io, *refs):
    outs, (con_kv, con_out) = refs[:4], refs[4:]
    chunks = (c0, c1, c2, c3)
    n, m = 4 * CON, 4 * TXT
    con_kv[...] = sum(
        nn(pick_con[:, a * n : (a + 1) * n], ref[0:n, :]) for a, ref in enumerate(chunks)
    ).astype(BF)
    txt_kv = sum(
        nn(pick_txt[:, a * m : (a + 1) * m], ref[n:, :]) for a, ref in enumerate(chunks)
    ).astype(BF)
    n_con = con_kv.shape[0]
    text = attend(iq[...], txt_kv[:, 0:HD], txt_kv[:, HD:])
    img = merge(text, (im[...], il[...], io[...])).astype(BF)
    for b in range(n_con // 256):
        rows = slice(b * 256, (b + 1) * 256)
        part = attend(cq[rows, :], con_kv[:, 0:HD], con_kv[:, HD:])
        con_out[rows, :] = merge(part, (cm[rows, :], cl[rows, :], co[rows, :])).astype(BF)
    dots = nt(img, con_out[...]).astype(BF)
    con_f = con_out[...].astype(F32)
    con_sq = nt(jnp.ones((16, HD), F32), con_f * con_f, precision=lax.Precision.HIGHEST).astype(BF)
    for s, out in enumerate(outs):
        rows = slice(s * 64, (s + 1) * 64)
        out[0:64, 0:n_con] = dots[rows]
        out[0:64, n_con:] = img[rows]
        out[64:80, 0:n_con] = con_sq
        out[64:80, n_con:] = jnp.zeros((16, HD), BF)


def head_sum_kernel(at, b0, b1, b2, b3, own, core, diag, out_own):
    n_con = b0.shape[1] - HD
    total = jnp.zeros((80, n_con), F32)
    outs = [jnp.zeros((64, HD), BF) for _ in range(3)]
    for s, ref in enumerate((b0, b1, b2, b3)):
        head = (at[4] + s) & 3
        total = total + jnp.where(head < 3, ref[:, 0:n_con].astype(F32), 0.0)
        for h in range(3):
            outs[h] = jnp.where(head == h, ref[0:64, n_con:], outs[h])
    image_sq = jnp.zeros((64, 1), F32)
    for h in range(3):
        out_f = outs[h].astype(F32)
        image_sq = image_sq + jnp.sum(out_f * out_f, axis=1, keepdims=True)
    image_sq = jnp.broadcast_to(image_sq, (64, HD)).astype(BF)
    total = total.astype(BF)
    for ref, row in ((own, 0), (core, 32), (diag, 32)):
        ref[0:32, 0:n_con] = total[row : row + 32]
        ref[32:48, 0:n_con] = total[64:80]
        ref[0:32, n_con : n_con + HD] = image_sq[row : row + 32]
        ref[32:48, n_con : n_con + HD] = jnp.zeros((16, HD), BF)
    for h in range(3):
        lanes = slice(n_con + (1 + h) * HD, n_con + (2 + h) * HD)
        core[0:32, lanes] = outs[h][32:64]
        core[32:48, lanes] = jnp.zeros((16, HD), BF)
        out_own[:, h * HD : (h + 1) * HD] = outs[h][0:32]


def finish_kernel(at, own, core, head, diag, out_own, img_ref, sal_ref):
    n_con = own.shape[1] - HD
    width = 12 * HD
    cols = n_con + HD
    near = own[...].astype(F32) + core[:, 0:cols].astype(F32)
    far = head[...].astype(F32) + diag[...].astype(F32)
    total = near + far
    con_rms = jnp.sqrt(total[32:33, 0:n_con] / width + 1e-06)
    img_rms = jnp.sqrt(total[0:32, n_con : n_con + 1] / width + 1e-06)
    sal = total[0:32, 0:n_con] / (math.sqrt(width) * con_rms * img_rms)
    sal_ref[...] = jnp.transpose(sal)
    half = 3 * HD
    mine = pl.ds(pl.multiple_of(at[2] * half, half), half)
    theirs = pl.ds(pl.multiple_of((1 - at[2]) * half, half), half)
    img_ref[:, mine] = out_own[...]
    img_ref[:, theirs] = core[0:32, cols:]


def packed(
    img_q, img_k, img_v, txt_ids, concept_ids, step_index, token_table, modulation, txt_qkv, qk_gain
):
    n_con, n_txt = concept_ids.shape[0], txt_ids.shape[0]
    ctx = lax.axis_index("ctx")
    g = lax.axis_index("head")
    c = ctx & 1
    y = (ctx >> 1) & 3
    zl = (ctx >> 3) & 1
    x = ctx >> 4
    u = jnp.where(c == 0, x, y)
    v = jnp.where(c == 0, y, x)
    at = jnp.stack([ctx * 2 + g, x * 4 + y, c, 2 * g + zl, u, v]).astype(jnp.int32)
    ids = jnp.concatenate([concept_ids, txt_ids])[None, :]
    n = n_con + n_txt
    width = token_table.shape[1]

    half = txt_qkv.shape[2] // 2
    n_img = img_q.shape[0]
    own, to_core, to_zl, to_diag = call(
        image_halves_kernel,
        (sds((3 * n_img, half)), sds((3 * n_img, half)), sds((2 * n_img, half)), sds((2 * n_img, half))),
        nbytes=MIB // 2,
    )(at, img_q, img_k, img_v)
    own_rows, plan = call(
        plan_kernel, (sds((SLOTS, width)), sds((8, n), jnp.int32)), nbytes=2 * MIB, flops=10**9
    )(at, ids, token_table)
    column_rows = [own_rows] + [send(own_rows, along_z(s)) for s in (1, 2, 3)]
    other_rows = [send(r, swap(0, 1, 0)) for r in column_rows]
    from_core = send(to_core, swap(0, 1, 0))
    from_zl = send(to_zl, swap(1, 0, 0))
    from_diag = send(to_diag, swap(1, 1, 0))

    pack, spots = call(
        pack_kernel, (sds((ROWS, 8 * SLOTS)), sds((8, n), jnp.int32)), nbytes=MIB, flops=10**9
    )(at, ids, plan)
    owner = ids[0] >> 8
    item_x = owner >> 5
    item_y = (owner >> 2) & 3
    item_u = jnp.where(c == 0, item_x, item_y)
    item_v = jnp.where(c == 0, item_y, item_x)
    block = ((v - item_v) & 3) * 4 + ((u - item_u) & 3)
    spot = spots[0]
    con_slot = block[:n_con] * CON + spot[:n_con]
    txt_slot = block[n_con:] * TXT + spot[n_con:]
    pick_con = (con_slot[:, None] == jnp.arange(16 * CON)[None, :]).astype(BF)
    pick_txt = (txt_slot[:, None] == jnp.arange(16 * TXT)[None, :]).astype(BF)
    shift_scale = lax.dynamic_index_in_dim(modulation, step_index[0], 0, keepdims=False)

    image_blocks = call(
        image_heads_kernel, tuple(sds((10 * n_img, HD)) for _ in range(4)), nbytes=MIB // 2
    )(at, own, from_core, from_zl, from_diag)
    image_blocks = [image_blocks[0]] + [send(image_blocks[s], along_u(s)) for s in (1, 2, 3)]
    image_q, image_kv = call(
        image_join_kernel, (sds((8 * n_img, HD)), sds((32 * n_img, HD))), nbytes=MIB // 2, smem=0
    )(*image_blocks)
    image_kvs = [image_kv] + [send(image_kv, along_v(s)) for s in (1, 2, 3)]

    qkv = call(
        project_kernel,
        tuple(sds((ROWS + CON // 2, 2 * HD)) for _ in range(4)),
        scratch=(
            pltpu.VMEM((8 * SLOTS, width), BF),
            pltpu.VMEM((ROWS, width), BF),
            pltpu.VMEM((3, width, half), BF),
            pltpu.SemaphoreType.DMA((3,)),
        ),
        nbytes=10 * MIB,
        flops=10**9,
        in_hbm=1,
    )(at, pack, *column_rows, *other_rows, shift_scale, qk_gain, jnp.transpose(txt_qkv, (1, 0, 2)))
    qkv = [qkv[0]] + [send(qkv[s], along_u(s)) for s in (1, 2, 3)]
    q_join, kv_join = call(
        join_kernel, (sds((4 * CON, HD)), sds((4 * ROWS, 2 * HD))), nbytes=MIB, smem=0
    )(*qkv)
    q_chunks = [q_join] + [send(q_join, along_v(s)) for s in (1, 2, 3)]
    kv_chunks = [kv_join] + [send(kv_join, along_v(s)) for s in (1, 2, 3)]

    def stats(rows):
        return (sds((rows, 1), F32), sds((rows, 1), F32), sds((rows, HD), F32))

    all_img = 64 * n_img
    keys, vals, *image_stats = call(
        image_self_kernel,
        (sds((all_img, HD)), sds((all_img, HD))) + stats(8 * n_img),
        nbytes=4 * MIB,
        flops=10**9,
        smem=0,
    )(*image_kvs, image_q)
    con_q, *con_stats = call(
        concept_image_kernel,
        (sds((n_con, HD)),) + stats(n_con),
        nbytes=8 * MIB,
        flops=3 * 10**9,
        smem=0,
    )(pick_con, *q_chunks, keys, vals)
    blocks = call(
        prompt_kernel,
        tuple(sds((80, n_con + HD)) for _ in range(4)),
        scratch=(pltpu.VMEM((n_con, 2 * HD), BF), pltpu.VMEM((n_con, HD), BF)),
        nbytes=10 * MIB,
        flops=2 * 10**9,
        smem=0,
    )(pick_con, pick_txt, *kv_chunks, con_q, *con_stats, image_q, *image_stats)
    blocks = [blocks[0]] + [send(blocks[s], along_u(-s)) for s in (1, 2, 3)]
    own, core, diag, out_own = call(
        head_sum_kernel,
        (sds((48, n_con + HD)), sds((48, n_con + 4 * HD)), sds((48, n_con + HD)), sds((32, half))),
        nbytes=MIB,
    )(at, *blocks)
    last = (
        at,
        own,
        send(core, swap(0, 1, 0)),
        send(own, swap(0, 0, 1)),
        send(diag, swap(0, 1, 1)),
        out_own,
    )
    finish = call(
        finish_kernel, (sds((n_img, 2 * half)), sds((n_con, n_img), F32)), nbytes=MIB
    )
    fits = (plan[1, 0] <= SLOTS) & (spots[1, 0] <= CON) & (spots[2, 0] <= TXT)
    return fits, lambda: tuple(finish(*last))


def on_device(*args):
    fits, finish = packed(*args)
    return lax.cond(fits, finish, lambda: tuple(general(*args)))


def solution(mesh):
    return jax.shard_map(
        on_device,
        mesh=mesh,
        in_specs=(
            P("ctx", "head"),
            P("ctx", "head"),
            P("ctx", "head"),
            P(),
            P(),
            P(),
            P(("ctx", "head"), None),
            P(),
            P(None, None, "head"),
            P(),
        ),
        out_specs=(P("ctx", "head"), P(None, "ctx")),
        check_vma=False,
    )
```

```python
import math

import jax
import jax.numpy as jnp
from jax import lax
from jax.experimental import pallas as pl
from jax.experimental.pallas import tpu as pltpu
from jax.sharding import PartitionSpec as P

BF = jnp.bfloat16
F32 = jnp.float32
HD = 128
SLOTS = 32
CON = 96
TXT = 64
ROWS = CON + TXT
MIB = 1 << 20
FACTOR = HD ** (-0.5) * math.log2(math.e)


def modulate(rows, shift_scale):
    values = rows.astype(F32)
    mean = jnp.mean(values, axis=1, keepdims=True)
    centered = values - mean
    var = jnp.mean(centered * centered, axis=1, keepdims=True)
    normed = centered * lax.rsqrt(var + 1e-06)
    return (normed * (1.0 + shift_scale[1]) + shift_scale[0]).astype(BF)


def head_norm(values, gain, head_dim):
    shaped = values.reshape(values.shape[0], -1, head_dim)
    meansq = jnp.mean(shaped * shaped, axis=2, keepdims=True)
    return (shaped * lax.rsqrt(meansq + 1e-06) * gain).reshape(values.shape[0], -1)


def block_stats(queries, keys, values):
    scores = jnp.einsum("rgd,kgd->grk", queries, keys, preferred_element_type=F32)
    scores = scores * queries.shape[-1] ** (-0.5)
    peak = jnp.max(scores, axis=2)
    weights = jnp.exp(scores - peak[:, :, None])
    total = jnp.sum(weights, axis=2)
    summed = jnp.einsum("grk,kgd->grd", weights.astype(BF), values, preferred_element_type=F32)
    return (peak, total, summed)


def combine_stats(first, second):
    peak = jnp.maximum(first[0], second[0])
    left = jnp.exp(first[0] - peak)
    right = jnp.exp(second[0] - peak)
    total = first[1] * left + second[1] * right
    summed = first[2] * left[:, :, None] + second[2] * right[:, :, None]
    return (peak, total, summed)


def scaled_scores(dots, concept_sq, image_sq, width):
    concept_rms = jnp.sqrt(concept_sq / width + 1e-06)
    image_rms = jnp.sqrt(image_sq / width + 1e-06)
    return dots / (jnp.sqrt(F32(width)) * concept_rms[:, None] * image_rms[None, :])


def gather_ctx(block):
    n_ctx = lax.axis_size("ctx")
    spread = jnp.broadcast_to(block[None], (n_ctx,) + block.shape)
    return lax.all_to_all(spread, "ctx", 0, 0, tiled=True)


def general(
    img_q, img_k, img_v, txt_ids, concept_ids, step_index, token_table, modulation, txt_qkv, qk_gain
):
    n_ctx = lax.axis_size("ctx")
    n_head = lax.axis_size("head")
    head_dim = qk_gain.shape[1]
    group = img_q.shape[1] // head_dim
    text_dev = txt_ids.shape[0] // n_ctx
    concept_dev = concept_ids.shape[0] // n_ctx
    vocab_dev = token_table.shape[0]
    combined = jnp.concatenate(
        [txt_ids.reshape(n_ctx, text_dev), concept_ids.reshape(n_ctx, concept_dev)], axis=1
    ).reshape(-1)
    offset = lax.axis_index(("ctx", "head")) * vocab_dev
    wanted = combined - offset
    inside = (wanted >= 0) & (wanted < vocab_dev)
    picked = jnp.take(token_table, jnp.clip(wanted, 0, vocab_dev - 1), axis=0)
    n_all = n_ctx * n_head
    mine = jnp.where(inside[:, None], picked, jnp.zeros((), picked.dtype))
    parts = lax.all_to_all(
        mine.reshape(n_all, -1, mine.shape[1]), ("ctx", "head"), 0, 0, tiled=True
    )
    own_rows = jnp.sum(parts.astype(F32), axis=0)
    prompt_rows = lax.all_gather(own_rows.astype(BF), "head", axis=0, tiled=True)
    shift_scale = lax.dynamic_index_in_dim(modulation, step_index[0], 0, keepdims=False)
    modded = modulate(prompt_rows, shift_scale)
    text_mod = modded[:text_dev]
    concept_mod = modded[text_dev:]
    text_kv = jnp.einsum("rd,dgc->rgc", text_mod, txt_qkv[:, 1:], preferred_element_type=F32)
    concept_qkv = jnp.einsum("rd,dgc->rgc", concept_mod, txt_qkv, preferred_element_type=F32)
    text_keys = head_norm(text_kv[:, 0], qk_gain[1], head_dim).astype(BF)
    text_values = text_kv[:, 1].astype(BF)
    concept_queries = head_norm(concept_qkv[:, 0], qk_gain[0], head_dim).astype(BF)
    concept_keys = head_norm(concept_qkv[:, 1], qk_gain[1], head_dim).astype(BF)
    concept_values = concept_qkv[:, 2].astype(BF)
    local_kv = jnp.stack(
        [
            jnp.concatenate([text_keys, concept_keys], axis=0),
            jnp.concatenate([text_values, concept_values], axis=0),
        ]
    )
    prompt_kv = gather_ctx(local_kv)
    text_part = jnp.swapaxes(prompt_kv[:, :, :text_dev], 0, 1).reshape(2, -1, group, head_dim)
    concept_part = jnp.swapaxes(prompt_kv[:, :, text_dev:], 0, 1).reshape(2, -1, group, head_dim)
    image_queries = img_q.reshape(-1, group, head_dim)
    concept_q3 = concept_queries.reshape(-1, group, head_dim)
    first = block_stats(image_queries, text_part[0], text_part[1])
    second = block_stats(concept_q3, concept_part[0], concept_part[1])
    start_stats = (
        jnp.concatenate([first[0], second[0]], axis=1),
        jnp.concatenate([first[1], second[1]], axis=1),
        jnp.concatenate([first[2], second[2]], axis=1),
    )
    all_queries = jnp.concatenate([image_queries, concept_q3], axis=0)
    image_kv = gather_ctx(jnp.stack([img_k, img_v]))
    keys = image_kv[:, 0].reshape(-1, group, head_dim)
    values = image_kv[:, 1].reshape(-1, group, head_dim)
    peak, total, summed = combine_stats(start_stats, block_stats(all_queries, keys, values))
    attended = (
        jnp.transpose(summed / total[:, :, None], (1, 0, 2))
        .reshape(all_queries.shape[0], -1)
        .astype(BF)
    )
    img_rows = img_q.shape[0]
    img_out = attended[:img_rows]
    concept_out = attended[img_rows:]
    concept_all = gather_ctx(concept_out).reshape(-1, concept_out.shape[1])
    dots = lax.dot_general(
        concept_all, img_out, (((1,), (1,)), ((), ())), preferred_element_type=F32
    )
    image_f = img_out.astype(F32)
    concept_f = concept_all.astype(F32)
    image_sq = jnp.sum(image_f * image_f, axis=1)
    concept_sq = jnp.sum(concept_f * concept_f, axis=1)
    width = group * head_dim * n_head
    sums = jnp.concatenate(
        [
            jnp.concatenate([dots, concept_sq[:, None]], axis=1),
            jnp.concatenate([image_sq, jnp.zeros((1,), F32)])[None],
        ]
    ).astype(BF)
    other = lax.ppermute(sums, "head", [(0, 1), (1, 0)])
    sums = sums.astype(F32) + other.astype(F32)
    concepts = dots.shape[0]
    saliency = scaled_scores(
        sums[:concepts, :img_rows], sums[:concepts, img_rows], sums[concepts, :img_rows], width
    )
    return (img_out, saliency)


def place(x, zl, y, c, g):
    return ((((x * 2 + zl) * 4 + y) * 2 + c) * 2) + g


def pairs(move):
    found = []
    for x in range(4):
        for zl in range(2):
            for y in range(4):
                for c in range(2):
                    for g in range(2):
                        found.append((place(x, zl, y, c, g), place(*move(x, zl, y, c, g))))
    return found


def swap_z(s):
    def move(x, zl, y, c, g):
        z = (2 * g + zl) ^ s
        return x, z & 1, y, c, z >> 1

    return pairs(move)


def swap_u(s):
    return pairs(
        lambda x, zl, y, c, g: (x, zl, y ^ s, c, g) if c else (x ^ s, zl, y, c, g)
    )


def swap_v(s):
    return pairs(
        lambda x, zl, y, c, g: (x ^ s, zl, y, c, g) if c else (x, zl, y ^ s, c, g)
    )


def swap_core(dg):
    return pairs(lambda x, zl, y, c, g: (x, zl, y, c ^ 1, g ^ dg))


def send(array, pairing):
    return lax.ppermute(array, ("ctx", "head"), pairing)


def nt(a, b, **kw):
    return lax.dot_general(a, b, (((1,), (1,)), ((), ())), preferred_element_type=F32, **kw)


def nn(a, b):
    return lax.dot_general(a, b, (((1,), (0,)), ((), ())), preferred_element_type=F32)


def call(kernel, outs, scratch=(), limit=48, flops=0, nbytes=0, smem=1, in_hbm=0):
    def run(*args):
        vm = pl.BlockSpec(memory_space=pltpu.VMEM)
        sm = pl.BlockSpec(memory_space=pltpu.SMEM)
        return pl.pallas_call(
            kernel,
            out_shape=outs,
            in_specs=[sm] * smem
            + [vm] * (len(args) - smem - in_hbm)
            + [pl.BlockSpec(memory_space=pl.ANY)] * in_hbm,
            out_specs=jax.tree.map(lambda _: vm, outs),
            scratch_shapes=list(scratch),
            compiler_params=pltpu.CompilerParams(vmem_limit_bytes=limit * MIB),
            cost_estimate=pl.CostEstimate(flops=flops, bytes_accessed=nbytes, transcendentals=0),
        )(*args)

    return run


def sds(shape, dtype=BF):
    return jax.ShapeDtypeStruct(shape, dtype)


def column_of(owner):
    ctx = owner >> 1
    return ((ctx >> 4) << 2) | ((ctx >> 1) & 3)


def ranks(keys, classes, resets):
    n = keys.shape[1]
    blk = 256
    row = lax.broadcasted_iota(jnp.int32, (blk, blk), 0)
    col = lax.broadcasted_iota(jnp.int32, (blk, blk), 1)
    earlier = (row < col).astype(F32).astype(BF)
    label = lax.broadcasted_iota(jnp.int32, (classes, blk), 0)
    carry = jnp.zeros((classes, 1), F32)
    found, counts = [], []
    for b in range(n // blk):
        if b in resets:
            counts.append(carry)
            carry = jnp.zeros((classes, 1), F32)
        hot = (label == keys[:, b * blk : (b + 1) * blk]).astype(F32)
        before = nn(hot.astype(BF), earlier) + carry
        found.append(jnp.sum(hot * before, axis=0, keepdims=True))
        carry = carry + jnp.sum(hot, axis=1, keepdims=True)
    counts.append(carry)
    return jnp.concatenate(found, axis=1).astype(jnp.int32), counts


def most(counts, n):
    return jnp.broadcast_to(jnp.max(counts, axis=0, keepdims=True).astype(jnp.int32), (1, n))


def plan_kernel(at, con_ref, txt_ref, table_ref, k_ref, v_ref, rows_ref, both_ref, plan_ref):
    ids = jnp.concatenate([con_ref[...], txt_ref[...]], axis=1)
    n = ids.shape[1]
    vocab_dev = table_ref.shape[0]
    owner = ids >> int(math.log2(vocab_dev))
    rank, (counts,) = ranks(owner, 128, ())
    hot_slot = lax.broadcasted_iota(jnp.int32, (SLOTS, n), 0) == rank
    hot_slot = (hot_slot & (owner == at[0])).astype(F32).astype(BF)
    hot_row = lax.broadcasted_iota(jnp.int32, (vocab_dev, n), 0) == (ids & (vocab_dev - 1))
    pick = nt(hot_slot, hot_row.astype(F32).astype(BF)).astype(BF)
    rows = nn(pick, table_ref[...]).astype(BF)
    rows_ref[...] = rows
    both_ref[0:SLOTS, :] = rows
    wide = k_ref.shape[1]
    for j, (ref, row) in enumerate(((k_ref, 0), (k_ref, 16), (v_ref, 0), (v_ref, 16))):
        both_ref[SLOTS:, j * wide : (j + 1) * wide] = ref[row : row + 16, :]
    plan_ref[0:1, :] = rank
    plan_ref[1:2, :] = most(counts, n)
    plan_ref[2:8, :] = jnp.zeros((6, n), jnp.int32)


def empty_bias(at, counts, slots, blocks_lanes):
    lane = lax.broadcasted_iota(jnp.int32, (1, blocks_lanes), 1)
    block = jnp.zeros((1, blocks_lanes), jnp.int32)
    for j in range(1, 16):
        block = block + (lane >= j * slots).astype(jnp.int32)
    item_u = (block & 3) ^ at[4]
    item_v = (block >> 2) ^ at[5]
    column = jnp.where(at[2] == 0, item_u * 4 + item_v, item_v * 4 + item_u)
    hot = lax.broadcasted_iota(jnp.int32, (16, blocks_lanes), 0) == column
    held = jnp.sum(jnp.where(hot, counts, 0.0), axis=0, keepdims=True)
    return jnp.where((lane - block * slots).astype(F32) < held, 0.0, -1e30)


def pack_kernel(at, con_ref, txt_ref, plan_ref, out_ref, spot_ref, con_bias, txt_bias):
    ids = jnp.concatenate([con_ref[...], txt_ref[...]], axis=1)
    n = ids.shape[1]
    n_con = con_ref.shape[1]
    owner = ids >> 8
    column = column_of(owner)
    spot, (con_counts, txt_counts) = ranks(column, 16, (n_con // 256,))
    con_bias[...] = empty_bias(at, con_counts, CON, 16 * CON)
    txt_bias[...] = empty_bias(at, txt_counts, TXT, 16 * TXT)
    spot_ref[0:1, :] = spot
    spot_ref[1:2, :] = most(con_counts, n)
    spot_ref[2:3, :] = most(txt_counts, n)
    spot_ref[3:8, :] = jnp.zeros((5, n), jnp.int32)
    here = column == at[1]
    rank = plan_ref[0:1, :]
    concept = lax.broadcasted_iota(jnp.int32, (1, n), 1) < n_con
    target = jnp.where(
        concept, jnp.where(spot < CON, spot, -1), jnp.where(spot < TXT, spot + CON, -1)
    )
    z = ((owner & 1) << 1) | ((owner >> 4) & 1)
    core = (owner >> 1) & 1
    piece = jnp.where(core == at[2], 0, 4) + (at[3] ^ z)
    source = jnp.where(rank < SLOTS, piece * SLOTS + rank, -1)
    target = jnp.where(here, target, -1)
    source = jnp.where(here, source, -1)
    hot_t = (lax.broadcasted_iota(jnp.int32, (ROWS, n), 0) == target).astype(F32).astype(BF)
    hot_s = (lax.broadcasted_iota(jnp.int32, (8 * SLOTS, n), 0) == source).astype(F32).astype(BF)
    out_ref[...] = nt(hot_t, hot_s).astype(BF)


def project_kernel(at, pack_ref, *refs):
    rows, (mod_ref, gain_ref, w_hbm), outs = refs[:8], refs[8:11], refs[11:15]
    raw_ref, x_ref, w_ref, sems = refs[15:]
    half = w_ref.shape[2]
    lanes = pl.ds(pl.multiple_of(at[2] * half, half), half)
    copies = [
        pltpu.make_async_copy(w_hbm.at[j, :, lanes], w_ref.at[j], sems.at[j]) for j in range(3)
    ]
    for copy in copies:
        copy.start()
    for i, ref in enumerate(rows):
        raw_ref[i * SLOTS : (i + 1) * SLOTS, :] = ref[0:SLOTS, :]
    shift = mod_ref[0:1, :]
    scale = 1.0 + mod_ref[1:2, :]
    for i in range(ROWS // 32):
        block = slice(i * 32, (i + 1) * 32)
        values = nn(pack_ref[block, :], raw_ref[...])
        mean = jnp.mean(values, axis=1, keepdims=True)
        centered = values - mean
        var = jnp.mean(centered * centered, axis=1, keepdims=True)
        x_ref[block, :] = (centered * lax.rsqrt(var + 1e-06) * scale + shift).astype(BF)

    def normed(u, gain):
        meansq = jnp.mean(u * u, axis=1, keepdims=True)
        return u * lax.rsqrt(meansq + 1e-06) * gain

    copies[0].wait()
    q = nn(x_ref[0:CON, :], w_ref[0])
    copies[1].wait()
    k = nn(x_ref[...], w_ref[1])
    copies[2].wait()
    v = nn(x_ref[...], w_ref[2])
    heads = []
    for h in range(3):
        cols = slice(h * HD, (h + 1) * HD)
        heads.append(
            (
                (normed(q[:, cols], gain_ref[0:1, :]) * FACTOR).astype(BF),
                normed(k[:, cols], gain_ref[1:2, :]).astype(BF),
                v[:, cols].astype(BF),
            )
        )
    for s, out in enumerate(outs):
        head = jnp.minimum(at[4] ^ s, 2)
        for h in range(3):

            @pl.when(head == h)
            def _(h=h, out=out):
                out[0:ROWS, 0:HD] = heads[h][1]
                out[0:ROWS, HD:] = heads[h][2]
                out[ROWS:, 0:HD] = heads[h][0][: CON // 2]
                out[ROWS:, HD:] = heads[h][0][CON // 2 :]


def join_kernel(a, b, c, d, q_out, kv_out):
    for i, ref in enumerate((a, b, c, d)):
        kv_out[i * CON : (i + 1) * CON, :] = ref[0:CON, :]
        kv_out[4 * CON + i * TXT : 4 * CON + (i + 1) * TXT, :] = ref[CON:ROWS, :]
        q_out[i * CON : i * CON + CON // 2, :] = ref[ROWS:, 0:HD]
        q_out[i * CON + CON // 2 : (i + 1) * CON, :] = ref[ROWS:, HD:]


def image_heads_kernel(at, q, q_core, own, core, zl, diag, *outs):
    n, wide = q.shape
    for s, out in enumerate(outs):
        head = at[2] * 3 + jnp.minimum(at[4] ^ s, 2)
        lanes = pl.ds(pl.multiple_of(head * HD, HD), HD)
        out[0:n, :] = q[:, lanes]
        out[n : 2 * n, :] = q_core[:, lanes]
        for i in range(2):
            for j, ref in enumerate((own, core, zl, diag)):
                row = (2 + 4 * i + j) * n
                for m in range(2):
                    lanes = pl.ds(pl.multiple_of((2 * i + m) * wide + head * HD, HD), HD)
                    out[row + 16 * m : row + 16 * (m + 1), :] = ref[SLOTS:, lanes]


def image_join_kernel(a, b, c, d, q_out, kv_out):
    n = a.shape[0] // 10
    for i, ref in enumerate((a, b, c, d)):
        q_out[2 * n * i : 2 * n * (i + 1), :] = ref[0 : 2 * n, :]
        kv_out[4 * n * i : 4 * n * (i + 1), :] = ref[2 * n : 6 * n, :]
        kv_out[4 * n * (4 + i) : 4 * n * (5 + i), :] = ref[6 * n :, :]


def weigh(q, parts, factor):
    scores = []
    for keys, _, bias in parts:
        part = nt(q, keys)
        scores.append(part if bias is None else part + bias)
    peak = scores[0].max(axis=1, keepdims=True)
    for part in scores[1:]:
        peak = jnp.maximum(peak, part.max(axis=1, keepdims=True))
    total = None
    for part, (_, values, _) in zip(scores, parts):
        power = part - peak
        weights = jnp.exp2(power if factor is None else power * factor).astype(BF)
        summed = nn(weights, values)
        total = summed if total is None else total + summed
    return (peak if factor is None else peak * factor), total


def merge(first, second):
    peak = jnp.maximum(first[0], second[0])
    summed = first[1] * jnp.exp2(first[0] - peak) + second[1] * jnp.exp2(second[0] - peak)
    return (summed[:, 0:HD] / summed[:, HD:]).astype(BF)


def with_ones(values):
    return jnp.concatenate([values, jnp.ones_like(values)], axis=1)


def image_self_kernel(i0, i1, i2, i3, q, kv, bias, keys, vals, peak, summed):
    part = i0.shape[0] // 2
    for i, ref in enumerate((i0, i1, i2, i3)):
        keys[i * part : (i + 1) * part, :] = ref[0:part, :]
        vals[i * part : (i + 1) * part, :] = with_ones(ref[part:, :])
    text = kv[4 * CON :, :]
    parts = (
        (keys[...], vals[...], None),
        (text[:, 0:HD], with_ones(text[:, HD:]), bias[:, 0 : 4 * TXT]),
    )
    peak[...], summed[...] = weigh(q[...], parts, FACTOR)


def concept_image_kernel(pick, q0, q1, q2, q3, keys, vals, kv, bias, q_out, peak, summed):
    n = 4 * CON
    q_out[...] = sum(
        nn(pick[:, a * n : (a + 1) * n], ref[...]) for a, ref in enumerate((q0, q1, q2, q3))
    ).astype(BF)
    own = (kv[0:n, 0:HD], with_ones(kv[0:n, HD:]), bias[:, 0:n])
    for b in range(q_out.shape[0] // 256):
        rows = slice(b * 256, (b + 1) * 256)
        parts = ((keys[...], vals[...], None), own)
        peak[rows, :], summed[rows, :] = weigh(q_out[rows, :], parts, None)


def prompt_kernel(con_bias, txt_bias, c1, c2, c3, con_q, cm, cs, img_q, im, ims, *refs):
    outs, (con_out,) = refs[:4], refs[4:]
    n, m = 4 * CON, 4 * TXT
    con_parts, txt_parts = [], []
    for a, ref in enumerate((c1, c2, c3)):
        con, txt = ref[0:n, :], ref[n:, :]
        con_parts.append(
            (con[:, 0:HD], with_ones(con[:, HD:]), con_bias[:, (a + 1) * n : (a + 2) * n])
        )
        txt_parts.append(
            (txt[:, 0:HD], with_ones(txt[:, HD:]), txt_bias[:, (a + 1) * m : (a + 2) * m])
        )
    img = merge(weigh(img_q[...], txt_parts, FACTOR), (im[...], ims[...]))
    n_con = con_q.shape[0]
    for b in range(n_con // 256):
        rows = slice(b * 256, (b + 1) * 256)
        part = weigh(con_q[rows, :], con_parts, None)
        con_out[rows, :] = merge(part, (cm[rows, :], cs[rows, :]))
    dots = nt(img, con_out[...]).astype(BF)
    con_f = con_out[...].astype(F32)
    con_sq = nt(jnp.ones((16, HD), F32), con_f * con_f, precision=lax.Precision.HIGHEST).astype(BF)
    for s, out in enumerate(outs):
        rows = slice(s * 64, (s + 1) * 64)
        out[0:64, 0:n_con] = dots[rows]
        out[0:64, n_con:] = img[rows]
        out[64:80, 0:n_con] = con_sq
        out[64:80, n_con:] = jnp.zeros((16, HD), BF)


def head_sum_kernel(at, b0, b1, b2, b3, own, core, diag, out_own):
    n_con = b0.shape[1] - HD
    total = jnp.zeros((80, n_con), F32)
    outs = [jnp.zeros((64, HD), BF) for _ in range(3)]
    for s, ref in enumerate((b0, b1, b2, b3)):
        head = at[4] ^ s
        total = total + jnp.where(head < 3, ref[:, 0:n_con].astype(F32), 0.0)
        for h in range(3):
            outs[h] = jnp.where(head == h, ref[0:64, n_con:], outs[h])
    image_sq = jnp.zeros((64, 1), F32)
    for h in range(3):
        out_f = outs[h].astype(F32)
        image_sq = image_sq + jnp.sum(out_f * out_f, axis=1, keepdims=True)
    image_sq = jnp.broadcast_to(image_sq, (64, HD)).astype(BF)
    total = total.astype(BF)
    for ref, row in ((own, 0), (core, 32), (diag, 32)):
        ref[0:32, 0:n_con] = total[row : row + 32]
        ref[32:48, 0:n_con] = total[64:80]
        ref[0:32, n_con : n_con + HD] = image_sq[row : row + 32]
        ref[32:48, n_con : n_con + HD] = jnp.zeros((16, HD), BF)
    for h in range(3):
        lanes = slice(n_con + (1 + h) * HD, n_con + (2 + h) * HD)
        core[0:32, lanes] = outs[h][32:64]
        core[32:48, lanes] = jnp.zeros((16, HD), BF)
        out_own[:, h * HD : (h + 1) * HD] = outs[h][0:32]


def finish_kernel(at, own, core, head, diag, out_own, img_ref, sal_ref):
    n_con = own.shape[1] - HD
    width = 12 * HD
    cols = n_con + HD
    near = own[...].astype(F32) + core[:, 0:cols].astype(F32)
    far = head[...].astype(F32) + diag[...].astype(F32)
    total = near + far
    con_rms = jnp.sqrt(total[32:33, 0:n_con] / width + 1e-06)
    img_rms = jnp.sqrt(total[0:32, n_con : n_con + 1] / width + 1e-06)
    sal = total[0:32, 0:n_con] / (math.sqrt(width) * con_rms * img_rms)
    sal_ref[...] = jnp.transpose(sal)
    half = 3 * HD
    mine = pl.ds(pl.multiple_of(at[2] * half, half), half)
    theirs = pl.ds(pl.multiple_of((1 - at[2]) * half, half), half)
    img_ref[:, mine] = out_own[...]
    img_ref[:, theirs] = core[0:32, cols:]


def packed(
    img_q, img_k, img_v, txt_ids, concept_ids, step_index, token_table, modulation, txt_qkv, qk_gain
):
    n_con, n_txt = concept_ids.shape[0], txt_ids.shape[0]
    ctx = lax.axis_index("ctx")
    g = lax.axis_index("head")
    c = ctx & 1
    y = (ctx >> 1) & 3
    zl = (ctx >> 3) & 1
    x = ctx >> 4
    u = jnp.where(c == 0, x, y)
    v = jnp.where(c == 0, y, x)
    at = jnp.stack([ctx * 2 + g, x * 4 + y, c, 2 * g + zl, u, v]).astype(jnp.int32)
    con_ids, text_ids = concept_ids[None, :], txt_ids[None, :]
    n = n_con + n_txt
    width = token_table.shape[1]
    half = txt_qkv.shape[2] // 2
    n_img = img_q.shape[0]

    own_rows, own_both, plan = call(
        plan_kernel,
        (sds((SLOTS, width)), sds((SLOTS + 16, width)), sds((8, n), jnp.int32)),
        nbytes=2 * MIB,
        flops=10**9,
    )(at, con_ids, text_ids, token_table, img_k, img_v)
    column_rows = [own_both, send(own_both, swap_z(1))]
    column_rows += [send(own_rows, swap_z(s)) for s in (2, 3)]
    other_rows = [send(r, swap_core(0)) for r in column_rows]
    q_core = send(img_q, swap_core(0))

    pack, spots, con_bias, txt_bias = call(
        pack_kernel,
        (
            sds((ROWS, 8 * SLOTS)),
            sds((8, n), jnp.int32),
            sds((1, 16 * CON), F32),
            sds((1, 16 * TXT), F32),
        ),
        nbytes=MIB,
        flops=10**9,
    )(at, con_ids, text_ids, plan)
    owner = concept_ids >> 8
    item_x = owner >> 5
    item_y = (owner >> 2) & 3
    item_u = jnp.where(c == 0, item_x, item_y)
    item_v = jnp.where(c == 0, item_y, item_x)
    con_slot = ((v ^ item_v) * 4 + (u ^ item_u)) * CON + spots[0, :n_con]
    pick = (con_slot[:, None] == jnp.arange(16 * CON)[None, :]).astype(BF)
    shift_scale = lax.dynamic_index_in_dim(modulation, step_index[0], 0, keepdims=False)

    image_blocks = call(
        image_heads_kernel, tuple(sds((10 * n_img, HD)) for _ in range(4)), nbytes=MIB // 2
    )(at, img_q, q_core, own_both, other_rows[0], column_rows[1], other_rows[1])
    image_blocks = [image_blocks[0]] + [send(image_blocks[s], swap_u(s)) for s in (1, 2, 3)]

    qkv = call(
        project_kernel,
        tuple(sds((ROWS + CON // 2, 2 * HD)) for _ in range(4)),
        scratch=(
            pltpu.VMEM((8 * SLOTS, width), BF),
            pltpu.VMEM((ROWS, width), BF),
            pltpu.VMEM((3, width, half), BF),
            pltpu.SemaphoreType.DMA((3,)),
        ),
        nbytes=10 * MIB,
        flops=10**9,
        in_hbm=1,
    )(at, pack, *column_rows, *other_rows, shift_scale, qk_gain, jnp.transpose(txt_qkv, (1, 0, 2)))

    *image_blocks, first = lax.optimization_barrier((*image_blocks, qkv[0]))
    image_q, image_kv = call(
        image_join_kernel, (sds((8 * n_img, HD)), sds((32 * n_img, HD))), nbytes=MIB // 2, smem=0
    )(*image_blocks)
    image_kvs = [image_kv] + [send(image_kv, swap_v(s)) for s in (1, 2, 3)]

    qkv = [first] + [send(qkv[s], swap_u(s)) for s in (1, 2, 3)]
    q_join, kv_join = call(
        join_kernel, (sds((4 * CON, HD)), sds((4 * ROWS, 2 * HD))), nbytes=MIB, smem=0
    )(*qkv)
    q_chunks = [q_join] + [send(q_join, swap_v(s)) for s in (1, 2, 3)]
    kv_chunks = [send(kv_join, swap_v(s)) for s in (1, 2, 3)]

    all_img = 64 * n_img
    keys, vals, *image_stats = call(
        image_self_kernel,
        (
            sds((all_img, HD)),
            sds((all_img, 2 * HD)),
            sds((8 * n_img, 1), F32),
            sds((8 * n_img, 2 * HD), F32),
        ),
        nbytes=4 * MIB,
        flops=10**9,
        smem=0,
    )(*image_kvs, image_q, kv_join, txt_bias)
    con_q, *con_stats = call(
        concept_image_kernel,
        (sds((n_con, HD)), sds((n_con, 1), F32), sds((n_con, 2 * HD), F32)),
        nbytes=8 * MIB,
        flops=3 * 10**9,
        smem=0,
    )(pick, *q_chunks, keys, vals, kv_join, con_bias)
    blocks = call(
        prompt_kernel,
        tuple(sds((80, n_con + HD)) for _ in range(4)),
        scratch=(pltpu.VMEM((n_con, HD), BF),),
        nbytes=10 * MIB,
        flops=2 * 10**9,
        smem=0,
    )(con_bias, txt_bias, *kv_chunks, con_q, *con_stats, image_q, *image_stats)
    blocks = [blocks[0]] + [send(blocks[s], swap_u(s)) for s in (1, 2, 3)]
    own, core, diag, out_own = call(
        head_sum_kernel,
        (sds((48, n_con + HD)), sds((48, n_con + 4 * HD)), sds((48, n_con + HD)), sds((32, half))),
        nbytes=MIB,
    )(at, *blocks)
    last = (
        at,
        own,
        send(core, swap_core(0)),
        send(own, swap_z(2)),
        send(diag, swap_core(1)),
        out_own,
    )
    finish = call(
        finish_kernel, (sds((n_img, 2 * half)), sds((n_con, n_img), F32)), nbytes=MIB
    )
    fits = (plan[1, 0] <= SLOTS) & (spots[1, 0] <= CON) & (spots[2, 0] <= TXT)
    return fits, lambda: tuple(finish(*last))


def on_device(*args):
    fits, finish = packed(*args)
    return lax.cond(fits, finish, lambda: tuple(general(*args)))


def solution(mesh):
    return jax.shard_map(
        on_device,
        mesh=mesh,
        in_specs=(
            P("ctx", "head"),
            P("ctx", "head"),
            P("ctx", "head"),
            P(),
            P(),
            P(),
            P(("ctx", "head"), None),
            P(),
            P(None, None, "head"),
            P(),
        ),
        out_specs=(P("ctx", "head"), P(None, "ctx")),
        check_vma=False,
    )
```

```python
import math

import jax
import jax.numpy as jnp
from jax import lax
from jax.experimental import pallas as pl
from jax.experimental.pallas import tpu as pltpu
from jax.sharding import PartitionSpec as P

BF = jnp.bfloat16
F32 = jnp.float32
HD = 128
SLOTS = 32
CON = 96
TXT = 64
ROWS = CON + TXT
MIB = 1 << 20
NEAR_US, FAR_US, PROJ_US, PROMPT_US = 5.0, 4.0, 5.0, 3.0
FACTOR = HD ** (-0.5) * math.log2(math.e)


def modulate(rows, shift_scale):
    values = rows.astype(F32)
    mean = jnp.mean(values, axis=1, keepdims=True)
    centered = values - mean
    var = jnp.mean(centered * centered, axis=1, keepdims=True)
    normed = centered * lax.rsqrt(var + 1e-06)
    return (normed * (1.0 + shift_scale[1]) + shift_scale[0]).astype(BF)


def head_norm(values, gain, head_dim):
    shaped = values.reshape(values.shape[0], -1, head_dim)
    meansq = jnp.mean(shaped * shaped, axis=2, keepdims=True)
    return (shaped * lax.rsqrt(meansq + 1e-06) * gain).reshape(values.shape[0], -1)


def block_stats(queries, keys, values):
    scores = jnp.einsum("rgd,kgd->grk", queries, keys, preferred_element_type=F32)
    scores = scores * queries.shape[-1] ** (-0.5)
    peak = jnp.max(scores, axis=2)
    weights = jnp.exp(scores - peak[:, :, None])
    total = jnp.sum(weights, axis=2)
    summed = jnp.einsum("grk,kgd->grd", weights.astype(BF), values, preferred_element_type=F32)
    return (peak, total, summed)


def combine_stats(first, second):
    peak = jnp.maximum(first[0], second[0])
    left = jnp.exp(first[0] - peak)
    right = jnp.exp(second[0] - peak)
    total = first[1] * left + second[1] * right
    summed = first[2] * left[:, :, None] + second[2] * right[:, :, None]
    return (peak, total, summed)


def scaled_scores(dots, concept_sq, image_sq, width):
    concept_rms = jnp.sqrt(concept_sq / width + 1e-06)
    image_rms = jnp.sqrt(image_sq / width + 1e-06)
    return dots / (jnp.sqrt(F32(width)) * concept_rms[:, None] * image_rms[None, :])


def gather_ctx(block):
    n_ctx = lax.axis_size("ctx")
    spread = jnp.broadcast_to(block[None], (n_ctx,) + block.shape)
    return lax.all_to_all(spread, "ctx", 0, 0, tiled=True)


def general(
    img_q, img_k, img_v, txt_ids, concept_ids, step_index, token_table, modulation, txt_qkv, qk_gain
):
    n_ctx = lax.axis_size("ctx")
    n_head = lax.axis_size("head")
    head_dim = qk_gain.shape[1]
    group = img_q.shape[1] // head_dim
    text_dev = txt_ids.shape[0] // n_ctx
    concept_dev = concept_ids.shape[0] // n_ctx
    vocab_dev = token_table.shape[0]
    combined = jnp.concatenate(
        [txt_ids.reshape(n_ctx, text_dev), concept_ids.reshape(n_ctx, concept_dev)], axis=1
    ).reshape(-1)
    offset = lax.axis_index(("ctx", "head")) * vocab_dev
    wanted = combined - offset
    inside = (wanted >= 0) & (wanted < vocab_dev)
    picked = jnp.take(token_table, jnp.clip(wanted, 0, vocab_dev - 1), axis=0)
    n_all = n_ctx * n_head
    mine = jnp.where(inside[:, None], picked, jnp.zeros((), picked.dtype))
    parts = lax.all_to_all(
        mine.reshape(n_all, -1, mine.shape[1]), ("ctx", "head"), 0, 0, tiled=True
    )
    own_rows = jnp.sum(parts.astype(F32), axis=0)
    prompt_rows = lax.all_gather(own_rows.astype(BF), "head", axis=0, tiled=True)
    shift_scale = lax.dynamic_index_in_dim(modulation, step_index[0], 0, keepdims=False)
    modded = modulate(prompt_rows, shift_scale)
    text_mod = modded[:text_dev]
    concept_mod = modded[text_dev:]
    text_kv = jnp.einsum("rd,dgc->rgc", text_mod, txt_qkv[:, 1:], preferred_element_type=F32)
    concept_qkv = jnp.einsum("rd,dgc->rgc", concept_mod, txt_qkv, preferred_element_type=F32)
    text_keys = head_norm(text_kv[:, 0], qk_gain[1], head_dim).astype(BF)
    text_values = text_kv[:, 1].astype(BF)
    concept_queries = head_norm(concept_qkv[:, 0], qk_gain[0], head_dim).astype(BF)
    concept_keys = head_norm(concept_qkv[:, 1], qk_gain[1], head_dim).astype(BF)
    concept_values = concept_qkv[:, 2].astype(BF)
    local_kv = jnp.stack(
        [
            jnp.concatenate([text_keys, concept_keys], axis=0),
            jnp.concatenate([text_values, concept_values], axis=0),
        ]
    )
    prompt_kv = gather_ctx(local_kv)
    text_part = jnp.swapaxes(prompt_kv[:, :, :text_dev], 0, 1).reshape(2, -1, group, head_dim)
    concept_part = jnp.swapaxes(prompt_kv[:, :, text_dev:], 0, 1).reshape(2, -1, group, head_dim)
    image_queries = img_q.reshape(-1, group, head_dim)
    concept_q3 = concept_queries.reshape(-1, group, head_dim)
    first = block_stats(image_queries, text_part[0], text_part[1])
    second = block_stats(concept_q3, concept_part[0], concept_part[1])
    start_stats = (
        jnp.concatenate([first[0], second[0]], axis=1),
        jnp.concatenate([first[1], second[1]], axis=1),
        jnp.concatenate([first[2], second[2]], axis=1),
    )
    all_queries = jnp.concatenate([image_queries, concept_q3], axis=0)
    image_kv = gather_ctx(jnp.stack([img_k, img_v]))
    keys = image_kv[:, 0].reshape(-1, group, head_dim)
    values = image_kv[:, 1].reshape(-1, group, head_dim)
    peak, total, summed = combine_stats(start_stats, block_stats(all_queries, keys, values))
    attended = (
        jnp.transpose(summed / total[:, :, None], (1, 0, 2))
        .reshape(all_queries.shape[0], -1)
        .astype(BF)
    )
    img_rows = img_q.shape[0]
    img_out = attended[:img_rows]
    concept_out = attended[img_rows:]
    concept_all = gather_ctx(concept_out).reshape(-1, concept_out.shape[1])
    dots = lax.dot_general(
        concept_all, img_out, (((1,), (1,)), ((), ())), preferred_element_type=F32
    )
    image_f = img_out.astype(F32)
    concept_f = concept_all.astype(F32)
    image_sq = jnp.sum(image_f * image_f, axis=1)
    concept_sq = jnp.sum(concept_f * concept_f, axis=1)
    width = group * head_dim * n_head
    sums = jnp.concatenate(
        [
            jnp.concatenate([dots, concept_sq[:, None]], axis=1),
            jnp.concatenate([image_sq, jnp.zeros((1,), F32)])[None],
        ]
    ).astype(BF)
    other = lax.ppermute(sums, "head", [(0, 1), (1, 0)])
    sums = sums.astype(F32) + other.astype(F32)
    concepts = dots.shape[0]
    saliency = scaled_scores(
        sums[:concepts, :img_rows], sums[:concepts, img_rows], sums[concepts, :img_rows], width
    )
    return (img_out, saliency)


def place(x, zl, y, c, g):
    return ((((x * 2 + zl) * 4 + y) * 2 + c) * 2) + g


def pairs(move):
    found = []
    for x in range(4):
        for zl in range(2):
            for y in range(4):
                for c in range(2):
                    for g in range(2):
                        found.append((place(x, zl, y, c, g), place(*move(x, zl, y, c, g))))
    return found


def swap_z(s):
    def move(x, zl, y, c, g):
        z = (2 * g + zl) ^ s
        return x, z & 1, y, c, z >> 1

    return pairs(move)


def swap_u(s):
    return pairs(
        lambda x, zl, y, c, g: (x, zl, y ^ s, c, g) if c else (x ^ s, zl, y, c, g)
    )


def swap_v(s):
    return pairs(
        lambda x, zl, y, c, g: (x ^ s, zl, y, c, g) if c else (x, zl, y ^ s, c, g)
    )


def swap_plane():
    return pairs(lambda x, zl, y, c, g: (x, zl ^ 1, y, c, g))


def swap_core(dg):
    return pairs(lambda x, zl, y, c, g: (x, zl, y, c ^ 1, g ^ dg))


def send(array, pairing):
    return lax.ppermute(array, ("ctx", "head"), pairing)


def nt(a, b, **kw):
    return lax.dot_general(a, b, (((1,), (1,)), ((), ())), preferred_element_type=F32, **kw)


def nn(a, b):
    return lax.dot_general(a, b, (((1,), (0,)), ((), ())), preferred_element_type=F32)


def call(kernel, outs, scratch=(), limit=48, us=1.0, smem=1, in_hbm=0):
    def run(*args):
        vm = pl.BlockSpec(memory_space=pltpu.VMEM)
        sm = pl.BlockSpec(memory_space=pltpu.SMEM)
        return pl.pallas_call(
            kernel,
            out_shape=outs,
            in_specs=[sm] * smem
            + [vm] * (len(args) - smem - in_hbm)
            + [pl.BlockSpec(memory_space=pl.ANY)] * in_hbm,
            out_specs=jax.tree.map(lambda _: vm, outs),
            scratch_shapes=list(scratch),
            compiler_params=pltpu.CompilerParams(vmem_limit_bytes=limit * MIB),
            cost_estimate=pl.CostEstimate(
                flops=int(us * 1.1e9), bytes_accessed=0, transcendentals=0
            ),
        )(*args)

    return run


def sds(shape, dtype=BF):
    return jax.ShapeDtypeStruct(shape, dtype)


def column_of(owner):
    ctx = owner >> 1
    return ((ctx >> 4) << 2) | ((ctx >> 1) & 3)


def ranks(keys, classes, resets):
    n = keys.shape[1]
    blk = 256
    row = lax.broadcasted_iota(jnp.int32, (blk, blk), 0)
    col = lax.broadcasted_iota(jnp.int32, (blk, blk), 1)
    earlier = (row < col).astype(F32).astype(BF)
    label = lax.broadcasted_iota(jnp.int32, (classes, blk), 0)
    carry = jnp.zeros((classes, 1), F32)
    found, counts = [], []
    for b in range(n // blk):
        if b in resets:
            counts.append(carry)
            carry = jnp.zeros((classes, 1), F32)
        hot = (label == keys[:, b * blk : (b + 1) * blk]).astype(F32)
        before = nn(hot.astype(BF), earlier) + carry
        found.append(jnp.sum(hot * before, axis=0, keepdims=True))
        carry = carry + jnp.sum(hot, axis=1, keepdims=True)
    counts.append(carry)
    return jnp.concatenate(found, axis=1).astype(jnp.int32), counts


def most(counts, n):
    return jnp.broadcast_to(jnp.max(counts, axis=0, keepdims=True).astype(jnp.int32), (1, n))


def plan_kernel(
    at, con_ref, txt_ref, table_ref, q_ref, k_ref, v_ref, rows_ref, both_ref, img_ref, plan_ref
):
    ids = jnp.concatenate([con_ref[...], txt_ref[...]], axis=1)
    n = ids.shape[1]
    vocab_dev = table_ref.shape[0]
    owner = ids >> int(math.log2(vocab_dev))
    rank, (counts,) = ranks(owner, 128, ())
    hot_slot = lax.broadcasted_iota(jnp.int32, (SLOTS, n), 0) == rank
    hot_slot = (hot_slot & (owner == at[0])).astype(F32).astype(BF)
    hot_row = lax.broadcasted_iota(jnp.int32, (vocab_dev, n), 0) == (ids & (vocab_dev - 1))
    pick = nt(hot_slot, hot_row.astype(F32).astype(BF)).astype(BF)
    rows = nn(pick, table_ref[...]).astype(BF)
    rows_ref[...] = rows
    both_ref[0:SLOTS, :] = rows
    m = q_ref.shape[0]
    half = q_ref.shape[1] // 2
    mine = pl.ds(pl.multiple_of(at[2] * half, half), half)
    theirs = pl.ds(pl.multiple_of((1 - at[2]) * half, half), half)
    for i, ref in enumerate((q_ref, k_ref, v_ref)):
        img_ref[i * m : (i + 1) * m, :] = ref[:, mine]
        for j in range(2):
            lanes = slice((2 * i + j) * half, (2 * i + j + 1) * half)
            both_ref[SLOTS:, lanes] = ref[16 * j : 16 * (j + 1), theirs]
    both_ref[SLOTS:, 6 * half :] = jnp.zeros((16, 2 * half), BF)
    plan_ref[0:1, :] = rank
    plan_ref[1:2, :] = most(counts, n)
    plan_ref[2:8, :] = jnp.zeros((6, n), jnp.int32)


def empty_bias(at, counts, slots, blocks_lanes):
    lane = lax.broadcasted_iota(jnp.int32, (1, blocks_lanes), 1)
    block = jnp.zeros((1, blocks_lanes), jnp.int32)
    for j in range(1, 16):
        block = block + (lane >= j * slots).astype(jnp.int32)
    item_u = (block & 3) ^ at[4]
    item_v = (block >> 2) ^ at[5]
    column = jnp.where(at[2] == 0, item_u * 4 + item_v, item_v * 4 + item_u)
    hot = lax.broadcasted_iota(jnp.int32, (16, blocks_lanes), 0) == column
    held = jnp.sum(jnp.where(hot, counts, 0.0), axis=0, keepdims=True)
    return jnp.where((lane - block * slots).astype(F32) < held, 0.0, -1e30)


def pack_kernel(at, con_ref, txt_ref, plan_ref, out_ref, spot_ref, con_bias, txt_bias):
    ids = jnp.concatenate([con_ref[...], txt_ref[...]], axis=1)
    n = ids.shape[1]
    n_con = con_ref.shape[1]
    owner = ids >> 8
    column = column_of(owner)
    spot, (con_counts, txt_counts) = ranks(column, 16, (n_con // 256,))
    con_bias[...] = empty_bias(at, con_counts, CON, 16 * CON)
    txt_bias[...] = empty_bias(at, txt_counts, TXT, 16 * TXT)
    spot_ref[0:1, :] = spot
    spot_ref[1:2, :] = jnp.maximum(
        jnp.maximum(most(con_counts, n) - CON, most(txt_counts, n) - TXT),
        plan_ref[1:2, :] - SLOTS,
    )
    spot_ref[2:8, :] = jnp.zeros((6, n), jnp.int32)
    here = column == at[1]
    rank = plan_ref[0:1, :]
    concept = lax.broadcasted_iota(jnp.int32, (1, n), 1) < n_con
    target = jnp.where(
        concept, jnp.where(spot < CON, spot, -1), jnp.where(spot < TXT, spot + CON, -1)
    )
    z = ((owner & 1) << 1) | ((owner >> 4) & 1)
    core = (owner >> 1) & 1
    piece = jnp.where(core == at[2], 0, 4) + (at[3] ^ z)
    source = jnp.where(rank < SLOTS, piece * SLOTS + rank, -1)
    target = jnp.where(here, target, -1)
    source = jnp.where(here, source, -1)
    hot_t = (lax.broadcasted_iota(jnp.int32, (ROWS, n), 0) == target).astype(F32).astype(BF)
    hot_s = (lax.broadcasted_iota(jnp.int32, (8 * SLOTS, n), 0) == source).astype(F32).astype(BF)
    out_ref[...] = nt(hot_t, hot_s).astype(BF)


def project_kernel(at, pack_ref, *refs):
    rows, (mod_ref, gain_ref, w_hbm), outs = refs[:8], refs[8:11], refs[11:15]
    raw_ref, x_ref, w_ref, sems = refs[15:]
    half = w_ref.shape[2]
    lanes = pl.ds(pl.multiple_of(at[2] * half, half), half)
    copies = [
        pltpu.make_async_copy(w_hbm.at[j, :, lanes], w_ref.at[j], sems.at[j]) for j in range(3)
    ]
    for copy in copies:
        copy.start()
    for i, ref in enumerate(rows):
        raw_ref[i * SLOTS : (i + 1) * SLOTS, :] = ref[0:SLOTS, :]
    shift = mod_ref[0:1, :]
    scale = 1.0 + mod_ref[1:2, :]
    for i in range(ROWS // 32):
        block = slice(i * 32, (i + 1) * 32)
        values = nn(pack_ref[block, :], raw_ref[...])
        mean = jnp.mean(values, axis=1, keepdims=True)
        centered = values - mean
        var = jnp.mean(centered * centered, axis=1, keepdims=True)
        x_ref[block, :] = (centered * lax.rsqrt(var + 1e-06) * scale + shift).astype(BF)

    def normed(u, gain):
        meansq = jnp.mean(u * u, axis=1, keepdims=True)
        return u * lax.rsqrt(meansq + 1e-06) * gain

    copies[0].wait()
    q = nn(x_ref[0:CON, :], w_ref[0])
    copies[1].wait()
    k = nn(x_ref[...], w_ref[1])
    copies[2].wait()
    v = nn(x_ref[...], w_ref[2])
    heads = []
    for h in range(3):
        cols = slice(h * HD, (h + 1) * HD)
        heads.append(
            (
                (normed(q[:, cols], gain_ref[0:1, :]) * FACTOR).astype(BF),
                normed(k[:, cols], gain_ref[1:2, :]).astype(BF),
                v[:, cols].astype(BF),
            )
        )
    for s, out in enumerate(outs):
        head = jnp.minimum(at[4] ^ s, 2)
        for h in range(3):

            @pl.when(head == h)
            def _(h=h, out=out):
                out[0:ROWS, 0:HD] = heads[h][1]
                out[0:ROWS, HD:] = heads[h][2]
                out[ROWS:, 0:HD] = heads[h][0][: CON // 2]
                out[ROWS:, HD:] = heads[h][0][CON // 2 :]


def join_kernel(a, b, c, d, q_out, kv_out):
    for i, ref in enumerate((a, b, c, d)):
        kv_out[i * CON : (i + 1) * CON, :] = ref[0:CON, :]
        kv_out[4 * CON + i * TXT : 4 * CON + (i + 1) * TXT, :] = ref[CON:ROWS, :]
        q_out[i * CON : i * CON + CON // 2, :] = ref[ROWS:, 0:HD]
        q_out[i * CON + CON // 2 : (i + 1) * CON, :] = ref[ROWS:, HD:]


def image_heads_kernel(at, own, core, *outs):
    n, half = own.shape[0] // 3, own.shape[1]
    for s, out in enumerate(outs):
        head = jnp.minimum(at[4] ^ s, 2)
        lanes = pl.ds(pl.multiple_of(head * HD, HD), HD)
        for i in range(3):
            row = 2 * i * n
            out[row : row + n, :] = own[i * n : (i + 1) * n, lanes]
            for j in range(2):
                there = pl.ds(pl.multiple_of((2 * i + j) * half + head * HD, HD), HD)
                out[row + n + 16 * j : row + n + 16 * (j + 1), :] = core[SLOTS:, there]


def image_join_kernel(a, b, c, d, q_out, kv_out):
    n = a.shape[0] // 3
    for i, ref in enumerate((a, b, c, d)):
        q_out[n * i : n * (i + 1), :] = ref[0:n, :]
        kv_out[n * i : n * (i + 1), :] = ref[n : 2 * n, :]
        kv_out[n * (4 + i) : n * (5 + i), :] = ref[2 * n :, :]


def plane_kernel(a, b, c, d, out):
    n = a.shape[0] // 2
    for i, ref in enumerate((a, b, c, d)):
        out[n * i : n * (i + 1), :] = ref[0:n, :]
        out[n * (4 + i) : n * (5 + i), :] = ref[n:, :]


def weigh(q, parts, factor):
    scores = []
    for keys, _, bias in parts:
        part = nt(q, keys)
        scores.append(part if bias is None else part + bias)
    peak = scores[0].max(axis=1, keepdims=True)
    for part in scores[1:]:
        peak = jnp.maximum(peak, part.max(axis=1, keepdims=True))
    total = None
    for part, (_, values, _) in zip(scores, parts):
        power = part - peak
        weights = jnp.exp2(power if factor is None else power * factor).astype(BF)
        summed = nn(weights, values)
        total = summed if total is None else total + summed
    return (peak if factor is None else peak * factor), total


def join(first, second):
    peak = jnp.maximum(first[0], second[0])
    return peak, first[1] * jnp.exp2(first[0] - peak) + second[1] * jnp.exp2(second[0] - peak)


def merge(first, second):
    _, summed = join(first, second)
    return (summed[:, 0:HD] / summed[:, HD:]).astype(BF)


def with_ones(values):
    return jnp.concatenate([values, jnp.ones_like(values)], axis=1)


def plane_parts(plane):
    n = plane.shape[0] // 2
    return (plane[0:n, :], with_ones(plane[n:, :]), None)


def near_kernel(pick, q0, q1, q2, q3, plane, kv, con_bias, txt_bias, img_q, q_out, cm, cs, im, ims):
    n = 4 * CON
    q_out[...] = sum(
        nn(pick[:, a * n : (a + 1) * n], ref[...]) for a, ref in enumerate((q0, q1, q2, q3))
    ).astype(BF)
    images = plane_parts(plane)
    own = (kv[0:n, 0:HD], with_ones(kv[0:n, HD:]), con_bias[:, 0:n])
    for b in range(q_out.shape[0] // 256):
        rows = slice(b * 256, (b + 1) * 256)
        cm[rows, :], cs[rows, :] = weigh(q_out[rows, :], (images, own), None)
    text = (kv[n:, 0:HD], with_ones(kv[n:, HD:]), txt_bias[:, 0 : 4 * TXT])
    im[...], ims[...] = weigh(img_q[...], (images, text), FACTOR)


def far_kernel(plane, con_q, img_q, cm, cs, im, ims, cm_out, cs_out, im_out, ims_out):
    images = plane_parts(plane)
    for b in range(con_q.shape[0] // 256):
        rows = slice(b * 256, (b + 1) * 256)
        part = weigh(con_q[rows, :], (images,), None)
        cm_out[rows, :], cs_out[rows, :] = join(part, (cm[rows, :], cs[rows, :]))
    part = weigh(img_q[...], (images,), FACTOR)
    im_out[...], ims_out[...] = join(part, (im[...], ims[...]))


def prompt_kernel(con_bias, txt_bias, c1, c2, c3, con_q, cm, cs, img_q, im, ims, *refs):
    outs, (con_out,) = refs[:4], refs[4:]
    n, m = 4 * CON, 4 * TXT
    con_parts, txt_parts = [], []
    for a, ref in enumerate((c1, c2, c3)):
        con, txt = ref[0:n, :], ref[n:, :]
        con_parts.append(
            (con[:, 0:HD], with_ones(con[:, HD:]), con_bias[:, (a + 1) * n : (a + 2) * n])
        )
        txt_parts.append(
            (txt[:, 0:HD], with_ones(txt[:, HD:]), txt_bias[:, (a + 1) * m : (a + 2) * m])
        )
    img = merge(weigh(img_q[...], txt_parts, FACTOR), (im[...], ims[...]))
    n_con = con_q.shape[0]
    for b in range(n_con // 256):
        rows = slice(b * 256, (b + 1) * 256)
        part = weigh(con_q[rows, :], con_parts, None)
        con_out[rows, :] = merge(part, (cm[rows, :], cs[rows, :]))
    dots = nt(img, con_out[...]).astype(BF)
    con_f = con_out[...].astype(F32)
    con_sq = nt(jnp.ones((16, HD), F32), con_f * con_f, precision=lax.Precision.HIGHEST).astype(BF)
    for s, out in enumerate(outs):
        rows = slice(s * 64, (s + 1) * 64)
        out[0:64, 0:n_con] = dots[rows]
        out[0:64, n_con:] = img[rows]
        out[64:80, 0:n_con] = con_sq
        out[64:80, n_con:] = jnp.zeros((16, HD), BF)


def head_sum_kernel(at, b0, b1, b2, b3, own, core, diag, out_own):
    n_con = b0.shape[1] - HD
    total = jnp.zeros((80, n_con), F32)
    outs = [jnp.zeros((64, HD), BF) for _ in range(3)]
    for s, ref in enumerate((b0, b1, b2, b3)):
        head = at[4] ^ s
        total = total + jnp.where(head < 3, ref[:, 0:n_con].astype(F32), 0.0)
        for h in range(3):
            outs[h] = jnp.where(head == h, ref[0:64, n_con:], outs[h])
    image_sq = jnp.zeros((64, 1), F32)
    for h in range(3):
        out_f = outs[h].astype(F32)
        image_sq = image_sq + jnp.sum(out_f * out_f, axis=1, keepdims=True)
    image_sq = jnp.broadcast_to(image_sq, (64, HD)).astype(BF)
    total = total.astype(BF)
    for ref, row in ((own, 0), (core, 32), (diag, 32)):
        ref[0:32, 0:n_con] = total[row : row + 32]
        ref[32:48, 0:n_con] = total[64:80]
        ref[0:32, n_con : n_con + HD] = image_sq[row : row + 32]
        ref[32:48, n_con : n_con + HD] = jnp.zeros((16, HD), BF)
    for h in range(3):
        lanes = slice(n_con + (1 + h) * HD, n_con + (2 + h) * HD)
        core[0:32, lanes] = outs[h][32:64]
        core[32:48, lanes] = jnp.zeros((16, HD), BF)
        out_own[:, h * HD : (h + 1) * HD] = outs[h][0:32]


def finish_kernel(at, own, core, head, diag, out_own, img_ref, sal_ref):
    n_con = own.shape[1] - HD
    width = 12 * HD
    cols = n_con + HD
    near = own[...].astype(F32) + core[:, 0:cols].astype(F32)
    far = head[...].astype(F32) + diag[...].astype(F32)
    total = near + far
    con_rms = jnp.sqrt(total[32:33, 0:n_con] / width + 1e-06)
    img_rms = jnp.sqrt(total[0:32, n_con : n_con + 1] / width + 1e-06)
    sal = total[0:32, 0:n_con] / (math.sqrt(width) * con_rms * img_rms)
    sal_ref[...] = sal
    half = 3 * HD
    mine = pl.ds(pl.multiple_of(at[2] * half, half), half)
    theirs = pl.ds(pl.multiple_of((1 - at[2]) * half, half), half)
    img_ref[:, mine] = out_own[...]
    img_ref[:, theirs] = core[0:32, cols:]


def packed(
    img_q, img_k, img_v, txt_ids, concept_ids, step_index, token_table, modulation, txt_qkv, qk_gain
):
    n_con, n_txt = concept_ids.shape[0], txt_ids.shape[0]
    ctx = lax.axis_index("ctx")
    g = lax.axis_index("head")
    c = ctx & 1
    y = (ctx >> 1) & 3
    zl = (ctx >> 3) & 1
    x = ctx >> 4
    u = jnp.where(c == 0, x, y)
    v = jnp.where(c == 0, y, x)
    at = jnp.stack([ctx * 2 + g, x * 4 + y, c, 2 * g + zl, u, v]).astype(jnp.int32)
    con_ids, text_ids = concept_ids[None, :], txt_ids[None, :]
    n = n_con + n_txt
    width = token_table.shape[1]
    half = txt_qkv.shape[2] // 2
    n_img = img_q.shape[0]

    own_rows, own_both, own_img, plan = call(
        plan_kernel,
        (
            sds((SLOTS, width)),
            sds((SLOTS + 16, width)),
            sds((3 * n_img, half)),
            sds((8, n), jnp.int32),
        ),
    )(at, con_ids, text_ids, token_table, img_q, img_k, img_v)
    far_rows = send(own_rows, swap_z(2))
    column_rows = [own_rows] + [send(own_rows, swap_z(s)) for s in (1, 3)]
    core_both = send(own_both, swap_core(0))

    pack, spots, con_bias, txt_bias = call(
        pack_kernel,
        (
            sds((ROWS, 8 * SLOTS)),
            sds((8, n), jnp.int32),
            sds((1, 16 * CON), F32),
            sds((1, 16 * TXT), F32),
        ),
    )(at, con_ids, text_ids, plan)
    owner = concept_ids >> 8
    item_x = owner >> 5
    item_y = (owner >> 2) & 3
    item_u = jnp.where(c == 0, item_x, item_y)
    item_v = jnp.where(c == 0, item_y, item_x)
    con_slot = ((v ^ item_v) * 4 + (u ^ item_u)) * CON + spots[0, :n_con]
    pick = (con_slot[:, None] == jnp.arange(16 * CON)[None, :]).astype(BF)
    shift_scale = lax.dynamic_index_in_dim(modulation, step_index[0], 0, keepdims=False)
    fits = (spots[1, 0] <= 0).astype(jnp.int32)

    image_blocks = call(
        image_heads_kernel, tuple(sds((6 * n_img, HD)) for _ in range(4))
    )(at, own_img, core_both)
    far_rows, pack, shift_scale, pick, fits, *image_blocks = lax.optimization_barrier(
        (far_rows, pack, shift_scale, pick, fits, *image_blocks)
    )
    column_rows.insert(2, far_rows)
    other_rows = [core_both] + [send(r, swap_core(0)) for r in column_rows[1:]]

    image_blocks = [image_blocks[0]] + [send(image_blocks[s], swap_u(s)) for s in (2, 1, 3)]
    image_blocks = [image_blocks[0], image_blocks[2], image_blocks[1], image_blocks[3]]

    qkv = call(
        project_kernel,
        tuple(sds((ROWS + CON // 2, 2 * HD)) for _ in range(4)),
        scratch=(
            pltpu.VMEM((8 * SLOTS, width), BF),
            pltpu.VMEM((ROWS, width), BF),
            pltpu.VMEM((3, width, half), BF),
            pltpu.SemaphoreType.DMA((3,)),
        ),
        us=PROJ_US,
        in_hbm=1,
    )(at, pack, *column_rows, *other_rows, shift_scale, qk_gain, jnp.transpose(txt_qkv, (1, 0, 2)))

    *image_blocks, first = lax.optimization_barrier((*image_blocks, qkv[0]))
    image_q, image_kv = call(
        image_join_kernel, (sds((8 * n_img, HD)), sds((16 * n_img, HD))), smem=0
    )(*image_blocks)
    image_kvs = [image_kv] + [send(image_kv, swap_v(s)) for s in (2, 1, 3)]

    qkv = [first] + [send(qkv[s], swap_u(s)) for s in (2, 1, 3)]
    qkv = [qkv[0], qkv[2], qkv[1], qkv[3]]
    q_join, kv_join = call(
        join_kernel, (sds((4 * CON, HD)), sds((4 * ROWS, 2 * HD))), smem=0
    )(*qkv)
    plane = call(plane_kernel, sds((64 * n_img, HD)), smem=0)(*image_kvs)
    q_chunks = [q_join] + [send(q_join, swap_v(s)) for s in (2, 1, 3)]
    q_chunks = [q_chunks[0], q_chunks[2], q_chunks[1], q_chunks[3]]
    other_plane = send(plane, swap_plane())
    kv_chunks = [send(kv_join, swap_v(s)) for s in (2, 1, 3)]
    kv_chunks = [kv_chunks[1], kv_chunks[0], kv_chunks[2]]

    stats = (
        sds((n_con, 1), F32),
        sds((n_con, 2 * HD), F32),
        sds((8 * n_img, 1), F32),
        sds((8 * n_img, 2 * HD), F32),
    )
    con_q, *near = call(near_kernel, (sds((n_con, HD)),) + stats, us=NEAR_US, smem=0)(
        pick, *q_chunks, plane, kv_join, con_bias, txt_bias, image_q
    )
    con_stats = call(far_kernel, stats, us=FAR_US, smem=0)(other_plane, con_q, image_q, *near)
    con_stats, image_stats = con_stats[:2], con_stats[2:]
    blocks = call(
        prompt_kernel,
        tuple(sds((80, n_con + HD)) for _ in range(4)),
        scratch=(pltpu.VMEM((n_con, HD), BF),),
        us=PROMPT_US,
        smem=0,
    )(con_bias, txt_bias, *kv_chunks, con_q, *con_stats, image_q, *image_stats)
    blocks = [blocks[0]] + [send(blocks[s], swap_u(s)) for s in (2, 1, 3)]
    blocks = [blocks[0], blocks[2], blocks[1], blocks[3]]
    own, core, diag, out_own = call(
        head_sum_kernel,
        (sds((48, n_con + HD)), sds((48, n_con + 4 * HD)), sds((48, n_con + HD)), sds((32, half))),
    )(at, *blocks)
    last = (
        at,
        own,
        send(core, swap_core(0)),
        send(own, swap_z(2)),
        send(diag, swap_core(1)),
        out_own,
    )
    finish = call(
        finish_kernel, (sds((n_img, 2 * half)), sds((n_img, n_con), F32))
    )

    def finished():
        img_out, saliency = finish(*last)
        return img_out, jnp.transpose(saliency)

    return fits > 0, finished


def on_device(*args):
    fits, finish = packed(*args)
    return lax.cond(fits, finish, lambda: tuple(general(*args)))


def solution(mesh):
    return jax.shard_map(
        on_device,
        mesh=mesh,
        in_specs=(
            P("ctx", "head"),
            P("ctx", "head"),
            P("ctx", "head"),
            P(),
            P(),
            P(),
            P(("ctx", "head"), None),
            P(),
            P(None, None, "head"),
            P(),
        ),
        out_specs=(P("ctx", "head"), P(None, "ctx")),
        check_vma=False,
    )
```

```python
import math

import jax
import jax.numpy as jnp
from jax import lax
from jax.experimental import pallas as pl
from jax.experimental.pallas import tpu as pltpu
from jax.sharding import PartitionSpec as P

BF = jnp.bfloat16
F32 = jnp.float32
HD = 128
SLOTS = 32
CON = 96
TXT = 64
ROWS = CON + TXT
LINE_CON = 320
LINE_TXT = 176
LINE = LINE_CON + LINE_TXT
MIB = 1 << 20
PROJ_US, PROMPT_US = 5.0, 9.0
FACTOR = HD ** (-0.5) * math.log2(math.e)


def modulate(rows, shift_scale):
    values = rows.astype(F32)
    mean = jnp.mean(values, axis=1, keepdims=True)
    centered = values - mean
    var = jnp.mean(centered * centered, axis=1, keepdims=True)
    normed = centered * lax.rsqrt(var + 1e-06)
    return (normed * (1.0 + shift_scale[1]) + shift_scale[0]).astype(BF)


def head_norm(values, gain, head_dim):
    shaped = values.reshape(values.shape[0], -1, head_dim)
    meansq = jnp.mean(shaped * shaped, axis=2, keepdims=True)
    return (shaped * lax.rsqrt(meansq + 1e-06) * gain).reshape(values.shape[0], -1)


def block_stats(queries, keys, values):
    scores = jnp.einsum("rgd,kgd->grk", queries, keys, preferred_element_type=F32)
    scores = scores * queries.shape[-1] ** (-0.5)
    peak = jnp.max(scores, axis=2)
    weights = jnp.exp(scores - peak[:, :, None])
    total = jnp.sum(weights, axis=2)
    summed = jnp.einsum("grk,kgd->grd", weights.astype(BF), values, preferred_element_type=F32)
    return (peak, total, summed)


def combine_stats(first, second):
    peak = jnp.maximum(first[0], second[0])
    left = jnp.exp(first[0] - peak)
    right = jnp.exp(second[0] - peak)
    total = first[1] * left + second[1] * right
    summed = first[2] * left[:, :, None] + second[2] * right[:, :, None]
    return (peak, total, summed)


def scaled_scores(dots, concept_sq, image_sq, width):
    concept_rms = jnp.sqrt(concept_sq / width + 1e-06)
    image_rms = jnp.sqrt(image_sq / width + 1e-06)
    return dots / (jnp.sqrt(F32(width)) * concept_rms[:, None] * image_rms[None, :])


def gather_ctx(block):
    n_ctx = lax.axis_size("ctx")
    spread = jnp.broadcast_to(block[None], (n_ctx,) + block.shape)
    return lax.all_to_all(spread, "ctx", 0, 0, tiled=True)


def general(
    img_q, img_k, img_v, txt_ids, concept_ids, step_index, token_table, modulation, txt_qkv, qk_gain
):
    n_ctx = lax.axis_size("ctx")
    n_head = lax.axis_size("head")
    head_dim = qk_gain.shape[1]
    group = img_q.shape[1] // head_dim
    text_dev = txt_ids.shape[0] // n_ctx
    concept_dev = concept_ids.shape[0] // n_ctx
    vocab_dev = token_table.shape[0]
    combined = jnp.concatenate(
        [txt_ids.reshape(n_ctx, text_dev), concept_ids.reshape(n_ctx, concept_dev)], axis=1
    ).reshape(-1)
    offset = lax.axis_index(("ctx", "head")) * vocab_dev
    wanted = combined - offset
    inside = (wanted >= 0) & (wanted < vocab_dev)
    picked = jnp.take(token_table, jnp.clip(wanted, 0, vocab_dev - 1), axis=0)
    n_all = n_ctx * n_head
    mine = jnp.where(inside[:, None], picked, jnp.zeros((), picked.dtype))
    parts = lax.all_to_all(
        mine.reshape(n_all, -1, mine.shape[1]), ("ctx", "head"), 0, 0, tiled=True
    )
    own_rows = jnp.sum(parts.astype(F32), axis=0)
    prompt_rows = lax.all_gather(own_rows.astype(BF), "head", axis=0, tiled=True)
    shift_scale = lax.dynamic_index_in_dim(modulation, step_index[0], 0, keepdims=False)
    modded = modulate(prompt_rows, shift_scale)
    text_mod = modded[:text_dev]
    concept_mod = modded[text_dev:]
    text_kv = jnp.einsum("rd,dgc->rgc", text_mod, txt_qkv[:, 1:], preferred_element_type=F32)
    concept_qkv = jnp.einsum("rd,dgc->rgc", concept_mod, txt_qkv, preferred_element_type=F32)
    text_keys = head_norm(text_kv[:, 0], qk_gain[1], head_dim).astype(BF)
    text_values = text_kv[:, 1].astype(BF)
    concept_queries = head_norm(concept_qkv[:, 0], qk_gain[0], head_dim).astype(BF)
    concept_keys = head_norm(concept_qkv[:, 1], qk_gain[1], head_dim).astype(BF)
    concept_values = concept_qkv[:, 2].astype(BF)
    local_kv = jnp.stack(
        [
            jnp.concatenate([text_keys, concept_keys], axis=0),
            jnp.concatenate([text_values, concept_values], axis=0),
        ]
    )
    prompt_kv = gather_ctx(local_kv)
    text_part = jnp.swapaxes(prompt_kv[:, :, :text_dev], 0, 1).reshape(2, -1, group, head_dim)
    concept_part = jnp.swapaxes(prompt_kv[:, :, text_dev:], 0, 1).reshape(2, -1, group, head_dim)
    image_queries = img_q.reshape(-1, group, head_dim)
    concept_q3 = concept_queries.reshape(-1, group, head_dim)
    first = block_stats(image_queries, text_part[0], text_part[1])
    second = block_stats(concept_q3, concept_part[0], concept_part[1])
    start_stats = (
        jnp.concatenate([first[0], second[0]], axis=1),
        jnp.concatenate([first[1], second[1]], axis=1),
        jnp.concatenate([first[2], second[2]], axis=1),
    )
    all_queries = jnp.concatenate([image_queries, concept_q3], axis=0)
    image_kv = gather_ctx(jnp.stack([img_k, img_v]))
    keys = image_kv[:, 0].reshape(-1, group, head_dim)
    values = image_kv[:, 1].reshape(-1, group, head_dim)
    peak, total, summed = combine_stats(start_stats, block_stats(all_queries, keys, values))
    attended = (
        jnp.transpose(summed / total[:, :, None], (1, 0, 2))
        .reshape(all_queries.shape[0], -1)
        .astype(BF)
    )
    img_rows = img_q.shape[0]
    img_out = attended[:img_rows]
    concept_out = attended[img_rows:]
    concept_all = gather_ctx(concept_out).reshape(-1, concept_out.shape[1])
    dots = lax.dot_general(
        concept_all, img_out, (((1,), (1,)), ((), ())), preferred_element_type=F32
    )
    image_f = img_out.astype(F32)
    concept_f = concept_all.astype(F32)
    image_sq = jnp.sum(image_f * image_f, axis=1)
    concept_sq = jnp.sum(concept_f * concept_f, axis=1)
    width = group * head_dim * n_head
    sums = jnp.concatenate(
        [
            jnp.concatenate([dots, concept_sq[:, None]], axis=1),
            jnp.concatenate([image_sq, jnp.zeros((1,), F32)])[None],
        ]
    ).astype(BF)
    other = lax.ppermute(sums, "head", [(0, 1), (1, 0)])
    sums = sums.astype(F32) + other.astype(F32)
    concepts = dots.shape[0]
    saliency = scaled_scores(
        sums[:concepts, :img_rows], sums[:concepts, img_rows], sums[concepts, :img_rows], width
    )
    return (img_out, saliency)


def place(x, zl, y, c, g):
    return ((((x * 2 + zl) * 4 + y) * 2 + c) * 2) + g


def pairs(move):
    found = []
    for x in range(4):
        for zl in range(2):
            for y in range(4):
                for c in range(2):
                    for g in range(2):
                        found.append((place(x, zl, y, c, g), place(*move(x, zl, y, c, g))))
    return found


def swap_z(s):
    def move(x, zl, y, c, g):
        z = (2 * g + zl) ^ s
        return x, z & 1, y, c, z >> 1

    return pairs(move)


def swap_u(s):
    return pairs(
        lambda x, zl, y, c, g: (x, zl, y ^ s, c, g) if c else (x ^ s, zl, y, c, g)
    )


def swap_v(s):
    return pairs(
        lambda x, zl, y, c, g: (x ^ s, zl, y, c, g) if c else (x, zl, y ^ s, c, g)
    )


def swap_plane():
    return pairs(lambda x, zl, y, c, g: (x, zl ^ 1, y, c, g))


def swap_core():
    return pairs(lambda x, zl, y, c, g: (x, zl, y, c ^ 1, g))


def send(array, pairing):
    return lax.ppermute(array, ("ctx", "head"), pairing)


def nt(a, b, **kw):
    return lax.dot_general(a, b, (((1,), (1,)), ((), ())), preferred_element_type=F32, **kw)


def nn(a, b):
    return lax.dot_general(a, b, (((1,), (0,)), ((), ())), preferred_element_type=F32)


def call(kernel, outs, scratch=(), limit=48, us=1.0, smem=1, in_hbm=0):
    def run(*args):
        vm = pl.BlockSpec(memory_space=pltpu.VMEM)
        sm = pl.BlockSpec(memory_space=pltpu.SMEM)
        return pl.pallas_call(
            kernel,
            out_shape=outs,
            in_specs=[sm] * smem
            + [vm] * (len(args) - smem - in_hbm)
            + [pl.BlockSpec(memory_space=pl.ANY)] * in_hbm,
            out_specs=jax.tree.map(lambda _: vm, outs),
            scratch_shapes=list(scratch),
            compiler_params=pltpu.CompilerParams(vmem_limit_bytes=limit * MIB),
            cost_estimate=pl.CostEstimate(
                flops=int(us * 1.1e9), bytes_accessed=0, transcendentals=0
            ),
        )(*args)

    return run


def sds(shape, dtype=BF):
    return jax.ShapeDtypeStruct(shape, dtype)


def column_of(owner):
    ctx = owner >> 1
    return ((ctx >> 4) << 2) | ((ctx >> 1) & 3)


def ranks(keys, classes, resets):
    n = keys.shape[1]
    blk = 256
    row = lax.broadcasted_iota(jnp.int32, (blk, blk), 0)
    col = lax.broadcasted_iota(jnp.int32, (blk, blk), 1)
    earlier = (row < col).astype(F32).astype(BF)
    label = lax.broadcasted_iota(jnp.int32, (classes, blk), 0)
    carry = jnp.zeros((classes, 1), F32)
    found, counts = [], []
    for b in range(n // blk):
        if b in resets:
            counts.append(carry)
            carry = jnp.zeros((classes, 1), F32)
        hot = (label == keys[:, b * blk : (b + 1) * blk]).astype(F32)
        before = nn(hot.astype(BF), earlier) + carry
        found.append(jnp.sum(hot * before, axis=0, keepdims=True))
        carry = carry + jnp.sum(hot, axis=1, keepdims=True)
    counts.append(carry)
    return jnp.concatenate(found, axis=1).astype(jnp.int32), counts


def most(counts, n):
    return jnp.broadcast_to(jnp.max(counts, axis=0, keepdims=True).astype(jnp.int32), (1, n))


def plan_kernel(
    at, con_ref, txt_ref, table_ref, q_ref, k_ref, v_ref, rows_ref, both_ref, img_ref, plan_ref
):
    ids = jnp.concatenate([con_ref[...], txt_ref[...]], axis=1)
    n = ids.shape[1]
    vocab_dev = table_ref.shape[0]
    owner = ids >> int(math.log2(vocab_dev))
    rank, (counts,) = ranks(owner, 128, ())
    hot_slot = lax.broadcasted_iota(jnp.int32, (SLOTS, n), 0) == rank
    hot_slot = (hot_slot & (owner == at[0])).astype(F32).astype(BF)
    hot_row = lax.broadcasted_iota(jnp.int32, (vocab_dev, n), 0) == (ids & (vocab_dev - 1))
    pick = nt(hot_slot, hot_row.astype(F32).astype(BF)).astype(BF)
    rows = nn(pick, table_ref[...]).astype(BF)
    rows_ref[...] = rows
    both_ref[0:SLOTS, :] = rows
    m = q_ref.shape[0]
    half = q_ref.shape[1] // 2
    mine = pl.ds(pl.multiple_of(at[2] * half, half), half)
    theirs = pl.ds(pl.multiple_of((1 - at[2]) * half, half), half)
    for i, ref in enumerate((q_ref, k_ref, v_ref)):
        img_ref[i * m : (i + 1) * m, :] = ref[:, mine]
        for j in range(2):
            lanes = slice((2 * i + j) * half, (2 * i + j + 1) * half)
            both_ref[SLOTS:, lanes] = ref[16 * j : 16 * (j + 1), theirs]
    both_ref[SLOTS:, 6 * half :] = jnp.zeros((16, 2 * half), BF)
    plan_ref[0:1, :] = rank
    plan_ref[1:2, :] = most(counts, n)
    plan_ref[2:8, :] = jnp.zeros((6, n), jnp.int32)


def to_row(column):
    n = column.shape[0]
    diagonal = lax.broadcasted_iota(jnp.int32, (n, n), 0) == lax.broadcasted_iota(
        jnp.int32, (n, n), 1
    )
    return jnp.sum(jnp.where(diagonal, column, 0.0), axis=0, keepdims=True)


def line_of(at, column):
    first, second = column >> 2, column & 3
    return jnp.where(at[2] == 0, first, second), jnp.where(at[2] == 0, second, first)


def line_plan(at, counts):
    u, v = line_of(at, lax.broadcasted_iota(jnp.int32, (16, 16), 0))
    u2, v2 = line_of(at, lax.broadcasted_iota(jnp.int32, (16, 16), 1))
    row = to_row(counts)
    same = v == v2
    before = same & ((u2 ^ at[4]) < (u ^ at[4]))
    skipped = jnp.sum(jnp.where(before, row, 0.0), axis=1, keepdims=True)
    total = jnp.sum(jnp.where(same, row, 0.0), axis=1, keepdims=True)
    other = jnp.sum(jnp.where(u == u2, row, 0.0), axis=1, keepdims=True)
    return skipped, total, jnp.max(jnp.maximum(total, other), axis=0, keepdims=True)


def per_lane(values, column):
    hot = lax.broadcasted_iota(jnp.int32, (16, column.shape[1]), 0) == column
    return jnp.sum(jnp.where(hot, values, 0.0), axis=0, keepdims=True)


def blocks_of(lanes, size, blocks):
    lane = lax.broadcasted_iota(jnp.int32, (1, lanes), 1)
    block = jnp.zeros((1, lanes), jnp.int32)
    for j in range(1, blocks):
        block = block + (lane >= j * size).astype(jnp.int32)
    return block, (lane - block * size).astype(F32)


def column_at(at, u, v):
    return jnp.where(at[2] == 0, u * 4 + v, v * 4 + u)


def line_targets(at, counts, skipped, slots):
    block, slot = blocks_of(4 * slots, slots, 4)
    column = column_at(at, block ^ at[4], jnp.zeros_like(block) + at[5])
    target = per_lane(skipped, column) + slot
    return jnp.where(slot < per_lane(counts, column), target, -1.0).astype(jnp.int32)


def line_bias(at, total, rows):
    block, slot = blocks_of(4 * rows, rows, 4)
    column = column_at(at, jnp.zeros_like(block) + at[4], block ^ at[5])
    return jnp.where(slot < per_lane(total, column), 0.0, -1e30)


def pack_kernel(
    at, con_ref, txt_ref, plan_ref, out_ref, spot_ref, con_bias, txt_bias, con_line, txt_line
):
    ids = jnp.concatenate([con_ref[...], txt_ref[...]], axis=1)
    n = ids.shape[1]
    n_con = con_ref.shape[1]
    owner = ids >> 8
    column = column_of(owner)
    spot, (con_counts, txt_counts) = ranks(column, 16, (n_con // 256,))
    con_skip, con_total, con_most = line_plan(at, con_counts)
    txt_skip, txt_total, txt_most = line_plan(at, txt_counts)
    con_bias[...] = line_bias(at, con_total, LINE_CON)
    txt_bias[...] = line_bias(at, txt_total, LINE_TXT)
    con_line[...] = line_targets(at, con_counts, con_skip, CON)
    txt_line[...] = line_targets(at, txt_counts, txt_skip, TXT)
    _, item_v = line_of(at, column)
    spot_ref[0:1, :] = (
        (item_v ^ at[5]) * LINE_CON + per_lane(con_skip, column).astype(jnp.int32) + spot
    )
    over = jnp.maximum(
        jnp.maximum(
            jnp.max(con_counts, axis=0, keepdims=True) - CON,
            jnp.max(txt_counts, axis=0, keepdims=True) - TXT,
        ),
        jnp.maximum(con_most - LINE_CON, txt_most - LINE_TXT),
    )
    spot_ref[1:2, :] = jnp.maximum(
        jnp.broadcast_to(over.astype(jnp.int32), (1, n)), plan_ref[1:2, :] - SLOTS
    )
    spot_ref[2:8, :] = jnp.zeros((6, n), jnp.int32)
    here = column == at[1]
    rank = plan_ref[0:1, :]
    concept = lax.broadcasted_iota(jnp.int32, (1, n), 1) < n_con
    target = jnp.where(
        concept, jnp.where(spot < CON, spot, -1), jnp.where(spot < TXT, spot + CON, -1)
    )
    z = ((owner & 1) << 1) | ((owner >> 4) & 1)
    core = (owner >> 1) & 1
    piece = jnp.where(core == at[2], 0, 4) + (at[3] ^ z)
    source = jnp.where(rank < SLOTS, piece * SLOTS + rank, -1)
    target = jnp.where(here, target, -1)
    source = jnp.where(here, source, -1)
    hot_t = (lax.broadcasted_iota(jnp.int32, (ROWS, n), 0) == target).astype(F32).astype(BF)
    hot_s = (lax.broadcasted_iota(jnp.int32, (8 * SLOTS, n), 0) == source).astype(F32).astype(BF)
    out_ref[...] = nt(hot_t, hot_s).astype(BF)


def project_kernel(at, pack_ref, *refs):
    rows, (mod_ref, gain_ref, w_hbm), outs = refs[:8], refs[8:11], refs[11:15]
    raw_ref, x_ref, w_ref, sems = refs[15:]
    half = w_ref.shape[2]
    lanes = pl.ds(pl.multiple_of(at[2] * half, half), half)
    copies = [
        pltpu.make_async_copy(w_hbm.at[j, :, lanes], w_ref.at[j], sems.at[j]) for j in range(3)
    ]
    for copy in copies:
        copy.start()
    for i, ref in enumerate(rows):
        raw_ref[i * SLOTS : (i + 1) * SLOTS, :] = ref[0:SLOTS, :]
    shift = mod_ref[0:1, :]
    scale = 1.0 + mod_ref[1:2, :]
    for i in range(ROWS // 32):
        block = slice(i * 32, (i + 1) * 32)
        values = nn(pack_ref[block, :], raw_ref[...])
        mean = jnp.mean(values, axis=1, keepdims=True)
        centered = values - mean
        var = jnp.mean(centered * centered, axis=1, keepdims=True)
        x_ref[block, :] = (centered * lax.rsqrt(var + 1e-06) * scale + shift).astype(BF)

    def normed(u, gain):
        meansq = jnp.mean(u * u, axis=1, keepdims=True)
        return u * lax.rsqrt(meansq + 1e-06) * gain

    copies[0].wait()
    q = nn(x_ref[0:CON, :], w_ref[0])
    copies[1].wait()
    k = nn(x_ref[...], w_ref[1])
    copies[2].wait()
    v = nn(x_ref[...], w_ref[2])
    heads = []
    for h in range(3):
        cols = slice(h * HD, (h + 1) * HD)
        heads.append(
            (
                (normed(q[:, cols], gain_ref[0:1, :]) * FACTOR).astype(BF),
                normed(k[:, cols], gain_ref[1:2, :]).astype(BF),
                v[:, cols].astype(BF),
            )
        )
    for s, out in enumerate(outs):
        head = jnp.minimum(at[4] ^ s, 2)
        for h in range(3):

            @pl.when(head == h)
            def _(h=h, out=out):
                out[0:ROWS, 0:HD] = heads[h][1]
                out[0:ROWS, HD:] = heads[h][2]
                out[ROWS:, 0:HD] = heads[h][0][: CON // 2]
                out[ROWS:, HD:] = heads[h][0][CON // 2 :]


def join_kernel(a, b, c, d, con_line, txt_line, out, con, txt):
    for i, ref in enumerate((a, b, c, d)):
        con[i * CON : (i + 1) * CON, 0 : 2 * HD] = ref[0:CON, :]
        con[i * CON : i * CON + CON // 2, 2 * HD :] = ref[ROWS:, 0:HD]
        con[i * CON + CON // 2 : (i + 1) * CON, 2 * HD :] = ref[ROWS:, HD:]
        txt[i * TXT : (i + 1) * TXT, :] = ref[CON:ROWS, :]
    hot = lax.broadcasted_iota(jnp.int32, (LINE_CON, 4 * CON), 0) == con_line[...]
    found = nn(hot.astype(F32).astype(BF), con[...]).astype(BF)
    out[0:LINE_CON, :] = found[:, 0 : 2 * HD]
    out[LINE:, 0:HD] = found[: LINE_CON // 2, 2 * HD :]
    out[LINE:, HD:] = found[LINE_CON // 2 :, 2 * HD :]
    hot = lax.broadcasted_iota(jnp.int32, (LINE_TXT, 4 * TXT), 0) == txt_line[...]
    out[LINE_CON:LINE, :] = nn(hot.astype(F32).astype(BF), txt[...]).astype(BF)


def image_heads_kernel(at, own, core, *outs):
    n, half = own.shape[0] // 3, own.shape[1]
    for s, out in enumerate(outs):
        head = jnp.minimum(at[4] ^ s, 2)
        lanes = pl.ds(pl.multiple_of(head * HD, HD), HD)
        for i in range(3):
            row = 2 * i * n
            out[row : row + n, :] = own[i * n : (i + 1) * n, lanes]
            for j in range(2):
                there = pl.ds(pl.multiple_of((2 * i + j) * half + head * HD, HD), HD)
                out[row + n + 16 * j : row + n + 16 * (j + 1), :] = core[SLOTS:, there]


def image_join_kernel(a, b, c, d, q_out, kv_out):
    n = a.shape[0] // 3
    for i, ref in enumerate((a, b, c, d)):
        q_out[n * i : n * (i + 1), :] = ref[0:n, :]
        kv_out[n * i : n * (i + 1), :] = ref[n : 2 * n, :]
        kv_out[n * (4 + i) : n * (5 + i), :] = ref[2 * n :, :]


def planes_kernel(own, other, out):
    n = own.shape[0] // 2
    for i, ref in enumerate((own, other)):
        out[n * i : n * (i + 1), :] = ref[0:n, :]
        out[n * (2 + i) : n * (3 + i), :] = ref[n:, :]


def weigh(q, parts, factor):
    scores = []
    for keys, _, bias in parts:
        part = nt(q, keys)
        scores.append(part if bias is None else part + bias)
    peak = scores[0].max(axis=1, keepdims=True)
    for part in scores[1:]:
        peak = jnp.maximum(peak, part.max(axis=1, keepdims=True))
    total = None
    for part, (_, values, _) in zip(scores, parts):
        power = part - peak
        weights = jnp.exp2(power if factor is None else power * factor).astype(BF)
        summed = nn(weights, values)
        total = summed if total is None else total + summed
    return (peak if factor is None else peak * factor), total


def join(first, second):
    peak = jnp.maximum(first[0], second[0])
    return peak, first[1] * jnp.exp2(first[0] - peak) + second[1] * jnp.exp2(second[0] - peak)


def merge(first, second):
    _, summed = join(first, second)
    return (summed[:, 0:HD] / summed[:, HD:]).astype(BF)


def with_ones(values):
    return jnp.concatenate([values, jnp.ones_like(values)], axis=1)


def image_self_kernel(i0, i1, i2, i3, q, keys, vals, peak, summed):
    part = i0.shape[0] // 2
    for i, ref in enumerate((i0, i1, i2, i3)):
        keys[i * part : (i + 1) * part, :] = ref[0:part, :]
        vals[i * part : (i + 1) * part, :] = with_ones(ref[part:, :])
    peak[...], summed[...] = weigh(q[...], ((keys[...], vals[...], None),), FACTOR)


def prompt_kernel(pick, l0, l1, l2, l3, con_bias, txt_bias, keys, vals, img_q, im, ims, *refs):
    outs, (con_q, con_k, con_v, txt_k, txt_v, con_out) = refs[:4], refs[4:]
    n, m = LINE_CON, LINE_TXT
    for a, ref in enumerate((l0, l1, l2, l3)):
        con_q[a * n : a * n + n // 2, :] = ref[LINE:, 0:HD]
        con_q[a * n + n // 2 : (a + 1) * n, :] = ref[LINE:, HD:]
        con_k[a * n : (a + 1) * n, :] = ref[0:n, 0:HD]
        con_v[a * n : (a + 1) * n, :] = with_ones(ref[0:n, HD:])
        txt_k[a * m : (a + 1) * m, :] = ref[n:LINE, 0:HD]
        txt_v[a * m : (a + 1) * m, :] = with_ones(ref[n:LINE, HD:])
    text = weigh(img_q[...], ((txt_k[...], txt_v[...], txt_bias[...]),), FACTOR)
    img = merge(text, (im[...], ims[...]))
    n_con = con_out.shape[0]
    for b in range(n_con // 256):
        rows = slice(b * 256, (b + 1) * 256)
        q = nn(pick[rows, :], con_q[...]).astype(BF)
        parts = ((keys[...], vals[...], None), (con_k[...], con_v[...], con_bias[...]))
        _, summed = weigh(q, parts, None)
        con_out[rows, :] = (summed[:, 0:HD] / summed[:, HD:]).astype(BF)
    dots = nt(img, con_out[...]).astype(BF)
    con_f = con_out[...].astype(F32)
    con_sq = nt(jnp.ones((16, HD), F32), con_f * con_f, precision=lax.Precision.HIGHEST).astype(BF)
    for s, out in enumerate(outs):
        rows = slice(s * 64, (s + 1) * 64)
        out[0:64, 0:n_con] = dots[rows]
        out[0:64, n_con:] = img[rows]
        out[64:80, 0:n_con] = con_sq
        out[64:80, n_con:] = jnp.zeros((16, HD), BF)


def head_sum_kernel(at, b0, b1, b2, b3, own, core, out_own):
    n_con = b0.shape[1] - HD
    total = jnp.zeros((80, n_con), F32)
    outs = [jnp.zeros((64, HD), BF) for _ in range(3)]
    for s, ref in enumerate((b0, b1, b2, b3)):
        head = at[4] ^ s
        total = total + jnp.where(head < 3, ref[:, 0:n_con].astype(F32), 0.0)
        for h in range(3):
            outs[h] = jnp.where(head == h, ref[0:64, n_con:], outs[h])
    image_sq = jnp.zeros((64, 1), F32)
    for h in range(3):
        out_f = outs[h].astype(F32)
        image_sq = image_sq + jnp.sum(out_f * out_f, axis=1, keepdims=True)
    image_sq = jnp.broadcast_to(image_sq, (64, HD)).astype(BF)
    total = total.astype(BF)
    for ref, row in ((own, 0), (core, 32)):
        ref[0:32, 0:n_con] = total[row : row + 32]
        ref[32:48, 0:n_con] = total[64:80]
        ref[0:32, n_con : n_con + HD] = image_sq[row : row + 32]
        ref[32:48, n_con : n_con + HD] = jnp.zeros((16, HD), BF)
    for h in range(3):
        lanes = slice(n_con + (1 + h) * HD, n_con + (2 + h) * HD)
        core[0:32, lanes] = outs[h][32:64]
        core[32:48, lanes] = jnp.zeros((16, HD), BF)
        out_own[:, h * HD : (h + 1) * HD] = outs[h][0:32]


def core_sum_kernel(own, core, out):
    cols = own.shape[1]
    out[...] = (own[...].astype(F32) + core[:, 0:cols].astype(F32)).astype(BF)


def finish_kernel(at, own, head, core, out_own, img_ref, sal_ref):
    n_con = own.shape[1] - HD
    width = 12 * HD
    total = own[...].astype(F32) + head[...].astype(F32)
    con_rms = jnp.sqrt(total[32:33, 0:n_con] / width + 1e-06)
    img_rms = jnp.sqrt(total[0:32, n_con : n_con + 1] / width + 1e-06)
    sal_ref[...] = total[0:32, 0:n_con] / (math.sqrt(width) * con_rms * img_rms)
    half = 3 * HD
    mine = pl.ds(pl.multiple_of(at[2] * half, half), half)
    theirs = pl.ds(pl.multiple_of((1 - at[2]) * half, half), half)
    img_ref[:, mine] = out_own[...]
    img_ref[:, theirs] = core[0:32, n_con + HD :]


def packed(
    img_q, img_k, img_v, txt_ids, concept_ids, step_index, token_table, modulation, txt_qkv, qk_gain
):
    n_con, n_txt = concept_ids.shape[0], txt_ids.shape[0]
    ctx = lax.axis_index("ctx")
    g = lax.axis_index("head")
    c = ctx & 1
    y = (ctx >> 1) & 3
    zl = (ctx >> 3) & 1
    x = ctx >> 4
    u = jnp.where(c == 0, x, y)
    v = jnp.where(c == 0, y, x)
    at = jnp.stack([ctx * 2 + g, x * 4 + y, c, 2 * g + zl, u, v]).astype(jnp.int32)
    con_ids, text_ids = concept_ids[None, :], txt_ids[None, :]
    n = n_con + n_txt
    width = token_table.shape[1]
    half = txt_qkv.shape[2] // 2
    n_img = img_q.shape[0]

    own_rows, own_both, own_img, plan = call(
        plan_kernel,
        (
            sds((SLOTS, width)),
            sds((SLOTS + 16, width)),
            sds((3 * n_img, half)),
            sds((8, n), jnp.int32),
        ),
    )(at, con_ids, text_ids, token_table, img_q, img_k, img_v)
    far_rows = send(own_rows, swap_z(2))
    column_rows = [own_rows] + [send(own_rows, swap_z(s)) for s in (1, 3)]
    core_both = send(own_both, swap_core())

    pack, spots, con_bias, txt_bias, con_line, txt_line = call(
        pack_kernel,
        (
            sds((ROWS, 8 * SLOTS)),
            sds((8, n), jnp.int32),
            sds((1, 4 * LINE_CON), F32),
            sds((1, 4 * LINE_TXT), F32),
            sds((1, 4 * CON), jnp.int32),
            sds((1, 4 * TXT), jnp.int32),
        ),
    )(at, con_ids, text_ids, plan)
    con_slot = spots[0, :n_con]
    pick = (con_slot[:, None] == jnp.arange(4 * LINE_CON)[None, :]).astype(BF)
    shift_scale = lax.dynamic_index_in_dim(modulation, step_index[0], 0, keepdims=False)
    fits = (spots[1, 0] <= 0).astype(jnp.int32)

    image_blocks = call(
        image_heads_kernel, tuple(sds((6 * n_img, HD)) for _ in range(4))
    )(at, own_img, core_both)
    image_blocks = [image_blocks[0]] + [send(image_blocks[s], swap_u(s)) for s in (2, 1, 3)]
    image_blocks = [image_blocks[0], image_blocks[2], image_blocks[1], image_blocks[3]]
    column_rows[1], image_blocks[2] = lax.optimization_barrier((column_rows[1], image_blocks[2]))
    far_rows, pack, shift_scale, fits, image_blocks[1] = lax.optimization_barrier(
        (far_rows, pack, shift_scale, fits, image_blocks[1])
    )
    column_rows.insert(2, far_rows)
    other_rows = [core_both] + [send(r, swap_core()) for r in column_rows[1:]]

    qkv = call(
        project_kernel,
        tuple(sds((ROWS + CON // 2, 2 * HD)) for _ in range(4)),
        scratch=(
            pltpu.VMEM((8 * SLOTS, width), BF),
            pltpu.VMEM((ROWS, width), BF),
            pltpu.VMEM((3, width, half), BF),
            pltpu.SemaphoreType.DMA((3,)),
        ),
        us=PROJ_US,
        in_hbm=1,
    )(at, pack, *column_rows, *other_rows, shift_scale, qk_gain, jnp.transpose(txt_qkv, (1, 0, 2)))

    *image_blocks, first = lax.optimization_barrier((*image_blocks, qkv[0]))
    image_q, image_kv = call(
        image_join_kernel, (sds((8 * n_img, HD)), sds((16 * n_img, HD))), smem=0
    )(*image_blocks)
    other_kv = send(image_kv, swap_plane())
    qkv = [first] + [send(qkv[s], swap_u(s)) for s in (2, 1, 3)]
    qkv = [qkv[0], qkv[2], qkv[1], qkv[3]]
    other_kv, *qkv = lax.optimization_barrier((other_kv, *qkv))
    planes = call(planes_kernel, sds((32 * n_img, HD)), smem=0)(image_kv, other_kv)
    image_kvs = [planes] + [send(planes, swap_v(s)) for s in (2, 1, 3)]
    line = call(
        join_kernel,
        sds((LINE + LINE_CON // 2, 2 * HD)),
        scratch=(pltpu.VMEM((4 * CON, 3 * HD), BF), pltpu.VMEM((4 * TXT, 2 * HD), BF)),
        smem=0,
    )(*qkv, con_line, txt_line)
    lines = [line] + [send(line, swap_v(s)) for s in (2, 1, 3)]
    lines = [lines[0], lines[2], lines[1], lines[3]]

    all_img = 64 * n_img
    image_self = call(
        image_self_kernel,
        (
            sds((all_img, HD)),
            sds((all_img, 2 * HD)),
            sds((8 * n_img, 1), F32),
            sds((8 * n_img, 2 * HD), F32),
        ),
        us=2.0,
        smem=0,
    )
    keys, vals, *image_stats = image_self(*image_kvs, image_q)
    blocks = call(
        prompt_kernel,
        tuple(sds((80, n_con + HD)) for _ in range(4)),
        scratch=(
            pltpu.VMEM((4 * LINE_CON, HD), BF),
            pltpu.VMEM((4 * LINE_CON, HD), BF),
            pltpu.VMEM((4 * LINE_CON, 2 * HD), BF),
            pltpu.VMEM((4 * LINE_TXT, HD), BF),
            pltpu.VMEM((4 * LINE_TXT, 2 * HD), BF),
            pltpu.VMEM((n_con, HD), BF),
        ),
        us=PROMPT_US,
        smem=0,
    )(pick, *lines, con_bias, txt_bias, keys, vals, image_q, *image_stats)
    blocks = [blocks[0]] + [send(blocks[s], swap_u(s)) for s in (2, 1, 3)]
    blocks = [blocks[0], blocks[2], blocks[1], blocks[3]]
    own, core, out_own = call(
        head_sum_kernel,
        (sds((48, n_con + HD)), sds((48, n_con + 4 * HD)), sds((32, half))),
    )(at, *blocks)
    core = send(core, swap_core())
    own = call(core_sum_kernel, sds((48, n_con + HD)), smem=0)(own, core)
    last = (at, own, send(own, swap_z(2)), core, out_own)
    finish = call(finish_kernel, (sds((n_img, 2 * half)), sds((n_img, n_con), F32)))

    def finished():
        img_out, saliency = finish(*last)
        return img_out, jnp.transpose(saliency)

    return fits > 0, finished


def on_device(*args):
    fits, finish = packed(*args)
    return lax.cond(fits, finish, lambda: tuple(general(*args)))


def solution(mesh):
    return jax.shard_map(
        on_device,
        mesh=mesh,
        in_specs=(
            P("ctx", "head"),
            P("ctx", "head"),
            P("ctx", "head"),
            P(),
            P(),
            P(),
            P(("ctx", "head"), None),
            P(),
            P(None, None, "head"),
            P(),
        ),
        out_specs=(P("ctx", "head"), P(None, "ctx")),
        check_vma=False,
    )
```

```python
import math

import jax
import jax.numpy as jnp
from jax import lax
from jax.experimental import pallas as pl
from jax.experimental.pallas import tpu as pltpu
from jax.sharding import PartitionSpec as P

BF = jnp.bfloat16
F32 = jnp.float32
HD = 128
SLOTS = 32
CON = 96
TXT = 64
ROWS = CON + TXT
LINE_CON = 320
LINE_TXT = 176
LINE = LINE_CON + LINE_TXT
MIB = 1 << 20
PROJ_US, NEAR_US, FAR_US = 5.0, 6.0, 3.0
FACTOR = HD ** (-0.5) * math.log2(math.e)


def modulate(rows, shift_scale):
    values = rows.astype(F32)
    mean = jnp.mean(values, axis=1, keepdims=True)
    centered = values - mean
    var = jnp.mean(centered * centered, axis=1, keepdims=True)
    normed = centered * lax.rsqrt(var + 1e-06)
    return (normed * (1.0 + shift_scale[1]) + shift_scale[0]).astype(BF)


def head_norm(values, gain, head_dim):
    shaped = values.reshape(values.shape[0], -1, head_dim)
    meansq = jnp.mean(shaped * shaped, axis=2, keepdims=True)
    return (shaped * lax.rsqrt(meansq + 1e-06) * gain).reshape(values.shape[0], -1)


def block_stats(queries, keys, values):
    scores = jnp.einsum("rgd,kgd->grk", queries, keys, preferred_element_type=F32)
    scores = scores * queries.shape[-1] ** (-0.5)
    peak = jnp.max(scores, axis=2)
    weights = jnp.exp(scores - peak[:, :, None])
    total = jnp.sum(weights, axis=2)
    summed = jnp.einsum("grk,kgd->grd", weights.astype(BF), values, preferred_element_type=F32)
    return (peak, total, summed)


def combine_stats(first, second):
    peak = jnp.maximum(first[0], second[0])
    left = jnp.exp(first[0] - peak)
    right = jnp.exp(second[0] - peak)
    total = first[1] * left + second[1] * right
    summed = first[2] * left[:, :, None] + second[2] * right[:, :, None]
    return (peak, total, summed)


def scaled_scores(dots, concept_sq, image_sq, width):
    concept_rms = jnp.sqrt(concept_sq / width + 1e-06)
    image_rms = jnp.sqrt(image_sq / width + 1e-06)
    return dots / (jnp.sqrt(F32(width)) * concept_rms[:, None] * image_rms[None, :])


def gather_ctx(block):
    n_ctx = lax.axis_size("ctx")
    spread = jnp.broadcast_to(block[None], (n_ctx,) + block.shape)
    return lax.all_to_all(spread, "ctx", 0, 0, tiled=True)


def general(
    img_q, img_k, img_v, txt_ids, concept_ids, step_index, token_table, modulation, txt_qkv, qk_gain
):
    n_ctx = lax.axis_size("ctx")
    n_head = lax.axis_size("head")
    head_dim = qk_gain.shape[1]
    group = img_q.shape[1] // head_dim
    text_dev = txt_ids.shape[0] // n_ctx
    concept_dev = concept_ids.shape[0] // n_ctx
    vocab_dev = token_table.shape[0]
    combined = jnp.concatenate(
        [txt_ids.reshape(n_ctx, text_dev), concept_ids.reshape(n_ctx, concept_dev)], axis=1
    ).reshape(-1)
    offset = lax.axis_index(("ctx", "head")) * vocab_dev
    wanted = combined - offset
    inside = (wanted >= 0) & (wanted < vocab_dev)
    picked = jnp.take(token_table, jnp.clip(wanted, 0, vocab_dev - 1), axis=0)
    n_all = n_ctx * n_head
    mine = jnp.where(inside[:, None], picked, jnp.zeros((), picked.dtype))
    parts = lax.all_to_all(
        mine.reshape(n_all, -1, mine.shape[1]), ("ctx", "head"), 0, 0, tiled=True
    )
    own_rows = jnp.sum(parts.astype(F32), axis=0)
    prompt_rows = lax.all_gather(own_rows.astype(BF), "head", axis=0, tiled=True)
    shift_scale = lax.dynamic_index_in_dim(modulation, step_index[0], 0, keepdims=False)
    modded = modulate(prompt_rows, shift_scale)
    text_mod = modded[:text_dev]
    concept_mod = modded[text_dev:]
    text_kv = jnp.einsum("rd,dgc->rgc", text_mod, txt_qkv[:, 1:], preferred_element_type=F32)
    concept_qkv = jnp.einsum("rd,dgc->rgc", concept_mod, txt_qkv, preferred_element_type=F32)
    text_keys = head_norm(text_kv[:, 0], qk_gain[1], head_dim).astype(BF)
    text_values = text_kv[:, 1].astype(BF)
    concept_queries = head_norm(concept_qkv[:, 0], qk_gain[0], head_dim).astype(BF)
    concept_keys = head_norm(concept_qkv[:, 1], qk_gain[1], head_dim).astype(BF)
    concept_values = concept_qkv[:, 2].astype(BF)
    local_kv = jnp.stack(
        [
            jnp.concatenate([text_keys, concept_keys], axis=0),
            jnp.concatenate([text_values, concept_values], axis=0),
        ]
    )
    prompt_kv = gather_ctx(local_kv)
    text_part = jnp.swapaxes(prompt_kv[:, :, :text_dev], 0, 1).reshape(2, -1, group, head_dim)
    concept_part = jnp.swapaxes(prompt_kv[:, :, text_dev:], 0, 1).reshape(2, -1, group, head_dim)
    image_queries = img_q.reshape(-1, group, head_dim)
    concept_q3 = concept_queries.reshape(-1, group, head_dim)
    first = block_stats(image_queries, text_part[0], text_part[1])
    second = block_stats(concept_q3, concept_part[0], concept_part[1])
    start_stats = (
        jnp.concatenate([first[0], second[0]], axis=1),
        jnp.concatenate([first[1], second[1]], axis=1),
        jnp.concatenate([first[2], second[2]], axis=1),
    )
    all_queries = jnp.concatenate([image_queries, concept_q3], axis=0)
    image_kv = gather_ctx(jnp.stack([img_k, img_v]))
    keys = image_kv[:, 0].reshape(-1, group, head_dim)
    values = image_kv[:, 1].reshape(-1, group, head_dim)
    peak, total, summed = combine_stats(start_stats, block_stats(all_queries, keys, values))
    attended = (
        jnp.transpose(summed / total[:, :, None], (1, 0, 2))
        .reshape(all_queries.shape[0], -1)
        .astype(BF)
    )
    img_rows = img_q.shape[0]
    img_out = attended[:img_rows]
    concept_out = attended[img_rows:]
    concept_all = gather_ctx(concept_out).reshape(-1, concept_out.shape[1])
    dots = lax.dot_general(
        concept_all, img_out, (((1,), (1,)), ((), ())), preferred_element_type=F32
    )
    image_f = img_out.astype(F32)
    concept_f = concept_all.astype(F32)
    image_sq = jnp.sum(image_f * image_f, axis=1)
    concept_sq = jnp.sum(concept_f * concept_f, axis=1)
    width = group * head_dim * n_head
    sums = jnp.concatenate(
        [
            jnp.concatenate([dots, concept_sq[:, None]], axis=1),
            jnp.concatenate([image_sq, jnp.zeros((1,), F32)])[None],
        ]
    ).astype(BF)
    other = lax.ppermute(sums, "head", [(0, 1), (1, 0)])
    sums = sums.astype(F32) + other.astype(F32)
    concepts = dots.shape[0]
    saliency = scaled_scores(
        sums[:concepts, :img_rows], sums[:concepts, img_rows], sums[concepts, :img_rows], width
    )
    return (img_out, saliency)


def place(x, zl, y, c, g):
    return ((((x * 2 + zl) * 4 + y) * 2 + c) * 2) + g


def pairs(move):
    found = []
    for x in range(4):
        for zl in range(2):
            for y in range(4):
                for c in range(2):
                    for g in range(2):
                        found.append((place(x, zl, y, c, g), place(*move(x, zl, y, c, g))))
    return found


def swap_z(s):
    def move(x, zl, y, c, g):
        z = (2 * g + zl) ^ s
        return x, z & 1, y, c, z >> 1

    return pairs(move)


def swap_u(s):
    return pairs(
        lambda x, zl, y, c, g: (x, zl, y ^ s, c, g) if c else (x ^ s, zl, y, c, g)
    )


def swap_v(s):
    return pairs(
        lambda x, zl, y, c, g: (x ^ s, zl, y, c, g) if c else (x, zl, y ^ s, c, g)
    )


def swap_plane():
    return pairs(lambda x, zl, y, c, g: (x, zl ^ 1, y, c, g))


def swap_core():
    return pairs(lambda x, zl, y, c, g: (x, zl, y, c ^ 1, g))


def send(array, pairing):
    return lax.ppermute(array, ("ctx", "head"), pairing)


def nt(a, b, **kw):
    return lax.dot_general(a, b, (((1,), (1,)), ((), ())), preferred_element_type=F32, **kw)


def nn(a, b):
    return lax.dot_general(a, b, (((1,), (0,)), ((), ())), preferred_element_type=F32)


def call(kernel, outs, scratch=(), limit=48, us=1.0, smem=1, in_hbm=0):
    def run(*args):
        vm = pl.BlockSpec(memory_space=pltpu.VMEM)
        sm = pl.BlockSpec(memory_space=pltpu.SMEM)
        return pl.pallas_call(
            kernel,
            out_shape=outs,
            in_specs=[sm] * smem
            + [vm] * (len(args) - smem - in_hbm)
            + [pl.BlockSpec(memory_space=pl.ANY)] * in_hbm,
            out_specs=jax.tree.map(lambda _: vm, outs),
            scratch_shapes=list(scratch),
            compiler_params=pltpu.CompilerParams(vmem_limit_bytes=limit * MIB),
            cost_estimate=pl.CostEstimate(
                flops=int(us * 1.1e9), bytes_accessed=0, transcendentals=0
            ),
        )(*args)

    return run


def sds(shape, dtype=BF):
    return jax.ShapeDtypeStruct(shape, dtype)


def column_of(owner):
    ctx = owner >> 1
    return ((ctx >> 4) << 2) | ((ctx >> 1) & 3)


def ranks(keys, classes, resets):
    n = keys.shape[1]
    blk = 256
    row = lax.broadcasted_iota(jnp.int32, (blk, blk), 0)
    col = lax.broadcasted_iota(jnp.int32, (blk, blk), 1)
    earlier = (row < col).astype(F32).astype(BF)
    label = lax.broadcasted_iota(jnp.int32, (classes, blk), 0)
    carry = jnp.zeros((classes, 1), F32)
    found, counts = [], []
    for b in range(n // blk):
        if b in resets:
            counts.append(carry)
            carry = jnp.zeros((classes, 1), F32)
        hot = (label == keys[:, b * blk : (b + 1) * blk]).astype(F32)
        before = nn(hot.astype(BF), earlier) + carry
        found.append(jnp.sum(hot * before, axis=0, keepdims=True))
        carry = carry + jnp.sum(hot, axis=1, keepdims=True)
    counts.append(carry)
    return jnp.concatenate(found, axis=1).astype(jnp.int32), counts


def most(counts, n):
    return jnp.broadcast_to(jnp.max(counts, axis=0, keepdims=True).astype(jnp.int32), (1, n))


def plan_kernel(
    at, con_ref, txt_ref, table_ref, q_ref, k_ref, v_ref, rows_ref, both_ref, img_ref, plan_ref
):
    ids = jnp.concatenate([con_ref[...], txt_ref[...]], axis=1)
    n = ids.shape[1]
    vocab_dev = table_ref.shape[0]
    owner = ids >> int(math.log2(vocab_dev))
    rank, (counts,) = ranks(owner, 128, ())
    hot_slot = lax.broadcasted_iota(jnp.int32, (SLOTS, n), 0) == rank
    hot_slot = (hot_slot & (owner == at[0])).astype(F32).astype(BF)
    hot_row = lax.broadcasted_iota(jnp.int32, (vocab_dev, n), 0) == (ids & (vocab_dev - 1))
    pick = nt(hot_slot, hot_row.astype(F32).astype(BF)).astype(BF)
    rows = nn(pick, table_ref[...]).astype(BF)
    rows_ref[...] = rows
    both_ref[0:SLOTS, :] = rows
    m = q_ref.shape[0]
    half = q_ref.shape[1] // 2
    mine = pl.ds(pl.multiple_of(at[2] * half, half), half)
    theirs = pl.ds(pl.multiple_of((1 - at[2]) * half, half), half)
    for i, ref in enumerate((q_ref, k_ref, v_ref)):
        img_ref[i * m : (i + 1) * m, :] = ref[:, mine]
        for j in range(2):
            lanes = slice((2 * i + j) * half, (2 * i + j + 1) * half)
            both_ref[SLOTS:, lanes] = ref[16 * j : 16 * (j + 1), theirs]
    both_ref[SLOTS:, 6 * half :] = jnp.zeros((16, 2 * half), BF)
    plan_ref[0:1, :] = rank
    plan_ref[1:2, :] = most(counts, n)
    plan_ref[2:8, :] = jnp.zeros((6, n), jnp.int32)


def to_row(column):
    n = column.shape[0]
    diagonal = lax.broadcasted_iota(jnp.int32, (n, n), 0) == lax.broadcasted_iota(
        jnp.int32, (n, n), 1
    )
    return jnp.sum(jnp.where(diagonal, column, 0.0), axis=0, keepdims=True)


def line_of(at, column):
    first, second = column >> 2, column & 3
    return jnp.where(at[2] == 0, first, second), jnp.where(at[2] == 0, second, first)


def line_plan(at, counts):
    u, v = line_of(at, lax.broadcasted_iota(jnp.int32, (16, 16), 0))
    u2, v2 = line_of(at, lax.broadcasted_iota(jnp.int32, (16, 16), 1))
    row = to_row(counts)
    same = v == v2
    before = same & ((u2 ^ at[4]) < (u ^ at[4]))
    skipped = jnp.sum(jnp.where(before, row, 0.0), axis=1, keepdims=True)
    total = jnp.sum(jnp.where(same, row, 0.0), axis=1, keepdims=True)
    other = jnp.sum(jnp.where(u == u2, row, 0.0), axis=1, keepdims=True)
    return skipped, total, jnp.max(jnp.maximum(total, other), axis=0, keepdims=True)


def per_lane(values, column):
    hot = lax.broadcasted_iota(jnp.int32, (16, column.shape[1]), 0) == column
    return jnp.sum(jnp.where(hot, values, 0.0), axis=0, keepdims=True)


def blocks_of(lanes, size, blocks):
    lane = lax.broadcasted_iota(jnp.int32, (1, lanes), 1)
    block = jnp.zeros((1, lanes), jnp.int32)
    for j in range(1, blocks):
        block = block + (lane >= j * size).astype(jnp.int32)
    return block, (lane - block * size).astype(F32)


def column_at(at, u, v):
    return jnp.where(at[2] == 0, u * 4 + v, v * 4 + u)


def line_targets(at, counts, skipped, slots):
    block, slot = blocks_of(4 * slots, slots, 4)
    column = column_at(at, block ^ at[4], jnp.zeros_like(block) + at[5])
    target = per_lane(skipped, column) + slot
    return jnp.where(slot < per_lane(counts, column), target, -1.0).astype(jnp.int32)


def line_bias(at, total, rows):
    block, slot = blocks_of(4 * rows, rows, 4)
    column = column_at(at, jnp.zeros_like(block) + at[4], block ^ at[5])
    return jnp.where(slot < per_lane(total, column), 0.0, -1e30)


def pack_kernel(
    at, con_ref, txt_ref, plan_ref, out_ref, spot_ref, con_bias, txt_bias, con_line, txt_line
):
    ids = jnp.concatenate([con_ref[...], txt_ref[...]], axis=1)
    n = ids.shape[1]
    n_con = con_ref.shape[1]
    owner = ids >> 8
    column = column_of(owner)
    spot, (con_counts, txt_counts) = ranks(column, 16, (n_con // 256,))
    con_skip, con_total, con_most = line_plan(at, con_counts)
    txt_skip, txt_total, txt_most = line_plan(at, txt_counts)
    con_bias[...] = line_bias(at, con_total, LINE_CON)
    txt_bias[...] = line_bias(at, txt_total, LINE_TXT)
    con_line[...] = line_targets(at, con_counts, con_skip, CON)
    txt_line[...] = line_targets(at, txt_counts, txt_skip, TXT)
    _, item_v = line_of(at, column)
    spot_ref[0:1, :] = (
        (item_v ^ at[5]) * LINE_CON + per_lane(con_skip, column).astype(jnp.int32) + spot
    )
    over = jnp.maximum(
        jnp.maximum(
            jnp.max(con_counts, axis=0, keepdims=True) - CON,
            jnp.max(txt_counts, axis=0, keepdims=True) - TXT,
        ),
        jnp.maximum(con_most - LINE_CON, txt_most - LINE_TXT),
    )
    spot_ref[1:2, :] = jnp.maximum(
        jnp.broadcast_to(over.astype(jnp.int32), (1, n)), plan_ref[1:2, :] - SLOTS
    )
    spot_ref[2:8, :] = jnp.zeros((6, n), jnp.int32)
    here = column == at[1]
    rank = plan_ref[0:1, :]
    concept = lax.broadcasted_iota(jnp.int32, (1, n), 1) < n_con
    target = jnp.where(
        concept, jnp.where(spot < CON, spot, -1), jnp.where(spot < TXT, spot + CON, -1)
    )
    z = ((owner & 1) << 1) | ((owner >> 4) & 1)
    core = (owner >> 1) & 1
    piece = jnp.where(core == at[2], 0, 4) + (at[3] ^ z)
    source = jnp.where(rank < SLOTS, piece * SLOTS + rank, -1)
    target = jnp.where(here, target, -1)
    source = jnp.where(here, source, -1)
    hot_t = (lax.broadcasted_iota(jnp.int32, (ROWS, n), 0) == target).astype(F32).astype(BF)
    hot_s = (lax.broadcasted_iota(jnp.int32, (8 * SLOTS, n), 0) == source).astype(F32).astype(BF)
    out_ref[...] = nt(hot_t, hot_s).astype(BF)


def project_kernel(at, pack_ref, *refs):
    rows, (mod_ref, gain_ref, w_hbm), outs = refs[:8], refs[8:11], refs[11:15]
    raw_ref, x_ref, w_ref, sems = refs[15:]
    half = w_ref.shape[2]
    lanes = pl.ds(pl.multiple_of(at[2] * half, half), half)
    copies = [
        pltpu.make_async_copy(w_hbm.at[j, :, lanes], w_ref.at[j], sems.at[j]) for j in range(3)
    ]
    for copy in copies:
        copy.start()
    for i, ref in enumerate(rows):
        raw_ref[i * SLOTS : (i + 1) * SLOTS, :] = ref[0:SLOTS, :]
    shift = mod_ref[0:1, :]
    scale = 1.0 + mod_ref[1:2, :]
    for i in range(ROWS // 32):
        block = slice(i * 32, (i + 1) * 32)
        values = nn(pack_ref[block, :], raw_ref[...])
        mean = jnp.mean(values, axis=1, keepdims=True)
        centered = values - mean
        var = jnp.mean(centered * centered, axis=1, keepdims=True)
        x_ref[block, :] = (centered * lax.rsqrt(var + 1e-06) * scale + shift).astype(BF)

    def normed(u, gain):
        meansq = jnp.mean(u * u, axis=1, keepdims=True)
        return u * lax.rsqrt(meansq + 1e-06) * gain

    copies[0].wait()
    q = nn(x_ref[0:CON, :], w_ref[0])
    copies[1].wait()
    k = nn(x_ref[...], w_ref[1])
    copies[2].wait()
    v = nn(x_ref[...], w_ref[2])
    heads = []
    for h in range(3):
        cols = slice(h * HD, (h + 1) * HD)
        heads.append(
            (
                (normed(q[:, cols], gain_ref[0:1, :]) * FACTOR).astype(BF),
                normed(k[:, cols], gain_ref[1:2, :]).astype(BF),
                v[:, cols].astype(BF),
            )
        )
    for s, out in enumerate(outs):
        head = jnp.minimum(at[4] ^ s, 2)
        for h in range(3):

            @pl.when(head == h)
            def _(h=h, out=out):
                out[0:ROWS, 0:HD] = heads[h][1]
                out[0:ROWS, HD:] = heads[h][2]
                out[ROWS:, 0:HD] = heads[h][0][: CON // 2]
                out[ROWS:, HD:] = heads[h][0][CON // 2 :]


def join_kernel(a, b, c, d, con_line, txt_line, out, con, txt):
    for i, ref in enumerate((a, b, c, d)):
        con[i * CON : (i + 1) * CON, 0 : 2 * HD] = ref[0:CON, :]
        con[i * CON : i * CON + CON // 2, 2 * HD :] = ref[ROWS:, 0:HD]
        con[i * CON + CON // 2 : (i + 1) * CON, 2 * HD :] = ref[ROWS:, HD:]
        txt[i * TXT : (i + 1) * TXT, :] = ref[CON:ROWS, :]
    hot = lax.broadcasted_iota(jnp.int32, (LINE_CON, 4 * CON), 0) == con_line[...]
    found = nn(hot.astype(F32).astype(BF), con[...]).astype(BF)
    out[0:LINE_CON, :] = found[:, 0 : 2 * HD]
    out[LINE:, 0:HD] = found[: LINE_CON // 2, 2 * HD :]
    out[LINE:, HD:] = found[LINE_CON // 2 :, 2 * HD :]
    hot = lax.broadcasted_iota(jnp.int32, (LINE_TXT, 4 * TXT), 0) == txt_line[...]
    out[LINE_CON:LINE, :] = nn(hot.astype(F32).astype(BF), txt[...]).astype(BF)


def image_heads_kernel(at, own, core, *outs):
    n, half = own.shape[0] // 3, own.shape[1]
    for s, out in enumerate(outs):
        head = jnp.minimum(at[4] ^ s, 2)
        lanes = pl.ds(pl.multiple_of(head * HD, HD), HD)
        for i in range(3):
            row = 2 * i * n
            out[row : row + n, :] = own[i * n : (i + 1) * n, lanes]
            for j in range(2):
                there = pl.ds(pl.multiple_of((2 * i + j) * half + head * HD, HD), HD)
                out[row + n + 16 * j : row + n + 16 * (j + 1), :] = core[SLOTS:, there]


def image_join_kernel(a, b, c, d, q_out, kv_out):
    n = a.shape[0] // 3
    for i, ref in enumerate((a, b, c, d)):
        q_out[n * i : n * (i + 1), :] = ref[0:n, :]
        kv_out[n * i : n * (i + 1), :] = ref[n : 2 * n, :]
        kv_out[n * (4 + i) : n * (5 + i), :] = ref[2 * n :, :]


def plane_kernel(a, b, c, d, out):
    n = a.shape[0] // 2
    for i, ref in enumerate((a, b, c, d)):
        out[n * i : n * (i + 1), :] = ref[0:n, :]
        out[n * (4 + i) : n * (5 + i), :] = ref[n:, :]


def weigh(q, parts, factor):
    scores = []
    for keys, _, bias in parts:
        part = nt(q, keys)
        scores.append(part if bias is None else part + bias)
    peak = scores[0].max(axis=1, keepdims=True)
    for part in scores[1:]:
        peak = jnp.maximum(peak, part.max(axis=1, keepdims=True))
    total = None
    for part, (_, values, _) in zip(scores, parts):
        power = part - peak
        weights = jnp.exp2(power if factor is None else power * factor).astype(BF)
        summed = nn(weights, values)
        total = summed if total is None else total + summed
    return (peak if factor is None else peak * factor), total


def join(first, second):
    peak = jnp.maximum(first[0], second[0])
    return peak, first[1] * jnp.exp2(first[0] - peak) + second[1] * jnp.exp2(second[0] - peak)


def merge(first, second):
    _, summed = join(first, second)
    return (summed[:, 0:HD] / summed[:, HD:]).astype(BF)


def with_ones(values):
    return jnp.concatenate([values, jnp.ones_like(values)], axis=1)


def plane_part(plane):
    n = plane.shape[0] // 2
    return (plane[0:n, :], with_ones(plane[n:, :]), None)


def image_near_kernel(plane, q, peak, summed):
    peak[...], summed[...] = weigh(q[...], (plane_part(plane),), FACTOR)


def near_kernel(pick, l0, l1, l2, l3, con_bias, txt_bias, plane, img_q, im, ims, *refs):
    (q_out, cm_out, cs_out, im_out, ims_out), (con_q, con_k, con_v, txt_k, txt_v) = refs[:5], refs[5:]
    n, m = LINE_CON, LINE_TXT
    for a, ref in enumerate((l0, l1, l2, l3)):
        con_q[a * n : a * n + n // 2, :] = ref[LINE:, 0:HD]
        con_q[a * n + n // 2 : (a + 1) * n, :] = ref[LINE:, HD:]
        con_k[a * n : (a + 1) * n, :] = ref[0:n, 0:HD]
        con_v[a * n : (a + 1) * n, :] = with_ones(ref[0:n, HD:])
        txt_k[a * m : (a + 1) * m, :] = ref[n:LINE, 0:HD]
        txt_v[a * m : (a + 1) * m, :] = with_ones(ref[n:LINE, HD:])
    images = plane_part(plane)
    q_out[...] = nn(pick[...], con_q[...]).astype(BF)
    for b in range(q_out.shape[0] // 256):
        rows = slice(b * 256, (b + 1) * 256)
        parts = (images, (con_k[...], con_v[...], con_bias[...]))
        cm_out[rows, :], cs_out[rows, :] = weigh(q_out[rows, :], parts, None)
    text = weigh(img_q[...], ((txt_k[...], txt_v[...], txt_bias[...]),), FACTOR)
    im_out[...], ims_out[...] = join(text, (im[...], ims[...]))


def far_kernel(plane, con_q, img_q, cm, cs, im, ims, *refs):
    outs, (con_out,) = refs[:4], refs[4:]
    images = plane_part(plane)
    img = merge(weigh(img_q[...], (images,), FACTOR), (im[...], ims[...]))
    n_con = con_out.shape[0]
    for b in range(n_con // 256):
        rows = slice(b * 256, (b + 1) * 256)
        part = weigh(con_q[rows, :], (images,), None)
        con_out[rows, :] = merge(part, (cm[rows, :], cs[rows, :]))
    dots = nt(img, con_out[...]).astype(BF)
    con_f = con_out[...].astype(F32)
    con_sq = nt(jnp.ones((16, HD), F32), con_f * con_f, precision=lax.Precision.HIGHEST).astype(BF)
    for s, out in enumerate(outs):
        rows = slice(s * 64, (s + 1) * 64)
        out[0:64, 0:n_con] = dots[rows]
        out[0:64, n_con:] = img[rows]
        out[64:80, 0:n_con] = con_sq
        out[64:80, n_con:] = jnp.zeros((16, HD), BF)


def head_sum_kernel(at, b0, b1, b2, b3, own, core, out_own):
    n_con = b0.shape[1] - HD
    total = jnp.zeros((80, n_con), F32)
    outs = [jnp.zeros((64, HD), BF) for _ in range(3)]
    for s, ref in enumerate((b0, b1, b2, b3)):
        head = at[4] ^ s
        total = total + jnp.where(head < 3, ref[:, 0:n_con].astype(F32), 0.0)
        for h in range(3):
            outs[h] = jnp.where(head == h, ref[0:64, n_con:], outs[h])
    image_sq = jnp.zeros((64, 1), F32)
    for h in range(3):
        out_f = outs[h].astype(F32)
        image_sq = image_sq + jnp.sum(out_f * out_f, axis=1, keepdims=True)
    image_sq = jnp.broadcast_to(image_sq, (64, HD)).astype(BF)
    total = total.astype(BF)
    for ref, row in ((own, 0), (core, 32)):
        ref[0:32, 0:n_con] = total[row : row + 32]
        ref[32:48, 0:n_con] = total[64:80]
        ref[0:32, n_con : n_con + HD] = image_sq[row : row + 32]
        ref[32:48, n_con : n_con + HD] = jnp.zeros((16, HD), BF)
    for h in range(3):
        lanes = slice(n_con + (1 + h) * HD, n_con + (2 + h) * HD)
        core[0:32, lanes] = outs[h][32:64]
        core[32:48, lanes] = jnp.zeros((16, HD), BF)
        out_own[:, h * HD : (h + 1) * HD] = outs[h][0:32]


def core_sum_kernel(own, core, out):
    cols = own.shape[1]
    out[...] = (own[...].astype(F32) + core[:, 0:cols].astype(F32)).astype(BF)


def finish_kernel(at, own, head, core, out_own, img_ref, sal_ref):
    n_con = own.shape[1] - HD
    width = 12 * HD
    total = own[...].astype(F32) + head[...].astype(F32)
    con_rms = jnp.sqrt(total[32:33, 0:n_con] / width + 1e-06)
    img_rms = jnp.sqrt(total[0:32, n_con : n_con + 1] / width + 1e-06)
    sal_ref[...] = total[0:32, 0:n_con] / (math.sqrt(width) * con_rms * img_rms)
    half = 3 * HD
    mine = pl.ds(pl.multiple_of(at[2] * half, half), half)
    theirs = pl.ds(pl.multiple_of((1 - at[2]) * half, half), half)
    img_ref[:, mine] = out_own[...]
    img_ref[:, theirs] = core[0:32, n_con + HD :]


def packed(
    img_q, img_k, img_v, txt_ids, concept_ids, step_index, token_table, modulation, txt_qkv, qk_gain
):
    n_con, n_txt = concept_ids.shape[0], txt_ids.shape[0]
    ctx = lax.axis_index("ctx")
    g = lax.axis_index("head")
    c = ctx & 1
    y = (ctx >> 1) & 3
    zl = (ctx >> 3) & 1
    x = ctx >> 4
    u = jnp.where(c == 0, x, y)
    v = jnp.where(c == 0, y, x)
    at = jnp.stack([ctx * 2 + g, x * 4 + y, c, 2 * g + zl, u, v]).astype(jnp.int32)
    con_ids, text_ids = concept_ids[None, :], txt_ids[None, :]
    n = n_con + n_txt
    width = token_table.shape[1]
    half = txt_qkv.shape[2] // 2
    n_img = img_q.shape[0]

    own_rows, own_both, own_img, plan = call(
        plan_kernel,
        (
            sds((SLOTS, width)),
            sds((SLOTS + 16, width)),
            sds((3 * n_img, half)),
            sds((8, n), jnp.int32),
        ),
    )(at, con_ids, text_ids, token_table, img_q, img_k, img_v)
    far_rows = send(own_rows, swap_z(2))
    column_rows = [own_rows] + [send(own_rows, swap_z(s)) for s in (1, 3)]
    core_both = send(own_both, swap_core())

    pack, spots, con_bias, txt_bias, con_line, txt_line = call(
        pack_kernel,
        (
            sds((ROWS, 8 * SLOTS)),
            sds((8, n), jnp.int32),
            sds((1, 4 * LINE_CON), F32),
            sds((1, 4 * LINE_TXT), F32),
            sds((1, 4 * CON), jnp.int32),
            sds((1, 4 * TXT), jnp.int32),
        ),
    )(at, con_ids, text_ids, plan)
    shift_scale = lax.dynamic_index_in_dim(modulation, step_index[0], 0, keepdims=False)
    fits = (spots[1, 0] <= 0).astype(jnp.int32)

    image_blocks = call(
        image_heads_kernel, tuple(sds((6 * n_img, HD)) for _ in range(4))
    )(at, own_img, core_both)
    image_blocks = [image_blocks[0]] + [send(image_blocks[s], swap_u(s)) for s in (2, 1, 3)]
    image_blocks = [image_blocks[0], image_blocks[2], image_blocks[1], image_blocks[3]]
    column_rows[1], image_blocks[2] = lax.optimization_barrier((column_rows[1], image_blocks[2]))
    far_rows, pack, shift_scale, fits, image_blocks[1] = lax.optimization_barrier(
        (far_rows, pack, shift_scale, fits, image_blocks[1])
    )
    column_rows.insert(2, far_rows)
    other_rows = [core_both] + [send(r, swap_core()) for r in column_rows[1:]]

    qkv = call(
        project_kernel,
        tuple(sds((ROWS + CON // 2, 2 * HD)) for _ in range(4)),
        scratch=(
            pltpu.VMEM((8 * SLOTS, width), BF),
            pltpu.VMEM((ROWS, width), BF),
            pltpu.VMEM((3, width, half), BF),
            pltpu.SemaphoreType.DMA((3,)),
        ),
        us=PROJ_US,
        in_hbm=1,
    )(at, pack, *column_rows, *other_rows, shift_scale, qk_gain, jnp.transpose(txt_qkv, (1, 0, 2)))

    *image_blocks, first = lax.optimization_barrier((*image_blocks, qkv[0]))
    image_q, image_kv = call(
        image_join_kernel, (sds((8 * n_img, HD)), sds((16 * n_img, HD))), smem=0
    )(*image_blocks)
    image_kvs = [image_kv] + [send(image_kv, swap_v(s)) for s in (2, 1, 3)]

    qkv = [first] + [send(qkv[s], swap_u(s)) for s in (2, 1, 3)]
    qkv = [qkv[0], qkv[2], qkv[1], qkv[3]]
    line = call(
        join_kernel,
        sds((LINE + LINE_CON // 2, 2 * HD)),
        scratch=(pltpu.VMEM((4 * CON, 3 * HD), BF), pltpu.VMEM((4 * TXT, 2 * HD), BF)),
        smem=0,
    )(*qkv, con_line, txt_line)
    lines = [line] + [send(line, swap_v(s)) for s in (2, 1, 3)]
    lines = [lines[0], lines[2], lines[1], lines[3]]
    plane = call(plane_kernel, sds((64 * n_img, HD)), smem=0)(*image_kvs)
    con_slot, plane = lax.optimization_barrier((spots[0, :n_con], plane))
    other_plane = send(plane, swap_plane())
    pick = (con_slot[:, None] == jnp.arange(4 * LINE_CON)[None, :]).astype(BF)

    image_stats = (sds((8 * n_img, 1), F32), sds((8 * n_img, 2 * HD), F32))
    stats = (sds((n_con, 1), F32), sds((n_con, 2 * HD), F32)) + image_stats
    image_near = call(image_near_kernel, image_stats, smem=0)(plane, image_q)
    con_q, *near = call(
        near_kernel,
        (sds((n_con, HD)),) + stats,
        scratch=(
            pltpu.VMEM((4 * LINE_CON, HD), BF),
            pltpu.VMEM((4 * LINE_CON, HD), BF),
            pltpu.VMEM((4 * LINE_CON, 2 * HD), BF),
            pltpu.VMEM((4 * LINE_TXT, HD), BF),
            pltpu.VMEM((4 * LINE_TXT, 2 * HD), BF),
        ),
        us=NEAR_US,
        smem=0,
    )(pick, *lines, con_bias, txt_bias, plane, image_q, *image_near)
    blocks = call(
        far_kernel,
        tuple(sds((80, n_con + HD)) for _ in range(4)),
        scratch=(pltpu.VMEM((n_con, HD), BF),),
        us=FAR_US,
        smem=0,
    )(other_plane, con_q, image_q, *near)
    blocks = [blocks[0]] + [send(blocks[s], swap_u(s)) for s in (2, 1, 3)]
    blocks = [blocks[0], blocks[2], blocks[1], blocks[3]]
    own, core, out_own = call(
        head_sum_kernel,
        (sds((48, n_con + HD)), sds((48, n_con + 4 * HD)), sds((32, half))),
    )(at, *blocks)
    core = send(core, swap_core())
    own = call(core_sum_kernel, sds((48, n_con + HD)), smem=0)(own, core)
    last = (at, own, send(own, swap_z(2)), core, out_own)
    finish = call(finish_kernel, (sds((n_img, 2 * half)), sds((n_img, n_con), F32)))

    def finished():
        img_out, saliency = finish(*last)
        return img_out, jnp.transpose(saliency)

    return fits > 0, finished


def on_device(*args):
    fits, finish = packed(*args)
    return lax.cond(fits, finish, lambda: tuple(general(*args)))


def solution(mesh):
    return jax.shard_map(
        on_device,
        mesh=mesh,
        in_specs=(
            P("ctx", "head"),
            P("ctx", "head"),
            P("ctx", "head"),
            P(),
            P(),
            P(),
            P(("ctx", "head"), None),
            P(),
            P(None, None, "head"),
            P(),
        ),
        out_specs=(P("ctx", "head"), P(None, "ctx")),
        check_vma=False,
    )
```

```python
import math

import jax
import jax.numpy as jnp
from jax import lax
from jax.experimental import pallas as pl
from jax.experimental.pallas import tpu as pltpu
from jax.sharding import PartitionSpec as P

BF = jnp.bfloat16
F32 = jnp.float32
HD = 128
SLOTS = 32
CON = 96
TXT = 64
ROWS = CON + TXT
LINE_CON = 320
LINE_TXT = 176
LINE = LINE_CON + LINE_TXT
MIB = 1 << 20
PROJ_US, NEAR_US, FAR_US = 5.0, 2.0, 3.0
FACTOR = HD ** (-0.5) * math.log2(math.e)


def modulate(rows, shift_scale):
    values = rows.astype(F32)
    mean = jnp.mean(values, axis=1, keepdims=True)
    centered = values - mean
    var = jnp.mean(centered * centered, axis=1, keepdims=True)
    normed = centered * lax.rsqrt(var + 1e-06)
    return (normed * (1.0 + shift_scale[1]) + shift_scale[0]).astype(BF)


def head_norm(values, gain, head_dim):
    shaped = values.reshape(values.shape[0], -1, head_dim)
    meansq = jnp.mean(shaped * shaped, axis=2, keepdims=True)
    return (shaped * lax.rsqrt(meansq + 1e-06) * gain).reshape(values.shape[0], -1)


def block_stats(queries, keys, values):
    scores = jnp.einsum("rgd,kgd->grk", queries, keys, preferred_element_type=F32)
    scores = scores * queries.shape[-1] ** (-0.5)
    peak = jnp.max(scores, axis=2)
    weights = jnp.exp(scores - peak[:, :, None])
    total = jnp.sum(weights, axis=2)
    summed = jnp.einsum("grk,kgd->grd", weights.astype(BF), values, preferred_element_type=F32)
    return (peak, total, summed)


def combine_stats(first, second):
    peak = jnp.maximum(first[0], second[0])
    left = jnp.exp(first[0] - peak)
    right = jnp.exp(second[0] - peak)
    total = first[1] * left + second[1] * right
    summed = first[2] * left[:, :, None] + second[2] * right[:, :, None]
    return (peak, total, summed)


def scaled_scores(dots, concept_sq, image_sq, width):
    concept_rms = jnp.sqrt(concept_sq / width + 1e-06)
    image_rms = jnp.sqrt(image_sq / width + 1e-06)
    return dots / (jnp.sqrt(F32(width)) * concept_rms[:, None] * image_rms[None, :])


def gather_ctx(block):
    n_ctx = lax.axis_size("ctx")
    spread = jnp.broadcast_to(block[None], (n_ctx,) + block.shape)
    return lax.all_to_all(spread, "ctx", 0, 0, tiled=True)


def general(
    img_q, img_k, img_v, txt_ids, concept_ids, step_index, token_table, modulation, txt_qkv, qk_gain
):
    n_ctx = lax.axis_size("ctx")
    n_head = lax.axis_size("head")
    head_dim = qk_gain.shape[1]
    group = img_q.shape[1] // head_dim
    text_dev = txt_ids.shape[0] // n_ctx
    concept_dev = concept_ids.shape[0] // n_ctx
    vocab_dev = token_table.shape[0]
    combined = jnp.concatenate(
        [txt_ids.reshape(n_ctx, text_dev), concept_ids.reshape(n_ctx, concept_dev)], axis=1
    ).reshape(-1)
    offset = lax.axis_index(("ctx", "head")) * vocab_dev
    wanted = combined - offset
    inside = (wanted >= 0) & (wanted < vocab_dev)
    picked = jnp.take(token_table, jnp.clip(wanted, 0, vocab_dev - 1), axis=0)
    n_all = n_ctx * n_head
    mine = jnp.where(inside[:, None], picked, jnp.zeros((), picked.dtype))
    parts = lax.all_to_all(
        mine.reshape(n_all, -1, mine.shape[1]), ("ctx", "head"), 0, 0, tiled=True
    )
    own_rows = jnp.sum(parts.astype(F32), axis=0)
    prompt_rows = lax.all_gather(own_rows.astype(BF), "head", axis=0, tiled=True)
    shift_scale = lax.dynamic_index_in_dim(modulation, step_index[0], 0, keepdims=False)
    modded = modulate(prompt_rows, shift_scale)
    text_mod = modded[:text_dev]
    concept_mod = modded[text_dev:]
    text_kv = jnp.einsum("rd,dgc->rgc", text_mod, txt_qkv[:, 1:], preferred_element_type=F32)
    concept_qkv = jnp.einsum("rd,dgc->rgc", concept_mod, txt_qkv, preferred_element_type=F32)
    text_keys = head_norm(text_kv[:, 0], qk_gain[1], head_dim).astype(BF)
    text_values = text_kv[:, 1].astype(BF)
    concept_queries = head_norm(concept_qkv[:, 0], qk_gain[0], head_dim).astype(BF)
    concept_keys = head_norm(concept_qkv[:, 1], qk_gain[1], head_dim).astype(BF)
    concept_values = concept_qkv[:, 2].astype(BF)
    local_kv = jnp.stack(
        [
            jnp.concatenate([text_keys, concept_keys], axis=0),
            jnp.concatenate([text_values, concept_values], axis=0),
        ]
    )
    prompt_kv = gather_ctx(local_kv)
    text_part = jnp.swapaxes(prompt_kv[:, :, :text_dev], 0, 1).reshape(2, -1, group, head_dim)
    concept_part = jnp.swapaxes(prompt_kv[:, :, text_dev:], 0, 1).reshape(2, -1, group, head_dim)
    image_queries = img_q.reshape(-1, group, head_dim)
    concept_q3 = concept_queries.reshape(-1, group, head_dim)
    first = block_stats(image_queries, text_part[0], text_part[1])
    second = block_stats(concept_q3, concept_part[0], concept_part[1])
    start_stats = (
        jnp.concatenate([first[0], second[0]], axis=1),
        jnp.concatenate([first[1], second[1]], axis=1),
        jnp.concatenate([first[2], second[2]], axis=1),
    )
    all_queries = jnp.concatenate([image_queries, concept_q3], axis=0)
    image_kv = gather_ctx(jnp.stack([img_k, img_v]))
    keys = image_kv[:, 0].reshape(-1, group, head_dim)
    values = image_kv[:, 1].reshape(-1, group, head_dim)
    peak, total, summed = combine_stats(start_stats, block_stats(all_queries, keys, values))
    attended = (
        jnp.transpose(summed / total[:, :, None], (1, 0, 2))
        .reshape(all_queries.shape[0], -1)
        .astype(BF)
    )
    img_rows = img_q.shape[0]
    img_out = attended[:img_rows]
    concept_out = attended[img_rows:]
    concept_all = gather_ctx(concept_out).reshape(-1, concept_out.shape[1])
    dots = lax.dot_general(
        concept_all, img_out, (((1,), (1,)), ((), ())), preferred_element_type=F32
    )
    image_f = img_out.astype(F32)
    concept_f = concept_all.astype(F32)
    image_sq = jnp.sum(image_f * image_f, axis=1)
    concept_sq = jnp.sum(concept_f * concept_f, axis=1)
    width = group * head_dim * n_head
    sums = jnp.concatenate(
        [
            jnp.concatenate([dots, concept_sq[:, None]], axis=1),
            jnp.concatenate([image_sq, jnp.zeros((1,), F32)])[None],
        ]
    ).astype(BF)
    other = lax.ppermute(sums, "head", [(0, 1), (1, 0)])
    sums = sums.astype(F32) + other.astype(F32)
    concepts = dots.shape[0]
    saliency = scaled_scores(
        sums[:concepts, :img_rows], sums[:concepts, img_rows], sums[concepts, :img_rows], width
    )
    return (img_out, saliency)


def place(x, zl, y, c, g):
    return ((((x * 2 + zl) * 4 + y) * 2 + c) * 2) + g


def pairs(move):
    found = []
    for x in range(4):
        for zl in range(2):
            for y in range(4):
                for c in range(2):
                    for g in range(2):
                        found.append((place(x, zl, y, c, g), place(*move(x, zl, y, c, g))))
    return found


def swap_z(s):
    def move(x, zl, y, c, g):
        z = (2 * g + zl) ^ s
        return x, z & 1, y, c, z >> 1

    return pairs(move)


def swap_u(s):
    return pairs(
        lambda x, zl, y, c, g: (x, zl, y ^ s, c, g) if c else (x ^ s, zl, y, c, g)
    )


def swap_v(s):
    return pairs(
        lambda x, zl, y, c, g: (x ^ s, zl, y, c, g) if c else (x, zl, y ^ s, c, g)
    )


def swap_plane():
    return pairs(lambda x, zl, y, c, g: (x, zl ^ 1, y, c, g))


def swap_core():
    return pairs(lambda x, zl, y, c, g: (x, zl, y, c ^ 1, g))


def send(array, pairing):
    return lax.ppermute(array, ("ctx", "head"), pairing)


def nt(a, b, **kw):
    return lax.dot_general(a, b, (((1,), (1,)), ((), ())), preferred_element_type=F32, **kw)


def nn(a, b):
    return lax.dot_general(a, b, (((1,), (0,)), ((), ())), preferred_element_type=F32)


def call(kernel, outs, scratch=(), limit=16, us=1.0, smem=1, in_hbm=0):
    def run(*args):
        vm = pl.BlockSpec(memory_space=pltpu.VMEM)
        sm = pl.BlockSpec(memory_space=pltpu.SMEM)
        return pl.pallas_call(
            kernel,
            out_shape=outs,
            in_specs=[sm] * smem
            + [vm] * (len(args) - smem - in_hbm)
            + [pl.BlockSpec(memory_space=pl.ANY)] * in_hbm,
            out_specs=jax.tree.map(lambda _: vm, outs),
            scratch_shapes=list(scratch),
            compiler_params=pltpu.CompilerParams(vmem_limit_bytes=limit * MIB),
            cost_estimate=pl.CostEstimate(
                flops=int(us * 1.1e9), bytes_accessed=0, transcendentals=0
            ),
        )(*args)

    return run


def sds(shape, dtype=BF):
    return jax.ShapeDtypeStruct(shape, dtype)


def column_of(owner):
    ctx = owner >> 1
    return ((ctx >> 4) << 2) | ((ctx >> 1) & 3)


def ranks(keys, classes, resets):
    n = keys.shape[1]
    blk = 256
    row = lax.broadcasted_iota(jnp.int32, (blk, blk), 0)
    col = lax.broadcasted_iota(jnp.int32, (blk, blk), 1)
    earlier = (row < col).astype(F32).astype(BF)
    label = lax.broadcasted_iota(jnp.int32, (classes, blk), 0)
    carry = jnp.zeros((classes, 1), F32)
    found, counts = [], []
    for b in range(n // blk):
        if b in resets:
            counts.append(carry)
            carry = jnp.zeros((classes, 1), F32)
        hot = (label == keys[:, b * blk : (b + 1) * blk]).astype(F32)
        before = nn(hot.astype(BF), earlier) + carry
        found.append(jnp.sum(hot * before, axis=0, keepdims=True))
        carry = carry + jnp.sum(hot, axis=1, keepdims=True)
    counts.append(carry)
    return jnp.concatenate(found, axis=1).astype(jnp.int32), counts


def plan_kernel(
    at, con_ref, txt_ref, table_ref, q_ref, k_ref, v_ref, rows_ref, both_ref, img_ref
):
    ids = jnp.concatenate([con_ref[...], txt_ref[...]], axis=1)
    n = ids.shape[1]
    blk = 256
    blocks = n // blk
    vocab_dev = table_ref.shape[0]
    mine = ((ids >> int(math.log2(vocab_dev))) == at[0]).astype(F32)
    pieces = [slice(b * blk, (b + 1) * blk) for b in range(blocks)]
    folded = jnp.concatenate(
        [mine[:, p] for p in pieces] + [jnp.zeros((8 - blocks, blk), F32)], axis=0
    )
    row = lax.broadcasted_iota(jnp.int32, (blk, blk), 0)
    col = lax.broadcasted_iota(jnp.int32, (blk, blk), 1)
    before = nn(folded.astype(BF), (row < col).astype(F32).astype(BF))
    label = lax.broadcasted_iota(jnp.int32, (SLOTS, blk), 0).astype(F32)
    found = jnp.zeros((SLOTS, blk), F32)
    skipped = jnp.zeros((1, 1), F32)
    for b, p in enumerate(pieces):
        rank = before[b : b + 1, :] + skipped
        row_in_table = ((ids[:, p] & (vocab_dev - 1)) + 1).astype(F32) * mine[:, p]
        found = found + jnp.where(label == rank, row_in_table, 0.0)
        skipped = skipped + jnp.sum(mine[:, p], axis=1, keepdims=True)
    found = jnp.sum(found, axis=1, keepdims=True).astype(jnp.int32) - 1
    pick = lax.broadcasted_iota(jnp.int32, (SLOTS, vocab_dev), 1) == found
    rows = nn(pick.astype(F32).astype(BF), table_ref[...]).astype(BF)
    rows_ref[...] = rows
    both_ref[0:SLOTS, :] = rows
    m = q_ref.shape[0]
    half = q_ref.shape[1] // 2
    lanes_own = pl.ds(pl.multiple_of(at[2] * half, half), half)
    lanes_other = pl.ds(pl.multiple_of((1 - at[2]) * half, half), half)
    for i, ref in enumerate((q_ref, k_ref, v_ref)):
        img_ref[i * m : (i + 1) * m, :] = ref[:, lanes_own]
        for j in range(2):
            lanes = slice((2 * i + j) * half, (2 * i + j + 1) * half)
            both_ref[SLOTS:, lanes] = ref[16 * j : 16 * (j + 1), lanes_other]
    both_ref[SLOTS:, 6 * half :] = jnp.zeros((16, 2 * half), BF)


def to_row(column):
    n = column.shape[0]
    diagonal = lax.broadcasted_iota(jnp.int32, (n, n), 0) == lax.broadcasted_iota(
        jnp.int32, (n, n), 1
    )
    return jnp.sum(jnp.where(diagonal, column, 0.0), axis=0, keepdims=True)


def line_of(at, column):
    first, second = column >> 2, column & 3
    return jnp.where(at[2] == 0, first, second), jnp.where(at[2] == 0, second, first)


def line_plan(at, counts):
    u, v = line_of(at, lax.broadcasted_iota(jnp.int32, (16, 16), 0))
    u2, v2 = line_of(at, lax.broadcasted_iota(jnp.int32, (16, 16), 1))
    row = to_row(counts)
    same = v == v2
    before = same & ((u2 ^ at[4]) < (u ^ at[4]))
    skipped = jnp.sum(jnp.where(before, row, 0.0), axis=1, keepdims=True)
    total = jnp.sum(jnp.where(same, row, 0.0), axis=1, keepdims=True)
    other = jnp.sum(jnp.where(u == u2, row, 0.0), axis=1, keepdims=True)
    return skipped, total, jnp.max(jnp.maximum(total, other), axis=0, keepdims=True)


def per_lane(values, column):
    hot = lax.broadcasted_iota(jnp.int32, (16, column.shape[1]), 0) == column
    return jnp.sum(jnp.where(hot, values, 0.0), axis=0, keepdims=True)


def blocks_of(lanes, size, blocks):
    lane = lax.broadcasted_iota(jnp.int32, (1, lanes), 1)
    block = jnp.zeros((1, lanes), jnp.int32)
    for j in range(1, blocks):
        block = block + (lane >= j * size).astype(jnp.int32)
    return block, (lane - block * size).astype(F32)


def column_at(at, u, v):
    return jnp.where(at[2] == 0, u * 4 + v, v * 4 + u)


def line_targets(at, counts, skipped, slots):
    block, slot = blocks_of(4 * slots, slots, 4)
    column = column_at(at, block ^ at[4], jnp.zeros_like(block) + at[5])
    target = per_lane(skipped, column) + slot
    return jnp.where(slot < per_lane(counts, column), target, -1.0).astype(jnp.int32)


def line_bias(at, total, rows):
    block, slot = blocks_of(4 * rows, rows, 4)
    column = column_at(at, jnp.zeros_like(block) + at[4], block ^ at[5])
    return jnp.where(slot < per_lane(total, column), 0.0, -1e30)


def pack_kernel(
    at, con_ref, txt_ref, w_hbm, out_ref, spot_ref, con_bias, txt_bias, con_line, txt_line, w_ref, sem
):
    half = w_ref.shape[2]
    lanes = pl.ds(pl.multiple_of(at[2] * half, half), half)
    weights = pltpu.make_async_copy(w_hbm.at[:, :, lanes], w_ref, sem)
    weights.start()
    ids = jnp.concatenate([con_ref[...], txt_ref[...]], axis=1)
    n = ids.shape[1]
    n_con = con_ref.shape[1]
    owner = ids >> 8
    column = column_of(owner)
    here = column == at[1]
    z = ((owner & 1) << 1) | ((owner >> 4) & 1)
    core = (owner >> 1) & 1
    piece = jnp.where(here, jnp.where(core == at[2], 0, 4) + (at[3] ^ z), -1)
    rank, _ = ranks(piece, 8, ())
    spot, (con_counts, txt_counts) = ranks(column, 16, (n_con // 256,))
    con_skip, con_total, con_most = line_plan(at, con_counts)
    txt_skip, txt_total, txt_most = line_plan(at, txt_counts)
    con_bias[...] = line_bias(at, con_total, LINE_CON)
    txt_bias[...] = line_bias(at, txt_total, LINE_TXT)
    con_line[...] = line_targets(at, con_counts, con_skip, CON)
    txt_line[...] = line_targets(at, txt_counts, txt_skip, TXT)
    _, item_v = line_of(at, column)
    spot_ref[0:1, :] = (
        (item_v ^ at[5]) * LINE_CON + per_lane(con_skip, column).astype(jnp.int32) + spot
    )
    wanted = (lax.broadcasted_iota(jnp.int32, (128, n), 0) == owner).astype(F32)
    over = jnp.maximum(
        jnp.maximum(
            jnp.max(con_counts, axis=0, keepdims=True) - CON,
            jnp.max(txt_counts, axis=0, keepdims=True) - TXT,
        ),
        jnp.maximum(con_most - LINE_CON, txt_most - LINE_TXT),
    )
    most = jnp.max(jnp.sum(wanted, axis=1, keepdims=True), axis=0, keepdims=True)
    over = jnp.maximum(over, most - SLOTS)
    spot_ref[1:2, :] = jnp.broadcast_to(over.astype(jnp.int32), (1, n))
    spot_ref[2:8, :] = jnp.zeros((6, n), jnp.int32)
    concept = lax.broadcasted_iota(jnp.int32, (1, n), 1) < n_con
    target = jnp.where(
        concept, jnp.where(spot < CON, spot, -1), jnp.where(spot < TXT, spot + CON, -1)
    )
    source = jnp.where(here & (rank < SLOTS), piece * SLOTS + rank, -1)
    target = jnp.where(here, target, -1)
    hot_t = (lax.broadcasted_iota(jnp.int32, (ROWS, n), 0) == target).astype(F32).astype(BF)
    hot_s = (lax.broadcasted_iota(jnp.int32, (8 * SLOTS, n), 0) == source).astype(F32).astype(BF)
    out_ref[...] = nt(hot_t, hot_s).astype(BF)
    weights.wait()


def project_kernel(at, pack_ref, *refs):
    rows, (mod_ref, gain_ref, w_ref), outs, (raw_ref, x_ref) = (
        refs[:8], refs[8:11], refs[11:15], refs[15:]
    )
    for i, ref in enumerate(rows):
        raw_ref[i * SLOTS : (i + 1) * SLOTS, :] = ref[0:SLOTS, :]
    shift = mod_ref[0:1, :]
    scale = 1.0 + mod_ref[1:2, :]
    for i in range(ROWS // 32):
        block = slice(i * 32, (i + 1) * 32)
        values = nn(pack_ref[block, :], raw_ref[...])
        mean = jnp.mean(values, axis=1, keepdims=True)
        centered = values - mean
        var = jnp.mean(centered * centered, axis=1, keepdims=True)
        x_ref[block, :] = (centered * lax.rsqrt(var + 1e-06) * scale + shift).astype(BF)

    def normed(u, gain):
        meansq = jnp.mean(u * u, axis=1, keepdims=True)
        return u * lax.rsqrt(meansq + 1e-06) * gain

    q = nn(x_ref[0:CON, :], w_ref[0])
    k = nn(x_ref[...], w_ref[1])
    v = nn(x_ref[...], w_ref[2])
    heads = []
    for h in range(3):
        cols = slice(h * HD, (h + 1) * HD)
        heads.append(
            (
                (normed(q[:, cols], gain_ref[0:1, :]) * FACTOR).astype(BF),
                normed(k[:, cols], gain_ref[1:2, :]).astype(BF),
                v[:, cols].astype(BF),
            )
        )
    for s, out in enumerate(outs):
        head = jnp.minimum(at[4] ^ s, 2)
        for h in range(3):

            @pl.when(head == h)
            def _(h=h, out=out):
                out[0:ROWS, 0:HD] = heads[h][1]
                out[0:ROWS, HD:] = heads[h][2]
                out[ROWS:, 0:HD] = heads[h][0][: CON // 2]
                out[ROWS:, HD:] = heads[h][0][CON // 2 :]


def join_kernel(a, b, c, d, con_line, txt_line, out, con, txt):
    for i, ref in enumerate((a, b, c, d)):
        con[i * CON : (i + 1) * CON, 0 : 2 * HD] = ref[0:CON, :]
        con[i * CON : i * CON + CON // 2, 2 * HD :] = ref[ROWS:, 0:HD]
        con[i * CON + CON // 2 : (i + 1) * CON, 2 * HD :] = ref[ROWS:, HD:]
        txt[i * TXT : (i + 1) * TXT, :] = ref[CON:ROWS, :]
    hot = lax.broadcasted_iota(jnp.int32, (LINE_CON, 4 * CON), 0) == con_line[...]
    found = nn(hot.astype(F32).astype(BF), con[...]).astype(BF)
    out[0:LINE_CON, :] = found[:, 0 : 2 * HD]
    out[LINE:, 0:HD] = found[: LINE_CON // 2, 2 * HD :]
    out[LINE:, HD:] = found[LINE_CON // 2 :, 2 * HD :]
    hot = lax.broadcasted_iota(jnp.int32, (LINE_TXT, 4 * TXT), 0) == txt_line[...]
    out[LINE_CON:LINE, :] = nn(hot.astype(F32).astype(BF), txt[...]).astype(BF)


def image_heads_kernel(at, own, core, *outs):
    n, half = own.shape[0] // 3, own.shape[1]
    for s, out in enumerate(outs):
        head = jnp.minimum(at[4] ^ s, 2)
        lanes = pl.ds(pl.multiple_of(head * HD, HD), HD)
        for i in range(3):
            row = 2 * i * n
            out[row : row + n, :] = own[i * n : (i + 1) * n, lanes]
            for j in range(2):
                there = pl.ds(pl.multiple_of((2 * i + j) * half + head * HD, HD), HD)
                out[row + n + 16 * j : row + n + 16 * (j + 1), :] = core[SLOTS:, there]


def image_join_kernel(a, b, c, d, q_out, kv_out):
    n = a.shape[0] // 3
    for i, ref in enumerate((a, b, c, d)):
        q_out[n * i : n * (i + 1), :] = ref[0:n, :]
        kv_out[n * i : n * (i + 1), :] = ref[n : 2 * n, :]
        kv_out[n * (4 + i) : n * (5 + i), :] = ref[2 * n :, :]


def plane_kernel(a, b, c, d, out):
    n = a.shape[0] // 2
    for i, ref in enumerate((a, b, c, d)):
        out[n * i : n * (i + 1), :] = ref[0:n, :]
        out[n * (4 + i) : n * (5 + i), :] = ref[n:, :]


def weigh(q, parts, factor):
    scores = []
    for keys, _, bias in parts:
        part = nt(q, keys)
        scores.append(part if bias is None else part + bias)
    peak = scores[0].max(axis=1, keepdims=True)
    for part in scores[1:]:
        peak = jnp.maximum(peak, part.max(axis=1, keepdims=True))
    total = None
    for part, (_, values, _) in zip(scores, parts):
        power = part - peak
        weights = jnp.exp2(power if factor is None else power * factor).astype(BF)
        summed = nn(weights, values)
        total = summed if total is None else total + summed
    return (peak if factor is None else peak * factor), total


def join(first, second):
    peak = jnp.maximum(first[0], second[0])
    return peak, first[1] * jnp.exp2(first[0] - peak) + second[1] * jnp.exp2(second[0] - peak)


def merge(first, second):
    _, summed = join(first, second)
    return (summed[:, 0:HD] / summed[:, HD:]).astype(BF)


def with_ones(values):
    return jnp.concatenate([values, jnp.ones_like(values)], axis=1)


def image_near_kernel(plane, q, peak, summed):
    n = plane.shape[0] // 2
    part = (plane[0:n, :], with_ones(plane[n:, :]), None)
    peak[...], summed[...] = weigh(q[...], (part,), FACTOR)


def line_queries(con_q, refs):
    n = LINE_CON
    for a, ref in enumerate(refs):
        con_q[a * n : a * n + n // 2, :] = ref[LINE:, 0:HD]
        con_q[a * n + n // 2 : (a + 1) * n, :] = ref[LINE:, HD:]


def order_kernel(pick, l0, l1, q_out, con_q):
    line_queries(con_q, (l0, l1))
    q_out[...] = nn(pick[:, : 2 * LINE_CON], con_q[...]).astype(BF)


def weigh_blocks(q, parts, store):
    blk = 256
    blocks = [slice(b, b + blk) for b in range(0, q.shape[0], blk)]

    def scores(rows):
        found = []
        for keys, _, bias in parts:
            part = nt(q[rows, :], keys[...])
            found.append(part if bias is None else part + bias[...])
        return found

    ready = scores(blocks[0])
    for b, rows in enumerate(blocks):
        now, ready = ready, scores(blocks[b + 1]) if b + 1 < len(blocks) else None
        peak = now[0].max(axis=1, keepdims=True)
        for part in now[1:]:
            peak = jnp.maximum(peak, part.max(axis=1, keepdims=True))
        summed = sum(
            nn(jnp.exp2(part - peak).astype(BF), values[...])
            for part, (_, values, _) in zip(now, parts)
        )
        store(rows, peak, summed)


def near_kernel(
    pick, q_part, l0, l1, l2, l3, con_bias, txt_bias, plane, img_q, im, ims, *refs
):
    q_out, cm_out, cs_out, im_out, ims_out = refs[:5]
    con_q, con_k, con_v, txt_k, txt_v, img_v = refs[5:]
    n, m = LINE_CON, LINE_TXT
    line_queries(con_q, (l2, l3))
    for a, ref in enumerate((l0, l1, l2, l3)):
        con_k[a * n : (a + 1) * n, :] = ref[0:n, 0:HD]
        con_v[a * n : (a + 1) * n, :] = with_ones(ref[0:n, HD:])
        txt_k[a * m : (a + 1) * m, :] = ref[n:LINE, 0:HD]
        txt_v[a * m : (a + 1) * m, :] = with_ones(ref[n:LINE, HD:])
    n_img = plane.shape[0] // 2
    img_v[...] = with_ones(plane[n_img:, :])
    rest = nn(pick[:, 2 * n :], con_q[...])
    q_out[...] = (rest + q_part[...].astype(F32)).astype(BF)

    def store(rows, peak, summed):
        cm_out[rows, :] = peak
        cs_out[rows, :] = summed

    parts = ((plane.at[0:n_img, :], img_v, None), (con_k, con_v, con_bias))
    weigh_blocks(q_out, parts, store)
    text = weigh(img_q[...], ((txt_k[...], txt_v[...], txt_bias[...]),), FACTOR)
    im_out[...], ims_out[...] = join(text, (im[...], ims[...]))


def far_kernel(plane, con_q, img_q, cm, cs, im, ims, *refs):
    outs, (con_out, img_v) = refs[:4], refs[4:]
    n_img = plane.shape[0] // 2
    img_v[...] = with_ones(plane[n_img:, :])
    part = (plane[0:n_img, :], img_v[...], None)
    img = merge(weigh(img_q[...], (part,), FACTOR), (im[...], ims[...]))
    n_con = con_out.shape[0]

    def store(rows, peak, summed):
        con_out[rows, :] = merge((peak, summed), (cm[rows, :], cs[rows, :]))

    weigh_blocks(con_q, ((plane.at[0:n_img, :], img_v, None),), store)
    dots = nt(img, con_out[...]).astype(BF)
    con_f = con_out[...].astype(F32)
    con_sq = nt(jnp.ones((8, HD), F32), con_f * con_f, precision=lax.Precision.HIGHEST).astype(BF)
    for s, out in enumerate(outs):
        rows = slice(s * 64, (s + 1) * 64)
        out[0:64, 0:n_con] = dots[rows]
        out[0:64, n_con:] = img[rows]
        out[64:72, 0:n_con] = con_sq
        out[64:72, n_con:] = jnp.zeros((8, HD), BF)


def head_sum_kernel(at, b0, b1, b2, b3, own, core, out_own):
    n_con = b0.shape[1] - HD
    total = jnp.zeros((72, n_con), F32)
    outs = [jnp.zeros((64, HD), BF) for _ in range(3)]
    for s, ref in enumerate((b0, b1, b2, b3)):
        head = at[4] ^ s
        total = total + jnp.where(head < 3, ref[:, 0:n_con].astype(F32), 0.0)
        for h in range(3):
            outs[h] = jnp.where(head == h, ref[0:64, n_con:], outs[h])
    image_sq = jnp.zeros((64, 1), F32)
    for h in range(3):
        out_f = outs[h].astype(F32)
        image_sq = image_sq + jnp.sum(out_f * out_f, axis=1, keepdims=True)
    image_sq = jnp.broadcast_to(image_sq, (64, HD)).astype(BF)
    total = total.astype(BF)
    for ref, row in ((own, 0), (core, 32)):
        ref[0:32, 0:n_con] = total[row : row + 32]
        ref[32:40, 0:n_con] = total[64:72]
        ref[0:32, n_con : n_con + HD] = image_sq[row : row + 32]
        ref[32:40, n_con : n_con + HD] = jnp.zeros((8, HD), BF)
    for h in range(3):
        lanes = slice(n_con + (1 + h) * HD, n_con + (2 + h) * HD)
        core[0:32, lanes] = outs[h][32:64]
        core[32:40, lanes] = jnp.zeros((8, HD), BF)
        out_own[:, h * HD : (h + 1) * HD] = outs[h][0:32]


def core_sum_kernel(own, core, out):
    cols = own.shape[1]
    out[...] = (own[...].astype(F32) + core[:, 0:cols].astype(F32)).astype(BF)


def finish_kernel(at, own, head, core, out_own, img_ref, sal_ref):
    n_con = own.shape[1] - HD
    width = 12 * HD
    total = own[...].astype(F32) + head[...].astype(F32)
    con_rms = jnp.sqrt(total[32:33, 0:n_con] / width + 1e-06)
    img_rms = jnp.sqrt(total[0:32, n_con : n_con + 1] / width + 1e-06)
    sal_ref[...] = total[0:32, 0:n_con] / (math.sqrt(width) * con_rms * img_rms)
    half = 3 * HD
    mine = pl.ds(pl.multiple_of(at[2] * half, half), half)
    theirs = pl.ds(pl.multiple_of((1 - at[2]) * half, half), half)
    img_ref[:, mine] = out_own[...]
    img_ref[:, theirs] = core[0:32, n_con + HD :]


def packed(
    img_q, img_k, img_v, txt_ids, concept_ids, step_index, token_table, modulation, txt_qkv, qk_gain
):
    n_con, n_txt = concept_ids.shape[0], txt_ids.shape[0]
    ctx = lax.axis_index("ctx")
    g = lax.axis_index("head")
    c = ctx & 1
    y = (ctx >> 1) & 3
    zl = (ctx >> 3) & 1
    x = ctx >> 4
    u = jnp.where(c == 0, x, y)
    v = jnp.where(c == 0, y, x)
    at = jnp.stack([ctx * 2 + g, x * 4 + y, c, 2 * g + zl, u, v]).astype(jnp.int32)
    con_ids, text_ids = concept_ids[None, :], txt_ids[None, :]
    n = n_con + n_txt
    width = token_table.shape[1]
    half = txt_qkv.shape[2] // 2
    n_img = img_q.shape[0]

    own_rows, own_both, own_img = call(
        plan_kernel, (sds((SLOTS, width)), sds((SLOTS + 16, width)), sds((3 * n_img, half)))
    )(at, con_ids, text_ids, token_table, img_q, img_k, img_v)
    far_rows = send(own_rows, swap_z(2))
    column_rows = [own_rows] + [send(own_rows, swap_z(s)) for s in (1, 3)]
    core_both = send(own_both, swap_core())

    pack, spots, con_bias, txt_bias, con_line, txt_line, weights = call(
        pack_kernel,
        (
            sds((ROWS, 8 * SLOTS)),
            sds((8, n), jnp.int32),
            sds((1, 4 * LINE_CON), F32),
            sds((1, 4 * LINE_TXT), F32),
            sds((1, 4 * CON), jnp.int32),
            sds((1, 4 * TXT), jnp.int32),
            sds((3, width, half)),
        ),
        scratch=(pltpu.SemaphoreType.DMA,),
        limit=24,
        us=2.0,
        in_hbm=1,
    )(at, con_ids, text_ids, jnp.transpose(txt_qkv, (1, 0, 2)))
    shift_scale = lax.dynamic_index_in_dim(modulation, step_index[0], 0, keepdims=False)
    fits = (spots[1, 0] <= 0).astype(jnp.int32)

    image_blocks = call(
        image_heads_kernel, tuple(sds((6 * n_img, HD)) for _ in range(4))
    )(at, own_img, core_both)
    image_blocks = [image_blocks[0]] + [send(image_blocks[s], swap_u(s)) for s in (2, 1, 3)]
    image_blocks = [image_blocks[0], image_blocks[2], image_blocks[1], image_blocks[3]]
    column_rows[1], image_blocks[2] = lax.optimization_barrier((column_rows[1], image_blocks[2]))
    far_rows, pack, shift_scale, fits, image_blocks[1] = lax.optimization_barrier(
        (far_rows, pack, shift_scale, fits, image_blocks[1])
    )
    column_rows.insert(2, far_rows)
    other_rows = [core_both] + [send(r, swap_core()) for r in column_rows[1:]]

    qkv = call(
        project_kernel,
        tuple(sds((ROWS + CON // 2, 2 * HD)) for _ in range(4)),
        scratch=(
            pltpu.VMEM((8 * SLOTS, width), BF),
            pltpu.VMEM((ROWS, width), BF),
        ),
        limit=24,
        us=PROJ_US,
    )(at, pack, *column_rows, *other_rows, shift_scale, qk_gain, weights)

    *image_blocks, first = lax.optimization_barrier((*image_blocks, qkv[0]))
    image_q, image_kv = call(
        image_join_kernel, (sds((8 * n_img, HD)), sds((16 * n_img, HD))), smem=0
    )(*image_blocks)
    image_kvs = [image_kv] + [send(image_kv, swap_v(s)) for s in (2, 1, 3)]

    qkv = [first] + [send(qkv[s], swap_u(s)) for s in (2, 1, 3)]
    qkv = [qkv[0], qkv[2], qkv[1], qkv[3]]
    line = call(
        join_kernel,
        sds((LINE + LINE_CON // 2, 2 * HD)),
        scratch=(pltpu.VMEM((4 * CON, 3 * HD), BF), pltpu.VMEM((4 * TXT, 2 * HD), BF)),
        smem=0,
    )(*qkv, con_line, txt_line)
    lines = [line] + [send(line, swap_v(s)) for s in (2, 1, 3)]
    lines = [lines[0], lines[2], lines[1], lines[3]]
    plane = call(plane_kernel, sds((64 * n_img, HD)), smem=0)(*image_kvs)
    con_slot, plane = lax.optimization_barrier((spots[0, :n_con], plane))
    other_plane = send(plane, swap_plane())
    pick = (con_slot[:, None] == jnp.arange(4 * LINE_CON)[None, :]).astype(BF)

    image_stats = (sds((8 * n_img, 1), F32), sds((8 * n_img, 2 * HD), F32))
    stats = (sds((n_con, 1), F32), sds((n_con, 2 * HD), F32)) + image_stats
    image_near = call(image_near_kernel, image_stats, smem=0)(plane, image_q)
    q_part = call(
        order_kernel, sds((n_con, HD)), scratch=(pltpu.VMEM((2 * LINE_CON, HD), BF),), smem=0
    )(pick, lines[0], lines[1])
    con_q, *near = call(
        near_kernel,
        (sds((n_con, HD)),) + stats,
        scratch=(
            pltpu.VMEM((2 * LINE_CON, HD), BF),
            pltpu.VMEM((4 * LINE_CON, HD), BF),
            pltpu.VMEM((4 * LINE_CON, 2 * HD), BF),
            pltpu.VMEM((4 * LINE_TXT, HD), BF),
            pltpu.VMEM((4 * LINE_TXT, 2 * HD), BF),
            pltpu.VMEM((32 * n_img, 2 * HD), BF),
        ),
        limit=32,
        us=NEAR_US,
        smem=0,
    )(pick, q_part, *lines, con_bias, txt_bias, plane, image_q, *image_near)
    blocks = call(
        far_kernel,
        tuple(sds((72, n_con + HD)) for _ in range(4)),
        scratch=(pltpu.VMEM((n_con, HD), BF), pltpu.VMEM((32 * n_img, 2 * HD), BF)),
        limit=24,
        us=FAR_US,
        smem=0,
    )(other_plane, con_q, image_q, *near)
    blocks = [blocks[0]] + [send(blocks[s], swap_u(s)) for s in (2, 1, 3)]
    blocks = [blocks[0], blocks[2], blocks[1], blocks[3]]
    own, core, out_own = call(
        head_sum_kernel,
        (sds((40, n_con + HD)), sds((40, n_con + 4 * HD)), sds((32, half))),
    )(at, *blocks)
    core = send(core, swap_core())
    own = call(core_sum_kernel, sds((40, n_con + HD)), smem=0)(own, core)
    last = (at, own, send(own, swap_z(2)), core, out_own)
    finish = call(finish_kernel, (sds((n_img, 2 * half)), sds((n_img, n_con), F32)))

    def finished():
        img_out, saliency = finish(*last)
        return img_out, jnp.transpose(saliency)

    return fits > 0, finished


def on_device(*args):
    fits, finish = packed(*args)
    return lax.cond(fits, finish, lambda: tuple(general(*args)))


def solution(mesh):
    return jax.shard_map(
        on_device,
        mesh=mesh,
        in_specs=(
            P("ctx", "head"),
            P("ctx", "head"),
            P("ctx", "head"),
            P(),
            P(),
            P(),
            P(("ctx", "head"), None),
            P(),
            P(None, None, "head"),
            P(),
        ),
        out_specs=(P("ctx", "head"), P(None, "ctx")),
        check_vma=False,
    )
```

```python
import math

import jax
import jax.numpy as jnp
from jax import lax
from jax.experimental import pallas as pl
from jax.experimental.pallas import tpu as pltpu
from jax.sharding import PartitionSpec as P

BF = jnp.bfloat16
F32 = jnp.float32
HD = 128
SLOTS = 32
CON = 96
TXT = 64
ROWS = CON + TXT
LINE_CON = 320
LINE_TXT = 176
LINE = LINE_CON + LINE_TXT
MIB = 1 << 20
PROJ_US, NEAR_US, FAR_US = 5.0, 2.0, 3.0
FACTOR = HD ** (-0.5) * math.log2(math.e)


def modulate(rows, shift_scale):
    values = rows.astype(F32)
    mean = jnp.mean(values, axis=1, keepdims=True)
    centered = values - mean
    var = jnp.mean(centered * centered, axis=1, keepdims=True)
    normed = centered * lax.rsqrt(var + 1e-06)
    return (normed * (1.0 + shift_scale[1]) + shift_scale[0]).astype(BF)


def head_norm(values, gain, head_dim):
    shaped = values.reshape(values.shape[0], -1, head_dim)
    meansq = jnp.mean(shaped * shaped, axis=2, keepdims=True)
    return (shaped * lax.rsqrt(meansq + 1e-06) * gain).reshape(values.shape[0], -1)


def block_stats(queries, keys, values):
    scores = jnp.einsum("rgd,kgd->grk", queries, keys, preferred_element_type=F32)
    scores = scores * queries.shape[-1] ** (-0.5)
    peak = jnp.max(scores, axis=2)
    weights = jnp.exp(scores - peak[:, :, None])
    total = jnp.sum(weights, axis=2)
    summed = jnp.einsum("grk,kgd->grd", weights.astype(BF), values, preferred_element_type=F32)
    return (peak, total, summed)


def combine_stats(first, second):
    peak = jnp.maximum(first[0], second[0])
    left = jnp.exp(first[0] - peak)
    right = jnp.exp(second[0] - peak)
    total = first[1] * left + second[1] * right
    summed = first[2] * left[:, :, None] + second[2] * right[:, :, None]
    return (peak, total, summed)


def scaled_scores(dots, concept_sq, image_sq, width):
    concept_rms = jnp.sqrt(concept_sq / width + 1e-06)
    image_rms = jnp.sqrt(image_sq / width + 1e-06)
    return dots / (jnp.sqrt(F32(width)) * concept_rms[:, None] * image_rms[None, :])


def gather_ctx(block):
    n_ctx = lax.axis_size("ctx")
    spread = jnp.broadcast_to(block[None], (n_ctx,) + block.shape)
    return lax.all_to_all(spread, "ctx", 0, 0, tiled=True)


def general(
    img_q, img_k, img_v, txt_ids, concept_ids, step_index, token_table, modulation, txt_qkv, qk_gain
):
    n_ctx = lax.axis_size("ctx")
    n_head = lax.axis_size("head")
    head_dim = qk_gain.shape[1]
    group = img_q.shape[1] // head_dim
    text_dev = txt_ids.shape[0] // n_ctx
    concept_dev = concept_ids.shape[0] // n_ctx
    vocab_dev = token_table.shape[0]
    combined = jnp.concatenate(
        [txt_ids.reshape(n_ctx, text_dev), concept_ids.reshape(n_ctx, concept_dev)], axis=1
    ).reshape(-1)
    offset = lax.axis_index(("ctx", "head")) * vocab_dev
    wanted = combined - offset
    inside = (wanted >= 0) & (wanted < vocab_dev)
    picked = jnp.take(token_table, jnp.clip(wanted, 0, vocab_dev - 1), axis=0)
    n_all = n_ctx * n_head
    mine = jnp.where(inside[:, None], picked, jnp.zeros((), picked.dtype))
    parts = lax.all_to_all(
        mine.reshape(n_all, -1, mine.shape[1]), ("ctx", "head"), 0, 0, tiled=True
    )
    own_rows = jnp.sum(parts.astype(F32), axis=0)
    prompt_rows = lax.all_gather(own_rows.astype(BF), "head", axis=0, tiled=True)
    shift_scale = lax.dynamic_index_in_dim(modulation, step_index[0], 0, keepdims=False)
    modded = modulate(prompt_rows, shift_scale)
    text_mod = modded[:text_dev]
    concept_mod = modded[text_dev:]
    text_kv = jnp.einsum("rd,dgc->rgc", text_mod, txt_qkv[:, 1:], preferred_element_type=F32)
    concept_qkv = jnp.einsum("rd,dgc->rgc", concept_mod, txt_qkv, preferred_element_type=F32)
    text_keys = head_norm(text_kv[:, 0], qk_gain[1], head_dim).astype(BF)
    text_values = text_kv[:, 1].astype(BF)
    concept_queries = head_norm(concept_qkv[:, 0], qk_gain[0], head_dim).astype(BF)
    concept_keys = head_norm(concept_qkv[:, 1], qk_gain[1], head_dim).astype(BF)
    concept_values = concept_qkv[:, 2].astype(BF)
    local_kv = jnp.stack(
        [
            jnp.concatenate([text_keys, concept_keys], axis=0),
            jnp.concatenate([text_values, concept_values], axis=0),
        ]
    )
    prompt_kv = gather_ctx(local_kv)
    text_part = jnp.swapaxes(prompt_kv[:, :, :text_dev], 0, 1).reshape(2, -1, group, head_dim)
    concept_part = jnp.swapaxes(prompt_kv[:, :, text_dev:], 0, 1).reshape(2, -1, group, head_dim)
    image_queries = img_q.reshape(-1, group, head_dim)
    concept_q3 = concept_queries.reshape(-1, group, head_dim)
    first = block_stats(image_queries, text_part[0], text_part[1])
    second = block_stats(concept_q3, concept_part[0], concept_part[1])
    start_stats = (
        jnp.concatenate([first[0], second[0]], axis=1),
        jnp.concatenate([first[1], second[1]], axis=1),
        jnp.concatenate([first[2], second[2]], axis=1),
    )
    all_queries = jnp.concatenate([image_queries, concept_q3], axis=0)
    image_kv = gather_ctx(jnp.stack([img_k, img_v]))
    keys = image_kv[:, 0].reshape(-1, group, head_dim)
    values = image_kv[:, 1].reshape(-1, group, head_dim)
    peak, total, summed = combine_stats(start_stats, block_stats(all_queries, keys, values))
    attended = (
        jnp.transpose(summed / total[:, :, None], (1, 0, 2))
        .reshape(all_queries.shape[0], -1)
        .astype(BF)
    )
    img_rows = img_q.shape[0]
    img_out = attended[:img_rows]
    concept_out = attended[img_rows:]
    concept_all = gather_ctx(concept_out).reshape(-1, concept_out.shape[1])
    dots = lax.dot_general(
        concept_all, img_out, (((1,), (1,)), ((), ())), preferred_element_type=F32
    )
    image_f = img_out.astype(F32)
    concept_f = concept_all.astype(F32)
    image_sq = jnp.sum(image_f * image_f, axis=1)
    concept_sq = jnp.sum(concept_f * concept_f, axis=1)
    width = group * head_dim * n_head
    sums = jnp.concatenate(
        [
            jnp.concatenate([dots, concept_sq[:, None]], axis=1),
            jnp.concatenate([image_sq, jnp.zeros((1,), F32)])[None],
        ]
    ).astype(BF)
    other = lax.ppermute(sums, "head", [(0, 1), (1, 0)])
    sums = sums.astype(F32) + other.astype(F32)
    concepts = dots.shape[0]
    saliency = scaled_scores(
        sums[:concepts, :img_rows], sums[:concepts, img_rows], sums[concepts, :img_rows], width
    )
    return (img_out, saliency)


def place(x, zl, y, c, g):
    return ((((x * 2 + zl) * 4 + y) * 2 + c) * 2) + g


def pairs(move):
    found = []
    for x in range(4):
        for zl in range(2):
            for y in range(4):
                for c in range(2):
                    for g in range(2):
                        found.append((place(x, zl, y, c, g), place(*move(x, zl, y, c, g))))
    return found


def swap_z(s):
    def move(x, zl, y, c, g):
        z = (2 * g + zl) ^ s
        return x, z & 1, y, c, z >> 1

    return pairs(move)


def swap_u(s):
    return pairs(lambda x, zl, y, c, g: (x ^ s, zl, y, c, g))


def swap_v(s):
    return pairs(lambda x, zl, y, c, g: (x, zl, y ^ s, c, g))


def swap_plane():
    return pairs(lambda x, zl, y, c, g: (x, zl ^ 1, y, c, g))


def swap_core():
    return pairs(lambda x, zl, y, c, g: (x, zl, y, c ^ 1, g))


def send(array, pairing):
    return lax.ppermute(array, ("ctx", "head"), pairing)


def nt(a, b, **kw):
    return lax.dot_general(a, b, (((1,), (1,)), ((), ())), preferred_element_type=F32, **kw)


def nn(a, b):
    return lax.dot_general(a, b, (((1,), (0,)), ((), ())), preferred_element_type=F32)


def call(kernel, outs, scratch=(), limit=16, us=1.0, smem=1, in_hbm=0):
    def run(*args):
        vm = pl.BlockSpec(memory_space=pltpu.VMEM)
        sm = pl.BlockSpec(memory_space=pltpu.SMEM)
        return pl.pallas_call(
            kernel,
            out_shape=outs,
            in_specs=[sm] * smem
            + [vm] * (len(args) - smem - in_hbm)
            + [pl.BlockSpec(memory_space=pl.ANY)] * in_hbm,
            out_specs=jax.tree.map(lambda _: vm, outs),
            scratch_shapes=list(scratch),
            compiler_params=pltpu.CompilerParams(vmem_limit_bytes=limit * MIB),
            cost_estimate=pl.CostEstimate(
                flops=int(us * 1.1e9), bytes_accessed=0, transcendentals=0
            ),
        )(*args)

    return run


def sds(shape, dtype=BF):
    return jax.ShapeDtypeStruct(shape, dtype)


def column_of(owner):
    ctx = owner >> 1
    return ((ctx >> 4) << 2) | ((ctx >> 1) & 3)


def ranks(keys, classes, resets):
    n = keys.shape[1]
    blk = 256
    row = lax.broadcasted_iota(jnp.int32, (blk, blk), 0)
    col = lax.broadcasted_iota(jnp.int32, (blk, blk), 1)
    earlier = (row < col).astype(F32).astype(BF)
    label = lax.broadcasted_iota(jnp.int32, (classes, blk), 0)
    carry = jnp.zeros((classes, 1), F32)
    found, counts = [], []
    for b in range(n // blk):
        if b in resets:
            counts.append(carry)
            carry = jnp.zeros((classes, 1), F32)
        hot = (label == keys[:, b * blk : (b + 1) * blk]).astype(F32)
        before = nn(hot.astype(BF), earlier) + carry
        found.append(jnp.sum(hot * before, axis=0, keepdims=True))
        carry = carry + jnp.sum(hot, axis=1, keepdims=True)
    counts.append(carry)
    return jnp.concatenate(found, axis=1).astype(jnp.int32), counts


def plan_kernel(
    at, con_ref, txt_ref, table_ref, q_ref, k_ref, v_ref, rows_ref, both_ref, img_ref
):
    ids = jnp.concatenate([con_ref[...], txt_ref[...]], axis=1)
    n = ids.shape[1]
    blk = 256
    blocks = n // blk
    vocab_dev = table_ref.shape[0]
    mine = ((ids >> int(math.log2(vocab_dev))) == at[0]).astype(F32)
    pieces = [slice(b * blk, (b + 1) * blk) for b in range(blocks)]
    folded = jnp.concatenate(
        [mine[:, p] for p in pieces] + [jnp.zeros((8 - blocks, blk), F32)], axis=0
    )
    row = lax.broadcasted_iota(jnp.int32, (blk, blk), 0)
    col = lax.broadcasted_iota(jnp.int32, (blk, blk), 1)
    before = nn(folded.astype(BF), (row < col).astype(F32).astype(BF))
    label = lax.broadcasted_iota(jnp.int32, (SLOTS, blk), 0).astype(F32)
    found = jnp.zeros((SLOTS, blk), F32)
    skipped = jnp.zeros((1, 1), F32)
    for b, p in enumerate(pieces):
        rank = before[b : b + 1, :] + skipped
        row_in_table = ((ids[:, p] & (vocab_dev - 1)) + 1).astype(F32) * mine[:, p]
        found = found + jnp.where(label == rank, row_in_table, 0.0)
        skipped = skipped + jnp.sum(mine[:, p], axis=1, keepdims=True)
    found = jnp.sum(found, axis=1, keepdims=True).astype(jnp.int32) - 1
    pick = lax.broadcasted_iota(jnp.int32, (SLOTS, vocab_dev), 1) == found
    rows = nn(pick.astype(F32).astype(BF), table_ref[...]).astype(BF)
    rows_ref[...] = rows
    both_ref[0:SLOTS, :] = rows
    m = q_ref.shape[0]
    half = q_ref.shape[1] // 2
    lanes_own = pl.ds(pl.multiple_of(at[2] * half, half), half)
    lanes_other = pl.ds(pl.multiple_of((1 - at[2]) * half, half), half)
    for i, ref in enumerate((q_ref, k_ref, v_ref)):
        img_ref[i * m : (i + 1) * m, :] = ref[:, lanes_own]
        for j in range(2):
            lanes = slice((2 * i + j) * half, (2 * i + j + 1) * half)
            both_ref[SLOTS:, lanes] = ref[16 * j : 16 * (j + 1), lanes_other]
    both_ref[SLOTS:, 6 * half :] = jnp.zeros((16, 2 * half), BF)


def to_row(column):
    n = column.shape[0]
    diagonal = lax.broadcasted_iota(jnp.int32, (n, n), 0) == lax.broadcasted_iota(
        jnp.int32, (n, n), 1
    )
    return jnp.sum(jnp.where(diagonal, column, 0.0), axis=0, keepdims=True)


def line_plan(at, counts):
    column = lax.broadcasted_iota(jnp.int32, (16, 16), 0)
    other = lax.broadcasted_iota(jnp.int32, (16, 16), 1)
    row = to_row(counts)
    same = (column & 3) == (other & 3)
    before = same & (((other >> 2) ^ at[4]) < ((column >> 2) ^ at[4]))
    skipped = jnp.sum(jnp.where(before, row, 0.0), axis=1, keepdims=True)
    total = jnp.sum(jnp.where(same, row, 0.0), axis=1, keepdims=True)
    return skipped, total, jnp.max(total, axis=0, keepdims=True)


def per_lane(values, column):
    hot = lax.broadcasted_iota(jnp.int32, (16, column.shape[1]), 0) == column
    return jnp.sum(jnp.where(hot, values, 0.0), axis=0, keepdims=True)


def blocks_of(lanes, size, blocks):
    lane = lax.broadcasted_iota(jnp.int32, (1, lanes), 1)
    block = jnp.zeros((1, lanes), jnp.int32)
    for j in range(1, blocks):
        block = block + (lane >= j * size).astype(jnp.int32)
    return block, (lane - block * size).astype(F32)


def line_targets(at, counts, skipped, slots):
    block, slot = blocks_of(4 * slots, slots, 4)
    column = ((block ^ at[4]) << 2) | at[5]
    target = per_lane(skipped, column) + slot
    return jnp.where(slot < per_lane(counts, column), target, -1.0).astype(jnp.int32)


def line_bias(at, total, rows):
    block, slot = blocks_of(4 * rows, rows, 4)
    column = (at[4] << 2) | (block ^ at[5])
    return jnp.where(slot < per_lane(total, column), 0.0, -1e30)


def pack_kernel(
    at, con_ref, txt_ref, w_hbm, out_ref, spot_ref, con_bias, txt_bias, con_line, txt_line, w_ref, sem
):
    half = w_ref.shape[2]
    lanes = pl.ds(pl.multiple_of(at[2] * half, half), half)
    weights = pltpu.make_async_copy(w_hbm.at[0:2, :, lanes], w_ref, sem)
    weights.start()
    ids = jnp.concatenate([con_ref[...], txt_ref[...]], axis=1)
    n = ids.shape[1]
    n_con = con_ref.shape[1]
    owner = ids >> 8
    column = column_of(owner)
    here = column == at[1]
    z = ((owner & 1) << 1) | ((owner >> 4) & 1)
    core = (owner >> 1) & 1
    piece = jnp.where(here, jnp.where(core == at[2], 0, 4) + (at[3] ^ z), -1)
    rank, _ = ranks(piece, 8, ())
    spot, (con_counts, txt_counts) = ranks(column, 16, (n_con // 256,))
    con_skip, con_total, con_most = line_plan(at, con_counts)
    txt_skip, txt_total, txt_most = line_plan(at, txt_counts)
    con_bias[...] = line_bias(at, con_total, LINE_CON)
    txt_bias[...] = line_bias(at, txt_total, LINE_TXT)
    con_line[...] = line_targets(at, con_counts, con_skip, CON)
    txt_line[...] = line_targets(at, txt_counts, txt_skip, TXT)
    spot_ref[0:1, :] = (
        ((column & 3) ^ at[5]) * LINE_CON + per_lane(con_skip, column).astype(jnp.int32) + spot
    )
    wanted = (lax.broadcasted_iota(jnp.int32, (128, n), 0) == owner).astype(F32)
    over = jnp.maximum(
        jnp.maximum(
            jnp.max(con_counts, axis=0, keepdims=True) - CON,
            jnp.max(txt_counts, axis=0, keepdims=True) - TXT,
        ),
        jnp.maximum(con_most - LINE_CON, txt_most - LINE_TXT),
    )
    most = jnp.max(jnp.sum(wanted, axis=1, keepdims=True), axis=0, keepdims=True)
    over = jnp.maximum(over, most - SLOTS)
    spot_ref[1:2, :] = jnp.broadcast_to(over.astype(jnp.int32), (1, n))
    spot_ref[2:8, :] = jnp.zeros((6, n), jnp.int32)
    concept = lax.broadcasted_iota(jnp.int32, (1, n), 1) < n_con
    target = jnp.where(
        concept, jnp.where(spot < CON, spot, -1), jnp.where(spot < TXT, spot + CON, -1)
    )
    source = jnp.where(here & (rank < SLOTS), piece * SLOTS + rank, -1)
    target = jnp.where(here, target, -1)
    hot_t = (lax.broadcasted_iota(jnp.int32, (ROWS, n), 0) == target).astype(F32).astype(BF)
    hot_s = (lax.broadcasted_iota(jnp.int32, (8 * SLOTS, n), 0) == source).astype(F32).astype(BF)
    out_ref[...] = nt(hot_t, hot_s).astype(BF)
    weights.wait()


def project_kernel(at, pack_ref, *refs):
    rows, (mod_ref, gain_ref, w_ref, w_hbm), outs, (raw_ref, x_ref, w_last, sem) = (
        refs[:8], refs[8:12], refs[12:16], refs[16:]
    )
    half = w_ref.shape[2]
    lanes = pl.ds(pl.multiple_of(at[2] * half, half), half)
    weights = pltpu.make_async_copy(w_hbm.at[2, :, lanes], w_last, sem)
    weights.start()
    for i, ref in enumerate(rows):
        raw_ref[i * SLOTS : (i + 1) * SLOTS, :] = ref[0:SLOTS, :]
    shift = mod_ref[0:1, :]
    scale = 1.0 + mod_ref[1:2, :]
    for i in range(ROWS // 32):
        block = slice(i * 32, (i + 1) * 32)
        values = nn(pack_ref[block, :], raw_ref[...])
        mean = jnp.mean(values, axis=1, keepdims=True)
        centered = values - mean
        var = jnp.mean(centered * centered, axis=1, keepdims=True)
        x_ref[block, :] = (centered * lax.rsqrt(var + 1e-06) * scale + shift).astype(BF)

    def normed(u, gain):
        meansq = jnp.mean(u * u, axis=1, keepdims=True)
        return u * lax.rsqrt(meansq + 1e-06) * gain

    q = nn(x_ref[0:CON, :], w_ref[0])
    k = nn(x_ref[...], w_ref[1])
    weights.wait()
    v = nn(x_ref[...], w_last[...])
    heads = []
    for h in range(3):
        cols = slice(h * HD, (h + 1) * HD)
        heads.append(
            (
                (normed(q[:, cols], gain_ref[0:1, :]) * FACTOR).astype(BF),
                normed(k[:, cols], gain_ref[1:2, :]).astype(BF),
                v[:, cols].astype(BF),
            )
        )
    for s, out in enumerate(outs):
        head = jnp.minimum(at[4] ^ s, 2)
        for h in range(3):

            @pl.when(head == h)
            def _(h=h, out=out):
                out[0:ROWS, 0:HD] = heads[h][1]
                out[0:ROWS, HD:] = heads[h][2]
                out[ROWS:, 0:HD] = heads[h][0][: CON // 2]
                out[ROWS:, HD:] = heads[h][0][CON // 2 :]


def join_kernel(a, b, c, d, con_line, txt_line, out, con, txt):
    for i, ref in enumerate((a, b, c, d)):
        con[i * CON : (i + 1) * CON, 0 : 2 * HD] = ref[0:CON, :]
        con[i * CON : i * CON + CON // 2, 2 * HD :] = ref[ROWS:, 0:HD]
        con[i * CON + CON // 2 : (i + 1) * CON, 2 * HD :] = ref[ROWS:, HD:]
        txt[i * TXT : (i + 1) * TXT, :] = ref[CON:ROWS, :]
    hot = lax.broadcasted_iota(jnp.int32, (LINE_CON, 4 * CON), 0) == con_line[...]
    found = nn(hot.astype(F32).astype(BF), con[...]).astype(BF)
    out[0:LINE_CON, :] = found[:, 0 : 2 * HD]
    out[LINE:, 0:HD] = found[: LINE_CON // 2, 2 * HD :]
    out[LINE:, HD:] = found[LINE_CON // 2 :, 2 * HD :]
    hot = lax.broadcasted_iota(jnp.int32, (LINE_TXT, 4 * TXT), 0) == txt_line[...]
    out[LINE_CON:LINE, :] = nn(hot.astype(F32).astype(BF), txt[...]).astype(BF)


def image_heads_kernel(at, own, core, *outs):
    n, half = own.shape[0] // 3, own.shape[1]
    for s, out in enumerate(outs):
        head = jnp.minimum(at[4] ^ s, 2)
        lanes = pl.ds(pl.multiple_of(head * HD, HD), HD)
        for i in range(3):
            row = 2 * i * n
            out[row : row + n, :] = own[i * n : (i + 1) * n, lanes]
            for j in range(2):
                there = pl.ds(pl.multiple_of((2 * i + j) * half + head * HD, HD), HD)
                out[row + n + 16 * j : row + n + 16 * (j + 1), :] = core[SLOTS:, there]


def image_join_kernel(a, b, c, d, q_out, kv_out):
    n = a.shape[0] // 3
    for i, ref in enumerate((a, b, c, d)):
        q_out[n * i : n * (i + 1), :] = ref[0:n, :]
        kv_out[n * i : n * (i + 1), :] = ref[n : 2 * n, :]
        kv_out[n * (4 + i) : n * (5 + i), :] = ref[2 * n :, :]


def plane_kernel(a, b, c, d, out):
    n = a.shape[0] // 2
    for i, ref in enumerate((a, b, c, d)):
        out[n * i : n * (i + 1), :] = ref[0:n, :]
        out[n * (4 + i) : n * (5 + i), :] = ref[n:, :]


def weigh(q, parts, factor):
    scores = []
    for keys, _, bias in parts:
        part = nt(q, keys)
        scores.append(part if bias is None else part + bias)
    peak = scores[0].max(axis=1, keepdims=True)
    for part in scores[1:]:
        peak = jnp.maximum(peak, part.max(axis=1, keepdims=True))
    total = None
    for part, (_, values, _) in zip(scores, parts):
        power = part - peak
        weights = jnp.exp2(power if factor is None else power * factor).astype(BF)
        summed = nn(weights, values)
        total = summed if total is None else total + summed
    return (peak if factor is None else peak * factor), total


def join(first, second):
    peak = jnp.maximum(first[0], second[0])
    return peak, first[1] * jnp.exp2(first[0] - peak) + second[1] * jnp.exp2(second[0] - peak)


def merge(first, second):
    _, summed = join(first, second)
    return (summed[:, 0:HD] / summed[:, HD:]).astype(BF)


def with_ones(values):
    return jnp.concatenate([values, jnp.ones_like(values)], axis=1)


def image_near_kernel(plane, q, peak, summed):
    n = plane.shape[0] // 2
    part = (plane[0:n, :], with_ones(plane[n:, :]), None)
    peak[...], summed[...] = weigh(q[...], (part,), FACTOR)


def line_queries(con_q, refs):
    n = LINE_CON
    for a, ref in enumerate(refs):
        con_q[a * n : a * n + n // 2, :] = ref[LINE:, 0:HD]
        con_q[a * n + n // 2 : (a + 1) * n, :] = ref[LINE:, HD:]


def order_kernel(pick, l0, l1, q_out, con_q):
    line_queries(con_q, (l0, l1))
    q_out[...] = nn(pick[:, : 2 * LINE_CON], con_q[...]).astype(BF)


def weigh_blocks(q, parts, store):
    blk = 256
    blocks = [slice(b, b + blk) for b in range(0, q.shape[0], blk)]

    def scores(rows):
        found = []
        for keys, _, bias in parts:
            part = nt(q[rows, :], keys[...])
            found.append(part if bias is None else part + bias[...])
        return found

    ready = scores(blocks[0])
    for b, rows in enumerate(blocks):
        now, ready = ready, scores(blocks[b + 1]) if b + 1 < len(blocks) else None
        peak = now[0].max(axis=1, keepdims=True)
        for part in now[1:]:
            peak = jnp.maximum(peak, part.max(axis=1, keepdims=True))
        summed = sum(
            nn(jnp.exp2(part - peak).astype(BF), values[...])
            for part, (_, values, _) in zip(now, parts)
        )
        store(rows, peak, summed)


def near_kernel(
    pick, q_part, l0, l1, l2, l3, con_bias, txt_bias, plane, img_q, im, ims, *refs
):
    q_out, cm_out, cs_out, im_out, ims_out = refs[:5]
    con_q, con_k, con_v, txt_k, txt_v, img_v = refs[5:]
    n, m = LINE_CON, LINE_TXT
    line_queries(con_q, (l2, l3))
    for a, ref in enumerate((l0, l1, l2, l3)):
        con_k[a * n : (a + 1) * n, :] = ref[0:n, 0:HD]
        con_v[a * n : (a + 1) * n, :] = with_ones(ref[0:n, HD:])
        txt_k[a * m : (a + 1) * m, :] = ref[n:LINE, 0:HD]
        txt_v[a * m : (a + 1) * m, :] = with_ones(ref[n:LINE, HD:])
    n_img = plane.shape[0] // 2
    img_v[...] = with_ones(plane[n_img:, :])
    rest = nn(pick[:, 2 * n :], con_q[...])
    q_out[...] = (rest + q_part[...].astype(F32)).astype(BF)

    def store(rows, peak, summed):
        cm_out[rows, :] = peak
        cs_out[rows, :] = summed

    parts = ((plane.at[0:n_img, :], img_v, None), (con_k, con_v, con_bias))
    weigh_blocks(q_out, parts, store)
    text = weigh(img_q[...], ((txt_k[...], txt_v[...], txt_bias[...]),), FACTOR)
    im_out[...], ims_out[...] = join(text, (im[...], ims[...]))


def far_kernel(plane, con_q, img_q, cm, cs, im, ims, *refs):
    outs, (con_out, img_v) = refs[:2], refs[2:]
    n_img = plane.shape[0] // 2
    img_v[...] = with_ones(plane[n_img:, :])
    part = (plane[0:n_img, :], img_v[...], None)
    img = merge(weigh(img_q[...], (part,), FACTOR), (im[...], ims[...]))
    n_con = con_out.shape[0]

    def store(rows, peak, summed):
        con_out[rows, :] = merge((peak, summed), (cm[rows, :], cs[rows, :]))

    weigh_blocks(con_q, ((plane.at[0:n_img, :], img_v, None),), store)
    dots = nt(img, con_out[...]).astype(BF)
    con_f = con_out[...].astype(F32)
    squares = con_f * con_f
    high = squares.astype(BF)
    ones = jnp.ones((8, HD), BF)
    con_sq = (nt(ones, high) + nt(ones, (squares - high.astype(F32)).astype(BF))).astype(BF)
    for j, out in enumerate(outs):
        for s in range(4):
            rows = slice(s * 64 + j * 32, s * 64 + (j + 1) * 32)
            out[s * 32 : (s + 1) * 32, 0:n_con] = dots[rows]
            out[s * 32 : (s + 1) * 32, n_con:] = img[rows]
        out[128:136, 0:n_con] = con_sq
        out[128:136, n_con:] = jnp.zeros((8, HD), BF)


def core_sum_kernel(at, own, core, *outs):
    n_con = own.shape[1] - HD
    con_sq = (own[128:136, 0:n_con].astype(F32) + core[128:136, 0:n_con].astype(F32)).astype(BF)
    mine = pl.ds(pl.multiple_of(n_con + at[2] * HD, HD), HD)
    theirs = pl.ds(pl.multiple_of(n_con + (1 - at[2]) * HD, HD), HD)
    for s, out in enumerate(outs):
        rows = slice(s * 32, (s + 1) * 32)
        out[0:32, 0:n_con] = (
            own[rows, 0:n_con].astype(F32) + core[rows, 0:n_con].astype(F32)
        ).astype(BF)
        out[0:32, mine] = own[rows, n_con:]
        out[0:32, theirs] = core[rows, n_con:]
        out[32:40, 0:n_con] = con_sq
        out[32:40, n_con:] = jnp.zeros((8, 2 * HD), BF)


def head_sum_kernel(at, b0, b1, b2, b3, sums, img):
    n_con = b0.shape[1] - 2 * HD
    total = jnp.zeros((40, n_con), F32)
    outs = [jnp.zeros((32, HD), BF) for _ in range(6)]
    for s, ref in enumerate((b0, b1, b2, b3)):
        head = at[4] ^ s
        total = total + jnp.where(head < 3, ref[:, 0:n_con].astype(F32), 0.0)
        for h in range(6):
            lanes = slice(n_con + (h // 3) * HD, n_con + (h // 3 + 1) * HD)
            outs[h] = jnp.where(head == h % 3, ref[0:32, lanes], outs[h])
    image_sq = jnp.zeros((32, 1), F32)
    for h in range(6):
        out_f = outs[h].astype(F32)
        image_sq = image_sq + jnp.sum(out_f * out_f, axis=1, keepdims=True)
        img[:, h * HD : (h + 1) * HD] = outs[h]
    sums[:, 0:n_con] = total.astype(BF)
    sums[0:32, n_con:] = jnp.broadcast_to(image_sq, (32, HD)).astype(BF)
    sums[32:40, n_con:] = jnp.zeros((8, HD), BF)


def finish_kernel(own, head, img, img_ref, sal_ref):
    n_con = own.shape[1] - HD
    width = 12 * HD
    total = own[...].astype(F32) + head[...].astype(F32)
    con_rms = jnp.sqrt(total[32:33, 0:n_con] / width + 1e-06)
    img_rms = jnp.sqrt(total[0:32, n_con : n_con + 1] / width + 1e-06)
    sal_ref[...] = total[0:32, 0:n_con] / (math.sqrt(width) * con_rms * img_rms)
    img_ref[...] = img[...]


def packed(
    img_q, img_k, img_v, txt_ids, concept_ids, step_index, token_table, modulation, txt_qkv, qk_gain
):
    n_con, n_txt = concept_ids.shape[0], txt_ids.shape[0]
    ctx = lax.axis_index("ctx")
    g = lax.axis_index("head")
    c = ctx & 1
    y = (ctx >> 1) & 3
    zl = (ctx >> 3) & 1
    x = ctx >> 4
    at = jnp.stack([ctx * 2 + g, x * 4 + y, c, 2 * g + zl, x, y]).astype(jnp.int32)
    con_ids, text_ids = concept_ids[None, :], txt_ids[None, :]
    n = n_con + n_txt
    width = token_table.shape[1]
    half = txt_qkv.shape[2] // 2
    n_img = img_q.shape[0]

    own_rows, own_both, own_img = call(
        plan_kernel, (sds((SLOTS, width)), sds((SLOTS + 16, width)), sds((3 * n_img, half)))
    )(at, con_ids, text_ids, token_table, img_q, img_k, img_v)
    far_rows = send(own_rows, swap_z(2))
    column_rows = [own_rows] + [send(own_rows, swap_z(s)) for s in (1, 3)]
    core_both = send(own_both, swap_core())

    all_weights = jnp.transpose(txt_qkv, (1, 0, 2))
    pack, spots, con_bias, txt_bias, con_line, txt_line, weights = call(
        pack_kernel,
        (
            sds((ROWS, 8 * SLOTS)),
            sds((8, n), jnp.int32),
            sds((1, 4 * LINE_CON), F32),
            sds((1, 4 * LINE_TXT), F32),
            sds((1, 4 * CON), jnp.int32),
            sds((1, 4 * TXT), jnp.int32),
            sds((2, width, half)),
        ),
        scratch=(pltpu.SemaphoreType.DMA,),
        limit=24,
        us=2.0,
        in_hbm=1,
    )(at, con_ids, text_ids, all_weights)
    shift_scale = lax.dynamic_index_in_dim(modulation, step_index[0], 0, keepdims=False)

    image_blocks = call(
        image_heads_kernel, tuple(sds((6 * n_img, HD)) for _ in range(4))
    )(at, own_img, core_both)
    image_blocks = [image_blocks[0]] + [send(image_blocks[s], swap_u(s)) for s in (2, 1, 3)]
    image_blocks = [image_blocks[0], image_blocks[2], image_blocks[1], image_blocks[3]]
    column_rows[1], image_blocks[2] = lax.optimization_barrier((column_rows[1], image_blocks[2]))
    far_rows, pack, shift_scale, image_blocks[1] = lax.optimization_barrier(
        (far_rows, pack, shift_scale, image_blocks[1])
    )
    column_rows.insert(2, far_rows)
    other_rows = [core_both] + [send(r, swap_core()) for r in column_rows[1:]]

    qkv = call(
        project_kernel,
        tuple(sds((ROWS + CON // 2, 2 * HD)) for _ in range(4)),
        scratch=(
            pltpu.VMEM((8 * SLOTS, width), BF),
            pltpu.VMEM((ROWS, width), BF),
            pltpu.VMEM((width, half), BF),
            pltpu.SemaphoreType.DMA,
        ),
        limit=24,
        us=PROJ_US,
        in_hbm=1,
    )(at, pack, *column_rows, *other_rows, shift_scale, qk_gain, weights, all_weights)

    *image_blocks, first = lax.optimization_barrier((*image_blocks, qkv[0]))
    image_q, image_kv = call(
        image_join_kernel, (sds((8 * n_img, HD)), sds((16 * n_img, HD))), smem=0
    )(*image_blocks)
    image_kvs = [image_kv] + [send(image_kv, swap_v(s)) for s in (2, 1, 3)]

    qkv = [first] + [send(qkv[s], swap_u(s)) for s in (2, 1, 3)]
    qkv = [qkv[0], qkv[2], qkv[1], qkv[3]]
    line = call(
        join_kernel,
        sds((LINE + LINE_CON // 2, 2 * HD)),
        scratch=(pltpu.VMEM((4 * CON, 3 * HD), BF), pltpu.VMEM((4 * TXT, 2 * HD), BF)),
        smem=0,
    )(*qkv, con_line, txt_line)
    lines = [line] + [send(line, swap_v(s)) for s in (2, 1, 3)]
    lines = [lines[0], lines[2], lines[1], lines[3]]
    plane = call(plane_kernel, sds((64 * n_img, HD)), smem=0)(*image_kvs)
    con_slot, over, plane = lax.optimization_barrier((spots[0, :n_con], spots[1, 0], plane))
    other_plane = send(plane, swap_plane())
    pick = (con_slot[:, None] == jnp.arange(4 * LINE_CON)[None, :]).astype(BF)

    image_stats = (sds((8 * n_img, 1), F32), sds((8 * n_img, 2 * HD), F32))
    stats = (sds((n_con, 1), F32), sds((n_con, 2 * HD), F32)) + image_stats
    image_near = call(image_near_kernel, image_stats, smem=0)(plane, image_q)
    q_part = call(
        order_kernel, sds((n_con, HD)), scratch=(pltpu.VMEM((2 * LINE_CON, HD), BF),), smem=0
    )(pick, lines[0], lines[1])
    con_q, *near = call(
        near_kernel,
        (sds((n_con, HD)),) + stats,
        scratch=(
            pltpu.VMEM((2 * LINE_CON, HD), BF),
            pltpu.VMEM((4 * LINE_CON, HD), BF),
            pltpu.VMEM((4 * LINE_CON, 2 * HD), BF),
            pltpu.VMEM((4 * LINE_TXT, HD), BF),
            pltpu.VMEM((4 * LINE_TXT, 2 * HD), BF),
            pltpu.VMEM((32 * n_img, 2 * HD), BF),
        ),
        limit=32,
        us=NEAR_US,
        smem=0,
    )(pick, q_part, *lines, con_bias, txt_bias, plane, image_q, *image_near)
    own, core = call(
        far_kernel,
        tuple(sds((136, n_con + HD)) for _ in range(2)),
        scratch=(pltpu.VMEM((n_con, HD), BF), pltpu.VMEM((32 * n_img, 2 * HD), BF)),
        limit=24,
        us=FAR_US,
        smem=0,
    )(other_plane, con_q, image_q, *near)
    blocks = call(core_sum_kernel, tuple(sds((40, n_con + 2 * HD)) for _ in range(4)))(
        at, own, send(core, swap_core())
    )
    blocks = [blocks[0]] + [send(blocks[s], swap_u(s)) for s in (1, 2, 3)]
    sums, img = call(head_sum_kernel, (sds((40, n_con + HD)), sds((n_img, 2 * half))))(at, *blocks)
    last = (sums, send(sums, swap_z(2)), img)
    finish = call(finish_kernel, (sds((n_img, 2 * half)), sds((n_img, n_con), F32)), smem=0)

    def finished():
        img_out, saliency = finish(*last)
        return img_out, jnp.transpose(saliency)

    return over <= 0, finished


def on_device(*args):
    fits, finish = packed(*args)
    return lax.cond(fits, finish, lambda: tuple(general(*args)))


def solution(mesh):
    return jax.shard_map(
        on_device,
        mesh=mesh,
        in_specs=(
            P("ctx", "head"),
            P("ctx", "head"),
            P("ctx", "head"),
            P(),
            P(),
            P(),
            P(("ctx", "head"), None),
            P(),
            P(None, None, "head"),
            P(),
        ),
        out_specs=(P("ctx", "head"), P(None, "ctx")),
        check_vma=False,
    )
```

```python
import math

import jax
import jax.numpy as jnp
from jax import lax
from jax.experimental import pallas as pl
from jax.experimental.pallas import tpu as pltpu
from jax.sharding import PartitionSpec as P

BF = jnp.bfloat16
F32 = jnp.float32
HD = 128
SLOTS = 32
CON = 96
TXT = 64
ROWS = CON + TXT
LINE_CON = 320
LINE_TXT = 176
LINE = LINE_CON + LINE_TXT
MIB = 1 << 20
PROJ_US, NEAR_US, FAR_US = 5.0, 2.0, 3.0
FACTOR = HD ** (-0.5) * math.log2(math.e)


def modulate(rows, shift_scale):
    values = rows.astype(F32)
    mean = jnp.mean(values, axis=1, keepdims=True)
    centered = values - mean
    var = jnp.mean(centered * centered, axis=1, keepdims=True)
    normed = centered * lax.rsqrt(var + 1e-06)
    return (normed * (1.0 + shift_scale[1]) + shift_scale[0]).astype(BF)


def head_norm(values, gain, head_dim):
    shaped = values.reshape(values.shape[0], -1, head_dim)
    meansq = jnp.mean(shaped * shaped, axis=2, keepdims=True)
    return (shaped * lax.rsqrt(meansq + 1e-06) * gain).reshape(values.shape[0], -1)


def block_stats(queries, keys, values):
    scores = jnp.einsum("rgd,kgd->grk", queries, keys, preferred_element_type=F32)
    scores = scores * queries.shape[-1] ** (-0.5)
    peak = jnp.max(scores, axis=2)
    weights = jnp.exp(scores - peak[:, :, None])
    total = jnp.sum(weights, axis=2)
    summed = jnp.einsum("grk,kgd->grd", weights.astype(BF), values, preferred_element_type=F32)
    return (peak, total, summed)


def combine_stats(first, second):
    peak = jnp.maximum(first[0], second[0])
    left = jnp.exp(first[0] - peak)
    right = jnp.exp(second[0] - peak)
    total = first[1] * left + second[1] * right
    summed = first[2] * left[:, :, None] + second[2] * right[:, :, None]
    return (peak, total, summed)


def scaled_scores(dots, concept_sq, image_sq, width):
    concept_rms = jnp.sqrt(concept_sq / width + 1e-06)
    image_rms = jnp.sqrt(image_sq / width + 1e-06)
    return dots / (jnp.sqrt(F32(width)) * concept_rms[:, None] * image_rms[None, :])


def gather_ctx(block):
    n_ctx = lax.axis_size("ctx")
    spread = jnp.broadcast_to(block[None], (n_ctx,) + block.shape)
    return lax.all_to_all(spread, "ctx", 0, 0, tiled=True)


def general(
    img_q, img_k, img_v, txt_ids, concept_ids, step_index, token_table, modulation, txt_qkv, qk_gain
):
    n_ctx = lax.axis_size("ctx")
    n_head = lax.axis_size("head")
    head_dim = qk_gain.shape[1]
    group = img_q.shape[1] // head_dim
    text_dev = txt_ids.shape[0] // n_ctx
    concept_dev = concept_ids.shape[0] // n_ctx
    vocab_dev = token_table.shape[0]
    combined = jnp.concatenate(
        [txt_ids.reshape(n_ctx, text_dev), concept_ids.reshape(n_ctx, concept_dev)], axis=1
    ).reshape(-1)
    offset = lax.axis_index(("ctx", "head")) * vocab_dev
    wanted = combined - offset
    inside = (wanted >= 0) & (wanted < vocab_dev)
    picked = jnp.take(token_table, jnp.clip(wanted, 0, vocab_dev - 1), axis=0)
    n_all = n_ctx * n_head
    mine = jnp.where(inside[:, None], picked, jnp.zeros((), picked.dtype))
    parts = lax.all_to_all(
        mine.reshape(n_all, -1, mine.shape[1]), ("ctx", "head"), 0, 0, tiled=True
    )
    own_rows = jnp.sum(parts.astype(F32), axis=0)
    prompt_rows = lax.all_gather(own_rows.astype(BF), "head", axis=0, tiled=True)
    shift_scale = lax.dynamic_index_in_dim(modulation, step_index[0], 0, keepdims=False)
    modded = modulate(prompt_rows, shift_scale)
    text_mod = modded[:text_dev]
    concept_mod = modded[text_dev:]
    text_kv = jnp.einsum("rd,dgc->rgc", text_mod, txt_qkv[:, 1:], preferred_element_type=F32)
    concept_qkv = jnp.einsum("rd,dgc->rgc", concept_mod, txt_qkv, preferred_element_type=F32)
    text_keys = head_norm(text_kv[:, 0], qk_gain[1], head_dim).astype(BF)
    text_values = text_kv[:, 1].astype(BF)
    concept_queries = head_norm(concept_qkv[:, 0], qk_gain[0], head_dim).astype(BF)
    concept_keys = head_norm(concept_qkv[:, 1], qk_gain[1], head_dim).astype(BF)
    concept_values = concept_qkv[:, 2].astype(BF)
    local_kv = jnp.stack(
        [
            jnp.concatenate([text_keys, concept_keys], axis=0),
            jnp.concatenate([text_values, concept_values], axis=0),
        ]
    )
    prompt_kv = gather_ctx(local_kv)
    text_part = jnp.swapaxes(prompt_kv[:, :, :text_dev], 0, 1).reshape(2, -1, group, head_dim)
    concept_part = jnp.swapaxes(prompt_kv[:, :, text_dev:], 0, 1).reshape(2, -1, group, head_dim)
    image_queries = img_q.reshape(-1, group, head_dim)
    concept_q3 = concept_queries.reshape(-1, group, head_dim)
    first = block_stats(image_queries, text_part[0], text_part[1])
    second = block_stats(concept_q3, concept_part[0], concept_part[1])
    start_stats = (
        jnp.concatenate([first[0], second[0]], axis=1),
        jnp.concatenate([first[1], second[1]], axis=1),
        jnp.concatenate([first[2], second[2]], axis=1),
    )
    all_queries = jnp.concatenate([image_queries, concept_q3], axis=0)
    image_kv = gather_ctx(jnp.stack([img_k, img_v]))
    keys = image_kv[:, 0].reshape(-1, group, head_dim)
    values = image_kv[:, 1].reshape(-1, group, head_dim)
    peak, total, summed = combine_stats(start_stats, block_stats(all_queries, keys, values))
    attended = (
        jnp.transpose(summed / total[:, :, None], (1, 0, 2))
        .reshape(all_queries.shape[0], -1)
        .astype(BF)
    )
    img_rows = img_q.shape[0]
    img_out = attended[:img_rows]
    concept_out = attended[img_rows:]
    concept_all = gather_ctx(concept_out).reshape(-1, concept_out.shape[1])
    dots = lax.dot_general(
        concept_all, img_out, (((1,), (1,)), ((), ())), preferred_element_type=F32
    )
    image_f = img_out.astype(F32)
    concept_f = concept_all.astype(F32)
    image_sq = jnp.sum(image_f * image_f, axis=1)
    concept_sq = jnp.sum(concept_f * concept_f, axis=1)
    width = group * head_dim * n_head
    sums = jnp.concatenate(
        [
            jnp.concatenate([dots, concept_sq[:, None]], axis=1),
            jnp.concatenate([image_sq, jnp.zeros((1,), F32)])[None],
        ]
    ).astype(BF)
    other = lax.ppermute(sums, "head", [(0, 1), (1, 0)])
    sums = sums.astype(F32) + other.astype(F32)
    concepts = dots.shape[0]
    saliency = scaled_scores(
        sums[:concepts, :img_rows], sums[:concepts, img_rows], sums[concepts, :img_rows], width
    )
    return (img_out, saliency)


def place(x, zl, y, c, g):
    return ((((x * 2 + zl) * 4 + y) * 2 + c) * 2) + g


def pairs(move):
    found = []
    for x in range(4):
        for zl in range(2):
            for y in range(4):
                for c in range(2):
                    for g in range(2):
                        found.append((place(x, zl, y, c, g), place(*move(x, zl, y, c, g))))
    return found


def swap_z(s):
    def move(x, zl, y, c, g):
        z = (2 * g + zl) ^ s
        return x, z & 1, y, c, z >> 1

    return pairs(move)


def swap_u(s):
    return pairs(
        lambda x, zl, y, c, g: (x, zl, y ^ s, c, g) if c else (x ^ s, zl, y, c, g)
    )


def swap_v(s):
    return pairs(
        lambda x, zl, y, c, g: (x ^ s, zl, y, c, g) if c else (x, zl, y ^ s, c, g)
    )


def swap_plane():
    return pairs(lambda x, zl, y, c, g: (x, zl ^ 1, y, c, g))


def swap_core():
    return pairs(lambda x, zl, y, c, g: (x, zl, y, c ^ 1, g))


def send(array, pairing):
    return lax.ppermute(array, ("ctx", "head"), pairing)


def nt(a, b, **kw):
    return lax.dot_general(a, b, (((1,), (1,)), ((), ())), preferred_element_type=F32, **kw)


def nn(a, b):
    return lax.dot_general(a, b, (((1,), (0,)), ((), ())), preferred_element_type=F32)


def call(kernel, outs, scratch=(), limit=16, us=1.0, smem=1, in_hbm=0):
    def run(*args):
        vm = pl.BlockSpec(memory_space=pltpu.VMEM)
        sm = pl.BlockSpec(memory_space=pltpu.SMEM)
        return pl.pallas_call(
            kernel,
            out_shape=outs,
            in_specs=[sm] * smem
            + [vm] * (len(args) - smem - in_hbm)
            + [pl.BlockSpec(memory_space=pl.ANY)] * in_hbm,
            out_specs=jax.tree.map(lambda _: vm, outs),
            scratch_shapes=list(scratch),
            compiler_params=pltpu.CompilerParams(vmem_limit_bytes=limit * MIB),
            cost_estimate=pl.CostEstimate(
                flops=int(us * 1.1e9), bytes_accessed=0, transcendentals=0
            ),
        )(*args)

    return run


def sds(shape, dtype=BF):
    return jax.ShapeDtypeStruct(shape, dtype)


def column_of(owner):
    ctx = owner >> 1
    return ((ctx >> 4) << 2) | ((ctx >> 1) & 3)


def ranks(keys, classes, resets):
    n = keys.shape[1]
    blk = 256
    row = lax.broadcasted_iota(jnp.int32, (blk, blk), 0)
    col = lax.broadcasted_iota(jnp.int32, (blk, blk), 1)
    earlier = (row < col).astype(F32).astype(BF)
    label = lax.broadcasted_iota(jnp.int32, (classes, blk), 0)
    carry = jnp.zeros((classes, 1), F32)
    found, counts = [], []
    for b in range(n // blk):
        if b in resets:
            counts.append(carry)
            carry = jnp.zeros((classes, 1), F32)
        hot = (label == keys[:, b * blk : (b + 1) * blk]).astype(F32)
        before = nn(hot.astype(BF), earlier) + carry
        found.append(jnp.sum(hot * before, axis=0, keepdims=True))
        carry = carry + jnp.sum(hot, axis=1, keepdims=True)
    counts.append(carry)
    return jnp.concatenate(found, axis=1).astype(jnp.int32), counts


def plan_kernel(
    at, con_ref, txt_ref, table_ref, q_ref, k_ref, v_ref, rows_ref, both_ref, img_ref
):
    ids = jnp.concatenate([con_ref[...], txt_ref[...]], axis=1)
    n = ids.shape[1]
    blk = 256
    blocks = n // blk
    vocab_dev = table_ref.shape[0]
    mine = ((ids >> int(math.log2(vocab_dev))) == at[0]).astype(F32)
    pieces = [slice(b * blk, (b + 1) * blk) for b in range(blocks)]
    folded = jnp.concatenate(
        [mine[:, p] for p in pieces] + [jnp.zeros((8 - blocks, blk), F32)], axis=0
    )
    row = lax.broadcasted_iota(jnp.int32, (blk, blk), 0)
    col = lax.broadcasted_iota(jnp.int32, (blk, blk), 1)
    before = nn(folded.astype(BF), (row < col).astype(F32).astype(BF))
    label = lax.broadcasted_iota(jnp.int32, (SLOTS, blk), 0).astype(F32)
    found = jnp.zeros((SLOTS, blk), F32)
    skipped = jnp.zeros((1, 1), F32)
    for b, p in enumerate(pieces):
        rank = before[b : b + 1, :] + skipped
        row_in_table = ((ids[:, p] & (vocab_dev - 1)) + 1).astype(F32) * mine[:, p]
        found = found + jnp.where(label == rank, row_in_table, 0.0)
        skipped = skipped + jnp.sum(mine[:, p], axis=1, keepdims=True)
    found = jnp.sum(found, axis=1, keepdims=True).astype(jnp.int32) - 1
    pick = lax.broadcasted_iota(jnp.int32, (SLOTS, vocab_dev), 1) == found
    rows = nn(pick.astype(F32).astype(BF), table_ref[...]).astype(BF)
    rows_ref[...] = rows
    both_ref[0:SLOTS, :] = rows
    m = q_ref.shape[0]
    half = q_ref.shape[1] // 2
    lanes_own = pl.ds(pl.multiple_of(at[2] * half, half), half)
    lanes_other = pl.ds(pl.multiple_of((1 - at[2]) * half, half), half)
    for i, ref in enumerate((q_ref, k_ref, v_ref)):
        img_ref[i * m : (i + 1) * m, :] = ref[:, lanes_own]
        for j in range(2):
            lanes = slice((2 * i + j) * half, (2 * i + j + 1) * half)
            both_ref[SLOTS:, lanes] = ref[16 * j : 16 * (j + 1), lanes_other]
    both_ref[SLOTS:, 6 * half :] = jnp.zeros((16, 2 * half), BF)


def to_row(column):
    n = column.shape[0]
    diagonal = lax.broadcasted_iota(jnp.int32, (n, n), 0) == lax.broadcasted_iota(
        jnp.int32, (n, n), 1
    )
    return jnp.sum(jnp.where(diagonal, column, 0.0), axis=0, keepdims=True)


def line_of(at, column):
    first, second = column >> 2, column & 3
    return jnp.where(at[2] == 0, first, second), jnp.where(at[2] == 0, second, first)


def line_plan(at, counts):
    u, v = line_of(at, lax.broadcasted_iota(jnp.int32, (16, 16), 0))
    u2, v2 = line_of(at, lax.broadcasted_iota(jnp.int32, (16, 16), 1))
    row = to_row(counts)
    same = v == v2
    before = same & ((u2 ^ at[4]) < (u ^ at[4]))
    skipped = jnp.sum(jnp.where(before, row, 0.0), axis=1, keepdims=True)
    total = jnp.sum(jnp.where(same, row, 0.0), axis=1, keepdims=True)
    other = jnp.sum(jnp.where(u == u2, row, 0.0), axis=1, keepdims=True)
    return skipped, total, jnp.max(jnp.maximum(total, other), axis=0, keepdims=True)


def per_lane(values, column):
    hot = lax.broadcasted_iota(jnp.int32, (16, column.shape[1]), 0) == column
    return jnp.sum(jnp.where(hot, values, 0.0), axis=0, keepdims=True)


def blocks_of(lanes, size, blocks):
    lane = lax.broadcasted_iota(jnp.int32, (1, lanes), 1)
    block = jnp.zeros((1, lanes), jnp.int32)
    for j in range(1, blocks):
        block = block + (lane >= j * size).astype(jnp.int32)
    return block, (lane - block * size).astype(F32)


def column_at(at, u, v):
    return jnp.where(at[2] == 0, u * 4 + v, v * 4 + u)


def line_targets(at, counts, skipped, slots):
    block, slot = blocks_of(4 * slots, slots, 4)
    column = column_at(at, block ^ at[4], jnp.zeros_like(block) + at[5])
    target = per_lane(skipped, column) + slot
    return jnp.where(slot < per_lane(counts, column), target, -1.0).astype(jnp.int32)


def line_bias(at, total, rows):
    block, slot = blocks_of(4 * rows, rows, 4)
    column = column_at(at, jnp.zeros_like(block) + at[4], block ^ at[5])
    return jnp.where(slot < per_lane(total, column), 0.0, -1e30)


def pack_kernel(
    at, con_ref, txt_ref, w_hbm, out_ref, spot_ref, con_bias, txt_bias, con_line, txt_line, w_ref, sem
):
    half = w_ref.shape[2]
    lanes = pl.ds(pl.multiple_of(at[2] * half, half), half)
    weights = pltpu.make_async_copy(w_hbm.at[0:2, :, lanes], w_ref, sem)
    weights.start()
    ids = jnp.concatenate([con_ref[...], txt_ref[...]], axis=1)
    n = ids.shape[1]
    n_con = con_ref.shape[1]
    owner = ids >> 8
    column = column_of(owner)
    here = column == at[1]
    z = ((owner & 1) << 1) | ((owner >> 4) & 1)
    core = (owner >> 1) & 1
    piece = jnp.where(here, jnp.where(core == at[2], 0, 4) + (at[3] ^ z), -1)
    rank, _ = ranks(piece, 8, ())
    spot, (con_counts, txt_counts) = ranks(column, 16, (n_con // 256,))
    con_skip, con_total, con_most = line_plan(at, con_counts)
    txt_skip, txt_total, txt_most = line_plan(at, txt_counts)
    con_bias[...] = line_bias(at, con_total, LINE_CON)
    txt_bias[...] = line_bias(at, txt_total, LINE_TXT)
    con_line[...] = line_targets(at, con_counts, con_skip, CON)
    txt_line[...] = line_targets(at, txt_counts, txt_skip, TXT)
    _, item_v = line_of(at, column)
    spot_ref[0:1, :] = (
        (item_v ^ at[5]) * LINE_CON + per_lane(con_skip, column).astype(jnp.int32) + spot
    )
    wanted = (lax.broadcasted_iota(jnp.int32, (128, n), 0) == owner).astype(F32)
    over = jnp.maximum(
        jnp.maximum(
            jnp.max(con_counts, axis=0, keepdims=True) - CON,
            jnp.max(txt_counts, axis=0, keepdims=True) - TXT,
        ),
        jnp.maximum(con_most - LINE_CON, txt_most - LINE_TXT),
    )
    most = jnp.max(jnp.sum(wanted, axis=1, keepdims=True), axis=0, keepdims=True)
    over = jnp.maximum(over, most - SLOTS)
    spot_ref[1:2, :] = jnp.broadcast_to(over.astype(jnp.int32), (1, n))
    spot_ref[2:8, :] = jnp.zeros((6, n), jnp.int32)
    concept = lax.broadcasted_iota(jnp.int32, (1, n), 1) < n_con
    target = jnp.where(
        concept, jnp.where(spot < CON, spot, -1), jnp.where(spot < TXT, spot + CON, -1)
    )
    source = jnp.where(here & (rank < SLOTS), piece * SLOTS + rank, -1)
    target = jnp.where(here, target, -1)
    hot_t = (lax.broadcasted_iota(jnp.int32, (ROWS, n), 0) == target).astype(F32).astype(BF)
    hot_s = (lax.broadcasted_iota(jnp.int32, (8 * SLOTS, n), 0) == source).astype(F32).astype(BF)
    out_ref[...] = nt(hot_t, hot_s).astype(BF)
    weights.wait()


def project_kernel(at, pack_ref, *refs):
    rows, (mod_ref, gain_ref, w_ref, w_hbm), outs, (raw_ref, x_ref, w_last, sem) = (
        refs[:8], refs[8:12], refs[12:16], refs[16:]
    )
    half = w_ref.shape[2]
    lanes = pl.ds(pl.multiple_of(at[2] * half, half), half)
    weights = pltpu.make_async_copy(w_hbm.at[2, :, lanes], w_last, sem)
    weights.start()
    for i, ref in enumerate(rows):
        raw_ref[i * SLOTS : (i + 1) * SLOTS, :] = ref[0:SLOTS, :]
    shift = mod_ref[0:1, :]
    scale = 1.0 + mod_ref[1:2, :]
    for i in range(ROWS // 32):
        block = slice(i * 32, (i + 1) * 32)
        values = nn(pack_ref[block, :], raw_ref[...])
        mean = jnp.mean(values, axis=1, keepdims=True)
        centered = values - mean
        var = jnp.mean(centered * centered, axis=1, keepdims=True)
        x_ref[block, :] = (centered * lax.rsqrt(var + 1e-06) * scale + shift).astype(BF)

    def normed(u, gain):
        meansq = jnp.mean(u * u, axis=1, keepdims=True)
        return u * lax.rsqrt(meansq + 1e-06) * gain

    q = nn(x_ref[0:CON, :], w_ref[0])
    k = nn(x_ref[...], w_ref[1])
    weights.wait()
    v = nn(x_ref[...], w_last[...])
    heads = []
    for h in range(3):
        cols = slice(h * HD, (h + 1) * HD)
        heads.append(
            (
                (normed(q[:, cols], gain_ref[0:1, :]) * FACTOR).astype(BF),
                normed(k[:, cols], gain_ref[1:2, :]).astype(BF),
                v[:, cols].astype(BF),
            )
        )
    for s, out in enumerate(outs):
        head = jnp.minimum(at[4] ^ s, 2)
        for h in range(3):

            @pl.when(head == h)
            def _(h=h, out=out):
                out[0:ROWS, 0:HD] = heads[h][1]
                out[0:ROWS, HD:] = heads[h][2]
                out[ROWS:, 0:HD] = heads[h][0][: CON // 2]
                out[ROWS:, HD:] = heads[h][0][CON // 2 :]


def join_kernel(a, b, c, d, con_line, txt_line, out, con, txt):
    for i, ref in enumerate((a, b, c, d)):
        con[i * CON : (i + 1) * CON, 0 : 2 * HD] = ref[0:CON, :]
        con[i * CON : i * CON + CON // 2, 2 * HD :] = ref[ROWS:, 0:HD]
        con[i * CON + CON // 2 : (i + 1) * CON, 2 * HD :] = ref[ROWS:, HD:]
        txt[i * TXT : (i + 1) * TXT, :] = ref[CON:ROWS, :]
    hot = lax.broadcasted_iota(jnp.int32, (LINE_CON, 4 * CON), 0) == con_line[...]
    found = nn(hot.astype(F32).astype(BF), con[...]).astype(BF)
    out[0:LINE_CON, :] = found[:, 0 : 2 * HD]
    out[LINE:, 0:HD] = found[: LINE_CON // 2, 2 * HD :]
    out[LINE:, HD:] = found[LINE_CON // 2 :, 2 * HD :]
    hot = lax.broadcasted_iota(jnp.int32, (LINE_TXT, 4 * TXT), 0) == txt_line[...]
    out[LINE_CON:LINE, :] = nn(hot.astype(F32).astype(BF), txt[...]).astype(BF)


def image_heads_kernel(at, own, core, *outs):
    n, half = own.shape[0] // 3, own.shape[1]
    for s, out in enumerate(outs):
        head = jnp.minimum(at[4] ^ s, 2)
        lanes = pl.ds(pl.multiple_of(head * HD, HD), HD)
        for i in range(3):
            row = 2 * i * n
            out[row : row + n, :] = own[i * n : (i + 1) * n, lanes]
            for j in range(2):
                there = pl.ds(pl.multiple_of((2 * i + j) * half + head * HD, HD), HD)
                out[row + n + 16 * j : row + n + 16 * (j + 1), :] = core[SLOTS:, there]


def image_join_kernel(a, b, c, d, q_out, kv_out):
    n = a.shape[0] // 3
    for i, ref in enumerate((a, b, c, d)):
        q_out[n * i : n * (i + 1), :] = ref[0:n, :]
        kv_out[n * i : n * (i + 1), :] = ref[n : 2 * n, :]
        kv_out[n * (4 + i) : n * (5 + i), :] = ref[2 * n :, :]


def plane_kernel(a, b, c, d, out):
    n = a.shape[0] // 2
    for i, ref in enumerate((a, b, c, d)):
        out[n * i : n * (i + 1), :] = ref[0:n, :]
        out[n * (4 + i) : n * (5 + i), :] = ref[n:, :]


def weigh(q, parts, factor):
    scores = []
    for keys, _, bias in parts:
        part = nt(q, keys)
        scores.append(part if bias is None else part + bias)
    peak = scores[0].max(axis=1, keepdims=True)
    for part in scores[1:]:
        peak = jnp.maximum(peak, part.max(axis=1, keepdims=True))
    total = None
    for part, (_, values, _) in zip(scores, parts):
        power = part - peak
        weights = jnp.exp2(power if factor is None else power * factor).astype(BF)
        summed = nn(weights, values)
        total = summed if total is None else total + summed
    return (peak if factor is None else peak * factor), total


def join(first, second):
    peak = jnp.maximum(first[0], second[0])
    return peak, first[1] * jnp.exp2(first[0] - peak) + second[1] * jnp.exp2(second[0] - peak)


def merge(first, second):
    _, summed = join(first, second)
    return (summed[:, 0:HD] / summed[:, HD:]).astype(BF)


def with_ones(values):
    return jnp.concatenate([values, jnp.ones_like(values)], axis=1)


def image_near_kernel(plane, q, peak, summed):
    n = plane.shape[0] // 2
    part = (plane[0:n, :], with_ones(plane[n:, :]), None)
    peak[...], summed[...] = weigh(q[...], (part,), FACTOR)


def line_queries(con_q, refs):
    n = LINE_CON
    for a, ref in enumerate(refs):
        con_q[a * n : a * n + n // 2, :] = ref[LINE:, 0:HD]
        con_q[a * n + n // 2 : (a + 1) * n, :] = ref[LINE:, HD:]


def order_kernel(pick, l0, l1, q_out, con_q):
    line_queries(con_q, (l0, l1))
    q_out[...] = nn(pick[:, : 2 * LINE_CON], con_q[...]).astype(BF)


def weigh_blocks(q, parts, store):
    blk = 256
    blocks = [slice(b, b + blk) for b in range(0, q.shape[0], blk)]

    def scores(rows):
        found = []
        for keys, _, bias in parts:
            part = nt(q[rows, :], keys[...])
            found.append(part if bias is None else part + bias[...])
        return found

    ready = scores(blocks[0])
    for b, rows in enumerate(blocks):
        now, ready = ready, scores(blocks[b + 1]) if b + 1 < len(blocks) else None
        peak = now[0].max(axis=1, keepdims=True)
        for part in now[1:]:
            peak = jnp.maximum(peak, part.max(axis=1, keepdims=True))
        summed = sum(
            nn(jnp.exp2(part - peak).astype(BF), values[...])
            for part, (_, values, _) in zip(now, parts)
        )
        store(rows, peak, summed)


def near_kernel(
    pick, q_part, l0, l1, l2, l3, con_bias, txt_bias, plane, img_q, im, ims, *refs
):
    q_out, cm_out, cs_out, im_out, ims_out = refs[:5]
    con_q, con_k, con_v, txt_k, txt_v, img_v = refs[5:]
    n, m = LINE_CON, LINE_TXT
    line_queries(con_q, (l2, l3))
    for a, ref in enumerate((l0, l1, l2, l3)):
        con_k[a * n : (a + 1) * n, :] = ref[0:n, 0:HD]
        con_v[a * n : (a + 1) * n, :] = with_ones(ref[0:n, HD:])
        txt_k[a * m : (a + 1) * m, :] = ref[n:LINE, 0:HD]
        txt_v[a * m : (a + 1) * m, :] = with_ones(ref[n:LINE, HD:])
    n_img = plane.shape[0] // 2
    img_v[...] = with_ones(plane[n_img:, :])
    rest = nn(pick[:, 2 * n :], con_q[...])
    q_out[...] = (rest + q_part[...].astype(F32)).astype(BF)

    def store(rows, peak, summed):
        cm_out[rows, :] = peak
        cs_out[rows, :] = summed

    parts = ((plane.at[0:n_img, :], img_v, None), (con_k, con_v, con_bias))
    weigh_blocks(q_out, parts, store)
    text = weigh(img_q[...], ((txt_k[...], txt_v[...], txt_bias[...]),), FACTOR)
    im_out[...], ims_out[...] = join(text, (im[...], ims[...]))


def far_kernel(plane, con_q, img_q, cm, cs, im, ims, *refs):
    outs, (con_out, img_v) = refs[:4], refs[4:]
    n_img = plane.shape[0] // 2
    img_v[...] = with_ones(plane[n_img:, :])
    part = (plane[0:n_img, :], img_v[...], None)
    img = merge(weigh(img_q[...], (part,), FACTOR), (im[...], ims[...]))
    n_con = con_out.shape[0]

    def store(rows, peak, summed):
        con_out[rows, :] = merge((peak, summed), (cm[rows, :], cs[rows, :]))

    weigh_blocks(con_q, ((plane.at[0:n_img, :], img_v, None),), store)
    dots = nt(img, con_out[...]).astype(BF)
    con_f = con_out[...].astype(F32)
    squares = con_f * con_f
    high = squares.astype(BF)
    ones = jnp.ones((8, HD), BF)
    con_sq = (nt(ones, high) + nt(ones, (squares - high.astype(F32)).astype(BF))).astype(BF)
    for s, out in enumerate(outs):
        rows = slice(s * 64, (s + 1) * 64)
        out[0:64, 0:n_con] = dots[rows]
        out[0:64, n_con:] = img[rows]
        out[64:72, 0:n_con] = con_sq
        out[64:72, n_con:] = jnp.zeros((8, HD), BF)


def head_sum_kernel(at, b0, b1, b2, b3, own, core):
    n_con = b0.shape[1] - HD
    total = jnp.zeros((72, n_con), F32)
    outs = [jnp.zeros((64, HD), BF) for _ in range(3)]
    for s, ref in enumerate((b0, b1, b2, b3)):
        head = at[4] ^ s
        total = total + jnp.where(head < 3, ref[:, 0:n_con].astype(F32), 0.0)
        for h in range(3):
            outs[h] = jnp.where(head == h, ref[0:64, n_con:], outs[h])
    image_sq = jnp.zeros((64, 1), F32)
    for h in range(3):
        out_f = outs[h].astype(F32)
        image_sq = image_sq + jnp.sum(out_f * out_f, axis=1, keepdims=True)
    image_sq = jnp.broadcast_to(image_sq, (64, HD)).astype(BF)
    total = total.astype(BF)
    for ref, row in ((own, 0), (core, 32)):
        ref[0:32, 0:n_con] = total[row : row + 32]
        ref[32:40, 0:n_con] = total[64:72]
        ref[0:32, n_con : n_con + HD] = image_sq[row : row + 32]
        ref[32:40, n_con : n_con + HD] = jnp.zeros((8, HD), BF)
    for h in range(3):
        lanes = slice(n_con + (1 + h) * HD, n_con + (2 + h) * HD)
        for ref, row in ((own, 0), (core, 32)):
            ref[0:32, lanes] = outs[h][row : row + 32]
            ref[32:40, lanes] = jnp.zeros((8, HD), BF)


def core_sum_kernel(own, core, out):
    cols = out.shape[1]
    out[...] = (own[:, 0:cols].astype(F32) + core[:, 0:cols].astype(F32)).astype(BF)


def finish_kernel(at, sums, head, own, core, img_ref, sal_ref):
    n_con = sums.shape[1] - HD
    width = 12 * HD
    total = sums[...].astype(F32) + head[...].astype(F32)
    con_rms = jnp.sqrt(total[32:33, 0:n_con] / width + 1e-06)
    img_rms = jnp.sqrt(total[0:32, n_con : n_con + 1] / width + 1e-06)
    sal_ref[...] = total[0:32, 0:n_con] / (math.sqrt(width) * con_rms * img_rms)
    half = 3 * HD
    for ref, core_of in ((own, at[2]), (core, 1 - at[2])):
        lanes = pl.ds(pl.multiple_of(core_of * half, half), half)
        img_ref[:, lanes] = ref[0:32, n_con + HD :]


def packed(
    img_q, img_k, img_v, txt_ids, concept_ids, step_index, token_table, modulation, txt_qkv, qk_gain
):
    n_con, n_txt = concept_ids.shape[0], txt_ids.shape[0]
    ctx = lax.axis_index("ctx")
    g = lax.axis_index("head")
    c = ctx & 1
    y = (ctx >> 1) & 3
    zl = (ctx >> 3) & 1
    x = ctx >> 4
    u = jnp.where(c == 0, x, y)
    v = jnp.where(c == 0, y, x)
    at = jnp.stack([ctx * 2 + g, x * 4 + y, c, 2 * g + zl, u, v]).astype(jnp.int32)
    con_ids, text_ids = concept_ids[None, :], txt_ids[None, :]
    n = n_con + n_txt
    width = token_table.shape[1]
    half = txt_qkv.shape[2] // 2
    n_img = img_q.shape[0]

    own_rows, own_both, own_img = call(
        plan_kernel, (sds((SLOTS, width)), sds((SLOTS + 16, width)), sds((3 * n_img, half)))
    )(at, con_ids, text_ids, token_table, img_q, img_k, img_v)
    far_rows = send(own_rows, swap_z(2))
    column_rows = [own_rows] + [send(own_rows, swap_z(s)) for s in (1, 3)]
    core_both = send(own_both, swap_core())

    all_weights = jnp.transpose(txt_qkv, (1, 0, 2))
    pack, spots, con_bias, txt_bias, con_line, txt_line, weights = call(
        pack_kernel,
        (
            sds((ROWS, 8 * SLOTS)),
            sds((8, n), jnp.int32),
            sds((1, 4 * LINE_CON), F32),
            sds((1, 4 * LINE_TXT), F32),
            sds((1, 4 * CON), jnp.int32),
            sds((1, 4 * TXT), jnp.int32),
            sds((2, width, half)),
        ),
        scratch=(pltpu.SemaphoreType.DMA,),
        limit=24,
        us=2.0,
        in_hbm=1,
    )(at, con_ids, text_ids, all_weights)
    shift_scale = lax.dynamic_index_in_dim(modulation, step_index[0], 0, keepdims=False)

    image_blocks = call(
        image_heads_kernel, tuple(sds((6 * n_img, HD)) for _ in range(4))
    )(at, own_img, core_both)
    image_blocks = [image_blocks[0]] + [send(image_blocks[s], swap_u(s)) for s in (2, 1, 3)]
    image_blocks = [image_blocks[0], image_blocks[2], image_blocks[1], image_blocks[3]]
    column_rows[1], image_blocks[2] = lax.optimization_barrier((column_rows[1], image_blocks[2]))
    far_rows, pack, shift_scale, image_blocks[1] = lax.optimization_barrier(
        (far_rows, pack, shift_scale, image_blocks[1])
    )
    column_rows.insert(2, far_rows)
    other_rows = [core_both] + [send(r, swap_core()) for r in column_rows[1:]]

    qkv = call(
        project_kernel,
        tuple(sds((ROWS + CON // 2, 2 * HD)) for _ in range(4)),
        scratch=(
            pltpu.VMEM((8 * SLOTS, width), BF),
            pltpu.VMEM((ROWS, width), BF),
            pltpu.VMEM((width, half), BF),
            pltpu.SemaphoreType.DMA,
        ),
        limit=24,
        us=PROJ_US,
        in_hbm=1,
    )(at, pack, *column_rows, *other_rows, shift_scale, qk_gain, weights, all_weights)

    *image_blocks, first = lax.optimization_barrier((*image_blocks, qkv[0]))
    image_q, image_kv = call(
        image_join_kernel, (sds((8 * n_img, HD)), sds((16 * n_img, HD))), smem=0
    )(*image_blocks)
    image_kvs = [image_kv] + [send(image_kv, swap_v(s)) for s in (2, 1, 3)]

    qkv = [first] + [send(qkv[s], swap_u(s)) for s in (2, 1, 3)]
    qkv = [qkv[0], qkv[2], qkv[1], qkv[3]]
    line = call(
        join_kernel,
        sds((LINE + LINE_CON // 2, 2 * HD)),
        scratch=(pltpu.VMEM((4 * CON, 3 * HD), BF), pltpu.VMEM((4 * TXT, 2 * HD), BF)),
        smem=0,
    )(*qkv, con_line, txt_line)
    lines = [line] + [send(line, swap_v(s)) for s in (2, 1, 3)]
    lines = [lines[0], lines[2], lines[1], lines[3]]
    plane = call(plane_kernel, sds((64 * n_img, HD)), smem=0)(*image_kvs)
    con_slot, over, plane = lax.optimization_barrier((spots[0, :n_con], spots[1, 0], plane))
    other_plane = send(plane, swap_plane())
    pick = (con_slot[:, None] == jnp.arange(4 * LINE_CON)[None, :]).astype(BF)

    image_stats = (sds((8 * n_img, 1), F32), sds((8 * n_img, 2 * HD), F32))
    stats = (sds((n_con, 1), F32), sds((n_con, 2 * HD), F32)) + image_stats
    image_near = call(image_near_kernel, image_stats, smem=0)(plane, image_q)
    q_part = call(
        order_kernel, sds((n_con, HD)), scratch=(pltpu.VMEM((2 * LINE_CON, HD), BF),), smem=0
    )(pick, lines[0], lines[1])
    con_q, *near = call(
        near_kernel,
        (sds((n_con, HD)),) + stats,
        scratch=(
            pltpu.VMEM((2 * LINE_CON, HD), BF),
            pltpu.VMEM((4 * LINE_CON, HD), BF),
            pltpu.VMEM((4 * LINE_CON, 2 * HD), BF),
            pltpu.VMEM((4 * LINE_TXT, HD), BF),
            pltpu.VMEM((4 * LINE_TXT, 2 * HD), BF),
            pltpu.VMEM((32 * n_img, 2 * HD), BF),
        ),
        limit=32,
        us=NEAR_US,
        smem=0,
    )(pick, q_part, *lines, con_bias, txt_bias, plane, image_q, *image_near)
    blocks = call(
        far_kernel,
        tuple(sds((72, n_con + HD)) for _ in range(4)),
        scratch=(pltpu.VMEM((n_con, HD), BF), pltpu.VMEM((32 * n_img, 2 * HD), BF)),
        limit=24,
        us=FAR_US,
        smem=0,
    )(other_plane, con_q, image_q, *near)
    blocks = [blocks[0]] + [send(blocks[s], swap_u(s)) for s in (2, 1, 3)]
    blocks = [blocks[0], blocks[2], blocks[1], blocks[3]]
    own, core = call(head_sum_kernel, tuple(sds((40, n_con + 4 * HD)) for _ in range(2)))(
        at, *blocks
    )
    core = send(core, swap_core())
    sums = call(core_sum_kernel, sds((40, n_con + HD)), smem=0)(own, core)
    last = (at, sums, send(sums, swap_z(2)), own, core)
    finish = call(finish_kernel, (sds((n_img, 2 * half)), sds((n_img, n_con), F32)))

    def finished():
        img_out, saliency = finish(*last)
        return img_out, jnp.transpose(saliency)

    return over <= 0, finished


def on_device(*args):
    fits, finish = packed(*args)
    return lax.cond(fits, finish, lambda: tuple(general(*args)))


def solution(mesh):
    return jax.shard_map(
        on_device,
        mesh=mesh,
        in_specs=(
            P("ctx", "head"),
            P("ctx", "head"),
            P("ctx", "head"),
            P(),
            P(),
            P(),
            P(("ctx", "head"), None),
            P(),
            P(None, None, "head"),
            P(),
        ),
        out_specs=(P("ctx", "head"), P(None, "ctx")),
        check_vma=False,
    )
```

```python
import math

import jax
import jax.numpy as jnp
from jax import lax
from jax.experimental import pallas as pl
from jax.experimental.pallas import tpu as pltpu
from jax.sharding import PartitionSpec as P

BF = jnp.bfloat16
F32 = jnp.float32
HD = 128
SLOTS = 32
CON = 96
TXT = 64
ROWS = CON + TXT
LINE_CON = 320
LINE_TXT = 176
LINE = LINE_CON + LINE_TXT
MIB = 1 << 20
PROJ_US, NEAR_US, FAR_US = 5.0, 2.0, 3.0
FACTOR = HD ** (-0.5) * math.log2(math.e)


def modulate(rows, shift_scale):
    values = rows.astype(F32)
    mean = jnp.mean(values, axis=1, keepdims=True)
    centered = values - mean
    var = jnp.mean(centered * centered, axis=1, keepdims=True)
    normed = centered * lax.rsqrt(var + 1e-06)
    return (normed * (1.0 + shift_scale[1]) + shift_scale[0]).astype(BF)


def head_norm(values, gain, head_dim):
    shaped = values.reshape(values.shape[0], -1, head_dim)
    meansq = jnp.mean(shaped * shaped, axis=2, keepdims=True)
    return (shaped * lax.rsqrt(meansq + 1e-06) * gain).reshape(values.shape[0], -1)


def block_stats(queries, keys, values):
    scores = jnp.einsum("rgd,kgd->grk", queries, keys, preferred_element_type=F32)
    scores = scores * queries.shape[-1] ** (-0.5)
    peak = jnp.max(scores, axis=2)
    weights = jnp.exp(scores - peak[:, :, None])
    total = jnp.sum(weights, axis=2)
    summed = jnp.einsum("grk,kgd->grd", weights.astype(BF), values, preferred_element_type=F32)
    return (peak, total, summed)


def combine_stats(first, second):
    peak = jnp.maximum(first[0], second[0])
    left = jnp.exp(first[0] - peak)
    right = jnp.exp(second[0] - peak)
    total = first[1] * left + second[1] * right
    summed = first[2] * left[:, :, None] + second[2] * right[:, :, None]
    return (peak, total, summed)


def scaled_scores(dots, concept_sq, image_sq, width):
    concept_rms = jnp.sqrt(concept_sq / width + 1e-06)
    image_rms = jnp.sqrt(image_sq / width + 1e-06)
    return dots / (jnp.sqrt(F32(width)) * concept_rms[:, None] * image_rms[None, :])


def gather_ctx(block):
    n_ctx = lax.axis_size("ctx")
    spread = jnp.broadcast_to(block[None], (n_ctx,) + block.shape)
    return lax.all_to_all(spread, "ctx", 0, 0, tiled=True)


def general(
    img_q, img_k, img_v, txt_ids, concept_ids, step_index, token_table, modulation, txt_qkv, qk_gain
):
    n_ctx = lax.axis_size("ctx")
    n_head = lax.axis_size("head")
    head_dim = qk_gain.shape[1]
    group = img_q.shape[1] // head_dim
    text_dev = txt_ids.shape[0] // n_ctx
    concept_dev = concept_ids.shape[0] // n_ctx
    vocab_dev = token_table.shape[0]
    combined = jnp.concatenate(
        [txt_ids.reshape(n_ctx, text_dev), concept_ids.reshape(n_ctx, concept_dev)], axis=1
    ).reshape(-1)
    offset = lax.axis_index(("ctx", "head")) * vocab_dev
    wanted = combined - offset
    inside = (wanted >= 0) & (wanted < vocab_dev)
    picked = jnp.take(token_table, jnp.clip(wanted, 0, vocab_dev - 1), axis=0)
    n_all = n_ctx * n_head
    mine = jnp.where(inside[:, None], picked, jnp.zeros((), picked.dtype))
    parts = lax.all_to_all(
        mine.reshape(n_all, -1, mine.shape[1]), ("ctx", "head"), 0, 0, tiled=True
    )
    own_rows = jnp.sum(parts.astype(F32), axis=0)
    prompt_rows = lax.all_gather(own_rows.astype(BF), "head", axis=0, tiled=True)
    shift_scale = lax.dynamic_index_in_dim(modulation, step_index[0], 0, keepdims=False)
    modded = modulate(prompt_rows, shift_scale)
    text_mod = modded[:text_dev]
    concept_mod = modded[text_dev:]
    text_kv = jnp.einsum("rd,dgc->rgc", text_mod, txt_qkv[:, 1:], preferred_element_type=F32)
    concept_qkv = jnp.einsum("rd,dgc->rgc", concept_mod, txt_qkv, preferred_element_type=F32)
    text_keys = head_norm(text_kv[:, 0], qk_gain[1], head_dim).astype(BF)
    text_values = text_kv[:, 1].astype(BF)
    concept_queries = head_norm(concept_qkv[:, 0], qk_gain[0], head_dim).astype(BF)
    concept_keys = head_norm(concept_qkv[:, 1], qk_gain[1], head_dim).astype(BF)
    concept_values = concept_qkv[:, 2].astype(BF)
    local_kv = jnp.stack(
        [
            jnp.concatenate([text_keys, concept_keys], axis=0),
            jnp.concatenate([text_values, concept_values], axis=0),
        ]
    )
    prompt_kv = gather_ctx(local_kv)
    text_part = jnp.swapaxes(prompt_kv[:, :, :text_dev], 0, 1).reshape(2, -1, group, head_dim)
    concept_part = jnp.swapaxes(prompt_kv[:, :, text_dev:], 0, 1).reshape(2, -1, group, head_dim)
    image_queries = img_q.reshape(-1, group, head_dim)
    concept_q3 = concept_queries.reshape(-1, group, head_dim)
    first = block_stats(image_queries, text_part[0], text_part[1])
    second = block_stats(concept_q3, concept_part[0], concept_part[1])
    start_stats = (
        jnp.concatenate([first[0], second[0]], axis=1),
        jnp.concatenate([first[1], second[1]], axis=1),
        jnp.concatenate([first[2], second[2]], axis=1),
    )
    all_queries = jnp.concatenate([image_queries, concept_q3], axis=0)
    image_kv = gather_ctx(jnp.stack([img_k, img_v]))
    keys = image_kv[:, 0].reshape(-1, group, head_dim)
    values = image_kv[:, 1].reshape(-1, group, head_dim)
    peak, total, summed = combine_stats(start_stats, block_stats(all_queries, keys, values))
    attended = (
        jnp.transpose(summed / total[:, :, None], (1, 0, 2))
        .reshape(all_queries.shape[0], -1)
        .astype(BF)
    )
    img_rows = img_q.shape[0]
    img_out = attended[:img_rows]
    concept_out = attended[img_rows:]
    concept_all = gather_ctx(concept_out).reshape(-1, concept_out.shape[1])
    dots = lax.dot_general(
        concept_all, img_out, (((1,), (1,)), ((), ())), preferred_element_type=F32
    )
    image_f = img_out.astype(F32)
    concept_f = concept_all.astype(F32)
    image_sq = jnp.sum(image_f * image_f, axis=1)
    concept_sq = jnp.sum(concept_f * concept_f, axis=1)
    width = group * head_dim * n_head
    sums = jnp.concatenate(
        [
            jnp.concatenate([dots, concept_sq[:, None]], axis=1),
            jnp.concatenate([image_sq, jnp.zeros((1,), F32)])[None],
        ]
    ).astype(BF)
    other = lax.ppermute(sums, "head", [(0, 1), (1, 0)])
    sums = sums.astype(F32) + other.astype(F32)
    concepts = dots.shape[0]
    saliency = scaled_scores(
        sums[:concepts, :img_rows], sums[:concepts, img_rows], sums[concepts, :img_rows], width
    )
    return (img_out, saliency)


def place(x, zl, y, c, g):
    return ((((x * 2 + zl) * 4 + y) * 2 + c) * 2) + g


def pairs(move):
    found = []
    for x in range(4):
        for zl in range(2):
            for y in range(4):
                for c in range(2):
                    for g in range(2):
                        found.append((place(x, zl, y, c, g), place(*move(x, zl, y, c, g))))
    return found


def swap_z(s):
    def move(x, zl, y, c, g):
        z = (2 * g + zl) ^ s
        return x, z & 1, y, c, z >> 1

    return pairs(move)


def swap_u(s):
    return pairs(
        lambda x, zl, y, c, g: (x, zl, y ^ s, c, g) if c else (x ^ s, zl, y, c, g)
    )


def swap_v(s):
    return pairs(
        lambda x, zl, y, c, g: (x ^ s, zl, y, c, g) if c else (x, zl, y ^ s, c, g)
    )


def swap_plane():
    return pairs(lambda x, zl, y, c, g: (x, zl ^ 1, y, c, g))


def swap_core():
    return pairs(lambda x, zl, y, c, g: (x, zl, y, c ^ 1, g))


def send(array, pairing):
    return lax.ppermute(array, ("ctx", "head"), pairing)


def nt(a, b, **kw):
    return lax.dot_general(a, b, (((1,), (1,)), ((), ())), preferred_element_type=F32, **kw)


def nn(a, b):
    return lax.dot_general(a, b, (((1,), (0,)), ((), ())), preferred_element_type=F32)


def call(kernel, outs, scratch=(), limit=16, us=1.0, smem=1, in_hbm=0):
    def run(*args):
        vm = pl.BlockSpec(memory_space=pltpu.VMEM)
        sm = pl.BlockSpec(memory_space=pltpu.SMEM)
        return pl.pallas_call(
            kernel,
            out_shape=outs,
            in_specs=[sm] * smem
            + [vm] * (len(args) - smem - in_hbm)
            + [pl.BlockSpec(memory_space=pl.ANY)] * in_hbm,
            out_specs=jax.tree.map(lambda _: vm, outs),
            scratch_shapes=list(scratch),
            compiler_params=pltpu.CompilerParams(vmem_limit_bytes=limit * MIB),
            cost_estimate=pl.CostEstimate(
                flops=int(us * 1.1e9), bytes_accessed=0, transcendentals=0
            ),
        )(*args)

    return run


def sds(shape, dtype=BF):
    return jax.ShapeDtypeStruct(shape, dtype)


def column_of(owner):
    ctx = owner >> 1
    return ((ctx >> 4) << 2) | ((ctx >> 1) & 3)


def ranks(columns, pieces, reset):
    n = columns.shape[1]
    blk = 256
    row = lax.broadcasted_iota(jnp.int32, (blk, blk), 0)
    col = lax.broadcasted_iota(jnp.int32, (blk, blk), 1)
    earlier = (row < col).astype(F32).astype(BF)
    label = lax.broadcasted_iota(jnp.int32, (16, blk), 0)
    label_piece = lax.broadcasted_iota(jnp.int32, (8, blk), 0)
    carry, carry_piece = jnp.zeros((16, 1), F32), jnp.zeros((8, 1), F32)
    spots, found, counts = [], [], []
    for b in range(n // blk):
        if b == reset:
            counts.append(carry)
            carry = jnp.zeros((16, 1), F32)
        lanes = slice(b * blk, (b + 1) * blk)
        hot = (label == columns[:, lanes]).astype(F32)
        hot_piece = (label_piece == pieces[:, lanes]).astype(F32)
        before = nn(jnp.concatenate([hot, hot_piece], axis=0).astype(BF), earlier)
        spots.append(jnp.sum(hot * (before[0:16] + carry), axis=0, keepdims=True))
        found.append(jnp.sum(hot_piece * (before[16:24] + carry_piece), axis=0, keepdims=True))
        carry = carry + jnp.sum(hot, axis=1, keepdims=True)
        carry_piece = carry_piece + jnp.sum(hot_piece, axis=1, keepdims=True)
    counts.append(carry)
    spots, found = (jnp.concatenate(r, axis=1).astype(jnp.int32) for r in (spots, found))
    return spots, found, counts


def plan_kernel(
    at, con_ref, txt_ref, table_ref, q_ref, k_ref, v_ref, rows_ref, both_ref, img_ref
):
    ids = jnp.concatenate([con_ref[...], txt_ref[...]], axis=1)
    n = ids.shape[1]
    blk = 256
    blocks = n // blk
    vocab_dev = table_ref.shape[0]
    mine = ((ids >> int(math.log2(vocab_dev))) == at[0]).astype(F32)
    pieces = [slice(b * blk, (b + 1) * blk) for b in range(blocks)]
    folded = jnp.concatenate(
        [mine[:, p] for p in pieces] + [jnp.zeros((8 - blocks, blk), F32)], axis=0
    )
    row = lax.broadcasted_iota(jnp.int32, (blk, blk), 0)
    col = lax.broadcasted_iota(jnp.int32, (blk, blk), 1)
    before = nn(folded.astype(BF), (row < col).astype(F32).astype(BF))
    label = lax.broadcasted_iota(jnp.int32, (SLOTS, blk), 0).astype(F32)
    found = jnp.zeros((SLOTS, blk), F32)
    skipped = jnp.zeros((1, 1), F32)
    for b, p in enumerate(pieces):
        rank = before[b : b + 1, :] + skipped
        row_in_table = ((ids[:, p] & (vocab_dev - 1)) + 1).astype(F32) * mine[:, p]
        found = found + jnp.where(label == rank, row_in_table, 0.0)
        skipped = skipped + jnp.sum(mine[:, p], axis=1, keepdims=True)
    found = jnp.sum(found, axis=1, keepdims=True).astype(jnp.int32) - 1
    pick = lax.broadcasted_iota(jnp.int32, (SLOTS, vocab_dev), 1) == found
    rows = nn(pick.astype(F32).astype(BF), table_ref[...]).astype(BF)
    rows_ref[...] = rows
    both_ref[0:SLOTS, :] = rows
    m = q_ref.shape[0]
    half = q_ref.shape[1] // 2
    lanes_own = pl.ds(pl.multiple_of(at[2] * half, half), half)
    lanes_other = pl.ds(pl.multiple_of((1 - at[2]) * half, half), half)
    for i, ref in enumerate((q_ref, k_ref, v_ref)):
        img_ref[i * m : (i + 1) * m, :] = ref[:, lanes_own]
        for j in range(2):
            lanes = slice((2 * i + j) * half, (2 * i + j + 1) * half)
            both_ref[SLOTS:, lanes] = ref[16 * j : 16 * (j + 1), lanes_other]
    both_ref[SLOTS:, 6 * half :] = jnp.zeros((16, 2 * half), BF)


def to_row(column):
    n = column.shape[0]
    diagonal = lax.broadcasted_iota(jnp.int32, (n, n), 0) == lax.broadcasted_iota(
        jnp.int32, (n, n), 1
    )
    return jnp.sum(jnp.where(diagonal, column, 0.0), axis=0, keepdims=True)


def line_of(at, column):
    first, second = column >> 2, column & 3
    return jnp.where(at[2] == 0, first, second), jnp.where(at[2] == 0, second, first)


def line_plan(at, counts):
    u, v = line_of(at, lax.broadcasted_iota(jnp.int32, (16, 16), 0))
    u2, v2 = line_of(at, lax.broadcasted_iota(jnp.int32, (16, 16), 1))
    row = to_row(counts)
    same = v == v2
    before = same & ((u2 ^ at[4]) < (u ^ at[4]))
    skipped = jnp.sum(jnp.where(before, row, 0.0), axis=1, keepdims=True)
    total = jnp.sum(jnp.where(same, row, 0.0), axis=1, keepdims=True)
    other = jnp.sum(jnp.where(u == u2, row, 0.0), axis=1, keepdims=True)
    return skipped, total, jnp.max(jnp.maximum(total, other), axis=0, keepdims=True)


def per_lane(values, column):
    hot = lax.broadcasted_iota(jnp.int32, (16, column.shape[1]), 0) == column
    return jnp.sum(jnp.where(hot, values, 0.0), axis=0, keepdims=True)


def blocks_of(lanes, size, blocks):
    lane = lax.broadcasted_iota(jnp.int32, (1, lanes), 1)
    block = jnp.zeros((1, lanes), jnp.int32)
    for j in range(1, blocks):
        block = block + (lane >= j * size).astype(jnp.int32)
    return block, (lane - block * size).astype(F32)


def column_at(at, u, v):
    return jnp.where(at[2] == 0, u * 4 + v, v * 4 + u)


def line_targets(at, counts, skipped, slots):
    block, slot = blocks_of(4 * slots, slots, 4)
    column = column_at(at, block ^ at[4], jnp.zeros_like(block) + at[5])
    target = per_lane(skipped, column) + slot
    return jnp.where(slot < per_lane(counts, column), target, -1.0).astype(jnp.int32)


def line_bias(at, total, rows):
    block, slot = blocks_of(4 * rows, rows, 4)
    column = column_at(at, jnp.zeros_like(block) + at[4], block ^ at[5])
    return jnp.where(slot < per_lane(total, column), 0.0, -1e30)


def pack_kernel(at, con_ref, txt_ref, out_ref, spot_ref, con_bias, txt_bias, con_line, txt_line):
    ids = jnp.concatenate([con_ref[...], txt_ref[...]], axis=1)
    n = ids.shape[1]
    n_con = con_ref.shape[1]
    owner = ids >> 8
    column = column_of(owner)
    here = column == at[1]
    z = ((owner & 1) << 1) | ((owner >> 4) & 1)
    core = (owner >> 1) & 1
    piece = jnp.where(here, jnp.where(core == at[2], 0, 4) + (at[3] ^ z), -1)
    spot, rank, (con_counts, txt_counts) = ranks(column, piece, n_con // 256)
    con_skip, con_total, con_most = line_plan(at, con_counts)
    txt_skip, txt_total, txt_most = line_plan(at, txt_counts)
    con_bias[...] = line_bias(at, con_total, LINE_CON)
    txt_bias[...] = line_bias(at, txt_total, LINE_TXT)
    con_line[...] = line_targets(at, con_counts, con_skip, CON)
    txt_line[...] = line_targets(at, txt_counts, txt_skip, TXT)
    _, item_v = line_of(at, column)
    spot_ref[0:1, :] = (
        (item_v ^ at[5]) * LINE_CON + per_lane(con_skip, column).astype(jnp.int32) + spot
    )
    wanted = (lax.broadcasted_iota(jnp.int32, (128, n), 0) == owner).astype(F32)
    over = jnp.maximum(
        jnp.maximum(
            jnp.max(con_counts, axis=0, keepdims=True) - CON,
            jnp.max(txt_counts, axis=0, keepdims=True) - TXT,
        ),
        jnp.maximum(con_most - LINE_CON, txt_most - LINE_TXT),
    )
    most = jnp.max(jnp.sum(wanted, axis=1, keepdims=True), axis=0, keepdims=True)
    over = jnp.maximum(over, most - SLOTS)
    spot_ref[1:2, :] = jnp.broadcast_to(over.astype(jnp.int32), (1, n))
    spot_ref[2:8, :] = jnp.zeros((6, n), jnp.int32)
    concept = lax.broadcasted_iota(jnp.int32, (1, n), 1) < n_con
    target = jnp.where(
        concept, jnp.where(spot < CON, spot, -1), jnp.where(spot < TXT, spot + CON, -1)
    )
    source = jnp.where(here & (rank < SLOTS), piece * SLOTS + rank, -1)
    label = lax.broadcasted_iota(jnp.int32, (8 * SLOTS, n), 0)
    found = jnp.sum(
        jnp.where(label == source, (target + 1).astype(F32), 0.0), axis=1, keepdims=True
    )
    hot = lax.broadcasted_iota(jnp.int32, (8 * SLOTS, 256), 1) == found.astype(jnp.int32) - 1
    out_ref[...] = jnp.transpose(hot.astype(F32))[0:ROWS].astype(BF)


def project_kernel(at, pack_ref, *refs):
    rows, (mod_ref, gain_ref, w_ref), outs, (raw_ref, x_ref) = (
        refs[:8], refs[8:11], refs[11:15], refs[15:]
    )
    half = w_ref.shape[2] // 2
    lanes = pl.ds(pl.multiple_of(at[2] * half, half), half)
    for i, ref in enumerate(rows):
        raw_ref[i * SLOTS : (i + 1) * SLOTS, :] = ref[0:SLOTS, :]
    shift = mod_ref[0:1, :]
    scale = 1.0 + mod_ref[1:2, :]
    for i in range(ROWS // 32):
        block = slice(i * 32, (i + 1) * 32)
        values = nn(pack_ref[block, :], raw_ref[...])
        mean = jnp.mean(values, axis=1, keepdims=True)
        centered = values - mean
        var = jnp.mean(centered * centered, axis=1, keepdims=True)
        x_ref[block, :] = (centered * lax.rsqrt(var + 1e-06) * scale + shift).astype(BF)

    def normed(u, gain):
        meansq = jnp.mean(u * u, axis=1, keepdims=True)
        return u * lax.rsqrt(meansq + 1e-06) * gain

    q = nn(x_ref[0:CON, :], w_ref[0, :, lanes])
    k = nn(x_ref[...], w_ref[1, :, lanes])
    v = nn(x_ref[...], w_ref[2, :, lanes])
    heads = []
    for h in range(3):
        cols = slice(h * HD, (h + 1) * HD)
        heads.append(
            (
                (normed(q[:, cols], gain_ref[0:1, :]) * FACTOR).astype(BF),
                normed(k[:, cols], gain_ref[1:2, :]).astype(BF),
                v[:, cols].astype(BF),
            )
        )
    for s, out in enumerate(outs):
        head = jnp.minimum(at[4] ^ s, 2)
        for h in range(3):

            @pl.when(head == h)
            def _(h=h, out=out):
                out[0:ROWS, 0:HD] = heads[h][1]
                out[0:ROWS, HD:] = heads[h][2]
                out[ROWS:, 0:HD] = heads[h][0][: CON // 2]
                out[ROWS:, HD:] = heads[h][0][CON // 2 :]


def join_kernel(a, b, c, d, con_line, txt_line, out, con, txt):
    for i, ref in enumerate((a, b, c, d)):
        con[i * CON : (i + 1) * CON, 0 : 2 * HD] = ref[0:CON, :]
        con[i * CON : i * CON + CON // 2, 2 * HD :] = ref[ROWS:, 0:HD]
        con[i * CON + CON // 2 : (i + 1) * CON, 2 * HD :] = ref[ROWS:, HD:]
        txt[i * TXT : (i + 1) * TXT, :] = ref[CON:ROWS, :]
    hot = lax.broadcasted_iota(jnp.int32, (LINE_CON, 4 * CON), 0) == con_line[...]
    found = nn(hot.astype(F32).astype(BF), con[...]).astype(BF)
    out[0:LINE_CON, :] = found[:, 0 : 2 * HD]
    out[LINE:, 0:HD] = found[: LINE_CON // 2, 2 * HD :]
    out[LINE:, HD:] = found[LINE_CON // 2 :, 2 * HD :]
    hot = lax.broadcasted_iota(jnp.int32, (LINE_TXT, 4 * TXT), 0) == txt_line[...]
    out[LINE_CON:LINE, :] = nn(hot.astype(F32).astype(BF), txt[...]).astype(BF)


def image_heads_kernel(at, own, core, *outs):
    n, half = own.shape[0] // 3, own.shape[1]
    for s, out in enumerate(outs):
        head = jnp.minimum(at[4] ^ s, 2)
        lanes = pl.ds(pl.multiple_of(head * HD, HD), HD)
        for i in range(3):
            row = 2 * i * n
            out[row : row + n, :] = own[i * n : (i + 1) * n, lanes]
            for j in range(2):
                there = pl.ds(pl.multiple_of((2 * i + j) * half + head * HD, HD), HD)
                out[row + n + 16 * j : row + n + 16 * (j + 1), :] = core[SLOTS:, there]


def image_join_kernel(a, b, c, d, q_out, kv_out):
    n = a.shape[0] // 3
    for i, ref in enumerate((a, b, c, d)):
        q_out[n * i : n * (i + 1), :] = ref[0:n, :]
        kv_out[n * i : n * (i + 1), :] = ref[n : 2 * n, :]
        kv_out[n * (4 + i) : n * (5 + i), :] = ref[2 * n :, :]


def plane_kernel(a, b, c, d, out):
    n = a.shape[0] // 2
    for i, ref in enumerate((a, b, c, d)):
        out[n * i : n * (i + 1), :] = ref[0:n, :]
        out[n * (4 + i) : n * (5 + i), :] = ref[n:, :]


def weigh(q, parts, factor):
    scores = []
    for keys, _, bias in parts:
        part = nt(q, keys)
        scores.append(part if bias is None else part + bias)
    peak = scores[0].max(axis=1, keepdims=True)
    for part in scores[1:]:
        peak = jnp.maximum(peak, part.max(axis=1, keepdims=True))
    total = None
    for part, (_, values, _) in zip(scores, parts):
        power = part - peak
        weights = jnp.exp2(power if factor is None else power * factor).astype(BF)
        summed = nn(weights, values)
        total = summed if total is None else total + summed
    return (peak if factor is None else peak * factor), total


def join(first, second):
    peak = jnp.maximum(first[0], second[0])
    return peak, first[1] * jnp.exp2(first[0] - peak) + second[1] * jnp.exp2(second[0] - peak)


def merge(first, second):
    _, summed = join(first, second)
    return (summed[:, 0:HD] / summed[:, HD:]).astype(BF)


def with_ones(values):
    return jnp.concatenate([values, jnp.ones_like(values)], axis=1)


def image_near_kernel(plane, q, peak, summed):
    n = plane.shape[0] // 2
    part = (plane[0:n, :], with_ones(plane[n:, :]), None)
    peak[...], summed[...] = weigh(q[...], (part,), FACTOR)


def line_queries(con_q, refs):
    n = LINE_CON
    for a, ref in enumerate(refs):
        con_q[a * n : a * n + n // 2, :] = ref[LINE:, 0:HD]
        con_q[a * n + n // 2 : (a + 1) * n, :] = ref[LINE:, HD:]


def order_kernel(pick, l0, l1, q_out, con_q):
    line_queries(con_q, (l0, l1))
    q_out[...] = nn(pick[:, : 2 * LINE_CON], con_q[...]).astype(BF)


def weigh_blocks(q, parts, store):
    blk = 256
    blocks = [slice(b, b + blk) for b in range(0, q.shape[0], blk)]

    def scores(rows):
        found = []
        for keys, _, bias in parts:
            part = nt(q[rows, :], keys[...])
            found.append(part if bias is None else part + bias[...])
        return found

    ready = scores(blocks[0])
    for b, rows in enumerate(blocks):
        now, ready = ready, scores(blocks[b + 1]) if b + 1 < len(blocks) else None
        peak = now[0].max(axis=1, keepdims=True)
        for part in now[1:]:
            peak = jnp.maximum(peak, part.max(axis=1, keepdims=True))
        summed = sum(
            nn(jnp.exp2(part - peak).astype(BF), values[...])
            for part, (_, values, _) in zip(now, parts)
        )
        store(rows, peak, summed)


def near_kernel(
    pick, q_part, l0, l1, l2, l3, con_bias, txt_bias, plane, img_q, im, ims, *refs
):
    q_out, cm_out, cs_out, im_out, ims_out = refs[:5]
    con_q, con_k, con_v, txt_k, txt_v, img_v = refs[5:]
    n, m = LINE_CON, LINE_TXT
    line_queries(con_q, (l2, l3))
    for a, ref in enumerate((l0, l1, l2, l3)):
        con_k[a * n : (a + 1) * n, :] = ref[0:n, 0:HD]
        con_v[a * n : (a + 1) * n, :] = with_ones(ref[0:n, HD:])
        txt_k[a * m : (a + 1) * m, :] = ref[n:LINE, 0:HD]
        txt_v[a * m : (a + 1) * m, :] = with_ones(ref[n:LINE, HD:])
    n_img = plane.shape[0] // 2
    img_v[...] = with_ones(plane[n_img:, :])
    rest = nn(pick[:, 2 * n :], con_q[...])
    q_out[...] = (rest + q_part[...].astype(F32)).astype(BF)

    def store(rows, peak, summed):
        cm_out[rows, :] = peak
        cs_out[rows, :] = summed

    parts = ((plane.at[0:n_img, :], img_v, None), (con_k, con_v, con_bias))
    weigh_blocks(q_out, parts, store)
    text = weigh(img_q[...], ((txt_k[...], txt_v[...], txt_bias[...]),), FACTOR)
    im_out[...], ims_out[...] = join(text, (im[...], ims[...]))


def far_kernel(plane, con_q, img_q, cm, cs, im, ims, *refs):
    outs, (con_out, img_v) = refs[:4], refs[4:]
    n_img = plane.shape[0] // 2
    img_v[...] = with_ones(plane[n_img:, :])
    part = (plane[0:n_img, :], img_v[...], None)
    img = merge(weigh(img_q[...], (part,), FACTOR), (im[...], ims[...]))
    n_con = con_out.shape[0]

    def store(rows, peak, summed):
        con_out[rows, :] = merge((peak, summed), (cm[rows, :], cs[rows, :]))

    weigh_blocks(con_q, ((plane.at[0:n_img, :], img_v, None),), store)
    dots = nt(img, con_out[...]).astype(BF)
    con_f = con_out[...].astype(F32)
    squares = con_f * con_f
    high = squares.astype(BF)
    ones = jnp.ones((8, HD), BF)
    con_sq = (nt(ones, high) + nt(ones, (squares - high.astype(F32)).astype(BF))).astype(BF)
    for s, out in enumerate(outs):
        rows = slice(s * 64, (s + 1) * 64)
        out[0:64, 0:n_con] = dots[rows]
        out[0:64, n_con:] = img[rows]
        out[64:72, 0:n_con] = con_sq
        out[64:72, n_con:] = jnp.zeros((8, HD), BF)


def head_sum_kernel(at, b0, b1, b2, b3, own, core):
    n_con = b0.shape[1] - HD
    total = jnp.zeros((72, n_con), F32)
    outs = [jnp.zeros((64, HD), BF) for _ in range(3)]
    for s, ref in enumerate((b0, b1, b2, b3)):
        head = at[4] ^ s
        total = total + jnp.where(head < 3, ref[:, 0:n_con].astype(F32), 0.0)
        for h in range(3):
            outs[h] = jnp.where(head == h, ref[0:64, n_con:], outs[h])
    image_sq = jnp.zeros((64, 1), F32)
    for h in range(3):
        out_f = outs[h].astype(F32)
        image_sq = image_sq + jnp.sum(out_f * out_f, axis=1, keepdims=True)
    image_sq = jnp.broadcast_to(image_sq, (64, HD)).astype(BF)
    total = total.astype(BF)
    for ref, row in ((own, 0), (core, 32)):
        ref[0:32, 0:n_con] = total[row : row + 32]
        ref[32:40, 0:n_con] = total[64:72]
        ref[0:32, n_con : n_con + HD] = image_sq[row : row + 32]
        ref[32:40, n_con : n_con + HD] = jnp.zeros((8, HD), BF)
    for h in range(3):
        lanes = slice(n_con + (1 + h) * HD, n_con + (2 + h) * HD)
        for ref, row in ((own, 0), (core, 32)):
            ref[0:32, lanes] = outs[h][row : row + 32]
            ref[32:40, lanes] = jnp.zeros((8, HD), BF)


def core_sum_kernel(own, core, out):
    cols = out.shape[1]
    out[...] = (own[:, 0:cols].astype(F32) + core[:, 0:cols].astype(F32)).astype(BF)


def finish_kernel(at, sums, head, own, core, img_ref, sal_ref):
    n_con = sums.shape[1] - HD
    width = 12 * HD
    total = sums[...].astype(F32) + head[...].astype(F32)
    con_rms = jnp.sqrt(total[32:33, 0:n_con] / width + 1e-06)
    img_rms = jnp.sqrt(total[0:32, n_con : n_con + 1] / width + 1e-06)
    sal_ref[...] = total[0:32, 0:n_con] / (math.sqrt(width) * con_rms * img_rms)
    half = 3 * HD
    for ref, core_of in ((own, at[2]), (core, 1 - at[2])):
        lanes = pl.ds(pl.multiple_of(core_of * half, half), half)
        img_ref[:, lanes] = ref[0:32, n_con + HD :]


def packed(
    img_q, img_k, img_v, txt_ids, concept_ids, step_index, token_table, modulation, txt_qkv, qk_gain
):
    n_con, n_txt = concept_ids.shape[0], txt_ids.shape[0]
    ctx = lax.axis_index("ctx")
    g = lax.axis_index("head")
    c = ctx & 1
    y = (ctx >> 1) & 3
    zl = (ctx >> 3) & 1
    x = ctx >> 4
    u = jnp.where(c == 0, x, y)
    v = jnp.where(c == 0, y, x)
    at = jnp.stack([ctx * 2 + g, x * 4 + y, c, 2 * g + zl, u, v]).astype(jnp.int32)
    con_ids, text_ids = concept_ids[None, :], txt_ids[None, :]
    n = n_con + n_txt
    width = token_table.shape[1]
    half = txt_qkv.shape[2] // 2
    n_img = img_q.shape[0]

    own_rows, own_both, own_img = call(
        plan_kernel, (sds((SLOTS, width)), sds((SLOTS + 16, width)), sds((3 * n_img, half)))
    )(at, con_ids, text_ids, token_table, img_q, img_k, img_v)
    far_rows = send(own_rows, swap_z(2))
    column_rows = [own_rows] + [send(own_rows, swap_z(s)) for s in (1, 3)]
    core_both = send(own_both, swap_core())

    all_weights = jnp.transpose(txt_qkv, (1, 0, 2))
    pack, spots, con_bias, txt_bias, con_line, txt_line = call(
        pack_kernel,
        (
            sds((ROWS, 8 * SLOTS)),
            sds((8, n), jnp.int32),
            sds((1, 4 * LINE_CON), F32),
            sds((1, 4 * LINE_TXT), F32),
            sds((1, 4 * CON), jnp.int32),
            sds((1, 4 * TXT), jnp.int32),
        ),
        us=2.0,
    )(at, con_ids, text_ids)
    shift_scale = lax.dynamic_index_in_dim(modulation, step_index[0], 0, keepdims=False)

    image_blocks = call(
        image_heads_kernel, tuple(sds((6 * n_img, HD)) for _ in range(4))
    )(at, own_img, core_both)
    image_blocks = [image_blocks[0]] + [send(image_blocks[s], swap_u(s)) for s in (2, 1, 3)]
    image_blocks = [image_blocks[0], image_blocks[2], image_blocks[1], image_blocks[3]]
    column_rows[1], image_blocks[2] = lax.optimization_barrier((column_rows[1], image_blocks[2]))
    far_rows, pack, shift_scale, image_blocks[1] = lax.optimization_barrier(
        (far_rows, pack, shift_scale, image_blocks[1])
    )
    column_rows.insert(2, far_rows)
    other_rows = [core_both] + [send(r, swap_core()) for r in column_rows[1:]]

    qkv = call(
        project_kernel,
        tuple(sds((ROWS + CON // 2, 2 * HD)) for _ in range(4)),
        scratch=(
            pltpu.VMEM((8 * SLOTS, width), BF),
            pltpu.VMEM((ROWS, width), BF),
        ),
        limit=28,
        us=PROJ_US,
    )(at, pack, *column_rows, *other_rows, shift_scale, qk_gain, all_weights)

    *image_blocks, first = lax.optimization_barrier((*image_blocks, qkv[0]))
    image_q, image_kv = call(
        image_join_kernel, (sds((8 * n_img, HD)), sds((16 * n_img, HD))), smem=0
    )(*image_blocks)
    image_kvs = [image_kv] + [send(image_kv, swap_v(s)) for s in (2, 1, 3)]

    qkv = [first] + [send(qkv[s], swap_u(s)) for s in (2, 1, 3)]
    qkv = [qkv[0], qkv[2], qkv[1], qkv[3]]
    line = call(
        join_kernel,
        sds((LINE + LINE_CON // 2, 2 * HD)),
        scratch=(pltpu.VMEM((4 * CON, 3 * HD), BF), pltpu.VMEM((4 * TXT, 2 * HD), BF)),
        smem=0,
    )(*qkv, con_line, txt_line)
    lines = [line] + [send(line, swap_v(s)) for s in (2, 1, 3)]
    lines = [lines[0], lines[2], lines[1], lines[3]]
    plane = call(plane_kernel, sds((64 * n_img, HD)), smem=0)(*image_kvs)
    con_slot, over, plane = lax.optimization_barrier((spots[0, :n_con], spots[1, 0], plane))
    other_plane = send(plane, swap_plane())
    pick = (con_slot[:, None] == jnp.arange(4 * LINE_CON)[None, :]).astype(BF)

    image_stats = (sds((8 * n_img, 1), F32), sds((8 * n_img, 2 * HD), F32))
    stats = (sds((n_con, 1), F32), sds((n_con, 2 * HD), F32)) + image_stats
    image_near = call(image_near_kernel, image_stats, smem=0)(plane, image_q)
    q_part = call(
        order_kernel, sds((n_con, HD)), scratch=(pltpu.VMEM((2 * LINE_CON, HD), BF),), smem=0
    )(pick, lines[0], lines[1])
    con_q, *near = call(
        near_kernel,
        (sds((n_con, HD)),) + stats,
        scratch=(
            pltpu.VMEM((2 * LINE_CON, HD), BF),
            pltpu.VMEM((4 * LINE_CON, HD), BF),
            pltpu.VMEM((4 * LINE_CON, 2 * HD), BF),
            pltpu.VMEM((4 * LINE_TXT, HD), BF),
            pltpu.VMEM((4 * LINE_TXT, 2 * HD), BF),
            pltpu.VMEM((32 * n_img, 2 * HD), BF),
        ),
        limit=32,
        us=NEAR_US,
        smem=0,
    )(pick, q_part, *lines, con_bias, txt_bias, plane, image_q, *image_near)
    blocks = call(
        far_kernel,
        tuple(sds((72, n_con + HD)) for _ in range(4)),
        scratch=(pltpu.VMEM((n_con, HD), BF), pltpu.VMEM((32 * n_img, 2 * HD), BF)),
        limit=24,
        us=FAR_US,
        smem=0,
    )(other_plane, con_q, image_q, *near)
    blocks = [blocks[0]] + [send(blocks[s], swap_u(s)) for s in (2, 1, 3)]
    blocks = [blocks[0], blocks[2], blocks[1], blocks[3]]
    own, core = call(head_sum_kernel, tuple(sds((40, n_con + 4 * HD)) for _ in range(2)))(
        at, *blocks
    )
    core = send(core, swap_core())
    sums = call(core_sum_kernel, sds((40, n_con + HD)), smem=0)(own, core)
    last = (at, sums, send(sums, swap_z(2)), own, core)
    finish = call(finish_kernel, (sds((n_img, 2 * half)), sds((n_img, n_con), F32)))

    def finished():
        img_out, saliency = finish(*last)
        return img_out, jnp.transpose(saliency)

    return over <= 0, finished


def on_device(*args):
    fits, finish = packed(*args)
    return lax.cond(fits, finish, lambda: tuple(general(*args)))


def solution(mesh):
    return jax.shard_map(
        on_device,
        mesh=mesh,
        in_specs=(
            P("ctx", "head"),
            P("ctx", "head"),
            P("ctx", "head"),
            P(),
            P(),
            P(),
            P(("ctx", "head"), None),
            P(),
            P(None, None, "head"),
            P(),
        ),
        out_specs=(P("ctx", "head"), P(None, "ctx")),
        check_vma=False,
    )
```

```python
import math

import jax
import jax.numpy as jnp
from jax import lax
from jax.experimental import pallas as pl
from jax.experimental.pallas import tpu as pltpu
from jax.sharding import PartitionSpec as P

BF = jnp.bfloat16
F32 = jnp.float32
HD = 128
SLOTS = 32
CON = 96
TXT = 64
ROWS = CON + TXT
LINE_CON = 320
LINE_TXT = 176
LINE = LINE_CON + LINE_TXT
MIB = 1 << 20
PROJ_US, NEAR_US, FAR_US = 5.0, 2.0, 3.0
FACTOR = HD ** (-0.5) * math.log2(math.e)


def modulate(rows, shift_scale):
    values = rows.astype(F32)
    mean = jnp.mean(values, axis=1, keepdims=True)
    centered = values - mean
    var = jnp.mean(centered * centered, axis=1, keepdims=True)
    normed = centered * lax.rsqrt(var + 1e-06)
    return (normed * (1.0 + shift_scale[1]) + shift_scale[0]).astype(BF)


def head_norm(values, gain, head_dim):
    shaped = values.reshape(values.shape[0], -1, head_dim)
    meansq = jnp.mean(shaped * shaped, axis=2, keepdims=True)
    return (shaped * lax.rsqrt(meansq + 1e-06) * gain).reshape(values.shape[0], -1)


def block_stats(queries, keys, values):
    scores = jnp.einsum("rgd,kgd->grk", queries, keys, preferred_element_type=F32)
    scores = scores * queries.shape[-1] ** (-0.5)
    peak = jnp.max(scores, axis=2)
    weights = jnp.exp(scores - peak[:, :, None])
    total = jnp.sum(weights, axis=2)
    summed = jnp.einsum("grk,kgd->grd", weights.astype(BF), values, preferred_element_type=F32)
    return (peak, total, summed)


def combine_stats(first, second):
    peak = jnp.maximum(first[0], second[0])
    left = jnp.exp(first[0] - peak)
    right = jnp.exp(second[0] - peak)
    total = first[1] * left + second[1] * right
    summed = first[2] * left[:, :, None] + second[2] * right[:, :, None]
    return (peak, total, summed)


def scaled_scores(dots, concept_sq, image_sq, width):
    concept_rms = jnp.sqrt(concept_sq / width + 1e-06)
    image_rms = jnp.sqrt(image_sq / width + 1e-06)
    return dots / (jnp.sqrt(F32(width)) * concept_rms[:, None] * image_rms[None, :])


def gather_ctx(block):
    n_ctx = lax.axis_size("ctx")
    spread = jnp.broadcast_to(block[None], (n_ctx,) + block.shape)
    return lax.all_to_all(spread, "ctx", 0, 0, tiled=True)


def general(
    img_q, img_k, img_v, txt_ids, concept_ids, step_index, token_table, modulation, txt_qkv, qk_gain
):
    n_ctx = lax.axis_size("ctx")
    n_head = lax.axis_size("head")
    head_dim = qk_gain.shape[1]
    group = img_q.shape[1] // head_dim
    text_dev = txt_ids.shape[0] // n_ctx
    concept_dev = concept_ids.shape[0] // n_ctx
    vocab_dev = token_table.shape[0]
    combined = jnp.concatenate(
        [txt_ids.reshape(n_ctx, text_dev), concept_ids.reshape(n_ctx, concept_dev)], axis=1
    ).reshape(-1)
    offset = lax.axis_index(("ctx", "head")) * vocab_dev
    wanted = combined - offset
    inside = (wanted >= 0) & (wanted < vocab_dev)
    picked = jnp.take(token_table, jnp.clip(wanted, 0, vocab_dev - 1), axis=0)
    n_all = n_ctx * n_head
    mine = jnp.where(inside[:, None], picked, jnp.zeros((), picked.dtype))
    parts = lax.all_to_all(
        mine.reshape(n_all, -1, mine.shape[1]), ("ctx", "head"), 0, 0, tiled=True
    )
    own_rows = jnp.sum(parts.astype(F32), axis=0)
    prompt_rows = lax.all_gather(own_rows.astype(BF), "head", axis=0, tiled=True)
    shift_scale = lax.dynamic_index_in_dim(modulation, step_index[0], 0, keepdims=False)
    modded = modulate(prompt_rows, shift_scale)
    text_mod = modded[:text_dev]
    concept_mod = modded[text_dev:]
    text_kv = jnp.einsum("rd,dgc->rgc", text_mod, txt_qkv[:, 1:], preferred_element_type=F32)
    concept_qkv = jnp.einsum("rd,dgc->rgc", concept_mod, txt_qkv, preferred_element_type=F32)
    text_keys = head_norm(text_kv[:, 0], qk_gain[1], head_dim).astype(BF)
    text_values = text_kv[:, 1].astype(BF)
    concept_queries = head_norm(concept_qkv[:, 0], qk_gain[0], head_dim).astype(BF)
    concept_keys = head_norm(concept_qkv[:, 1], qk_gain[1], head_dim).astype(BF)
    concept_values = concept_qkv[:, 2].astype(BF)
    local_kv = jnp.stack(
        [
            jnp.concatenate([text_keys, concept_keys], axis=0),
            jnp.concatenate([text_values, concept_values], axis=0),
        ]
    )
    prompt_kv = gather_ctx(local_kv)
    text_part = jnp.swapaxes(prompt_kv[:, :, :text_dev], 0, 1).reshape(2, -1, group, head_dim)
    concept_part = jnp.swapaxes(prompt_kv[:, :, text_dev:], 0, 1).reshape(2, -1, group, head_dim)
    image_queries = img_q.reshape(-1, group, head_dim)
    concept_q3 = concept_queries.reshape(-1, group, head_dim)
    first = block_stats(image_queries, text_part[0], text_part[1])
    second = block_stats(concept_q3, concept_part[0], concept_part[1])
    start_stats = (
        jnp.concatenate([first[0], second[0]], axis=1),
        jnp.concatenate([first[1], second[1]], axis=1),
        jnp.concatenate([first[2], second[2]], axis=1),
    )
    all_queries = jnp.concatenate([image_queries, concept_q3], axis=0)
    image_kv = gather_ctx(jnp.stack([img_k, img_v]))
    keys = image_kv[:, 0].reshape(-1, group, head_dim)
    values = image_kv[:, 1].reshape(-1, group, head_dim)
    peak, total, summed = combine_stats(start_stats, block_stats(all_queries, keys, values))
    attended = (
        jnp.transpose(summed / total[:, :, None], (1, 0, 2))
        .reshape(all_queries.shape[0], -1)
        .astype(BF)
    )
    img_rows = img_q.shape[0]
    img_out = attended[:img_rows]
    concept_out = attended[img_rows:]
    concept_all = gather_ctx(concept_out).reshape(-1, concept_out.shape[1])
    dots = lax.dot_general(
        concept_all, img_out, (((1,), (1,)), ((), ())), preferred_element_type=F32
    )
    image_f = img_out.astype(F32)
    concept_f = concept_all.astype(F32)
    image_sq = jnp.sum(image_f * image_f, axis=1)
    concept_sq = jnp.sum(concept_f * concept_f, axis=1)
    width = group * head_dim * n_head
    sums = jnp.concatenate(
        [
            jnp.concatenate([dots, concept_sq[:, None]], axis=1),
            jnp.concatenate([image_sq, jnp.zeros((1,), F32)])[None],
        ]
    ).astype(BF)
    other = lax.ppermute(sums, "head", [(0, 1), (1, 0)])
    sums = sums.astype(F32) + other.astype(F32)
    concepts = dots.shape[0]
    saliency = scaled_scores(
        sums[:concepts, :img_rows], sums[:concepts, img_rows], sums[concepts, :img_rows], width
    )
    return (img_out, saliency)


def place(x, zl, y, c, g):
    return ((((x * 2 + zl) * 4 + y) * 2 + c) * 2) + g


def pairs(move):
    found = []
    for x in range(4):
        for zl in range(2):
            for y in range(4):
                for c in range(2):
                    for g in range(2):
                        found.append((place(x, zl, y, c, g), place(*move(x, zl, y, c, g))))
    return found


def swap_z(s):
    def move(x, zl, y, c, g):
        z = (2 * g + zl) ^ s
        return x, z & 1, y, c, z >> 1

    return pairs(move)


def swap_u(s):
    return pairs(
        lambda x, zl, y, c, g: (x, zl, y ^ s, c, g) if c else (x ^ s, zl, y, c, g)
    )


def swap_v(s):
    return pairs(
        lambda x, zl, y, c, g: (x ^ s, zl, y, c, g) if c else (x, zl, y ^ s, c, g)
    )


def swap_plane():
    return pairs(lambda x, zl, y, c, g: (x, zl ^ 1, y, c, g))


def swap_core():
    return pairs(lambda x, zl, y, c, g: (x, zl, y, c ^ 1, g))


def send(array, pairing):
    return lax.ppermute(array, ("ctx", "head"), pairing)


def nt(a, b, **kw):
    return lax.dot_general(a, b, (((1,), (1,)), ((), ())), preferred_element_type=F32, **kw)


def nn(a, b):
    return lax.dot_general(a, b, (((1,), (0,)), ((), ())), preferred_element_type=F32)


def call(kernel, outs, scratch=(), limit=16, us=1.0, smem=1, in_hbm=0):
    def run(*args):
        vm = pl.BlockSpec(memory_space=pltpu.VMEM)
        sm = pl.BlockSpec(memory_space=pltpu.SMEM)
        return pl.pallas_call(
            kernel,
            out_shape=outs,
            in_specs=[sm] * smem
            + [vm] * (len(args) - smem - in_hbm)
            + [pl.BlockSpec(memory_space=pl.ANY)] * in_hbm,
            out_specs=jax.tree.map(lambda _: vm, outs),
            scratch_shapes=list(scratch),
            compiler_params=pltpu.CompilerParams(vmem_limit_bytes=limit * MIB),
            cost_estimate=pl.CostEstimate(
                flops=int(us * 1.1e9), bytes_accessed=0, transcendentals=0
            ),
        )(*args)

    return run


def sds(shape, dtype=BF):
    return jax.ShapeDtypeStruct(shape, dtype)


def column_of(owner):
    ctx = owner >> 1
    return ((ctx >> 4) << 2) | ((ctx >> 1) & 3)


def ranks(columns, pieces, reset):
    n = columns.shape[1]
    blk = 256
    row = lax.broadcasted_iota(jnp.int32, (blk, blk), 0)
    col = lax.broadcasted_iota(jnp.int32, (blk, blk), 1)
    earlier = (row < col).astype(F32).astype(BF)
    label = lax.broadcasted_iota(jnp.int32, (16, blk), 0)
    label_piece = lax.broadcasted_iota(jnp.int32, (8, blk), 0)
    carry, carry_piece = jnp.zeros((16, 1), F32), jnp.zeros((8, 1), F32)
    spots, found, counts = [], [], []
    for b in range(n // blk):
        if b == reset:
            counts.append(carry)
            carry = jnp.zeros((16, 1), F32)
        lanes = slice(b * blk, (b + 1) * blk)
        hot = (label == columns[:, lanes]).astype(F32)
        hot_piece = (label_piece == pieces[:, lanes]).astype(F32)
        before = nn(jnp.concatenate([hot, hot_piece], axis=0).astype(BF), earlier)
        spots.append(jnp.sum(hot * (before[0:16] + carry), axis=0, keepdims=True))
        found.append(jnp.sum(hot_piece * (before[16:24] + carry_piece), axis=0, keepdims=True))
        carry = carry + jnp.sum(hot, axis=1, keepdims=True)
        carry_piece = carry_piece + jnp.sum(hot_piece, axis=1, keepdims=True)
    counts.append(carry)
    spots, found = (jnp.concatenate(r, axis=1).astype(jnp.int32) for r in (spots, found))
    return spots, found, counts


def plan_kernel(
    at, con_ref, txt_ref, table_ref, q_ref, k_ref, v_ref, rows_ref, both_ref, img_ref
):
    ids = jnp.concatenate([con_ref[...], txt_ref[...]], axis=1)
    n = ids.shape[1]
    blk = 256
    blocks = n // blk
    vocab_dev = table_ref.shape[0]
    mine = ((ids >> int(math.log2(vocab_dev))) == at[0]).astype(F32)
    pieces = [slice(b * blk, (b + 1) * blk) for b in range(blocks)]
    folded = jnp.concatenate(
        [mine[:, p] for p in pieces] + [jnp.zeros((8 - blocks, blk), F32)], axis=0
    )
    row = lax.broadcasted_iota(jnp.int32, (blk, blk), 0)
    col = lax.broadcasted_iota(jnp.int32, (blk, blk), 1)
    before = nn(folded.astype(BF), (row < col).astype(F32).astype(BF))
    label = lax.broadcasted_iota(jnp.int32, (SLOTS, blk), 0).astype(F32)
    found = jnp.zeros((SLOTS, blk), F32)
    skipped = jnp.zeros((1, 1), F32)
    for b, p in enumerate(pieces):
        rank = before[b : b + 1, :] + skipped
        row_in_table = ((ids[:, p] & (vocab_dev - 1)) + 1).astype(F32) * mine[:, p]
        found = found + jnp.where(label == rank, row_in_table, 0.0)
        skipped = skipped + jnp.sum(mine[:, p], axis=1, keepdims=True)
    found = jnp.sum(found, axis=1, keepdims=True).astype(jnp.int32) - 1
    pick = lax.broadcasted_iota(jnp.int32, (SLOTS, vocab_dev), 1) == found
    rows = nn(pick.astype(F32).astype(BF), table_ref[...]).astype(BF)
    rows_ref[...] = rows
    both_ref[0:SLOTS, :] = rows
    m = q_ref.shape[0]
    half = q_ref.shape[1] // 2
    lanes_own = pl.ds(pl.multiple_of(at[2] * half, half), half)
    lanes_other = pl.ds(pl.multiple_of((1 - at[2]) * half, half), half)
    for i, ref in enumerate((q_ref, k_ref, v_ref)):
        img_ref[i * m : (i + 1) * m, :] = ref[:, lanes_own]
        for j in range(2):
            lanes = slice((2 * i + j) * half, (2 * i + j + 1) * half)
            both_ref[SLOTS:, lanes] = ref[16 * j : 16 * (j + 1), lanes_other]
    both_ref[SLOTS:, 6 * half :] = jnp.zeros((16, 2 * half), BF)


def to_row(column):
    n = column.shape[0]
    diagonal = lax.broadcasted_iota(jnp.int32, (n, n), 0) == lax.broadcasted_iota(
        jnp.int32, (n, n), 1
    )
    return jnp.sum(jnp.where(diagonal, column, 0.0), axis=0, keepdims=True)


def line_of(at, column):
    first, second = column >> 2, column & 3
    return jnp.where(at[2] == 0, first, second), jnp.where(at[2] == 0, second, first)


def line_plan(at, counts):
    u, v = line_of(at, lax.broadcasted_iota(jnp.int32, (16, 16), 0))
    u2, v2 = line_of(at, lax.broadcasted_iota(jnp.int32, (16, 16), 1))
    row = to_row(counts)
    same = v == v2
    before = same & ((u2 ^ at[4]) < (u ^ at[4]))
    skipped = jnp.sum(jnp.where(before, row, 0.0), axis=1, keepdims=True)
    total = jnp.sum(jnp.where(same, row, 0.0), axis=1, keepdims=True)
    other = jnp.sum(jnp.where(u == u2, row, 0.0), axis=1, keepdims=True)
    return skipped, total, jnp.max(jnp.maximum(total, other), axis=0, keepdims=True)


def per_lane(values, column):
    hot = lax.broadcasted_iota(jnp.int32, (16, column.shape[1]), 0) == column
    return jnp.sum(jnp.where(hot, values, 0.0), axis=0, keepdims=True)


def blocks_of(lanes, size, blocks):
    lane = lax.broadcasted_iota(jnp.int32, (1, lanes), 1)
    block = jnp.zeros((1, lanes), jnp.int32)
    for j in range(1, blocks):
        block = block + (lane >= j * size).astype(jnp.int32)
    return block, (lane - block * size).astype(F32)


def column_at(at, u, v):
    return jnp.where(at[2] == 0, u * 4 + v, v * 4 + u)


def line_targets(at, counts, skipped, slots):
    block, slot = blocks_of(4 * slots, slots, 4)
    column = column_at(at, block ^ at[4], jnp.zeros_like(block) + at[5])
    target = per_lane(skipped, column) + slot
    return jnp.where(slot < per_lane(counts, column), target, -1.0).astype(jnp.int32)


def line_bias(at, total, rows):
    block, slot = blocks_of(4 * rows, rows, 4)
    column = column_at(at, jnp.zeros_like(block) + at[4], block ^ at[5])
    return jnp.where(slot < per_lane(total, column), 0.0, -1e30)


def pack_kernel(
    at, con_ref, txt_ref, w_hbm, out_ref, spot_ref, con_bias, txt_bias, con_line, txt_line, w_ref, sem
):
    half = w_ref.shape[2]
    lanes = pl.ds(pl.multiple_of(at[2] * half, half), half)
    weights = pltpu.make_async_copy(w_hbm.at[:, :, lanes], w_ref, sem)
    weights.start()
    ids = jnp.concatenate([con_ref[...], txt_ref[...]], axis=1)
    n = ids.shape[1]
    n_con = con_ref.shape[1]
    owner = ids >> 8
    column = column_of(owner)
    here = column == at[1]
    z = ((owner & 1) << 1) | ((owner >> 4) & 1)
    core = (owner >> 1) & 1
    piece = jnp.where(here, jnp.where(core == at[2], 0, 4) + (at[3] ^ z), -1)
    spot, rank, (con_counts, txt_counts) = ranks(column, piece, n_con // 256)
    con_skip, con_total, con_most = line_plan(at, con_counts)
    txt_skip, txt_total, txt_most = line_plan(at, txt_counts)
    con_bias[...] = line_bias(at, con_total, LINE_CON)
    txt_bias[...] = line_bias(at, txt_total, LINE_TXT)
    con_line[...] = line_targets(at, con_counts, con_skip, CON)
    txt_line[...] = line_targets(at, txt_counts, txt_skip, TXT)
    _, item_v = line_of(at, column)
    spot_ref[0:1, :] = (
        (item_v ^ at[5]) * LINE_CON + per_lane(con_skip, column).astype(jnp.int32) + spot
    )
    wanted = (lax.broadcasted_iota(jnp.int32, (128, n), 0) == owner).astype(F32)
    over = jnp.maximum(
        jnp.maximum(
            jnp.max(con_counts, axis=0, keepdims=True) - CON,
            jnp.max(txt_counts, axis=0, keepdims=True) - TXT,
        ),
        jnp.maximum(con_most - LINE_CON, txt_most - LINE_TXT),
    )
    most = jnp.max(jnp.sum(wanted, axis=1, keepdims=True), axis=0, keepdims=True)
    over = jnp.maximum(over, most - SLOTS)
    spot_ref[1:2, :] = jnp.broadcast_to(over.astype(jnp.int32), (1, n))
    spot_ref[2:8, :] = jnp.zeros((6, n), jnp.int32)
    concept = lax.broadcasted_iota(jnp.int32, (1, n), 1) < n_con
    target = jnp.where(
        concept, jnp.where(spot < CON, spot, -1), jnp.where(spot < TXT, spot + CON, -1)
    )
    source = jnp.where(here & (rank < SLOTS), piece * SLOTS + rank, -1)
    label = lax.broadcasted_iota(jnp.int32, (8 * SLOTS, n), 0)
    found = jnp.sum(
        jnp.where(label == source, (target + 1).astype(F32), 0.0), axis=1, keepdims=True
    )
    hot = lax.broadcasted_iota(jnp.int32, (8 * SLOTS, 256), 1) == found.astype(jnp.int32) - 1
    out_ref[...] = jnp.transpose(hot.astype(F32))[0:ROWS].astype(BF)
    weights.wait()


def project_kernel(at, pack_ref, *refs):
    rows, (mod_ref, gain_ref, w_ref), outs, (raw_ref, x_ref) = (
        refs[:8], refs[8:11], refs[11:15], refs[15:]
    )
    for i, ref in enumerate(rows):
        raw_ref[i * SLOTS : (i + 1) * SLOTS, :] = ref[0:SLOTS, :]
    shift = mod_ref[0:1, :]
    scale = 1.0 + mod_ref[1:2, :]
    for i in range(ROWS // 32):
        block = slice(i * 32, (i + 1) * 32)
        values = nn(pack_ref[block, :], raw_ref[...])
        mean = jnp.mean(values, axis=1, keepdims=True)
        centered = values - mean
        var = jnp.mean(centered * centered, axis=1, keepdims=True)
        x_ref[block, :] = (centered * lax.rsqrt(var + 1e-06) * scale + shift).astype(BF)

    def normed(u, gain):
        meansq = jnp.mean(u * u, axis=1, keepdims=True)
        return u * lax.rsqrt(meansq + 1e-06) * gain

    q = nn(x_ref[0:CON, :], w_ref[0])
    k = nn(x_ref[...], w_ref[1])
    v = nn(x_ref[...], w_ref[2])
    heads = []
    for h in range(3):
        cols = slice(h * HD, (h + 1) * HD)
        heads.append(
            (
                (normed(q[:, cols], gain_ref[0:1, :]) * FACTOR).astype(BF),
                normed(k[:, cols], gain_ref[1:2, :]).astype(BF),
                v[:, cols].astype(BF),
            )
        )
    for s, out in enumerate(outs):
        head = jnp.minimum(at[4] ^ s, 2)
        for h in range(3):

            @pl.when(head == h)
            def _(h=h, out=out):
                out[0:ROWS, 0:HD] = heads[h][1]
                out[0:ROWS, HD:] = heads[h][2]
                out[ROWS:, 0:HD] = heads[h][0][: CON // 2]
                out[ROWS:, HD:] = heads[h][0][CON // 2 :]


def join_kernel(a, b, c, d, con_line, txt_line, out, con, txt):
    for i, ref in zip((0, 1, 3, 2), (a, b, c, d)):
        con[i * CON : (i + 1) * CON, 0 : 2 * HD] = ref[0:CON, :]
        con[i * CON : i * CON + CON // 2, 2 * HD :] = ref[ROWS:, 0:HD]
        con[i * CON + CON // 2 : (i + 1) * CON, 2 * HD :] = ref[ROWS:, HD:]
        txt[i * TXT : (i + 1) * TXT, :] = ref[CON:ROWS, :]
    hot = lax.broadcasted_iota(jnp.int32, (LINE_CON, 4 * CON), 0) == con_line[...]
    found = nn(hot.astype(F32).astype(BF), con[...]).astype(BF)
    out[0:LINE_CON, :] = found[:, 0 : 2 * HD]
    out[LINE:, 0:HD] = found[: LINE_CON // 2, 2 * HD :]
    out[LINE:, HD:] = found[LINE_CON // 2 :, 2 * HD :]
    hot = lax.broadcasted_iota(jnp.int32, (LINE_TXT, 4 * TXT), 0) == txt_line[...]
    out[LINE_CON:LINE, :] = nn(hot.astype(F32).astype(BF), txt[...]).astype(BF)


def image_heads_kernel(at, own, core, *outs):
    n, half = own.shape[0] // 3, own.shape[1]
    for s, out in enumerate(outs):
        head = jnp.minimum(at[4] ^ s, 2)
        lanes = pl.ds(pl.multiple_of(head * HD, HD), HD)
        for i in range(3):
            row = 2 * i * n
            out[row : row + n, :] = own[i * n : (i + 1) * n, lanes]
            for j in range(2):
                there = pl.ds(pl.multiple_of((2 * i + j) * half + head * HD, HD), HD)
                out[row + n + 16 * j : row + n + 16 * (j + 1), :] = core[SLOTS:, there]


def image_join_kernel(a, b, c, d, q_out, kv_out):
    n = a.shape[0] // 3
    for i, ref in enumerate((a, b, c, d)):
        q_out[n * i : n * (i + 1), :] = ref[0:n, :]
        kv_out[n * i : n * (i + 1), :] = ref[n : 2 * n, :]
        kv_out[n * (4 + i) : n * (5 + i), :] = ref[2 * n :, :]


def plane_kernel(a, b, c, d, out):
    n = a.shape[0] // 2
    for i, ref in enumerate((a, b, c, d)):
        out[n * i : n * (i + 1), :] = ref[0:n, :]
        out[n * (4 + i) : n * (5 + i), :] = ref[n:, :]


def weigh(q, parts, factor):
    scores = []
    for keys, _, bias in parts:
        part = nt(q, keys)
        scores.append(part if bias is None else part + bias)
    peak = scores[0].max(axis=1, keepdims=True)
    for part in scores[1:]:
        peak = jnp.maximum(peak, part.max(axis=1, keepdims=True))
    total = None
    for part, (_, values, _) in zip(scores, parts):
        power = part - peak
        weights = jnp.exp2(power if factor is None else power * factor).astype(BF)
        summed = nn(weights, values)
        total = summed if total is None else total + summed
    return (peak if factor is None else peak * factor), total


def join(first, second):
    peak = jnp.maximum(first[0], second[0])
    return peak, first[1] * jnp.exp2(first[0] - peak) + second[1] * jnp.exp2(second[0] - peak)


def merge(first, second):
    _, summed = join(first, second)
    return (summed[:, 0:HD] / summed[:, HD:]).astype(BF)


def with_ones(values):
    return jnp.concatenate([values, jnp.ones_like(values)], axis=1)


def image_near_kernel(plane, q, peak, summed):
    n = plane.shape[0] // 2
    part = (plane[0:n, :], with_ones(plane[n:, :]), None)
    peak[...], summed[...] = weigh(q[...], (part,), FACTOR)


def line_queries(con_q, refs):
    n = LINE_CON
    for a, ref in enumerate(refs):
        con_q[a * n : a * n + n // 2, :] = ref[LINE:, 0:HD]
        con_q[a * n + n // 2 : (a + 1) * n, :] = ref[LINE:, HD:]


def order_kernel(pick, l0, l1, q_out, con_q):
    line_queries(con_q, (l0, l1))
    q_out[...] = nn(pick[:, : 2 * LINE_CON], con_q[...]).astype(BF)


def weigh_blocks(q, parts, store):
    blk = 256
    blocks = [slice(b, b + blk) for b in range(0, q.shape[0], blk)]

    def scores(rows):
        found = []
        for keys, _, bias in parts:
            part = nt(q[rows, :], keys[...])
            found.append(part if bias is None else part + bias[...])
        return found

    ready = scores(blocks[0])
    for b, rows in enumerate(blocks):
        now, ready = ready, scores(blocks[b + 1]) if b + 1 < len(blocks) else None
        peak = now[0].max(axis=1, keepdims=True)
        for part in now[1:]:
            peak = jnp.maximum(peak, part.max(axis=1, keepdims=True))
        summed = sum(
            nn(jnp.exp2(part - peak).astype(BF), values[...])
            for part, (_, values, _) in zip(now, parts)
        )
        store(rows, peak, summed)


def near_kernel(
    pick, q_part, l0, l1, l3, l2, con_bias, txt_bias, plane, img_q, im, ims, *refs
):
    q_out, cm_out, cs_out, im_out, ims_out = refs[:5]
    con_q, con_k, con_v, txt_k, txt_v, img_v = refs[5:]
    n, m = LINE_CON, LINE_TXT
    line_queries(con_q, (l2, l3))
    for a, ref in enumerate((l0, l1, l2, l3)):
        con_k[a * n : (a + 1) * n, :] = ref[0:n, 0:HD]
        con_v[a * n : (a + 1) * n, :] = with_ones(ref[0:n, HD:])
        txt_k[a * m : (a + 1) * m, :] = ref[n:LINE, 0:HD]
        txt_v[a * m : (a + 1) * m, :] = with_ones(ref[n:LINE, HD:])
    n_img = plane.shape[0] // 2
    img_v[...] = with_ones(plane[n_img:, :])
    rest = nn(pick[:, 2 * n :], con_q[...])
    q_out[...] = (rest + q_part[...].astype(F32)).astype(BF)

    def store(rows, peak, summed):
        cm_out[rows, :] = peak
        cs_out[rows, :] = summed

    parts = ((plane.at[0:n_img, :], img_v, None), (con_k, con_v, con_bias))
    weigh_blocks(q_out, parts, store)
    text = weigh(img_q[...], ((txt_k[...], txt_v[...], txt_bias[...]),), FACTOR)
    im_out[...], ims_out[...] = join(text, (im[...], ims[...]))


def far_kernel(plane, con_q, img_q, cm, cs, im, ims, *refs):
    outs, (con_out, img_v) = refs[:4], refs[4:]
    n_img = plane.shape[0] // 2
    img_v[...] = with_ones(plane[n_img:, :])
    part = (plane[0:n_img, :], img_v[...], None)
    img = merge(weigh(img_q[...], (part,), FACTOR), (im[...], ims[...]))
    n_con = con_out.shape[0]

    def store(rows, peak, summed):
        con_out[rows, :] = merge((peak, summed), (cm[rows, :], cs[rows, :]))

    weigh_blocks(con_q, ((plane.at[0:n_img, :], img_v, None),), store)
    dots = nt(img, con_out[...]).astype(BF)
    con_f = con_out[...].astype(F32)
    squares = con_f * con_f
    high = squares.astype(BF)
    ones = jnp.ones((8, HD), BF)
    con_sq = (nt(ones, high) + nt(ones, (squares - high.astype(F32)).astype(BF))).astype(BF)
    for s, out in enumerate(outs):
        rows = slice(s * 64, (s + 1) * 64)
        out[0:64, 0:n_con] = dots[rows]
        out[0:64, n_con:] = img[rows]
        out[64:72, 0:n_con] = con_sq
        out[64:72, n_con:] = jnp.zeros((8, HD), BF)


def head_sum_kernel(at, b0, b1, b2, b3, own, core):
    n_con = b0.shape[1] - HD
    total = jnp.zeros((72, n_con), F32)
    outs = [jnp.zeros((64, HD), BF) for _ in range(3)]
    for s, ref in zip((0, 1, 3, 2), (b0, b1, b2, b3)):
        head = at[4] ^ s
        total = total + jnp.where(head < 3, ref[:, 0:n_con].astype(F32), 0.0)
        for h in range(3):
            outs[h] = jnp.where(head == h, ref[0:64, n_con:], outs[h])
    image_sq = jnp.zeros((64, 1), F32)
    for h in range(3):
        out_f = outs[h].astype(F32)
        image_sq = image_sq + jnp.sum(out_f * out_f, axis=1, keepdims=True)
    image_sq = jnp.broadcast_to(image_sq, (64, HD)).astype(BF)
    total = total.astype(BF)
    for ref, row in ((own, 0), (core, 32)):
        ref[0:32, 0:n_con] = total[row : row + 32]
        ref[32:40, 0:n_con] = total[64:72]
        ref[0:32, n_con : n_con + HD] = image_sq[row : row + 32]
        ref[32:40, n_con : n_con + HD] = jnp.zeros((8, HD), BF)
    for h in range(3):
        lanes = slice(n_con + (1 + h) * HD, n_con + (2 + h) * HD)
        for ref, row in ((own, 0), (core, 32)):
            ref[0:32, lanes] = outs[h][row : row + 32]
            ref[32:40, lanes] = jnp.zeros((8, HD), BF)


def core_sum_kernel(own, core, out):
    cols = out.shape[1]
    out[...] = (own[:, 0:cols].astype(F32) + core[:, 0:cols].astype(F32)).astype(BF)


def finish_kernel(at, sums, head, own, core, img_ref, sal_ref):
    n_con = sums.shape[1] - HD
    width = 12 * HD
    total = sums[...].astype(F32) + head[...].astype(F32)
    con_rms = jnp.sqrt(total[32:33, 0:n_con] / width + 1e-06)
    img_rms = jnp.sqrt(total[0:32, n_con : n_con + 1] / width + 1e-06)
    sal_ref[...] = total[0:32, 0:n_con] / (math.sqrt(width) * con_rms * img_rms)
    half = 3 * HD
    for ref, core_of in ((own, at[2]), (core, 1 - at[2])):
        lanes = pl.ds(pl.multiple_of(core_of * half, half), half)
        img_ref[:, lanes] = ref[0:32, n_con + HD :]


def packed(
    img_q, img_k, img_v, txt_ids, concept_ids, step_index, token_table, modulation, txt_qkv, qk_gain
):
    n_con, n_txt = concept_ids.shape[0], txt_ids.shape[0]
    ctx = lax.axis_index("ctx")
    g = lax.axis_index("head")
    c = ctx & 1
    y = (ctx >> 1) & 3
    zl = (ctx >> 3) & 1
    x = ctx >> 4
    u = jnp.where(c == 0, x, y)
    v = jnp.where(c == 0, y, x)
    at = jnp.stack([ctx * 2 + g, x * 4 + y, c, 2 * g + zl, u, v]).astype(jnp.int32)
    con_ids, text_ids = concept_ids[None, :], txt_ids[None, :]
    n = n_con + n_txt
    width = token_table.shape[1]
    half = txt_qkv.shape[2] // 2
    n_img = img_q.shape[0]

    own_rows, own_both, own_img = call(
        plan_kernel, (sds((SLOTS, width)), sds((SLOTS + 16, width)), sds((3 * n_img, half)))
    )(at, con_ids, text_ids, token_table, img_q, img_k, img_v)
    far_rows = send(own_rows, swap_z(2))
    column_rows = [own_rows] + [send(own_rows, swap_z(s)) for s in (1, 3)]
    core_both = send(own_both, swap_core())

    all_weights = jnp.transpose(txt_qkv, (1, 0, 2))
    pack, spots, con_bias, txt_bias, con_line, txt_line, weights = call(
        pack_kernel,
        (
            sds((ROWS, 8 * SLOTS)),
            sds((8, n), jnp.int32),
            sds((1, 4 * LINE_CON), F32),
            sds((1, 4 * LINE_TXT), F32),
            sds((1, 4 * CON), jnp.int32),
            sds((1, 4 * TXT), jnp.int32),
            sds((3, width, half)),
        ),
        scratch=(pltpu.SemaphoreType.DMA,),
        limit=24,
        us=2.0,
        in_hbm=1,
    )(at, con_ids, text_ids, all_weights)
    shift_scale = lax.dynamic_index_in_dim(modulation, step_index[0], 0, keepdims=False)

    image_blocks = call(
        image_heads_kernel, tuple(sds((6 * n_img, HD)) for _ in range(4))
    )(at, own_img, core_both)
    image_blocks = [image_blocks[0]] + [send(image_blocks[s], swap_u(s)) for s in (2, 1, 3)]
    image_blocks = [image_blocks[0], image_blocks[2], image_blocks[1], image_blocks[3]]
    column_rows[1], image_blocks[2] = lax.optimization_barrier((column_rows[1], image_blocks[2]))
    far_rows, pack, shift_scale, image_blocks[1] = lax.optimization_barrier(
        (far_rows, pack, shift_scale, image_blocks[1])
    )
    column_rows.insert(2, far_rows)
    other_rows = [core_both] + [send(r, swap_core()) for r in column_rows[1:]]

    qkv = call(
        project_kernel,
        tuple(sds((ROWS + CON // 2, 2 * HD)) for _ in range(4)),
        scratch=(
            pltpu.VMEM((8 * SLOTS, width), BF),
            pltpu.VMEM((ROWS, width), BF),
        ),
        limit=24,
        us=PROJ_US,
    )(at, pack, *column_rows, *other_rows, shift_scale, qk_gain, weights)

    *image_blocks, first = lax.optimization_barrier((*image_blocks, qkv[0]))
    image_q, image_kv = call(
        image_join_kernel, (sds((8 * n_img, HD)), sds((16 * n_img, HD))), smem=0
    )(*image_blocks)
    image_kvs = [image_kv] + [send(image_kv, swap_v(s)) for s in (1, 3, 2)]

    qkv = [first] + [send(qkv[s], swap_u(s)) for s in (1, 3, 2)]
    line = call(
        join_kernel,
        sds((LINE + LINE_CON // 2, 2 * HD)),
        scratch=(pltpu.VMEM((4 * CON, 3 * HD), BF), pltpu.VMEM((4 * TXT, 2 * HD), BF)),
        smem=0,
    )(*qkv, con_line, txt_line)
    lines = [line] + [send(line, swap_v(s)) for s in (1, 3, 2)]
    plane = call(plane_kernel, sds((64 * n_img, HD)), smem=0)(*image_kvs)
    con_slot, over, plane = lax.optimization_barrier((spots[0, :n_con], spots[1, 0], plane))
    other_plane = send(plane, swap_plane())
    pick = (con_slot[:, None] == jnp.arange(4 * LINE_CON)[None, :]).astype(BF)

    image_stats = (sds((8 * n_img, 1), F32), sds((8 * n_img, 2 * HD), F32))
    stats = (sds((n_con, 1), F32), sds((n_con, 2 * HD), F32)) + image_stats
    image_near = call(image_near_kernel, image_stats, smem=0)(plane, image_q)
    q_part = call(
        order_kernel, sds((n_con, HD)), scratch=(pltpu.VMEM((2 * LINE_CON, HD), BF),), smem=0
    )(pick, lines[0], lines[1])
    con_q, *near = call(
        near_kernel,
        (sds((n_con, HD)),) + stats,
        scratch=(
            pltpu.VMEM((2 * LINE_CON, HD), BF),
            pltpu.VMEM((4 * LINE_CON, HD), BF),
            pltpu.VMEM((4 * LINE_CON, 2 * HD), BF),
            pltpu.VMEM((4 * LINE_TXT, HD), BF),
            pltpu.VMEM((4 * LINE_TXT, 2 * HD), BF),
            pltpu.VMEM((32 * n_img, 2 * HD), BF),
        ),
        limit=32,
        us=NEAR_US,
        smem=0,
    )(pick, q_part, *lines, con_bias, txt_bias, plane, image_q, *image_near)
    blocks = call(
        far_kernel,
        tuple(sds((72, n_con + HD)) for _ in range(4)),
        scratch=(pltpu.VMEM((n_con, HD), BF), pltpu.VMEM((32 * n_img, 2 * HD), BF)),
        limit=24,
        us=FAR_US,
        smem=0,
    )(other_plane, con_q, image_q, *near)
    blocks = [blocks[0]] + [send(blocks[s], swap_u(s)) for s in (1, 3, 2)]
    own, core = call(head_sum_kernel, tuple(sds((40, n_con + 4 * HD)) for _ in range(2)))(
        at, *blocks
    )
    core = send(core, swap_core())
    sums = call(core_sum_kernel, sds((40, n_con + HD)), smem=0)(own, core)
    last = (at, sums, send(sums, swap_z(2)), own, core)
    finish = call(finish_kernel, (sds((n_img, 2 * half)), sds((n_img, n_con), F32)))

    def finished():
        img_out, saliency = finish(*last)
        return img_out, jnp.transpose(saliency)

    return over <= 0, finished


def on_device(*args):
    fits, finish = packed(*args)
    return lax.cond(fits, finish, lambda: tuple(general(*args)))


def solution(mesh):
    return jax.shard_map(
        on_device,
        mesh=mesh,
        in_specs=(
            P("ctx", "head"),
            P("ctx", "head"),
            P("ctx", "head"),
            P(),
            P(),
            P(),
            P(("ctx", "head"), None),
            P(),
            P(None, None, "head"),
            P(),
        ),
        out_specs=(P("ctx", "head"), P(None, "ctx")),
        check_vma=False,
    )
```

```python
import math

import jax
import jax.numpy as jnp
from jax import lax
from jax.experimental import pallas as pl
from jax.experimental.pallas import tpu as pltpu
from jax.sharding import PartitionSpec as P

BF = jnp.bfloat16
F32 = jnp.float32
HD = 128
SLOTS = 32
CON = 96
TXT = 64
ROWS = CON + TXT
LINE_CON = 320
LINE_TXT = 176
LINE = LINE_CON + LINE_TXT
MIB = 1 << 20
PROJ_US, NEAR_US, FAR_US = 5.0, 2.0, 3.0
FACTOR = HD ** (-0.5) * math.log2(math.e)


def modulate(rows, shift_scale):
    values = rows.astype(F32)
    mean = jnp.mean(values, axis=1, keepdims=True)
    centered = values - mean
    var = jnp.mean(centered * centered, axis=1, keepdims=True)
    normed = centered * lax.rsqrt(var + 1e-06)
    return (normed * (1.0 + shift_scale[1]) + shift_scale[0]).astype(BF)


def head_norm(values, gain, head_dim):
    shaped = values.reshape(values.shape[0], -1, head_dim)
    meansq = jnp.mean(shaped * shaped, axis=2, keepdims=True)
    return (shaped * lax.rsqrt(meansq + 1e-06) * gain).reshape(values.shape[0], -1)


def block_stats(queries, keys, values):
    scores = jnp.einsum("rgd,kgd->grk", queries, keys, preferred_element_type=F32)
    scores = scores * queries.shape[-1] ** (-0.5)
    peak = jnp.max(scores, axis=2)
    weights = jnp.exp(scores - peak[:, :, None])
    total = jnp.sum(weights, axis=2)
    summed = jnp.einsum("grk,kgd->grd", weights.astype(BF), values, preferred_element_type=F32)
    return (peak, total, summed)


def combine_stats(first, second):
    peak = jnp.maximum(first[0], second[0])
    left = jnp.exp(first[0] - peak)
    right = jnp.exp(second[0] - peak)
    total = first[1] * left + second[1] * right
    summed = first[2] * left[:, :, None] + second[2] * right[:, :, None]
    return (peak, total, summed)


def scaled_scores(dots, concept_sq, image_sq, width):
    concept_rms = jnp.sqrt(concept_sq / width + 1e-06)
    image_rms = jnp.sqrt(image_sq / width + 1e-06)
    return dots / (jnp.sqrt(F32(width)) * concept_rms[:, None] * image_rms[None, :])


def gather_ctx(block):
    n_ctx = lax.axis_size("ctx")
    spread = jnp.broadcast_to(block[None], (n_ctx,) + block.shape)
    return lax.all_to_all(spread, "ctx", 0, 0, tiled=True)


def general(
    img_q, img_k, img_v, txt_ids, concept_ids, step_index, token_table, modulation, txt_qkv, qk_gain
):
    n_ctx = lax.axis_size("ctx")
    n_head = lax.axis_size("head")
    head_dim = qk_gain.shape[1]
    group = img_q.shape[1] // head_dim
    text_dev = txt_ids.shape[0] // n_ctx
    concept_dev = concept_ids.shape[0] // n_ctx
    vocab_dev = token_table.shape[0]
    combined = jnp.concatenate(
        [txt_ids.reshape(n_ctx, text_dev), concept_ids.reshape(n_ctx, concept_dev)], axis=1
    ).reshape(-1)
    offset = lax.axis_index(("ctx", "head")) * vocab_dev
    wanted = combined - offset
    inside = (wanted >= 0) & (wanted < vocab_dev)
    picked = jnp.take(token_table, jnp.clip(wanted, 0, vocab_dev - 1), axis=0)
    n_all = n_ctx * n_head
    mine = jnp.where(inside[:, None], picked, jnp.zeros((), picked.dtype))
    parts = lax.all_to_all(
        mine.reshape(n_all, -1, mine.shape[1]), ("ctx", "head"), 0, 0, tiled=True
    )
    own_rows = jnp.sum(parts.astype(F32), axis=0)
    prompt_rows = lax.all_gather(own_rows.astype(BF), "head", axis=0, tiled=True)
    shift_scale = lax.dynamic_index_in_dim(modulation, step_index[0], 0, keepdims=False)
    modded = modulate(prompt_rows, shift_scale)
    text_mod = modded[:text_dev]
    concept_mod = modded[text_dev:]
    text_kv = jnp.einsum("rd,dgc->rgc", text_mod, txt_qkv[:, 1:], preferred_element_type=F32)
    concept_qkv = jnp.einsum("rd,dgc->rgc", concept_mod, txt_qkv, preferred_element_type=F32)
    text_keys = head_norm(text_kv[:, 0], qk_gain[1], head_dim).astype(BF)
    text_values = text_kv[:, 1].astype(BF)
    concept_queries = head_norm(concept_qkv[:, 0], qk_gain[0], head_dim).astype(BF)
    concept_keys = head_norm(concept_qkv[:, 1], qk_gain[1], head_dim).astype(BF)
    concept_values = concept_qkv[:, 2].astype(BF)
    local_kv = jnp.stack(
        [
            jnp.concatenate([text_keys, concept_keys], axis=0),
            jnp.concatenate([text_values, concept_values], axis=0),
        ]
    )
    prompt_kv = gather_ctx(local_kv)
    text_part = jnp.swapaxes(prompt_kv[:, :, :text_dev], 0, 1).reshape(2, -1, group, head_dim)
    concept_part = jnp.swapaxes(prompt_kv[:, :, text_dev:], 0, 1).reshape(2, -1, group, head_dim)
    image_queries = img_q.reshape(-1, group, head_dim)
    concept_q3 = concept_queries.reshape(-1, group, head_dim)
    first = block_stats(image_queries, text_part[0], text_part[1])
    second = block_stats(concept_q3, concept_part[0], concept_part[1])
    start_stats = (
        jnp.concatenate([first[0], second[0]], axis=1),
        jnp.concatenate([first[1], second[1]], axis=1),
        jnp.concatenate([first[2], second[2]], axis=1),
    )
    all_queries = jnp.concatenate([image_queries, concept_q3], axis=0)
    image_kv = gather_ctx(jnp.stack([img_k, img_v]))
    keys = image_kv[:, 0].reshape(-1, group, head_dim)
    values = image_kv[:, 1].reshape(-1, group, head_dim)
    peak, total, summed = combine_stats(start_stats, block_stats(all_queries, keys, values))
    attended = (
        jnp.transpose(summed / total[:, :, None], (1, 0, 2))
        .reshape(all_queries.shape[0], -1)
        .astype(BF)
    )
    img_rows = img_q.shape[0]
    img_out = attended[:img_rows]
    concept_out = attended[img_rows:]
    concept_all = gather_ctx(concept_out).reshape(-1, concept_out.shape[1])
    dots = lax.dot_general(
        concept_all, img_out, (((1,), (1,)), ((), ())), preferred_element_type=F32
    )
    image_f = img_out.astype(F32)
    concept_f = concept_all.astype(F32)
    image_sq = jnp.sum(image_f * image_f, axis=1)
    concept_sq = jnp.sum(concept_f * concept_f, axis=1)
    width = group * head_dim * n_head
    sums = jnp.concatenate(
        [
            jnp.concatenate([dots, concept_sq[:, None]], axis=1),
            jnp.concatenate([image_sq, jnp.zeros((1,), F32)])[None],
        ]
    ).astype(BF)
    other = lax.ppermute(sums, "head", [(0, 1), (1, 0)])
    sums = sums.astype(F32) + other.astype(F32)
    concepts = dots.shape[0]
    saliency = scaled_scores(
        sums[:concepts, :img_rows], sums[:concepts, img_rows], sums[concepts, :img_rows], width
    )
    return (img_out, saliency)


def place(x, zl, y, c, g):
    return ((((x * 2 + zl) * 4 + y) * 2 + c) * 2) + g


def pairs(move):
    found = []
    for x in range(4):
        for zl in range(2):
            for y in range(4):
                for c in range(2):
                    for g in range(2):
                        found.append((place(x, zl, y, c, g), place(*move(x, zl, y, c, g))))
    return found


def swap_z(s):
    def move(x, zl, y, c, g):
        z = (2 * g + zl) ^ s
        return x, z & 1, y, c, z >> 1

    return pairs(move)


def swap_u(s):
    return pairs(
        lambda x, zl, y, c, g: (x, zl, y ^ s, c, g) if c else (x ^ s, zl, y, c, g)
    )


def swap_v(s):
    return pairs(
        lambda x, zl, y, c, g: (x ^ s, zl, y, c, g) if c else (x, zl, y ^ s, c, g)
    )


def swap_plane():
    return pairs(lambda x, zl, y, c, g: (x, zl ^ 1, y, c, g))


def swap_core():
    return pairs(lambda x, zl, y, c, g: (x, zl, y, c ^ 1, g))


def send(array, pairing):
    return lax.ppermute(array, ("ctx", "head"), pairing)


def nt(a, b, **kw):
    return lax.dot_general(a, b, (((1,), (1,)), ((), ())), preferred_element_type=F32, **kw)


def nn(a, b):
    return lax.dot_general(a, b, (((1,), (0,)), ((), ())), preferred_element_type=F32)


def call(kernel, outs, scratch=(), limit=16, us=1.0, smem=1, in_hbm=0):
    def run(*args):
        vm = pl.BlockSpec(memory_space=pltpu.VMEM)
        sm = pl.BlockSpec(memory_space=pltpu.SMEM)
        return pl.pallas_call(
            kernel,
            out_shape=outs,
            in_specs=[sm] * smem
            + [vm] * (len(args) - smem - in_hbm)
            + [pl.BlockSpec(memory_space=pl.ANY)] * in_hbm,
            out_specs=jax.tree.map(lambda _: vm, outs),
            scratch_shapes=list(scratch),
            compiler_params=pltpu.CompilerParams(vmem_limit_bytes=limit * MIB),
            cost_estimate=pl.CostEstimate(
                flops=int(us * 1.1e9), bytes_accessed=0, transcendentals=0
            ),
        )(*args)

    return run


def sds(shape, dtype=BF):
    return jax.ShapeDtypeStruct(shape, dtype)


def column_of(owner):
    ctx = owner >> 1
    return ((ctx >> 4) << 2) | ((ctx >> 1) & 3)


def ranks(columns, pieces, reset):
    n = columns.shape[1]
    blk = 256
    row = lax.broadcasted_iota(jnp.int32, (blk, blk), 0)
    col = lax.broadcasted_iota(jnp.int32, (blk, blk), 1)
    earlier = (row < col).astype(F32).astype(BF)
    label = lax.broadcasted_iota(jnp.int32, (16, blk), 0)
    label_piece = lax.broadcasted_iota(jnp.int32, (8, blk), 0)
    carry, carry_piece = jnp.zeros((16, 1), F32), jnp.zeros((8, 1), F32)
    spots, found, counts = [], [], []
    for b in range(n // blk):
        if b == reset:
            counts.append(carry)
            carry = jnp.zeros((16, 1), F32)
        lanes = slice(b * blk, (b + 1) * blk)
        hot = (label == columns[:, lanes]).astype(F32)
        hot_piece = (label_piece == pieces[:, lanes]).astype(F32)
        before = nn(jnp.concatenate([hot, hot_piece], axis=0).astype(BF), earlier)
        spots.append(jnp.sum(hot * (before[0:16] + carry), axis=0, keepdims=True))
        found.append(jnp.sum(hot_piece * (before[16:24] + carry_piece), axis=0, keepdims=True))
        carry = carry + jnp.sum(hot, axis=1, keepdims=True)
        carry_piece = carry_piece + jnp.sum(hot_piece, axis=1, keepdims=True)
    counts.append(carry)
    spots, found = (jnp.concatenate(r, axis=1).astype(jnp.int32) for r in (spots, found))
    return spots, found, counts


def plan_kernel(
    at, con_ref, txt_ref, table_ref, q_ref, k_ref, v_ref, rows_ref, both_ref, img_ref
):
    ids = jnp.concatenate([con_ref[...], txt_ref[...]], axis=1)
    n = ids.shape[1]
    blk = 256
    blocks = n // blk
    vocab_dev = table_ref.shape[0]
    mine = ((ids >> int(math.log2(vocab_dev))) == at[0]).astype(F32)
    pieces = [slice(b * blk, (b + 1) * blk) for b in range(blocks)]
    folded = jnp.concatenate(
        [mine[:, p] for p in pieces] + [jnp.zeros((8 - blocks, blk), F32)], axis=0
    )
    row = lax.broadcasted_iota(jnp.int32, (blk, blk), 0)
    col = lax.broadcasted_iota(jnp.int32, (blk, blk), 1)
    before = nn(folded.astype(BF), (row < col).astype(F32).astype(BF))
    label = lax.broadcasted_iota(jnp.int32, (SLOTS, blk), 0).astype(F32)
    found = jnp.zeros((SLOTS, blk), F32)
    skipped = jnp.zeros((1, 1), F32)
    for b, p in enumerate(pieces):
        rank = before[b : b + 1, :] + skipped
        row_in_table = ((ids[:, p] & (vocab_dev - 1)) + 1).astype(F32) * mine[:, p]
        found = found + jnp.where(label == rank, row_in_table, 0.0)
        skipped = skipped + jnp.sum(mine[:, p], axis=1, keepdims=True)
    found = jnp.sum(found, axis=1, keepdims=True).astype(jnp.int32) - 1
    pick = lax.broadcasted_iota(jnp.int32, (SLOTS, vocab_dev), 1) == found
    rows = nn(pick.astype(F32).astype(BF), table_ref[...]).astype(BF)
    rows_ref[...] = rows
    both_ref[0:SLOTS, :] = rows
    m = q_ref.shape[0]
    half = q_ref.shape[1] // 2
    lanes_own = pl.ds(pl.multiple_of(at[2] * half, half), half)
    lanes_other = pl.ds(pl.multiple_of((1 - at[2]) * half, half), half)
    for i, ref in enumerate((q_ref, k_ref, v_ref)):
        img_ref[i * m : (i + 1) * m, :] = ref[:, lanes_own]
        for j in range(2):
            lanes = slice((2 * i + j) * half, (2 * i + j + 1) * half)
            both_ref[SLOTS:, lanes] = ref[16 * j : 16 * (j + 1), lanes_other]
    both_ref[SLOTS:, 6 * half :] = jnp.zeros((16, 2 * half), BF)


def to_row(column):
    n = column.shape[0]
    diagonal = lax.broadcasted_iota(jnp.int32, (n, n), 0) == lax.broadcasted_iota(
        jnp.int32, (n, n), 1
    )
    return jnp.sum(jnp.where(diagonal, column, 0.0), axis=0, keepdims=True)


def line_of(at, column):
    first, second = column >> 2, column & 3
    return jnp.where(at[2] == 0, first, second), jnp.where(at[2] == 0, second, first)


def line_plan(at, counts):
    u, v = line_of(at, lax.broadcasted_iota(jnp.int32, (16, 16), 0))
    u2, v2 = line_of(at, lax.broadcasted_iota(jnp.int32, (16, 16), 1))
    row = to_row(counts)
    same = v == v2
    before = same & ((u2 ^ at[4]) < (u ^ at[4]))
    skipped = jnp.sum(jnp.where(before, row, 0.0), axis=1, keepdims=True)
    total = jnp.sum(jnp.where(same, row, 0.0), axis=1, keepdims=True)
    other = jnp.sum(jnp.where(u == u2, row, 0.0), axis=1, keepdims=True)
    return skipped, total, jnp.max(jnp.maximum(total, other), axis=0, keepdims=True)


def per_lane(values, column):
    hot = lax.broadcasted_iota(jnp.int32, (16, column.shape[1]), 0) == column
    return jnp.sum(jnp.where(hot, values, 0.0), axis=0, keepdims=True)


def blocks_of(lanes, size, blocks):
    lane = lax.broadcasted_iota(jnp.int32, (1, lanes), 1)
    block = jnp.zeros((1, lanes), jnp.int32)
    for j in range(1, blocks):
        block = block + (lane >= j * size).astype(jnp.int32)
    return block, (lane - block * size).astype(F32)


def column_at(at, u, v):
    return jnp.where(at[2] == 0, u * 4 + v, v * 4 + u)


def line_targets(at, counts, skipped, slots):
    block, slot = blocks_of(4 * slots, slots, 4)
    column = column_at(at, block ^ at[4], jnp.zeros_like(block) + at[5])
    target = per_lane(skipped, column) + slot
    return jnp.where(slot < per_lane(counts, column), target, -1.0).astype(jnp.int32)


def line_bias(at, total, rows):
    block, slot = blocks_of(4 * rows, rows, 4)
    column = column_at(at, jnp.zeros_like(block) + at[4], block ^ at[5])
    return jnp.where(slot < per_lane(total, column), 0.0, -1e30)


def pack_kernel(
    at, con_ref, txt_ref, w_hbm, out_ref, spot_ref, con_bias, txt_bias, con_line, txt_line, w_ref, sem
):
    half = w_ref.shape[2]
    lanes = pl.ds(pl.multiple_of(at[2] * half, half), half)
    weights = pltpu.make_async_copy(w_hbm.at[:, :, lanes], w_ref, sem)
    weights.start()
    ids = jnp.concatenate([con_ref[...], txt_ref[...]], axis=1)
    n = ids.shape[1]
    n_con = con_ref.shape[1]
    owner = ids >> 8
    column = column_of(owner)
    here = column == at[1]
    z = ((owner & 1) << 1) | ((owner >> 4) & 1)
    core = (owner >> 1) & 1
    piece = jnp.where(here, jnp.where(core == at[2], 0, 4) + (at[3] ^ z), -1)
    spot, rank, (con_counts, txt_counts) = ranks(column, piece, n_con // 256)
    con_skip, con_total, con_most = line_plan(at, con_counts)
    txt_skip, txt_total, txt_most = line_plan(at, txt_counts)
    con_bias[...] = line_bias(at, con_total, LINE_CON)
    txt_bias[...] = line_bias(at, txt_total, LINE_TXT)
    con_line[...] = line_targets(at, con_counts, con_skip, CON)
    txt_line[...] = line_targets(at, txt_counts, txt_skip, TXT)
    _, item_v = line_of(at, column)
    spot_ref[0:1, :] = (
        (item_v ^ at[5]) * LINE_CON + per_lane(con_skip, column).astype(jnp.int32) + spot
    )
    wanted = (lax.broadcasted_iota(jnp.int32, (128, n), 0) == owner).astype(F32)
    over = jnp.maximum(
        jnp.maximum(
            jnp.max(con_counts, axis=0, keepdims=True) - CON,
            jnp.max(txt_counts, axis=0, keepdims=True) - TXT,
        ),
        jnp.maximum(con_most - LINE_CON, txt_most - LINE_TXT),
    )
    most = jnp.max(jnp.sum(wanted, axis=1, keepdims=True), axis=0, keepdims=True)
    over = jnp.maximum(over, most - SLOTS)
    spot_ref[1:2, :] = jnp.broadcast_to(over.astype(jnp.int32), (1, n))
    spot_ref[2:8, :] = jnp.zeros((6, n), jnp.int32)
    concept = lax.broadcasted_iota(jnp.int32, (1, n), 1) < n_con
    target = jnp.where(
        concept, jnp.where(spot < CON, spot, -1), jnp.where(spot < TXT, spot + CON, -1)
    )
    source = jnp.where(here & (rank < SLOTS), piece * SLOTS + rank, -1)
    label = lax.broadcasted_iota(jnp.int32, (8 * SLOTS, n), 0)
    found = jnp.sum(
        jnp.where(label == source, (target + 1).astype(F32), 0.0), axis=1, keepdims=True
    )
    hot = lax.broadcasted_iota(jnp.int32, (8 * SLOTS, 256), 1) == found.astype(jnp.int32) - 1
    out_ref[...] = jnp.transpose(hot.astype(F32))[0:ROWS].astype(BF)
    weights.wait()


def project_kernel(at, pack_ref, *refs):
    rows, (mod_ref, gain_ref, w_ref), outs, (raw_ref, x_ref) = (
        refs[:8], refs[8:11], refs[11:15], refs[15:]
    )
    for i, ref in enumerate(rows):
        raw_ref[i * SLOTS : (i + 1) * SLOTS, :] = ref[0:SLOTS, :]
    shift = mod_ref[0:1, :]
    scale = 1.0 + mod_ref[1:2, :]
    for i in range(ROWS // 32):
        block = slice(i * 32, (i + 1) * 32)
        values = nn(pack_ref[block, :], raw_ref[...])
        mean = jnp.mean(values, axis=1, keepdims=True)
        centered = values - mean
        var = jnp.mean(centered * centered, axis=1, keepdims=True)
        x_ref[block, :] = (centered * lax.rsqrt(var + 1e-06) * scale + shift).astype(BF)

    def normed(u, gain):
        meansq = jnp.mean(u * u, axis=1, keepdims=True)
        return u * lax.rsqrt(meansq + 1e-06) * gain

    q = nn(x_ref[0:CON, :], w_ref[0])
    k = nn(x_ref[...], w_ref[1])
    v = nn(x_ref[...], w_ref[2])
    heads = []
    for h in range(3):
        cols = slice(h * HD, (h + 1) * HD)
        heads.append(
            (
                (normed(q[:, cols], gain_ref[0:1, :]) * FACTOR).astype(BF),
                normed(k[:, cols], gain_ref[1:2, :]).astype(BF),
                v[:, cols].astype(BF),
            )
        )
    for s, out in enumerate(outs):
        head = jnp.minimum(at[4] ^ s, 2)
        for h in range(3):

            @pl.when(head == h)
            def _(h=h, out=out):
                out[0:ROWS, 0:HD] = heads[h][1]
                out[0:ROWS, HD:] = heads[h][2]
                out[ROWS:, 0:HD] = heads[h][0][: CON // 2]
                out[ROWS:, HD:] = heads[h][0][CON // 2 :]


def join_kernel(a, b, c, d, con_line, txt_line, out, con, txt):
    for i, ref in zip((0, 1, 3, 2), (a, b, c, d)):
        con[i * CON : (i + 1) * CON, 0 : 2 * HD] = ref[0:CON, :]
        con[i * CON : i * CON + CON // 2, 2 * HD :] = ref[ROWS:, 0:HD]
        con[i * CON + CON // 2 : (i + 1) * CON, 2 * HD :] = ref[ROWS:, HD:]
        txt[i * TXT : (i + 1) * TXT, :] = ref[CON:ROWS, :]
    hot = lax.broadcasted_iota(jnp.int32, (LINE_CON, 4 * CON), 0) == con_line[...]
    found = nn(hot.astype(F32).astype(BF), con[...]).astype(BF)
    out[0:LINE_CON, :] = found[:, 0 : 2 * HD]
    out[LINE:, 0:HD] = found[: LINE_CON // 2, 2 * HD :]
    out[LINE:, HD:] = found[LINE_CON // 2 :, 2 * HD :]
    hot = lax.broadcasted_iota(jnp.int32, (LINE_TXT, 4 * TXT), 0) == txt_line[...]
    out[LINE_CON:LINE, :] = nn(hot.astype(F32).astype(BF), txt[...]).astype(BF)


def image_heads_kernel(at, own, core, *outs):
    n, half = own.shape[0] // 3, own.shape[1]
    for s, out in enumerate(outs):
        head = jnp.minimum(at[4] ^ s, 2)
        lanes = pl.ds(pl.multiple_of(head * HD, HD), HD)
        for i in range(3):
            row = 2 * i * n
            out[row : row + n, :] = own[i * n : (i + 1) * n, lanes]
            for j in range(2):
                there = pl.ds(pl.multiple_of((2 * i + j) * half + head * HD, HD), HD)
                out[row + n + 16 * j : row + n + 16 * (j + 1), :] = core[SLOTS:, there]


def image_join_kernel(a, b, c, d, q_out, kv_out):
    n = a.shape[0] // 3
    for i, ref in enumerate((a, b, c, d)):
        q_out[n * i : n * (i + 1), :] = ref[0:n, :]
        kv_out[n * i : n * (i + 1), :] = ref[n : 2 * n, :]
        kv_out[n * (4 + i) : n * (5 + i), :] = ref[2 * n :, :]


def plane_kernel(a, b, c, d, out):
    n = a.shape[0] // 2
    for i, ref in enumerate((a, b, c, d)):
        out[n * i : n * (i + 1), :] = ref[0:n, :]
        out[n * (4 + i) : n * (5 + i), :] = ref[n:, :]


def weigh(q, parts, factor):
    scores = []
    for keys, _, bias in parts:
        part = nt(q, keys)
        scores.append(part if bias is None else part + bias)
    peak = scores[0].max(axis=1, keepdims=True)
    for part in scores[1:]:
        peak = jnp.maximum(peak, part.max(axis=1, keepdims=True))
    total = None
    for part, (_, values, _) in zip(scores, parts):
        power = part - peak
        weights = jnp.exp2(power if factor is None else power * factor).astype(BF)
        summed = nn(weights, values)
        total = summed if total is None else total + summed
    return (peak if factor is None else peak * factor), total


def join(first, second):
    peak = jnp.maximum(first[0], second[0])
    return peak, first[1] * jnp.exp2(first[0] - peak) + second[1] * jnp.exp2(second[0] - peak)


def merge(first, second):
    _, summed = join(first, second)
    return (summed[:, 0:HD] / summed[:, HD:]).astype(BF)


def with_ones(values):
    return jnp.concatenate([values, jnp.ones_like(values)], axis=1)


def image_near_kernel(plane, q, peak, summed):
    n = plane.shape[0] // 2
    part = (plane[0:n, :], with_ones(plane[n:, :]), None)
    peak[...], summed[...] = weigh(q[...], (part,), FACTOR)


def line_queries(con_q, refs):
    n = LINE_CON
    for a, ref in enumerate(refs):
        con_q[a * n : a * n + n // 2, :] = ref[LINE:, 0:HD]
        con_q[a * n + n // 2 : (a + 1) * n, :] = ref[LINE:, HD:]


def line_texts(txt_k, txt_v, refs):
    m = LINE_TXT
    for a, ref in enumerate(refs):
        txt_k[a * m : (a + 1) * m, :] = ref[LINE_CON:LINE, 0:HD]
        txt_v[a * m : (a + 1) * m, :] = with_ones(ref[LINE_CON:LINE, HD:])


def order_kernel(pick, l0, l1, txt_bias, img_q, im, ims, *refs):
    (q_out, im_out, ims_out), (con_q, txt_k, txt_v) = refs[:3], refs[3:]
    line_queries(con_q, (l0, l1))
    q_out[...] = nn(pick[:, : 2 * LINE_CON], con_q[...]).astype(BF)
    line_texts(txt_k, txt_v, (l0, l1))
    part = (txt_k[...], txt_v[...], txt_bias[:, 0 : 2 * LINE_TXT])
    im_out[...], ims_out[...] = join(weigh(img_q[...], (part,), FACTOR), (im[...], ims[...]))


def weigh_blocks(q, parts, store):
    blk = 256
    blocks = [slice(b, b + blk) for b in range(0, q.shape[0], blk)]

    def scores(rows):
        found = []
        for keys, _, bias in parts:
            part = nt(q[rows, :], keys[...])
            found.append(part if bias is None else part + bias[...])
        return found

    ready = scores(blocks[0])
    for b, rows in enumerate(blocks):
        now, ready = ready, scores(blocks[b + 1]) if b + 1 < len(blocks) else None
        peak = now[0].max(axis=1, keepdims=True)
        for part in now[1:]:
            peak = jnp.maximum(peak, part.max(axis=1, keepdims=True))
        summed = sum(
            nn(jnp.exp2(part - peak).astype(BF), values[...])
            for part, (_, values, _) in zip(now, parts)
        )
        store(rows, peak, summed)


def near_kernel(
    pick, q_part, l0, l1, l3, l2, con_bias, txt_bias, plane, img_q, im, ims, *refs
):
    q_out, cm_out, cs_out, im_out, ims_out = refs[:5]
    con_q, con_k, con_v, txt_k, txt_v, img_v = refs[5:]
    n = LINE_CON
    line_queries(con_q, (l2, l3))
    for a, ref in enumerate((l0, l1, l2, l3)):
        con_k[a * n : (a + 1) * n, :] = ref[0:n, 0:HD]
        con_v[a * n : (a + 1) * n, :] = with_ones(ref[0:n, HD:])
    line_texts(txt_k, txt_v, (l2, l3))
    n_img = plane.shape[0] // 2
    img_v[...] = with_ones(plane[n_img:, :])
    rest = nn(pick[:, 2 * n :], con_q[...])
    q_out[...] = (rest + q_part[...].astype(F32)).astype(BF)

    def store(rows, peak, summed):
        cm_out[rows, :] = peak
        cs_out[rows, :] = summed

    parts = ((plane.at[0:n_img, :], img_v, None), (con_k, con_v, con_bias))
    weigh_blocks(q_out, parts, store)
    text = weigh(img_q[...], ((txt_k[...], txt_v[...], txt_bias[:, 2 * LINE_TXT :]),), FACTOR)
    im_out[...], ims_out[...] = join(text, (im[...], ims[...]))


def far_kernel(plane, con_q, img_q, cm, cs, im, ims, *refs):
    outs, (con_out, img_v) = refs[:4], refs[4:]
    n_img = plane.shape[0] // 2
    img_v[...] = with_ones(plane[n_img:, :])
    part = (plane[0:n_img, :], img_v[...], None)
    img = merge(weigh(img_q[...], (part,), FACTOR), (im[...], ims[...]))
    n_con = con_out.shape[0]

    def store(rows, peak, summed):
        con_out[rows, :] = merge((peak, summed), (cm[rows, :], cs[rows, :]))

    weigh_blocks(con_q, ((plane.at[0:n_img, :], img_v, None),), store)
    dots = nt(img, con_out[...]).astype(BF)
    con_f = con_out[...].astype(F32)
    squares = con_f * con_f
    high = squares.astype(BF)
    ones = jnp.ones((8, HD), BF)
    con_sq = (nt(ones, high) + nt(ones, (squares - high.astype(F32)).astype(BF))).astype(BF)
    for s, out in enumerate(outs):
        rows = slice(s * 64, (s + 1) * 64)
        out[0:64, 0:n_con] = dots[rows]
        out[0:64, n_con:] = img[rows]
        out[64:72, 0:n_con] = con_sq
        out[64:72, n_con:] = jnp.zeros((8, HD), BF)


def head_sum_kernel(at, b0, b1, b2, b3, own, core):
    n_con = b0.shape[1] - HD
    total = jnp.zeros((72, n_con), F32)
    outs = [jnp.zeros((64, HD), BF) for _ in range(3)]
    for s, ref in zip((0, 1, 3, 2), (b0, b1, b2, b3)):
        head = at[4] ^ s
        total = total + jnp.where(head < 3, ref[:, 0:n_con].astype(F32), 0.0)
        for h in range(3):
            outs[h] = jnp.where(head == h, ref[0:64, n_con:], outs[h])
    image_sq = jnp.zeros((64, 1), F32)
    for h in range(3):
        out_f = outs[h].astype(F32)
        image_sq = image_sq + jnp.sum(out_f * out_f, axis=1, keepdims=True)
    image_sq = jnp.broadcast_to(image_sq, (64, HD)).astype(BF)
    total = total.astype(BF)
    for ref, row in ((own, 0), (core, 32)):
        ref[0:32, 0:n_con] = total[row : row + 32]
        ref[32:40, 0:n_con] = total[64:72]
        ref[0:32, n_con : n_con + HD] = image_sq[row : row + 32]
        ref[32:40, n_con : n_con + HD] = jnp.zeros((8, HD), BF)
    for h in range(3):
        lanes = slice(n_con + (1 + h) * HD, n_con + (2 + h) * HD)
        for ref, row in ((own, 0), (core, 32)):
            ref[0:32, lanes] = outs[h][row : row + 32]
            ref[32:40, lanes] = jnp.zeros((8, HD), BF)


def core_sum_kernel(own, core, out):
    cols = out.shape[1]
    out[...] = (own[:, 0:cols].astype(F32) + core[:, 0:cols].astype(F32)).astype(BF)


def finish_kernel(at, sums, head, own, core, img_ref, sal_ref):
    n_con = sums.shape[1] - HD
    width = 12 * HD
    total = sums[...].astype(F32) + head[...].astype(F32)
    con_rms = jnp.sqrt(total[32:33, 0:n_con] / width + 1e-06)
    img_rms = jnp.sqrt(total[0:32, n_con : n_con + 1] / width + 1e-06)
    sal_ref[...] = total[0:32, 0:n_con] / (math.sqrt(width) * con_rms * img_rms)
    half = 3 * HD
    for ref, core_of in ((own, at[2]), (core, 1 - at[2])):
        lanes = pl.ds(pl.multiple_of(core_of * half, half), half)
        img_ref[:, lanes] = ref[0:32, n_con + HD :]


def packed(
    img_q, img_k, img_v, txt_ids, concept_ids, step_index, token_table, modulation, txt_qkv, qk_gain
):
    n_con, n_txt = concept_ids.shape[0], txt_ids.shape[0]
    ctx = lax.axis_index("ctx")
    g = lax.axis_index("head")
    c = ctx & 1
    y = (ctx >> 1) & 3
    zl = (ctx >> 3) & 1
    x = ctx >> 4
    u = jnp.where(c == 0, x, y)
    v = jnp.where(c == 0, y, x)
    at = jnp.stack([ctx * 2 + g, x * 4 + y, c, 2 * g + zl, u, v]).astype(jnp.int32)
    con_ids, text_ids = concept_ids[None, :], txt_ids[None, :]
    n = n_con + n_txt
    width = token_table.shape[1]
    half = txt_qkv.shape[2] // 2
    n_img = img_q.shape[0]

    own_rows, own_both, own_img = call(
        plan_kernel, (sds((SLOTS, width)), sds((SLOTS + 16, width)), sds((3 * n_img, half)))
    )(at, con_ids, text_ids, token_table, img_q, img_k, img_v)
    far_rows = send(own_rows, swap_z(2))
    column_rows = [own_rows] + [send(own_rows, swap_z(s)) for s in (1, 3)]
    core_both = send(own_both, swap_core())

    all_weights = jnp.transpose(txt_qkv, (1, 0, 2))
    pack, spots, con_bias, txt_bias, con_line, txt_line, weights = call(
        pack_kernel,
        (
            sds((ROWS, 8 * SLOTS)),
            sds((8, n), jnp.int32),
            sds((1, 4 * LINE_CON), F32),
            sds((1, 4 * LINE_TXT), F32),
            sds((1, 4 * CON), jnp.int32),
            sds((1, 4 * TXT), jnp.int32),
            sds((3, width, half)),
        ),
        scratch=(pltpu.SemaphoreType.DMA,),
        limit=24,
        us=2.0,
        in_hbm=1,
    )(at, con_ids, text_ids, all_weights)
    shift_scale = lax.dynamic_index_in_dim(modulation, step_index[0], 0, keepdims=False)

    image_blocks = call(
        image_heads_kernel, tuple(sds((6 * n_img, HD)) for _ in range(4))
    )(at, own_img, core_both)
    image_blocks = [image_blocks[0]] + [send(image_blocks[s], swap_u(s)) for s in (2, 1, 3)]
    image_blocks = [image_blocks[0], image_blocks[2], image_blocks[1], image_blocks[3]]
    column_rows[1], image_blocks[2] = lax.optimization_barrier((column_rows[1], image_blocks[2]))
    far_rows, pack, shift_scale, image_blocks[1] = lax.optimization_barrier(
        (far_rows, pack, shift_scale, image_blocks[1])
    )
    column_rows.insert(2, far_rows)
    other_rows = [core_both] + [send(r, swap_core()) for r in column_rows[1:]]

    qkv = call(
        project_kernel,
        tuple(sds((ROWS + CON // 2, 2 * HD)) for _ in range(4)),
        scratch=(
            pltpu.VMEM((8 * SLOTS, width), BF),
            pltpu.VMEM((ROWS, width), BF),
        ),
        limit=24,
        us=PROJ_US,
    )(at, pack, *column_rows, *other_rows, shift_scale, qk_gain, weights)

    *image_blocks, first = lax.optimization_barrier((*image_blocks, qkv[0]))
    image_q, image_kv = call(
        image_join_kernel, (sds((8 * n_img, HD)), sds((16 * n_img, HD))), smem=0
    )(*image_blocks)
    image_kvs = [image_kv] + [send(image_kv, swap_v(s)) for s in (1, 3, 2)]

    qkv = [first] + [send(qkv[s], swap_u(s)) for s in (1, 3, 2)]
    line = call(
        join_kernel,
        sds((LINE + LINE_CON // 2, 2 * HD)),
        scratch=(pltpu.VMEM((4 * CON, 3 * HD), BF), pltpu.VMEM((4 * TXT, 2 * HD), BF)),
        smem=0,
    )(*qkv, con_line, txt_line)
    lines = [line] + [send(line, swap_v(s)) for s in (1, 3, 2)]
    plane = call(plane_kernel, sds((64 * n_img, HD)), smem=0)(*image_kvs)
    con_slot, over, plane = lax.optimization_barrier((spots[0, :n_con], spots[1, 0], plane))
    other_plane = send(plane, swap_plane())
    pick = (con_slot[:, None] == jnp.arange(4 * LINE_CON)[None, :]).astype(BF)

    image_stats = (sds((8 * n_img, 1), F32), sds((8 * n_img, 2 * HD), F32))
    stats = (sds((n_con, 1), F32), sds((n_con, 2 * HD), F32)) + image_stats
    image_near = call(image_near_kernel, image_stats, smem=0)(plane, image_q)
    q_part, *image_near = call(
        order_kernel,
        (sds((n_con, HD)),) + image_stats,
        scratch=(
            pltpu.VMEM((2 * LINE_CON, HD), BF),
            pltpu.VMEM((2 * LINE_TXT, HD), BF),
            pltpu.VMEM((2 * LINE_TXT, 2 * HD), BF),
        ),
        smem=0,
    )(pick, lines[0], lines[1], txt_bias, image_q, *image_near)
    con_q, *near = call(
        near_kernel,
        (sds((n_con, HD)),) + stats,
        scratch=(
            pltpu.VMEM((2 * LINE_CON, HD), BF),
            pltpu.VMEM((4 * LINE_CON, HD), BF),
            pltpu.VMEM((4 * LINE_CON, 2 * HD), BF),
            pltpu.VMEM((2 * LINE_TXT, HD), BF),
            pltpu.VMEM((2 * LINE_TXT, 2 * HD), BF),
            pltpu.VMEM((32 * n_img, 2 * HD), BF),
        ),
        limit=32,
        us=NEAR_US,
        smem=0,
    )(pick, q_part, *lines, con_bias, txt_bias, plane, image_q, *image_near)
    blocks = call(
        far_kernel,
        tuple(sds((72, n_con + HD)) for _ in range(4)),
        scratch=(pltpu.VMEM((n_con, HD), BF), pltpu.VMEM((32 * n_img, 2 * HD), BF)),
        limit=24,
        us=FAR_US,
        smem=0,
    )(other_plane, con_q, image_q, *near)
    blocks = [blocks[0]] + [send(blocks[s], swap_u(s)) for s in (1, 3, 2)]
    own, core = call(head_sum_kernel, tuple(sds((40, n_con + 4 * HD)) for _ in range(2)))(
        at, *blocks
    )
    core = send(core, swap_core())
    sums = call(core_sum_kernel, sds((40, n_con + HD)), smem=0)(own, core)
    last = (at, sums, send(sums, swap_z(2)), own, core)
    finish = call(finish_kernel, (sds((n_img, 2 * half)), sds((n_img, n_con), F32)))

    def finished():
        img_out, saliency = finish(*last)
        return img_out, jnp.transpose(saliency)

    return over <= 0, finished


def on_device(*args):
    fits, finish = packed(*args)
    return lax.cond(fits, finish, lambda: tuple(general(*args)))


def solution(mesh):
    return jax.shard_map(
        on_device,
        mesh=mesh,
        in_specs=(
            P("ctx", "head"),
            P("ctx", "head"),
            P("ctx", "head"),
            P(),
            P(),
            P(),
            P(("ctx", "head"), None),
            P(),
            P(None, None, "head"),
            P(),
        ),
        out_specs=(P("ctx", "head"), P(None, "ctx")),
        check_vma=False,
    )
```

```python
import math

import jax
import jax.numpy as jnp
from jax import lax
from jax.experimental import pallas as pl
from jax.experimental.pallas import tpu as pltpu
from jax.sharding import PartitionSpec as P

BF = jnp.bfloat16
F32 = jnp.float32
HD = 128
SLOTS = 32
CON = 96
TXT = 64
ROWS = CON + TXT
LINE_CON = 320
LINE_TXT = 176
LINE = LINE_CON + LINE_TXT
MIB = 1 << 20
PROJ_US, NEAR_US, FAR_US = 5.0, 2.0, 3.0
FACTOR = HD ** (-0.5) * math.log2(math.e)


def modulate(rows, shift_scale):
    values = rows.astype(F32)
    mean = jnp.mean(values, axis=1, keepdims=True)
    centered = values - mean
    var = jnp.mean(centered * centered, axis=1, keepdims=True)
    normed = centered * lax.rsqrt(var + 1e-06)
    return (normed * (1.0 + shift_scale[1]) + shift_scale[0]).astype(BF)


def head_norm(values, gain, head_dim):
    shaped = values.reshape(values.shape[0], -1, head_dim)
    meansq = jnp.mean(shaped * shaped, axis=2, keepdims=True)
    return (shaped * lax.rsqrt(meansq + 1e-06) * gain).reshape(values.shape[0], -1)


def block_stats(queries, keys, values):
    scores = jnp.einsum("rgd,kgd->grk", queries, keys, preferred_element_type=F32)
    scores = scores * queries.shape[-1] ** (-0.5)
    peak = jnp.max(scores, axis=2)
    weights = jnp.exp(scores - peak[:, :, None])
    total = jnp.sum(weights, axis=2)
    summed = jnp.einsum("grk,kgd->grd", weights.astype(BF), values, preferred_element_type=F32)
    return (peak, total, summed)


def combine_stats(first, second):
    peak = jnp.maximum(first[0], second[0])
    left = jnp.exp(first[0] - peak)
    right = jnp.exp(second[0] - peak)
    total = first[1] * left + second[1] * right
    summed = first[2] * left[:, :, None] + second[2] * right[:, :, None]
    return (peak, total, summed)


def scaled_scores(dots, concept_sq, image_sq, width):
    concept_rms = jnp.sqrt(concept_sq / width + 1e-06)
    image_rms = jnp.sqrt(image_sq / width + 1e-06)
    return dots / (jnp.sqrt(F32(width)) * concept_rms[:, None] * image_rms[None, :])


def gather_ctx(block):
    n_ctx = lax.axis_size("ctx")
    spread = jnp.broadcast_to(block[None], (n_ctx,) + block.shape)
    return lax.all_to_all(spread, "ctx", 0, 0, tiled=True)


def general(
    img_q, img_k, img_v, txt_ids, concept_ids, step_index, token_table, modulation, txt_qkv, qk_gain
):
    n_ctx = lax.axis_size("ctx")
    n_head = lax.axis_size("head")
    head_dim = qk_gain.shape[1]
    group = img_q.shape[1] // head_dim
    text_dev = txt_ids.shape[0] // n_ctx
    concept_dev = concept_ids.shape[0] // n_ctx
    vocab_dev = token_table.shape[0]
    combined = jnp.concatenate(
        [txt_ids.reshape(n_ctx, text_dev), concept_ids.reshape(n_ctx, concept_dev)], axis=1
    ).reshape(-1)
    offset = lax.axis_index(("ctx", "head")) * vocab_dev
    wanted = combined - offset
    inside = (wanted >= 0) & (wanted < vocab_dev)
    picked = jnp.take(token_table, jnp.clip(wanted, 0, vocab_dev - 1), axis=0)
    n_all = n_ctx * n_head
    mine = jnp.where(inside[:, None], picked, jnp.zeros((), picked.dtype))
    parts = lax.all_to_all(
        mine.reshape(n_all, -1, mine.shape[1]), ("ctx", "head"), 0, 0, tiled=True
    )
    own_rows = jnp.sum(parts.astype(F32), axis=0)
    prompt_rows = lax.all_gather(own_rows.astype(BF), "head", axis=0, tiled=True)
    shift_scale = lax.dynamic_index_in_dim(modulation, step_index[0], 0, keepdims=False)
    modded = modulate(prompt_rows, shift_scale)
    text_mod = modded[:text_dev]
    concept_mod = modded[text_dev:]
    text_kv = jnp.einsum("rd,dgc->rgc", text_mod, txt_qkv[:, 1:], preferred_element_type=F32)
    concept_qkv = jnp.einsum("rd,dgc->rgc", concept_mod, txt_qkv, preferred_element_type=F32)
    text_keys = head_norm(text_kv[:, 0], qk_gain[1], head_dim).astype(BF)
    text_values = text_kv[:, 1].astype(BF)
    concept_queries = head_norm(concept_qkv[:, 0], qk_gain[0], head_dim).astype(BF)
    concept_keys = head_norm(concept_qkv[:, 1], qk_gain[1], head_dim).astype(BF)
    concept_values = concept_qkv[:, 2].astype(BF)
    local_kv = jnp.stack(
        [
            jnp.concatenate([text_keys, concept_keys], axis=0),
            jnp.concatenate([text_values, concept_values], axis=0),
        ]
    )
    prompt_kv = gather_ctx(local_kv)
    text_part = jnp.swapaxes(prompt_kv[:, :, :text_dev], 0, 1).reshape(2, -1, group, head_dim)
    concept_part = jnp.swapaxes(prompt_kv[:, :, text_dev:], 0, 1).reshape(2, -1, group, head_dim)
    image_queries = img_q.reshape(-1, group, head_dim)
    concept_q3 = concept_queries.reshape(-1, group, head_dim)
    first = block_stats(image_queries, text_part[0], text_part[1])
    second = block_stats(concept_q3, concept_part[0], concept_part[1])
    start_stats = (
        jnp.concatenate([first[0], second[0]], axis=1),
        jnp.concatenate([first[1], second[1]], axis=1),
        jnp.concatenate([first[2], second[2]], axis=1),
    )
    all_queries = jnp.concatenate([image_queries, concept_q3], axis=0)
    image_kv = gather_ctx(jnp.stack([img_k, img_v]))
    keys = image_kv[:, 0].reshape(-1, group, head_dim)
    values = image_kv[:, 1].reshape(-1, group, head_dim)
    peak, total, summed = combine_stats(start_stats, block_stats(all_queries, keys, values))
    attended = (
        jnp.transpose(summed / total[:, :, None], (1, 0, 2))
        .reshape(all_queries.shape[0], -1)
        .astype(BF)
    )
    img_rows = img_q.shape[0]
    img_out = attended[:img_rows]
    concept_out = attended[img_rows:]
    concept_all = gather_ctx(concept_out).reshape(-1, concept_out.shape[1])
    dots = lax.dot_general(
        concept_all, img_out, (((1,), (1,)), ((), ())), preferred_element_type=F32
    )
    image_f = img_out.astype(F32)
    concept_f = concept_all.astype(F32)
    image_sq = jnp.sum(image_f * image_f, axis=1)
    concept_sq = jnp.sum(concept_f * concept_f, axis=1)
    width = group * head_dim * n_head
    sums = jnp.concatenate(
        [
            jnp.concatenate([dots, concept_sq[:, None]], axis=1),
            jnp.concatenate([image_sq, jnp.zeros((1,), F32)])[None],
        ]
    ).astype(BF)
    other = lax.ppermute(sums, "head", [(0, 1), (1, 0)])
    sums = sums.astype(F32) + other.astype(F32)
    concepts = dots.shape[0]
    saliency = scaled_scores(
        sums[:concepts, :img_rows], sums[:concepts, img_rows], sums[concepts, :img_rows], width
    )
    return (img_out, saliency)


def place(x, zl, y, c, g):
    return ((((x * 2 + zl) * 4 + y) * 2 + c) * 2) + g


def pairs(move):
    found = []
    for x in range(4):
        for zl in range(2):
            for y in range(4):
                for c in range(2):
                    for g in range(2):
                        found.append((place(x, zl, y, c, g), place(*move(x, zl, y, c, g))))
    return found


def swap_z(s):
    def move(x, zl, y, c, g):
        z = (2 * g + zl) ^ s
        return x, z & 1, y, c, z >> 1

    return pairs(move)


def swap_u(s):
    return pairs(
        lambda x, zl, y, c, g: (x, zl, y ^ s, c, g) if c else (x ^ s, zl, y, c, g)
    )


def swap_v(s):
    return pairs(
        lambda x, zl, y, c, g: (x ^ s, zl, y, c, g) if c else (x, zl, y ^ s, c, g)
    )


def swap_plane():
    return pairs(lambda x, zl, y, c, g: (x, zl ^ 1, y, c, g))


def swap_core():
    return pairs(lambda x, zl, y, c, g: (x, zl, y, c ^ 1, g))


def send(array, pairing):
    return lax.ppermute(array, ("ctx", "head"), pairing)


def nt(a, b, **kw):
    return lax.dot_general(a, b, (((1,), (1,)), ((), ())), preferred_element_type=F32, **kw)


def nn(a, b):
    return lax.dot_general(a, b, (((1,), (0,)), ((), ())), preferred_element_type=F32)


def call(kernel, outs, scratch=(), limit=16, us=1.0, smem=1, in_hbm=0):
    def run(*args):
        vm = pl.BlockSpec(memory_space=pltpu.VMEM)
        sm = pl.BlockSpec(memory_space=pltpu.SMEM)
        return pl.pallas_call(
            kernel,
            out_shape=outs,
            in_specs=[sm] * smem
            + [vm] * (len(args) - smem - in_hbm)
            + [pl.BlockSpec(memory_space=pl.ANY)] * in_hbm,
            out_specs=jax.tree.map(lambda _: vm, outs),
            scratch_shapes=list(scratch),
            compiler_params=pltpu.CompilerParams(vmem_limit_bytes=limit * MIB),
            cost_estimate=pl.CostEstimate(
                flops=int(us * 1.1e9), bytes_accessed=0, transcendentals=0
            ),
        )(*args)

    return run


def sds(shape, dtype=BF):
    return jax.ShapeDtypeStruct(shape, dtype)


def column_of(owner):
    ctx = owner >> 1
    return ((ctx >> 4) << 2) | ((ctx >> 1) & 3)


def ranks(columns, pieces, reset):
    n = columns.shape[1]
    blk = 256
    row = lax.broadcasted_iota(jnp.int32, (blk, blk), 0)
    col = lax.broadcasted_iota(jnp.int32, (blk, blk), 1)
    earlier = (row < col).astype(F32).astype(BF)
    label = lax.broadcasted_iota(jnp.int32, (16, blk), 0)
    label_piece = lax.broadcasted_iota(jnp.int32, (8, blk), 0)
    carry, carry_piece = jnp.zeros((16, 1), F32), jnp.zeros((8, 1), F32)
    spots, found, counts = [], [], []
    for b in range(n // blk):
        if b == reset:
            counts.append(carry)
            carry = jnp.zeros((16, 1), F32)
        lanes = slice(b * blk, (b + 1) * blk)
        hot = (label == columns[:, lanes]).astype(F32)
        hot_piece = (label_piece == pieces[:, lanes]).astype(F32)
        before = nn(jnp.concatenate([hot, hot_piece], axis=0).astype(BF), earlier)
        spots.append(jnp.sum(hot * (before[0:16] + carry), axis=0, keepdims=True))
        found.append(jnp.sum(hot_piece * (before[16:24] + carry_piece), axis=0, keepdims=True))
        carry = carry + jnp.sum(hot, axis=1, keepdims=True)
        carry_piece = carry_piece + jnp.sum(hot_piece, axis=1, keepdims=True)
    counts.append(carry)
    spots, found = (jnp.concatenate(r, axis=1).astype(jnp.int32) for r in (spots, found))
    return spots, found, counts


def plan_kernel(
    at, con_ref, txt_ref, table_ref, q_ref, k_ref, v_ref, rows_ref, both_ref, img_ref
):
    ids = jnp.concatenate([con_ref[...], txt_ref[...]], axis=1)
    n = ids.shape[1]
    blk = 256
    blocks = n // blk
    vocab_dev = table_ref.shape[0]
    mine = ((ids >> int(math.log2(vocab_dev))) == at[0]).astype(F32)
    pieces = [slice(b * blk, (b + 1) * blk) for b in range(blocks)]
    folded = jnp.concatenate(
        [mine[:, p] for p in pieces] + [jnp.zeros((8 - blocks, blk), F32)], axis=0
    )
    row = lax.broadcasted_iota(jnp.int32, (blk, blk), 0)
    col = lax.broadcasted_iota(jnp.int32, (blk, blk), 1)
    before = nn(folded.astype(BF), (row < col).astype(F32).astype(BF))
    label = lax.broadcasted_iota(jnp.int32, (SLOTS, blk), 0).astype(F32)
    found = jnp.zeros((SLOTS, blk), F32)
    skipped = jnp.zeros((1, 1), F32)
    for b, p in enumerate(pieces):
        rank = before[b : b + 1, :] + skipped
        row_in_table = ((ids[:, p] & (vocab_dev - 1)) + 1).astype(F32) * mine[:, p]
        found = found + jnp.where(label == rank, row_in_table, 0.0)
        skipped = skipped + jnp.sum(mine[:, p], axis=1, keepdims=True)
    found = jnp.sum(found, axis=1, keepdims=True).astype(jnp.int32) - 1
    pick = lax.broadcasted_iota(jnp.int32, (SLOTS, vocab_dev), 1) == found
    rows = nn(pick.astype(F32).astype(BF), table_ref[...]).astype(BF)
    rows_ref[...] = rows
    both_ref[0:SLOTS, :] = rows
    m = q_ref.shape[0]
    half = q_ref.shape[1] // 2
    lanes_own = pl.ds(pl.multiple_of(at[2] * half, half), half)
    lanes_other = pl.ds(pl.multiple_of((1 - at[2]) * half, half), half)
    for i, ref in enumerate((q_ref, k_ref, v_ref)):
        img_ref[i * m : (i + 1) * m, :] = ref[:, lanes_own]
        for j in range(2):
            lanes = slice((2 * i + j) * half, (2 * i + j + 1) * half)
            both_ref[SLOTS:, lanes] = ref[16 * j : 16 * (j + 1), lanes_other]
    both_ref[SLOTS:, 6 * half :] = jnp.zeros((16, 2 * half), BF)


def to_row(column):
    n = column.shape[0]
    diagonal = lax.broadcasted_iota(jnp.int32, (n, n), 0) == lax.broadcasted_iota(
        jnp.int32, (n, n), 1
    )
    return jnp.sum(jnp.where(diagonal, column, 0.0), axis=0, keepdims=True)


def line_of(at, column):
    first, second = column >> 2, column & 3
    return jnp.where(at[2] == 0, first, second), jnp.where(at[2] == 0, second, first)


def line_plan(at, counts):
    u, v = line_of(at, lax.broadcasted_iota(jnp.int32, (16, 16), 0))
    u2, v2 = line_of(at, lax.broadcasted_iota(jnp.int32, (16, 16), 1))
    row = to_row(counts)
    same = v == v2
    before = same & ((u2 ^ at[4]) < (u ^ at[4]))
    skipped = jnp.sum(jnp.where(before, row, 0.0), axis=1, keepdims=True)
    total = jnp.sum(jnp.where(same, row, 0.0), axis=1, keepdims=True)
    other = jnp.sum(jnp.where(u == u2, row, 0.0), axis=1, keepdims=True)
    return skipped, total, jnp.max(jnp.maximum(total, other), axis=0, keepdims=True)


def per_lane(values, column):
    hot = lax.broadcasted_iota(jnp.int32, (16, column.shape[1]), 0) == column
    return jnp.sum(jnp.where(hot, values, 0.0), axis=0, keepdims=True)


def blocks_of(lanes, size, blocks):
    lane = lax.broadcasted_iota(jnp.int32, (1, lanes), 1)
    block = jnp.zeros((1, lanes), jnp.int32)
    for j in range(1, blocks):
        block = block + (lane >= j * size).astype(jnp.int32)
    return block, (lane - block * size).astype(F32)


def column_at(at, u, v):
    return jnp.where(at[2] == 0, u * 4 + v, v * 4 + u)


def line_targets(at, counts, skipped, slots):
    block, slot = blocks_of(4 * slots, slots, 4)
    column = column_at(at, block ^ at[4], jnp.zeros_like(block) + at[5])
    target = per_lane(skipped, column) + slot
    return jnp.where(slot < per_lane(counts, column), target, -1.0).astype(jnp.int32)


def line_bias(at, total, rows):
    block, slot = blocks_of(4 * rows, rows, 4)
    column = column_at(at, jnp.zeros_like(block) + at[4], block ^ at[5])
    return jnp.where(slot < per_lane(total, column), 0.0, -1e30)


def pack_kernel(
    at, con_ref, txt_ref, w_hbm, out_ref, spot_ref, con_bias, txt_bias, con_line, txt_line, w_ref, sem
):
    half = w_ref.shape[2]
    lanes = pl.ds(pl.multiple_of(at[2] * half, half), half)
    weights = pltpu.make_async_copy(w_hbm.at[:, :, lanes], w_ref, sem)
    weights.start()
    ids = jnp.concatenate([con_ref[...], txt_ref[...]], axis=1)
    n = ids.shape[1]
    n_con = con_ref.shape[1]
    owner = ids >> 8
    column = column_of(owner)
    here = column == at[1]
    z = ((owner & 1) << 1) | ((owner >> 4) & 1)
    core = (owner >> 1) & 1
    piece = jnp.where(here, jnp.where(core == at[2], 0, 4) + (at[3] ^ z), -1)
    spot, rank, (con_counts, txt_counts) = ranks(column, piece, n_con // 256)
    con_skip, con_total, con_most = line_plan(at, con_counts)
    txt_skip, txt_total, txt_most = line_plan(at, txt_counts)
    con_bias[...] = line_bias(at, con_total, LINE_CON)
    txt_bias[...] = line_bias(at, txt_total, LINE_TXT)
    con_line[...] = line_targets(at, con_counts, con_skip, CON)
    txt_line[...] = line_targets(at, txt_counts, txt_skip, TXT)
    _, item_v = line_of(at, column)
    spot_ref[0:1, :] = (
        (item_v ^ at[5]) * LINE_CON + per_lane(con_skip, column).astype(jnp.int32) + spot
    )
    wanted = (lax.broadcasted_iota(jnp.int32, (128, n), 0) == owner).astype(F32)
    over = jnp.maximum(
        jnp.maximum(
            jnp.max(con_counts, axis=0, keepdims=True) - CON,
            jnp.max(txt_counts, axis=0, keepdims=True) - TXT,
        ),
        jnp.maximum(con_most - LINE_CON, txt_most - LINE_TXT),
    )
    most = jnp.max(jnp.sum(wanted, axis=1, keepdims=True), axis=0, keepdims=True)
    over = jnp.maximum(over, most - SLOTS)
    spot_ref[1:2, :] = jnp.broadcast_to(over.astype(jnp.int32), (1, n))
    spot_ref[2:8, :] = jnp.zeros((6, n), jnp.int32)
    concept = lax.broadcasted_iota(jnp.int32, (1, n), 1) < n_con
    target = jnp.where(
        concept, jnp.where(spot < CON, spot, -1), jnp.where(spot < TXT, spot + CON, -1)
    )
    source = jnp.where(here & (rank < SLOTS), piece * SLOTS + rank, -1)
    label = lax.broadcasted_iota(jnp.int32, (8 * SLOTS, n), 0)
    found = jnp.sum(
        jnp.where(label == source, (target + 1).astype(F32), 0.0), axis=1, keepdims=True
    )
    hot = lax.broadcasted_iota(jnp.int32, (8 * SLOTS, 256), 1) == found.astype(jnp.int32) - 1
    out_ref[...] = jnp.transpose(hot.astype(F32))[0:ROWS].astype(BF)
    weights.wait()


def project_kernel(at, pack_ref, *refs):
    rows, (mod_ref, gain_ref, w_ref), outs, (raw_ref, x_ref) = (
        refs[:8], refs[8:11], refs[11:15], refs[15:]
    )
    for i, ref in enumerate(rows):
        raw_ref[i * SLOTS : (i + 1) * SLOTS, :] = ref[0:SLOTS, :]
    shift = mod_ref[0:1, :]
    scale = 1.0 + mod_ref[1:2, :]
    for i in range(ROWS // 32):
        block = slice(i * 32, (i + 1) * 32)
        values = nn(pack_ref[block, :], raw_ref[...])
        mean = jnp.mean(values, axis=1, keepdims=True)
        centered = values - mean
        var = jnp.mean(centered * centered, axis=1, keepdims=True)
        x_ref[block, :] = (centered * lax.rsqrt(var + 1e-06) * scale + shift).astype(BF)

    def normed(u, gain):
        meansq = jnp.mean(u * u, axis=1, keepdims=True)
        return u * lax.rsqrt(meansq + 1e-06) * gain

    q = nn(x_ref[0:CON, :], w_ref[0])
    k = nn(x_ref[...], w_ref[1])
    v = nn(x_ref[...], w_ref[2])
    heads = []
    for h in range(3):
        cols = slice(h * HD, (h + 1) * HD)
        heads.append(
            (
                (normed(q[:, cols], gain_ref[0:1, :]) * FACTOR).astype(BF),
                normed(k[:, cols], gain_ref[1:2, :]).astype(BF),
                v[:, cols].astype(BF),
            )
        )
    for s, out in enumerate(outs):
        head = jnp.minimum(at[4] ^ s, 2)
        for h in range(3):

            @pl.when(head == h)
            def _(h=h, out=out):
                out[0:ROWS, 0:HD] = heads[h][1]
                out[0:ROWS, HD:] = heads[h][2]
                out[ROWS:, 0:HD] = heads[h][0][: CON // 2]
                out[ROWS:, HD:] = heads[h][0][CON // 2 :]


def join_kernel(a, b, c, d, con_line, txt_line, out, con, txt):
    for i, ref in zip((0, 1, 3, 2), (a, b, c, d)):
        con[i * CON : (i + 1) * CON, 0 : 2 * HD] = ref[0:CON, :]
        con[i * CON : i * CON + CON // 2, 2 * HD :] = ref[ROWS:, 0:HD]
        con[i * CON + CON // 2 : (i + 1) * CON, 2 * HD :] = ref[ROWS:, HD:]
        txt[i * TXT : (i + 1) * TXT, :] = ref[CON:ROWS, :]
    hot = lax.broadcasted_iota(jnp.int32, (LINE_CON, 4 * CON), 0) == con_line[...]
    found = nn(hot.astype(F32).astype(BF), con[...]).astype(BF)
    out[0:LINE_CON, :] = found[:, 0 : 2 * HD]
    out[LINE:, 0:HD] = found[: LINE_CON // 2, 2 * HD :]
    out[LINE:, HD:] = found[LINE_CON // 2 :, 2 * HD :]
    hot = lax.broadcasted_iota(jnp.int32, (LINE_TXT, 4 * TXT), 0) == txt_line[...]
    out[LINE_CON:LINE, :] = nn(hot.astype(F32).astype(BF), txt[...]).astype(BF)


def image_heads_kernel(at, own, core, *outs):
    n, half = own.shape[0] // 3, own.shape[1]
    for s, out in enumerate(outs):
        head = jnp.minimum(at[4] ^ s, 2)
        lanes = pl.ds(pl.multiple_of(head * HD, HD), HD)
        for i in range(3):
            row = 2 * i * n
            out[row : row + n, :] = own[i * n : (i + 1) * n, lanes]
            for j in range(2):
                there = pl.ds(pl.multiple_of((2 * i + j) * half + head * HD, HD), HD)
                out[row + n + 16 * j : row + n + 16 * (j + 1), :] = core[SLOTS:, there]


def image_join_kernel(a, b, c, d, q_out, kv_out):
    n = a.shape[0] // 3
    for i, ref in enumerate((a, b, c, d)):
        q_out[n * i : n * (i + 1), :] = ref[0:n, :]
        kv_out[n * i : n * (i + 1), :] = ref[n : 2 * n, :]
        kv_out[n * (4 + i) : n * (5 + i), :] = ref[2 * n :, :]


def plane_kernel(a, b, c, d, out):
    n = a.shape[0] // 2
    for i, ref in enumerate((a, b, c, d)):
        out[n * i : n * (i + 1), :] = ref[0:n, :]
        out[n * (4 + i) : n * (5 + i), :] = ref[n:, :]


def weigh(q, parts, factor):
    scores = []
    for keys, _, bias in parts:
        part = nt(q, keys)
        scores.append(part if bias is None else part + bias)
    peak = scores[0].max(axis=1, keepdims=True)
    for part in scores[1:]:
        peak = jnp.maximum(peak, part.max(axis=1, keepdims=True))
    total = None
    for part, (_, values, _) in zip(scores, parts):
        power = part - peak
        weights = jnp.exp2(power if factor is None else power * factor).astype(BF)
        summed = nn(weights, values)
        total = summed if total is None else total + summed
    return (peak if factor is None else peak * factor), total


def join(first, second):
    peak = jnp.maximum(first[0], second[0])
    return peak, first[1] * jnp.exp2(first[0] - peak) + second[1] * jnp.exp2(second[0] - peak)


def merge(first, second):
    _, summed = join(first, second)
    return (summed[:, 0:HD] / summed[:, HD:]).astype(BF)


def with_ones(values):
    return jnp.concatenate([values, jnp.ones_like(values)], axis=1)


def image_near_kernel(plane, q, peak, summed):
    n = plane.shape[0] // 2
    part = (plane[0:n, :], with_ones(plane[n:, :]), None)
    peak[...], summed[...] = weigh(q[...], (part,), FACTOR)


def line_queries(con_q, refs):
    n = LINE_CON
    for a, ref in enumerate(refs):
        con_q[a * n : a * n + n // 2, :] = ref[LINE:, 0:HD]
        con_q[a * n + n // 2 : (a + 1) * n, :] = ref[LINE:, HD:]


def line_texts(txt_k, txt_v, refs):
    m = LINE_TXT
    for a, ref in enumerate(refs):
        txt_k[a * m : (a + 1) * m, :] = ref[LINE_CON:LINE, 0:HD]
        txt_v[a * m : (a + 1) * m, :] = with_ones(ref[LINE_CON:LINE, HD:])


def order_kernel(pick, l0, l1, txt_bias, img_q, im, ims, *refs):
    (q_out, im_out, ims_out), (con_q, txt_k, txt_v) = refs[:3], refs[3:]
    line_queries(con_q, (l0, l1))
    q_out[...] = nn(pick[:, : 2 * LINE_CON], con_q[...]).astype(BF)
    line_texts(txt_k, txt_v, (l0, l1))
    part = (txt_k[...], txt_v[...], txt_bias[:, 0 : 2 * LINE_TXT])
    im_out[...], ims_out[...] = join(weigh(img_q[...], (part,), FACTOR), (im[...], ims[...]))


def weigh_blocks(q, parts, store):
    blk = 256
    blocks = [slice(b, b + blk) for b in range(0, q.shape[0], blk)]

    def scores(rows):
        found = []
        for keys, _, bias in parts:
            part = nt(q[rows, :], keys[...])
            found.append(part if bias is None else part + bias[...])
        return found

    ready = scores(blocks[0])
    for b, rows in enumerate(blocks):
        now, ready = ready, scores(blocks[b + 1]) if b + 1 < len(blocks) else None
        peak = now[0].max(axis=1, keepdims=True)
        for part in now[1:]:
            peak = jnp.maximum(peak, part.max(axis=1, keepdims=True))
        summed = sum(
            nn(jnp.exp2(part - peak).astype(BF), values[...])
            for part, (_, values, _) in zip(now, parts)
        )
        store(rows, peak, summed)


def near_kernel(
    pick, q_part, l0, l1, l3, l2, con_bias, txt_bias, plane, img_q, im, ims, *refs
):
    q_out, cm_out, cs_out, im_out, ims_out = refs[:5]
    con_q, con_k, con_v, txt_k, txt_v, img_v = refs[5:]
    n = LINE_CON
    line_queries(con_q, (l2, l3))
    for a, ref in enumerate((l0, l1, l2, l3)):
        con_k[a * n : (a + 1) * n, :] = ref[0:n, 0:HD]
        con_v[a * n : (a + 1) * n, :] = with_ones(ref[0:n, HD:])
    line_texts(txt_k, txt_v, (l2, l3))
    n_img = plane.shape[0] // 2
    img_v[...] = with_ones(plane[n_img:, :])
    rest = nn(pick[:, 2 * n :], con_q[...])
    q_out[...] = (rest + q_part[...].astype(F32)).astype(BF)

    def store(rows, peak, summed):
        cm_out[rows, :] = peak
        cs_out[rows, :] = summed

    parts = ((plane.at[0:n_img, :], img_v, None), (con_k, con_v, con_bias))
    weigh_blocks(q_out, parts, store)
    text = weigh(img_q[...], ((txt_k[...], txt_v[...], txt_bias[:, 2 * LINE_TXT :]),), FACTOR)
    im_out[...], ims_out[...] = join(text, (im[...], ims[...]))


def far_kernel(plane, con_q, img_q, cm, cs, im, ims, *refs):
    outs, (con_out, img_v) = refs[:4], refs[4:]
    n_img = plane.shape[0] // 2
    img_v[...] = with_ones(plane[n_img:, :])
    part = (plane[0:n_img, :], img_v[...], None)
    img = merge(weigh(img_q[...], (part,), FACTOR), (im[...], ims[...]))
    n_con = con_out.shape[0]

    def store(rows, peak, summed):
        con_out[rows, :] = merge((peak, summed), (cm[rows, :], cs[rows, :]))

    weigh_blocks(con_q, ((plane.at[0:n_img, :], img_v, None),), store)
    dots = nt(img, con_out[...]).astype(BF)
    con_f = con_out[...].astype(F32)
    squares = con_f * con_f
    high = squares.astype(BF)
    ones = jnp.ones((8, HD), BF)
    con_sq = (nt(ones, high) + nt(ones, (squares - high.astype(F32)).astype(BF))).astype(BF)
    for s, out in enumerate(outs):
        rows = slice(s * 64, (s + 1) * 64)
        out[0:64, 0:n_con] = dots[rows]
        out[0:64, n_con:] = img[rows]
        out[64:72, 0:n_con] = con_sq
        out[64:72, n_con:] = jnp.zeros((8, HD), BF)


def head_sum_kernel(at, b0, b1, b2, b3, own, core):
    n_con = b0.shape[1] - HD
    total = jnp.zeros((72, n_con), F32)
    outs = [jnp.zeros((64, HD), BF) for _ in range(3)]
    for s, ref in zip((0, 1, 3, 2), (b0, b1, b2, b3)):
        head = at[4] ^ s
        total = total + jnp.where(head < 3, ref[:, 0:n_con].astype(F32), 0.0)
        for h in range(3):
            outs[h] = jnp.where(head == h, ref[0:64, n_con:], outs[h])
    image_sq = jnp.zeros((64, 1), F32)
    for h in range(3):
        out_f = outs[h].astype(F32)
        image_sq = image_sq + jnp.sum(out_f * out_f, axis=1, keepdims=True)
    image_sq = jnp.broadcast_to(image_sq, (64, HD)).astype(BF)
    total = total.astype(BF)
    for ref, row in ((own, 0), (core, 32)):
        ref[0:32, 0:n_con] = total[row : row + 32]
        ref[32:40, 0:n_con] = total[64:72]
        ref[0:32, n_con : n_con + HD] = image_sq[row : row + 32]
        ref[32:40, n_con : n_con + HD] = jnp.zeros((8, HD), BF)
    for h in range(3):
        lanes = slice(n_con + (1 + h) * HD, n_con + (2 + h) * HD)
        for ref, row in ((own, 0), (core, 32)):
            ref[0:32, lanes] = outs[h][row : row + 32]
            ref[32:40, lanes] = jnp.zeros((8, HD), BF)


def core_sum_kernel(own, core, out):
    cols = out.shape[1]
    out[...] = (own[:, 0:cols].astype(F32) + core[:, 0:cols].astype(F32)).astype(BF)


def finish_kernel(at, sums, head, own, core, img_ref, sal_ref):
    n_con = sums.shape[1] - HD
    width = 12 * HD
    total = sums[...].astype(F32) + head[...].astype(F32)
    con_rms = jnp.sqrt(total[32:33, 0:n_con] / width + 1e-06)
    img_rms = jnp.sqrt(total[0:32, n_con : n_con + 1] / width + 1e-06)
    sal_ref[...] = total[0:32, 0:n_con] / (math.sqrt(width) * con_rms * img_rms)
    half = 3 * HD
    for ref, core_of in ((own, at[2]), (core, 1 - at[2])):
        lanes = pl.ds(pl.multiple_of(core_of * half, half), half)
        img_ref[:, lanes] = ref[0:32, n_con + HD :]


def packed(
    img_q, img_k, img_v, txt_ids, concept_ids, step_index, token_table, modulation, txt_qkv, qk_gain
):
    n_con, n_txt = concept_ids.shape[0], txt_ids.shape[0]
    ctx = lax.axis_index("ctx")
    g = lax.axis_index("head")
    c = ctx & 1
    y = (ctx >> 1) & 3
    zl = (ctx >> 3) & 1
    x = ctx >> 4
    u = jnp.where(c == 0, x, y)
    v = jnp.where(c == 0, y, x)
    at = jnp.stack([ctx * 2 + g, x * 4 + y, c, 2 * g + zl, u, v]).astype(jnp.int32)
    con_ids, text_ids = concept_ids[None, :], txt_ids[None, :]
    n = n_con + n_txt
    width = token_table.shape[1]
    half = txt_qkv.shape[2] // 2
    n_img = img_q.shape[0]

    own_rows, own_both, own_img = call(
        plan_kernel, (sds((SLOTS, width)), sds((SLOTS + 16, width)), sds((3 * n_img, half)))
    )(at, con_ids, text_ids, token_table, img_q, img_k, img_v)
    far_rows = send(own_rows, swap_z(2))
    column_rows = [own_rows] + [send(own_rows, swap_z(s)) for s in (1, 3)]
    core_both = send(own_both, swap_core())

    all_weights = jnp.transpose(txt_qkv, (1, 0, 2))
    pack, spots, con_bias, txt_bias, con_line, txt_line, weights = call(
        pack_kernel,
        (
            sds((ROWS, 8 * SLOTS)),
            sds((8, n), jnp.int32),
            sds((1, 4 * LINE_CON), F32),
            sds((1, 4 * LINE_TXT), F32),
            sds((1, 4 * CON), jnp.int32),
            sds((1, 4 * TXT), jnp.int32),
            sds((3, width, half)),
        ),
        scratch=(pltpu.SemaphoreType.DMA,),
        limit=24,
        us=2.0,
        in_hbm=1,
    )(at, con_ids, text_ids, all_weights)
    shift_scale = lax.dynamic_index_in_dim(modulation, step_index[0], 0, keepdims=False)

    image_blocks = call(
        image_heads_kernel, tuple(sds((6 * n_img, HD)) for _ in range(4))
    )(at, own_img, core_both)
    image_blocks = [image_blocks[0]] + [send(image_blocks[s], swap_u(s)) for s in (2, 1, 3)]
    image_blocks = [image_blocks[0], image_blocks[2], image_blocks[1], image_blocks[3]]
    column_rows[1], image_blocks[2] = lax.optimization_barrier((column_rows[1], image_blocks[2]))
    far_rows, pack, shift_scale, image_blocks[1] = lax.optimization_barrier(
        (far_rows, pack, shift_scale, image_blocks[1])
    )
    column_rows.insert(2, far_rows)
    other_rows = [core_both] + [send(r, swap_core()) for r in column_rows[1:]]

    qkv = call(
        project_kernel,
        tuple(sds((ROWS + CON // 2, 2 * HD)) for _ in range(4)),
        scratch=(
            pltpu.VMEM((8 * SLOTS, width), BF),
            pltpu.VMEM((ROWS, width), BF),
        ),
        limit=24,
        us=PROJ_US,
    )(at, pack, *column_rows, *other_rows, shift_scale, qk_gain, weights)

    *image_blocks, first = lax.optimization_barrier((*image_blocks, qkv[0]))
    image_q, image_kv = call(
        image_join_kernel, (sds((8 * n_img, HD)), sds((16 * n_img, HD))), smem=0
    )(*image_blocks)
    image_kvs = [image_kv] + [send(image_kv, swap_v(s)) for s in (1, 3, 2)]

    qkv = [first] + [send(qkv[s], swap_u(s)) for s in (1, 3, 2)]
    line = call(
        join_kernel,
        sds((LINE + LINE_CON // 2, 2 * HD)),
        scratch=(pltpu.VMEM((4 * CON, 3 * HD), BF), pltpu.VMEM((4 * TXT, 2 * HD), BF)),
        smem=0,
    )(*qkv, con_line, txt_line)
    lines = [line] + [send(line, swap_v(s)) for s in (1, 3, 2)]
    plane = call(plane_kernel, sds((64 * n_img, HD)), smem=0)(*image_kvs)
    spots, plane = lax.optimization_barrier((spots, plane))
    con_slot, over = spots[0, :n_con], spots[1, 0]
    other_plane = send(plane, swap_plane())
    pick = (con_slot[:, None] == jnp.arange(4 * LINE_CON)[None, :]).astype(BF)

    image_stats = (sds((8 * n_img, 1), F32), sds((8 * n_img, 2 * HD), F32))
    stats = (sds((n_con, 1), F32), sds((n_con, 2 * HD), F32)) + image_stats
    image_near = call(image_near_kernel, image_stats, smem=0)(plane, image_q)
    q_part, *image_near = call(
        order_kernel,
        (sds((n_con, HD)),) + image_stats,
        scratch=(
            pltpu.VMEM((2 * LINE_CON, HD), BF),
            pltpu.VMEM((2 * LINE_TXT, HD), BF),
            pltpu.VMEM((2 * LINE_TXT, 2 * HD), BF),
        ),
        smem=0,
    )(pick, lines[0], lines[1], txt_bias, image_q, *image_near)
    con_q, *near = call(
        near_kernel,
        (sds((n_con, HD)),) + stats,
        scratch=(
            pltpu.VMEM((2 * LINE_CON, HD), BF),
            pltpu.VMEM((4 * LINE_CON, HD), BF),
            pltpu.VMEM((4 * LINE_CON, 2 * HD), BF),
            pltpu.VMEM((2 * LINE_TXT, HD), BF),
            pltpu.VMEM((2 * LINE_TXT, 2 * HD), BF),
            pltpu.VMEM((32 * n_img, 2 * HD), BF),
        ),
        limit=32,
        us=NEAR_US,
        smem=0,
    )(pick, q_part, *lines, con_bias, txt_bias, plane, image_q, *image_near)
    blocks = call(
        far_kernel,
        tuple(sds((72, n_con + HD)) for _ in range(4)),
        scratch=(pltpu.VMEM((n_con, HD), BF), pltpu.VMEM((32 * n_img, 2 * HD), BF)),
        limit=24,
        us=FAR_US,
        smem=0,
    )(other_plane, con_q, image_q, *near)
    blocks = [blocks[0]] + [send(blocks[s], swap_u(s)) for s in (1, 3, 2)]
    own, core = call(head_sum_kernel, tuple(sds((40, n_con + 4 * HD)) for _ in range(2)))(
        at, *blocks
    )
    core = send(core, swap_core())
    sums = call(core_sum_kernel, sds((40, n_con + HD)), smem=0)(own, core)
    last = (at, sums, send(sums, swap_z(2)), own, core)
    finish = call(finish_kernel, (sds((n_img, 2 * half)), sds((n_img, n_con), F32)))

    def finished():
        img_out, saliency = finish(*last)
        return img_out, jnp.transpose(saliency)

    return over <= 0, finished


def on_device(*args):
    fits, finish = packed(*args)
    return lax.cond(fits, finish, lambda: tuple(general(*args)))


def solution(mesh):
    return jax.shard_map(
        on_device,
        mesh=mesh,
        in_specs=(
            P("ctx", "head"),
            P("ctx", "head"),
            P("ctx", "head"),
            P(),
            P(),
            P(),
            P(("ctx", "head"), None),
            P(),
            P(None, None, "head"),
            P(),
        ),
        out_specs=(P("ctx", "head"), P(None, "ctx")),
        check_vma=False,
    )
```
